32 devices in a mesh: seq: 32 (over z, y, x, core).
Axes of the slice: x: 2, y: 2, z: 4, core: 2. Of those that a mesh axis runs over, the one named last changes fastest.
Arguments:
- tokens_in: bfloat16 [16384, 1024], P('seq'), may hold values from -6 to 6
- w_router: bfloat16 [1024], replicated, may hold values from -0.1875 to 0.1875
- gain_attn: bfloat16 [1024], replicated, may hold values from 0.25 to 1.75
- w_query: bfloat16 [1024, 1024], replicated, may hold values from -0.1875 to 0.1875
- w_key: bfloat16 [1024, 1024], replicated, may hold values from -0.1875 to 0.1875
- w_value: bfloat16 [1024, 1024], replicated, may hold values from -0.1875 to 0.1875
- w_out: bfloat16 [1024, 1024], replicated, may hold values from -3 to 3
- gain_mlp: bfloat16 [1024], replicated, may hold values from 0.25 to 1.75
- w_up: bfloat16 [1024, 4096], replicated, may hold values from -0.1875 to 0.1875
- w_down: bfloat16 [4096, 1024], replicated, may hold values from -0.09375 to 0.09375
- out_grad: bfloat16 [16384, 1024], P('seq'), may hold values from -6 to 6
- lengths: int32 [4], replicated, may hold values from 96 to 16000, as said below
- counts: int32 [32], replicated, may hold values from 16 to 64, as said below
- chosen: int32 [2048], replicated, may hold values from 0 to 511, as said below
Outputs:
- output: bfloat16 [16384, 1024], P('seq')
- input_grad: bfloat16 [16384, 1024], P('seq')
- grad_router: float32 [1024], P('seq')
- grad_gain_attn: float32 [1024], P('seq')
- grad_query: float32 [1024, 1024], P('seq')
- grad_key: float32 [1024, 1024], P('seq')
- grad_value: float32 [1024, 1024], P('seq')
- grad_out: float32 [1024, 1024], P('seq')
- grad_gain_mlp: float32 [1024], P('seq')
- grad_up: float32 [1024, 4096], P('seq')
- grad_down: float32 [4096, 1024], P('seq')
The draws below stay inside these ranges and needn't reach their ends.
Inputs may be any that keep to these rules, and one draw needn't show every extreme that they name: The lengths sum to 16384; one sequence, at a place drawn from the seed, starts among the first device's tokens and ends among the last device's. `counts`: every block holds at most 64 routed tokens, and some block exactly 64. `chosen`: each block's 64 slots hold distinct offsets; its first counts slots are the routed tokens in rising order, the others are unused.
All inputs are finite; a program needn't handle non-finite values.
Results may differ from the reference program's by a relative error of at most 0.023.
Values may be sent and summed in bfloat16 or wider, within the bound.
No kernel may reach another device: no remote copies, remote signals or barrier semaphores. Data moves between devices by JAX's collectives and lax.ppermute only.
A program may use at most 256 MiB of HBM per device.

```python
import math
import jax
import jax.numpy as jnp
from jax import lax

D = 1024
HEADS = 16
HEAD_DIM = 64
FF = 4096
TOK_DEV = 512
SEQUENCES = 4
CAP = 64
TOKENS = 16384
N_SEQ = 32


def routed_counts(key):
    key = jax.random.fold_in(key, 11)
    spread_key, fullest_key = jax.random.split(key)
    device_rank = jnp.arange(N_SEQ, dtype=jnp.int32)
    floor_count = CAP // 4 + CAP // 2 * device_rank // max(N_SEQ - 1, 1)
    drawn = floor_count + jax.random.randint(spread_key, (N_SEQ,), 0, CAP // 4 + 1)
    fullest = N_SEQ // 2 + jax.random.randint(fullest_key, (), 0, N_SEQ - N_SEQ // 2)
    return jnp.where(device_rank == fullest, CAP, drawn).astype(jnp.int32)


def draw_counts(key, part):
    shared = routed_counts(key)
    return shared


def draw_chosen(key, part):
    shared = routed_counts(key)
    key = jax.random.fold_in(key, 23)
    picks = jax.random.randint(key, (N_SEQ, TOK_DEV), 0, 1 << 19)
    offset_ids = jnp.arange(TOK_DEV, dtype=jnp.int32)
    shuffled = jnp.argsort(picks * TOK_DEV + offset_ids[None, :], axis=1)
    ranking = jnp.argsort(shuffled, axis=1)
    taken = ranking < shared[:, None]
    listed = jnp.argsort(jnp.where(taken, 0, TOK_DEV) + offset_ids[None, :], axis=1)
    return listed[:, :CAP].reshape(-1).astype(jnp.int32)


def draw_lengths(key, part):
    key = jax.random.fold_in(key, 37)
    delta_key, sign_key, longest_key = jax.random.split(key, 3)
    base_len = TOK_DEV // 4
    reach = TOK_DEV // 16
    other_count = SEQUENCES - 1
    pair_count = max(other_count // 2, 1)
    deltas = jax.random.randint(delta_key, (pair_count,), -reach, reach + 1)
    first_sign = 2 * jax.random.randint(sign_key, (), 0, 2) - 1
    deltas = deltas.at[0].set(first_sign * reach)
    other_ids = jnp.arange(other_count, dtype=jnp.int32)
    pair_ids = jnp.minimum(other_ids // 2, pair_count - 1)
    paired = other_ids < 2 * (other_count // 2)
    signs = jnp.where(other_ids % 2 == 0, 1, -1)
    others = base_len + jnp.where(paired, signs * deltas[pair_ids], 0)
    longest = jax.random.randint(longest_key, (), 0, SEQUENCES)
    seq_ids = jnp.arange(SEQUENCES, dtype=jnp.int32)
    long_len = TOKENS - other_count * base_len
    source = jnp.clip(jnp.where(seq_ids < longest, seq_ids, seq_ids - 1), 0, max(other_count - 1, 0))
    return jnp.where(seq_ids == longest, long_len, others[source]).astype(jnp.int32)


def levels(stream_key, extent, shards, low, high):
    factor_of, own = 1.0, jax.random.fold_in(stream_key, 6)
    for position, parts in shards:
        steps = jnp.exp(jax.random.uniform(jax.random.fold_in(own, position), (parts,), jnp.float32, low / len(shards), high / len(shards)))
        factor_of = factor_of * jnp.repeat(steps, extent[position] // parts).reshape([-1 if axis == position else 1 for axis in range(len(extent))])
    return factor_of


def scatter_about(stream_key, shape, deviation, bound, shards=(), held_as=jnp.bfloat16):
    level = levels(stream_key, shape, shards, -0.22, 0.18) if shards else 1.0
    entries = jax.random.normal(stream_key, shape, jnp.float32) * deviation * level
    return jnp.minimum(jnp.maximum(entries, -bound), bound).astype(held_as)


def setup_inputs(seed: int = 0) -> dict:
    key_of = jax.random.split(jax.random.key(seed), 15)
    return {
        "tokens_in": scatter_about(key_of[0], (TOKENS, D), 1.0, 6.0, ((0, 32),)),
        "w_router": scatter_about(key_of[1], (D,), D ** -0.5, 0.1875),
        "gain_attn": jnp.clip(1.0 + 0.15 * jax.random.normal(key_of[2], (D,), jnp.float32), 0.25, 1.75).astype(jnp.bfloat16),
        "w_query": scatter_about(key_of[3], (D, D), D ** -0.5, 0.1875),
        "w_key": scatter_about(key_of[4], (D, D), D ** -0.5, 0.1875),
        "w_value": scatter_about(key_of[5], (D, D), D ** -0.5, 0.1875),
        "w_out": scatter_about(key_of[6], (D, D), (max(1, D // 256)) ** -0.5, 3.0),
        "gain_mlp": jnp.clip(1.0 + 0.15 * jax.random.normal(key_of[7], (D,), jnp.float32), 0.25, 1.75).astype(jnp.bfloat16),
        "w_up": scatter_about(key_of[8], (D, FF), D ** -0.5, 0.1875),
        "w_down": scatter_about(key_of[9], (FF, D), FF ** -0.5, 0.09375),
        "out_grad": scatter_about(key_of[10], (TOKENS, D), 1.0, 6.0, ((0, 32),)),
        "lengths": draw_lengths(jax.random.fold_in(key_of[14], 71), 0),
        "counts": draw_counts(jax.random.fold_in(key_of[14], 71), 0),
        "chosen": draw_chosen(jax.random.fold_in(key_of[14], 71), 0),
    }


highest = lax.Precision.HIGHEST
masked_score = -1e+30
eps_norm = 1e-05

@jax.custom_vjp
def low(v):
    return lax.optimization_barrier(v.astype(jnp.bfloat16)).astype(jnp.float32)

@jax.custom_vjp
def low_back(v):
    return v

def low_keep(v):
    return (low(v), None)

def low_pass(kept, grad):
    return (grad,)

def back_keep(v):
    return (v, None)

def back_low(kept, grad):
    return (low(grad),)
low.defvjp(low_keep, low_pass)
low_back.defvjp(back_keep, back_low)

def rms_scale(values, gain):
    return values * lax.rsqrt(lax.optimization_barrier(jnp.mean(values * values, axis=-1, keepdims=True)) + eps_norm) * gain

def attend(query_heads, key_heads, value_heads, places, query_segs, key_segs):
    slot_total = query_heads.shape[0]
    block_rows = math.gcd(slot_total, 512)
    factor = HEAD_DIM ** (-0.5)

    def one_block(pieces):
        block_query, block_pos, block_seg = pieces
        logits = jnp.einsum('qhd,khd->hqk', block_query, key_heads, precision=highest) * factor
        logits = low_back(logits)
        allowed = ((block_seg[:, None] == key_segs[None, :]) & (places[None, :] <= block_pos[:, None]))[None]
        logits = jnp.where(allowed, logits, masked_score)
        peak = lax.optimization_barrier(jnp.max(logits, axis=-1, keepdims=True))
        weights_block = jnp.where(allowed, jnp.exp(logits - peak), 0.0)
        row_total = lax.optimization_barrier(jnp.sum(weights_block, axis=-1, keepdims=True))
        probs = low(weights_block / jnp.where(row_total > 0, row_total, 1.0))
        return jnp.einsum('hqk,khd->qhd', probs, value_heads, precision=highest)
    mapped = lax.map(jax.checkpoint(one_block), (query_heads.reshape(slot_total // block_rows, block_rows, HEADS, HEAD_DIM), places.reshape(-1, block_rows), query_segs.reshape(-1, block_rows)))
    return mapped.reshape(slot_total, HEADS * HEAD_DIM)

def reference(tokens_in, w_router, gain_attn, w_query, w_key, w_value, w_out, gain_mlp, w_up, w_down, out_grad, lengths, counts, chosen):
    slot_ids = jnp.arange(CAP, dtype=jnp.int32)
    places = (jnp.arange(N_SEQ, dtype=jnp.int32)[:, None] * TOK_DEV + chosen.reshape(N_SEQ, CAP).astype(jnp.int32)).reshape(-1).astype(jnp.int32)
    live = (slot_ids[None, :] < counts[:, None]).reshape(-1)
    seq_ends = jnp.cumsum(lengths).astype(jnp.int32)
    segment = lax.optimization_barrier(jnp.sum((places[:, None] >= seq_ends[None, :]).astype(jnp.int32), axis=1)).astype(jnp.int32)
    key_segs = jnp.where(live, segment, -1).astype(jnp.int32)
    query_segs = jnp.where(live, segment, -2).astype(jnp.int32)
    chosen_total = jnp.sum(counts).astype(jnp.float32)

    def split_heads(matrix):
        return matrix.reshape(matrix.shape[0], HEADS, HEAD_DIM)

    def forward(tokens, router, attn_gain, query_w, key_w, value_w, out_w, mlp_gain, up_w, down_w):
        routed = tokens[places]
        gate_prob = jax.nn.sigmoid(jnp.dot(routed, router, precision=highest))
        score_total = jnp.sum(jnp.where(live, gate_prob, 0.0))
        scaling = gate_prob * (chosen_total / score_total)
        normed = low(rms_scale(routed, attn_gain))
        queries = low_back(low(jnp.dot(normed, query_w, precision=highest)))
        keys_all = low_back(low(jnp.dot(normed, key_w, precision=highest)))
        values_all = low_back(low(jnp.dot(normed, value_w, precision=highest)))
        mixed = attend(split_heads(queries), split_heads(keys_all), split_heads(values_all), places, query_segs, key_segs)
        mixed = low_back(low(mixed))
        attn_out = low_back(jnp.dot(mixed, out_w, precision=highest))
        middle = routed + attn_out
        normed_mlp = low(rms_scale(middle, mlp_gain))
        hidden = low_back(jnp.dot(normed_mlp, up_w, precision=highest))
        active = low(jax.nn.gelu(hidden, approximate=True))
        mlp_out = low_back(jnp.dot(active, down_w, precision=highest))
        branch = attn_out + mlp_out
        update_rows = jnp.where(live[:, None], scaling[:, None] * branch, 0.0)
        return tokens.at[places].add(update_rows)
    output, pullback = jax.vjp(forward, tokens_in.astype(jnp.float32), w_router.astype(jnp.float32), gain_attn.astype(jnp.float32), w_query.astype(jnp.float32), w_key.astype(jnp.float32), w_value.astype(jnp.float32), w_out.astype(jnp.float32), gain_mlp.astype(jnp.float32), w_up.astype(jnp.float32), w_down.astype(jnp.float32))
    grads = pullback(out_grad.astype(jnp.float32))
    return (output.astype(jnp.bfloat16), grads[0].astype(jnp.bfloat16), grads[1], grads[2], grads[3], grads[4], grads[5], grads[6], grads[7], grads[8], grads[9])
```

```python
import functools
import jax
import jax.numpy as jnp
from jax import lax
from jax.experimental import pallas as pl
from jax.experimental.pallas import tpu as pltpu
from jax.sharding import PartitionSpec as P

HEADS = 16
HEAD_DIM = 64
LANES = 128
BLOCK = 128

masked_score = -1e30
eps_norm = 1e-05
far_away = 1e9

f32 = jnp.float32
bf16 = jnp.bfloat16


def nt(left, right):
    return lax.dot_general(left, right, (((1,), (1,)), ((), ())), preferred_element_type=f32)


def nn(left, right):
    return lax.dot_general(left, right, (((1,), (0,)), ((), ())), preferred_element_type=f32)


def rms_scale(values, gain):
    return values * lax.rsqrt(jnp.mean(values * values, axis=-1, keepdims=True) + eps_norm) * gain


def three_parts(value):
    high = lax.reduce_precision(value, 8, 7)
    rest = value - high
    middle = lax.reduce_precision(rest, 8, 7)
    return jnp.stack([high, middle, rest - middle]).astype(bf16)


def spread_rows(packed, upper):
    lanes = lax.broadcasted_iota(jnp.int32, packed.shape, 1)
    zero = jnp.zeros_like(packed)
    rolled = jnp.concatenate([packed[:, HEAD_DIM:], packed[:, :HEAD_DIM]], axis=1)
    if upper:
        return jnp.concatenate(
            [jnp.where(lanes >= HEAD_DIM, rolled, zero), jnp.where(lanes >= HEAD_DIM, packed, zero)], axis=0
        )
    return jnp.concatenate(
        [jnp.where(lanes < HEAD_DIM, packed, zero), jnp.where(lanes < HEAD_DIM, rolled, zero)], axis=0
    )


def pack_columns(turned):
    return jnp.concatenate([turned[:, :BLOCK], turned[:, BLOCK:]], axis=0)


def key_columns(kpos_ref, member, extent):
    row = kpos_ref[member : member + 1, :extent]
    column = jnp.transpose(jnp.broadcast_to(row, (LANES, extent)))
    return jnp.concatenate([column, column], axis=1)


def attend_kernel(factor, q_ref, kv_ref, kpos_ref, qpos_ref, qlow_ref, mixed_ref, turned_ref, lse_ref):
    members, key_rows, _ = kv_ref.shape
    blocks = q_ref.shape[0] // BLOCK
    kv_turned = [jnp.transpose(kv_ref[m]) for m in range(members)]
    for b in range(blocks):
        extent = key_rows * (b + 1) // blocks
        packed = (q_ref[b * BLOCK : (b + 1) * BLOCK, :].astype(f32) * factor).astype(bf16)
        wide = spread_rows(packed, False)
        qpos = qpos_ref[b : b + 1, :]
        qlow = qlow_ref[b : b + 1, :]
        scores = []
        for m in range(members):
            score = nt(kv_ref[m, :extent, :], wide)
            kpos = key_columns(kpos_ref, m, extent)
            score = jnp.where((kpos <= qpos) & (kpos >= qlow), score, masked_score)
            scores.append(score)
        peak = jnp.max(scores[0], axis=0, keepdims=True)
        for score in scores[1:]:
            peak = jnp.maximum(peak, jnp.max(score, axis=0, keepdims=True))
        peak = jnp.maximum(peak, 0.1 * masked_score)
        total = jnp.zeros_like(peak)
        mixed = jnp.zeros((LANES, 2 * BLOCK), f32)
        for m in range(members):
            prob = jnp.exp(scores[m] - peak)
            total = total + jnp.sum(prob, axis=0, keepdims=True)
            mixed = mixed + nn(kv_turned[m][:, :extent], prob.astype(bf16))
        safe = jnp.where(total > 0, total, 1.0)
        lse_ref[b : b + 1, :] = peak + jnp.log(safe)
        turned = pack_columns(mixed[HEAD_DIM:, :] / safe)
        turned_ref[b * BLOCK : (b + 1) * BLOCK, :] = turned
        mixed_ref[b * BLOCK : (b + 1) * BLOCK, :] = jnp.transpose(turned).astype(bf16)


def attend_back_kernel(
    factor, q_ref, do_ref, kv_ref, kpos_ref, qpos_ref, qlow_ref, turned_ref, lse_ref, dq_ref, dkv_ref
):
    members, key_rows, _ = kv_ref.shape
    blocks = q_ref.shape[0] // BLOCK
    kv_turned = [jnp.transpose(kv_ref[m]) for m in range(members)]
    for b in range(blocks - 1, -1, -1):
        extent = key_rows * (b + 1) // blocks
        rows = slice(b * BLOCK, (b + 1) * BLOCK)
        packed = (q_ref[rows, :].astype(f32) * factor).astype(bf16)
        grads = do_ref[rows, :]
        wide = jnp.concatenate([spread_rows(packed, False), spread_rows(grads, True)], axis=0)
        product = jnp.transpose(grads.astype(f32)) * turned_ref[rows, :]
        delta = jnp.concatenate(
            [
                jnp.sum(product[:HEAD_DIM], axis=0, keepdims=True),
                jnp.sum(product[HEAD_DIM:], axis=0, keepdims=True),
            ],
            axis=1,
        )
        qpos = qpos_ref[b : b + 1, :]
        qlow = qlow_ref[b : b + 1, :]
        lse = lse_ref[b : b + 1, :]
        dquery = jnp.zeros((LANES, 2 * BLOCK), f32)
        for m in range(members):
            both = nt(kv_ref[m, :extent, :], wide)
            kpos = key_columns(kpos_ref, m, extent)
            prob = jnp.exp(
                jnp.where((kpos <= qpos) & (kpos >= qlow), both[:, : 2 * BLOCK] - lse, masked_score)
            )
            dlogit = (prob * (both[:, 2 * BLOCK :] - delta)).astype(bf16)
            dquery = dquery + nn(kv_turned[m][:, :extent], dlogit)
            update = nn(jnp.concatenate([dlogit, prob.astype(bf16)], axis=1), wide)
            if b == blocks - 1:
                dkv_ref[m, :extent, :] = update
            else:
                dkv_ref[m, :extent, :] += update
        dq_ref[rows, :] = jnp.transpose(pack_columns(dquery[:HEAD_DIM, :] * factor)).astype(bf16)


vmem = pl.BlockSpec(memory_space=pltpu.VMEM)
vmem_limit = 56 * 1024 * 1024


def attend(factor, queries, kv, kpos, qpos, qlow):
    rows = queries.shape[0]
    return pl.pallas_call(
        functools.partial(attend_kernel, factor),
        out_shape=(
            jax.ShapeDtypeStruct((rows, LANES), bf16),
            jax.ShapeDtypeStruct((rows, LANES), f32),
            jax.ShapeDtypeStruct(qpos.shape, f32),
        ),
        in_specs=[vmem] * 5,
        out_specs=(vmem,) * 3,
        compiler_params=pltpu.CompilerParams(vmem_limit_bytes=vmem_limit),
        name="attend",
    )(queries, kv, kpos, qpos, qlow)


def attend_back(factor, queries, dmixed, kv, kpos, qpos, qlow, turned, lse):
    rows = queries.shape[0]
    return pl.pallas_call(
        functools.partial(attend_back_kernel, factor),
        out_shape=(
            jax.ShapeDtypeStruct((rows, LANES), bf16),
            jax.ShapeDtypeStruct(kv.shape, f32),
        ),
        in_specs=[vmem] * 8,
        out_specs=(vmem,) * 2,
        compiler_params=pltpu.CompilerParams(vmem_limit_bytes=vmem_limit),
        name="attend_back",
    )(queries, dmixed, kv, kpos, qpos, qlow, turned, lse)


def per_device(
    tokens_in,
    w_router,
    gain_attn,
    w_query,
    w_key,
    w_value,
    w_out,
    gain_mlp,
    w_up,
    w_down,
    out_grad,
    lengths,
    counts,
    chosen,
):
    devices = lax.axis_size("seq")
    own = lax.axis_index("seq")
    capacity = chosen.shape[0] // devices
    tok_rows, width = tokens_in.shape
    hidden_width = w_up.shape[1]
    group = devices // HEADS
    share = capacity // group
    half = share // 2
    member = own % group
    slots = devices * capacity
    factor = HEAD_DIM ** (-0.5)
    attn_gain = gain_attn.astype(f32)
    mlp_gain = gain_mlp.astype(f32)

    def swap(value):
        return lax.all_to_all(value, "seq", split_axis=0, concat_axis=0, tiled=True)

    groups = [[h * group + m for m in range(group)] for h in range(HEADS)]

    def across_group(value):
        if group == 2:
            other = lax.ppermute(value, "seq", [(s, s ^ 1) for s in range(devices)])
            return jnp.stack([value, other])
        return lax.all_gather(value, "seq", axis_index_groups=groups)

    def sum_over_group(value):
        if group == 2:
            return value[0] + lax.ppermute(value[1], "seq", [(s, s ^ 1) for s in range(devices)])
        return lax.psum_scatter(value, "seq", scatter_dimension=0, axis_index_groups=groups)

    def member_order(value):
        if group == 2:
            return jnp.where(member == 0, value, value[::-1])
        return value

    slot_ids = jnp.arange(capacity, dtype=jnp.int32)
    places = jnp.arange(devices, dtype=jnp.int32)[:, None] * tok_rows + chosen.reshape(devices, capacity)
    live_all = slot_ids[None, :] < counts[:, None]
    seq_ends = jnp.cumsum(lengths)
    starts = jnp.max(jnp.where(places[..., None] >= seq_ends, seq_ends, 0), axis=-1)
    kpos = jnp.where(live_all, places.astype(f32), far_away)
    kpos = member_order(kpos.reshape(devices, group, share).swapaxes(0, 1).reshape(group, devices * share))
    blocks = devices * half // BLOCK

    def query_order(value):
        value = lax.dynamic_index_in_dim(value.reshape(devices, group, share), member, 1, False)
        return value.reshape(blocks, devices // blocks, 2, half).swapaxes(1, 2).reshape(blocks, 2 * BLOCK)

    qpos = query_order(jnp.where(live_all, places, -1).astype(f32))
    qlow = query_order(starts.astype(f32))

    offsets = lax.dynamic_slice_in_dim(chosen, own * capacity, capacity)
    live = slot_ids < counts[own]
    pick = (offsets[:, None] == jnp.arange(tok_rows, dtype=jnp.int32)[None, :]).astype(bf16)
    routed = nn(pick, tokens_in)
    upstream = jnp.where(live[:, None], nn(pick, out_grad), 0.0)
    gate = jax.nn.sigmoid(jnp.sum(routed * w_router.astype(f32)[None, :], axis=1))
    gate_sum = jnp.sum(jnp.where(live, gate, 0.0))
    normed = rms_scale(routed, attn_gain).astype(bf16)
    normed_all = lax.all_gather(normed, "seq", axis=0, tiled=True)
    queries = nn(normed, w_query).astype(bf16)
    keys = nn(normed, w_key).astype(bf16)
    values = nn(normed, w_value).astype(bf16)

    def note(value):
        parts = jnp.pad(three_parts(value), (0, LANES - 3))
        return jnp.broadcast_to(parts, (devices, 8, LANES))

    def read_note(rows):
        return jnp.sum(rows[:, 0, :3].astype(f32))

    def to_heads(value, per_row):
        if per_row == 2:
            value = value.reshape(group, 2, half, HEADS, HEAD_DIM).transpose(3, 0, 2, 1, 4)
            return value.reshape(devices, half, LANES)
        return value

    def pair_to_heads(first, second):
        both = jnp.stack([first, second], axis=1).reshape(group, share, 2, HEADS, HEAD_DIM)
        return both.transpose(3, 0, 1, 2, 4).reshape(devices, share, LANES)

    def from_heads(value):
        value = value.reshape(HEADS, group, half, 2, HEAD_DIM).transpose(1, 3, 2, 0, 4)
        return value.reshape(capacity, HEADS * HEAD_DIM)

    def pair_from_heads(value):
        value = value.reshape(HEADS, group, share, 2, HEAD_DIM).transpose(3, 1, 2, 0, 4)
        value = value.reshape(2, capacity, HEADS * HEAD_DIM)
        return value[0], value[1]

    sent = jnp.concatenate([to_heads(queries, 2), pair_to_heads(keys, values), note(gate_sum)], axis=1)
    got = swap(sent)
    score_total = read_note(got[:, half + share :])
    chosen_total = jnp.sum(counts).astype(f32)
    ratio = chosen_total / score_total
    scaling = gate * ratio
    head_queries = got[:, :half].reshape(devices * half, LANES)
    kv = across_group(got[:, half : half + share].reshape(devices * share, LANES))
    mixed_packed, mixed_turned, lse = attend(factor, head_queries, kv, kpos, qpos, qlow)
    mixed = from_heads(swap(mixed_packed.reshape(devices, half, LANES)))

    attn_out = nn(mixed, w_out)
    middle = routed + attn_out
    normed_mlp = rms_scale(middle, mlp_gain).astype(bf16)
    dbranch = scaling[:, None] * upstream
    dmlp = dbranch.astype(bf16)
    gathered = lax.all_gather(
        jnp.concatenate([mixed, normed_mlp, dmlp], axis=1), "seq", axis=0, tiled=True
    )
    mixed_all = gathered[:, :width]
    normed_mlp_all = gathered[:, width : 2 * width]
    dmlp_all = gathered[:, 2 * width :]
    hidden = nn(normed_mlp, w_up)
    active = jax.nn.gelu(hidden, approximate=True).astype(bf16)
    branch = attn_out + nn(active, w_down)
    dweight = jnp.sum(upstream * branch, axis=1)

    def gelu_of(values):
        return jax.nn.gelu(values, approximate=True)

    dactive = nt(dmlp, w_down)
    dhidden = jax.vjp(gelu_of, hidden)[1](dactive)[0].astype(bf16)
    dnormed_mlp = nt(dhidden, w_up)
    dmiddle = jax.vjp(lambda v: rms_scale(v, mlp_gain), middle)[1](dnormed_mlp)[0]
    dattn = (dbranch + dmiddle).astype(bf16)
    dmixed = nt(dattn, w_out).astype(bf16)
    out_cols = width // devices
    dattn_split = dattn.reshape(capacity, devices, out_cols).swapaxes(0, 1)
    dattn_split = dattn_split.reshape(devices, capacity * out_cols // LANES, LANES)
    got = swap(
        jnp.concatenate(
            [to_heads(dmixed, 2), dattn_split, note(jnp.sum(jnp.where(live, dweight * gate, 0.0)))], axis=1
        )
    )
    dattn_own = got[:, half : half + capacity * out_cols // LANES].reshape(slots, out_cols)
    coefficient = read_note(got[:, half + capacity * out_cols // LANES :])
    dq_packed, dkv_parts = attend_back(
        factor,
        head_queries,
        got[:, :half].reshape(devices * half, LANES),
        kv,
        kpos,
        qpos,
        qlow,
        mixed_turned,
        lse,
    )
    dkv = sum_over_group(dkv_parts).astype(bf16)

    dscore = dweight * ratio - coefficient * chosen_total / (score_total * score_total)
    dlogit_router = jnp.where(live, dscore * gate * (1.0 - gate), 0.0)
    router_part = jnp.sum(dlogit_router[:, None] * routed, axis=0).reshape(devices, out_cols)
    router_parts = three_parts(router_part).swapaxes(0, 1).reshape(devices, 1, 3 * out_cols)
    router_note = jnp.pad(router_parts, ((0, 0), (0, 7), (0, LANES - 3 * out_cols)))
    got = swap(
        jnp.concatenate(
            [dq_packed.reshape(devices, half, LANES), dkv.reshape(devices, share, LANES), router_note], axis=1
        )
    )
    dquery = from_heads(got[:, :half])
    dkey, dvalue = pair_from_heads(got[:, half : half + share])
    grad_router = jnp.sum(got[:, half + share, : 3 * out_cols].astype(f32), axis=0)
    grad_router = jnp.sum(grad_router.reshape(3, out_cols), axis=0)

    normed_own = lax.dynamic_index_in_dim(normed_all.reshape(devices, group, share, width), member, 1, False)
    normed_own = normed_own.reshape(devices * share, width)
    dq_rows = dq_packed.reshape(devices, half, 2, HEAD_DIM).swapaxes(1, 2).reshape(devices * share, HEAD_DIM)
    dqkv = jnp.concatenate([dq_rows, dkv], axis=1)
    grad_qkv = lax.dot_general(normed_own, dqkv, (((0,), (0,)), ((), ())), preferred_element_type=f32)
    head_cols = 3 * HEAD_DIM // group
    grad_qkv = member_order(grad_qkv.reshape(width, group, head_cols).swapaxes(0, 1))
    grad_qkv = sum_over_group(grad_qkv).astype(bf16)
    grad_out = lax.dot_general(mixed_all, dattn_own, (((0,), (0,)), ((), ())), preferred_element_type=f32)

    hidden_cols = hidden_width // devices
    up_own = lax.dynamic_slice_in_dim(w_up, own * hidden_cols, hidden_cols, 1)
    down_own = lax.dynamic_slice_in_dim(w_down, own * hidden_cols, hidden_cols, 0)
    hidden_own = nn(normed_mlp_all, up_own)
    dactive_own = nt(dmlp_all, down_own)
    active_own, gelu_back = jax.vjp(gelu_of, hidden_own)
    dhidden_own = gelu_back(dactive_own)[0].astype(bf16)
    active_own = active_own.astype(bf16)
    grad_down = lax.dot_general(active_own, dmlp_all, (((0,), (0,)), ((), ())), preferred_element_type=f32)
    grad_up = lax.dot_general(
        normed_mlp_all, dhidden_own, (((0,), (0,)), ((), ())), preferred_element_type=f32
    )
    sent = jnp.concatenate([grad_up.astype(bf16), grad_qkv, grad_out.astype(bf16)], axis=1)
    got = swap(sent.reshape(devices, out_cols, sent.shape[1])).astype(f32)
    grad_up = got[:, :, :hidden_cols].swapaxes(0, 1).reshape(out_cols, hidden_width)
    grad_qkv = got[:, :, hidden_cols : hidden_cols + head_cols].reshape(HEADS, group, out_cols, head_cols)
    grad_qkv = grad_qkv.transpose(2, 0, 1, 3).reshape(out_cols, HEADS, 3, HEAD_DIM)
    grad_query = grad_qkv[:, :, 0].reshape(out_cols, width)
    grad_key = grad_qkv[:, :, 1].reshape(out_cols, width)
    grad_value = grad_qkv[:, :, 2].reshape(out_cols, width)
    grad_out = got[:, :, hidden_cols + head_cols :].swapaxes(0, 1).reshape(out_cols, width)

    def own_rows(value):
        return lax.dynamic_slice_in_dim(value, own * out_cols, out_cols, 0).astype(f32)

    grad_gain_attn = jnp.sum(
        own_rows(w_query) * grad_query + own_rows(w_key) * grad_key + own_rows(w_value) * grad_value, axis=1
    ) / own_rows(attn_gain)
    grad_gain_mlp = jnp.sum(own_rows(w_up) * grad_up, axis=1) / own_rows(mlp_gain)

    dnormed = nt(dquery, w_query) + nt(dkey, w_key) + nt(dvalue, w_value)
    drows = jax.vjp(lambda v: rms_scale(v, attn_gain), routed)[1](dnormed)[0]
    droutes = drows + dmiddle + dlogit_router[:, None] * w_router.astype(f32)[None, :]
    new_rows = (routed + scaling[:, None] * branch).astype(bf16)
    new_grads = (upstream + droutes).astype(bf16)
    put = (jnp.arange(tok_rows, dtype=jnp.int32)[:, None] == offsets[None, :]) & live[None, :]
    hit = jnp.any(put, axis=1, keepdims=True)
    put = put.astype(bf16)
    output = jnp.where(hit, nn(put, new_rows).astype(bf16), tokens_in)
    input_grad = jnp.where(hit, nn(put, new_grads).astype(bf16), out_grad)
    return (
        output,
        input_grad,
        grad_router,
        grad_gain_attn,
        grad_query,
        grad_key,
        grad_value,
        grad_out,
        grad_gain_mlp,
        grad_up,
        grad_down,
    )


def solution(mesh):
    placed = (P("seq", None),) + (P(),) * 9 + (P("seq", None),) + (P(),) * 3
    rows = P("seq", None)
    return jax.shard_map(
        per_device,
        mesh=mesh,
        in_specs=placed,
        out_specs=(rows, rows, P("seq"), P("seq"), rows, rows, rows, rows, P("seq"), rows, rows),
        check_vma=False,
    )
```

```python
import functools
import jax
import jax.numpy as jnp
from jax import lax
from jax.experimental import pallas as pl
from jax.experimental.pallas import tpu as pltpu
from jax.sharding import PartitionSpec as P

HEADS = 16
HEAD_DIM = 64
LANES = 128
BLOCK = 128

masked_score = -1e30
eps_norm = 1e-05
far_away = 1e9

f32 = jnp.float32
bf16 = jnp.bfloat16


def nt(left, right):
    return lax.dot_general(left, right, (((1,), (1,)), ((), ())), preferred_element_type=f32)


def nn(left, right):
    return lax.dot_general(left, right, (((1,), (0,)), ((), ())), preferred_element_type=f32)


def rms_scale(values, gain):
    return values * lax.rsqrt(jnp.mean(values * values, axis=-1, keepdims=True) + eps_norm) * gain


def three_parts(value):
    high = lax.reduce_precision(value, 8, 7)
    rest = value - high
    middle = lax.reduce_precision(rest, 8, 7)
    return jnp.stack([high, middle, rest - middle]).astype(bf16)


def spread_rows(packed, upper):
    lanes = lax.broadcasted_iota(jnp.int32, packed.shape, 1)
    zero = jnp.zeros_like(packed)
    rolled = jnp.concatenate([packed[:, HEAD_DIM:], packed[:, :HEAD_DIM]], axis=1)
    if upper:
        return jnp.concatenate(
            [jnp.where(lanes >= HEAD_DIM, rolled, zero), jnp.where(lanes >= HEAD_DIM, packed, zero)], axis=0
        )
    return jnp.concatenate(
        [jnp.where(lanes < HEAD_DIM, packed, zero), jnp.where(lanes < HEAD_DIM, rolled, zero)], axis=0
    )


def pack_columns(turned):
    return jnp.concatenate([turned[:, :BLOCK], turned[:, BLOCK:]], axis=0)


def key_columns(kpos_ref, member, extent):
    row = kpos_ref[member : member + 1, :extent]
    column = jnp.transpose(jnp.broadcast_to(row, (LANES, extent)))
    return jnp.concatenate([column, column], axis=1)


def attend_core(factor, load_query, load_kv, members, blocks, key_rows, kpos_ref, qpos_ref, qlow_ref, mixed_ref, turned_ref, lse_ref):
    kv_turned = [jnp.transpose(load_kv(m, key_rows)) for m in range(members)]
    for b in range(blocks):
        extent = key_rows * (b + 1) // blocks
        packed = (load_query(b).astype(f32) * factor).astype(bf16)
        wide = spread_rows(packed, False)
        qpos = qpos_ref[b : b + 1, :]
        qlow = qlow_ref[b : b + 1, :]
        scores = []
        for m in range(members):
            score = nt(load_kv(m, extent), wide)
            kpos = key_columns(kpos_ref, m, extent)
            score = jnp.where((kpos <= qpos) & (kpos >= qlow), score, masked_score)
            scores.append(score)
        peak = jnp.max(scores[0], axis=0, keepdims=True)
        for score in scores[1:]:
            peak = jnp.maximum(peak, jnp.max(score, axis=0, keepdims=True))
        peak = jnp.maximum(peak, 0.1 * masked_score)
        total = jnp.zeros_like(peak)
        mixed = jnp.zeros((LANES, 2 * BLOCK), f32)
        for m in range(members):
            prob = jnp.exp(scores[m] - peak)
            total = total + jnp.sum(prob, axis=0, keepdims=True)
            mixed = mixed + nn(kv_turned[m][:, :extent], prob.astype(bf16))
        safe = jnp.where(total > 0, total, 1.0)
        lse_ref[b : b + 1, :] = peak + jnp.log(safe)
        turned = pack_columns(mixed[HEAD_DIM:, :] / safe)
        turned_ref[b * BLOCK : (b + 1) * BLOCK, :] = turned
        mixed_ref[b * BLOCK : (b + 1) * BLOCK, :] = jnp.transpose(turned).astype(bf16)


def attend_back_core(
    factor, load_query, load_grad, load_kv, members, blocks, key_rows, kpos_ref, qpos_ref, qlow_ref, turned_ref, lse_ref,
    dq_ref, add_dkv,
):
    kv_turned = [jnp.transpose(load_kv(m, key_rows)) for m in range(members)]
    for b in range(blocks - 1, -1, -1):
        extent = key_rows * (b + 1) // blocks
        rows = slice(b * BLOCK, (b + 1) * BLOCK)
        packed = (load_query(b).astype(f32) * factor).astype(bf16)
        grads = load_grad(b)
        wide = jnp.concatenate([spread_rows(packed, False), spread_rows(grads, True)], axis=0)
        product = jnp.transpose(grads.astype(f32)) * turned_ref[rows, :]
        delta = jnp.concatenate(
            [
                jnp.sum(product[:HEAD_DIM], axis=0, keepdims=True),
                jnp.sum(product[HEAD_DIM:], axis=0, keepdims=True),
            ],
            axis=1,
        )
        qpos = qpos_ref[b : b + 1, :]
        qlow = qlow_ref[b : b + 1, :]
        lse = lse_ref[b : b + 1, :]
        dquery = jnp.zeros((LANES, 2 * BLOCK), f32)
        for m in range(members):
            both = nt(load_kv(m, extent), wide)
            kpos = key_columns(kpos_ref, m, extent)
            prob = jnp.exp(
                jnp.where((kpos <= qpos) & (kpos >= qlow), both[:, : 2 * BLOCK] - lse, masked_score)
            )
            dlogit = (prob * (both[:, 2 * BLOCK :] - delta)).astype(bf16)
            dquery = dquery + nn(kv_turned[m][:, :extent], dlogit)
            add_dkv(m, extent, b == blocks - 1, nn(jnp.concatenate([dlogit, prob.astype(bf16)], axis=1), wide))
        dq_ref[rows, :] = jnp.transpose(pack_columns(dquery[:HEAD_DIM, :] * factor)).astype(bf16)


def attend_kernel(factor, q_ref, kv_ref, kpos_ref, qpos_ref, qlow_ref, mixed_ref, turned_ref, lse_ref):
    members, key_rows, _ = kv_ref.shape
    attend_core(
        factor,
        lambda b: q_ref[b * BLOCK : (b + 1) * BLOCK, :],
        lambda m, extent: kv_ref[m, :extent, :],
        members, q_ref.shape[0] // BLOCK, key_rows, kpos_ref, qpos_ref, qlow_ref, mixed_ref, turned_ref, lse_ref,
    )


def attend_back_kernel(
    factor, q_ref, do_ref, kv_ref, kpos_ref, qpos_ref, qlow_ref, turned_ref, lse_ref, dq_ref, dkv_ref
):
    members, key_rows, _ = kv_ref.shape

    def add_dkv(m, extent, first, update):
        if first:
            dkv_ref[m, :extent, :] = update
        else:
            dkv_ref[m, :extent, :] += update

    attend_back_core(
        factor,
        lambda b: q_ref[b * BLOCK : (b + 1) * BLOCK, :],
        lambda b: do_ref[b * BLOCK : (b + 1) * BLOCK, :],
        lambda m, extent: kv_ref[m, :extent, :],
        members, q_ref.shape[0] // BLOCK, key_rows, kpos_ref, qpos_ref, qlow_ref, turned_ref, lse_ref, dq_ref, add_dkv,
    )


vmem = pl.BlockSpec(memory_space=pltpu.VMEM)
vmem_limit = 56 * 1024 * 1024


def attend(factor, queries, kv, kpos, qpos, qlow):
    rows = queries.shape[0]
    return pl.pallas_call(
        functools.partial(attend_kernel, factor),
        out_shape=(
            jax.ShapeDtypeStruct((rows, LANES), bf16),
            jax.ShapeDtypeStruct((rows, LANES), f32),
            jax.ShapeDtypeStruct(qpos.shape, f32),
        ),
        in_specs=[vmem] * 5,
        out_specs=(vmem,) * 3,
        compiler_params=pltpu.CompilerParams(vmem_limit_bytes=vmem_limit),
        name="attend",
    )(queries, kv, kpos, qpos, qlow)


def attend_back(factor, queries, dmixed, kv, kpos, qpos, qlow, turned, lse):
    rows = queries.shape[0]
    return pl.pallas_call(
        functools.partial(attend_back_kernel, factor),
        out_shape=(
            jax.ShapeDtypeStruct((rows, LANES), bf16),
            jax.ShapeDtypeStruct(kv.shape, f32),
        ),
        in_specs=[vmem] * 8,
        out_specs=(vmem,) * 2,
        compiler_params=pltpu.CompilerParams(vmem_limit_bytes=vmem_limit),
        name="attend_back",
    )(queries, dmixed, kv, kpos, qpos, qlow, turned, lse)


def general(
    tokens_in,
    w_router,
    gain_attn,
    w_query,
    w_key,
    w_value,
    w_out,
    gain_mlp,
    w_up,
    w_down,
    out_grad,
    lengths,
    counts,
    chosen,
):
    devices = lax.axis_size("seq")
    own = lax.axis_index("seq")
    capacity = chosen.shape[0] // devices
    tok_rows, width = tokens_in.shape
    hidden_width = w_up.shape[1]
    group = devices // HEADS
    share = capacity // group
    half = share // 2
    member = own % group
    slots = devices * capacity
    factor = HEAD_DIM ** (-0.5)
    attn_gain = gain_attn.astype(f32)
    mlp_gain = gain_mlp.astype(f32)

    def swap(value):
        return lax.all_to_all(value, "seq", split_axis=0, concat_axis=0, tiled=True)

    groups = [[h * group + m for m in range(group)] for h in range(HEADS)]

    def across_group(value):
        if group == 2:
            other = lax.ppermute(value, "seq", [(s, s ^ 1) for s in range(devices)])
            return jnp.stack([value, other])
        return lax.all_gather(value, "seq", axis_index_groups=groups)

    def sum_over_group(value):
        if group == 2:
            return value[0] + lax.ppermute(value[1], "seq", [(s, s ^ 1) for s in range(devices)])
        return lax.psum_scatter(value, "seq", scatter_dimension=0, axis_index_groups=groups)

    def member_order(value):
        if group == 2:
            return jnp.where(member == 0, value, value[::-1])
        return value

    slot_ids = jnp.arange(capacity, dtype=jnp.int32)
    places = jnp.arange(devices, dtype=jnp.int32)[:, None] * tok_rows + chosen.reshape(devices, capacity)
    live_all = slot_ids[None, :] < counts[:, None]
    seq_ends = jnp.cumsum(lengths)
    starts = jnp.max(jnp.where(places[..., None] >= seq_ends, seq_ends, 0), axis=-1)
    kpos = jnp.where(live_all, places.astype(f32), far_away)
    kpos = member_order(kpos.reshape(devices, group, share).swapaxes(0, 1).reshape(group, devices * share))
    blocks = devices * half // BLOCK

    def query_order(value):
        value = lax.dynamic_index_in_dim(value.reshape(devices, group, share), member, 1, False)
        return value.reshape(blocks, devices // blocks, 2, half).swapaxes(1, 2).reshape(blocks, 2 * BLOCK)

    qpos = query_order(jnp.where(live_all, places, -1).astype(f32))
    qlow = query_order(starts.astype(f32))

    offsets = lax.dynamic_slice_in_dim(chosen, own * capacity, capacity)
    live = slot_ids < counts[own]
    pick = (offsets[:, None] == jnp.arange(tok_rows, dtype=jnp.int32)[None, :]).astype(bf16)
    routed = nn(pick, tokens_in)
    upstream = jnp.where(live[:, None], nn(pick, out_grad), 0.0)
    gate = jax.nn.sigmoid(jnp.sum(routed * w_router.astype(f32)[None, :], axis=1))
    gate_sum = jnp.sum(jnp.where(live, gate, 0.0))
    normed = rms_scale(routed, attn_gain).astype(bf16)
    normed_all = lax.all_gather(normed, "seq", axis=0, tiled=True)
    queries = nn(normed, w_query).astype(bf16)
    keys = nn(normed, w_key).astype(bf16)
    values = nn(normed, w_value).astype(bf16)

    def note(value):
        parts = jnp.pad(three_parts(value), (0, LANES - 3))
        return jnp.broadcast_to(parts, (devices, 8, LANES))

    def read_note(rows):
        return jnp.sum(rows[:, 0, :3].astype(f32))

    def to_heads(value, per_row):
        if per_row == 2:
            value = value.reshape(group, 2, half, HEADS, HEAD_DIM).transpose(3, 0, 2, 1, 4)
            return value.reshape(devices, half, LANES)
        return value

    def pair_to_heads(first, second):
        both = jnp.stack([first, second], axis=1).reshape(group, share, 2, HEADS, HEAD_DIM)
        return both.transpose(3, 0, 1, 2, 4).reshape(devices, share, LANES)

    def from_heads(value):
        value = value.reshape(HEADS, group, half, 2, HEAD_DIM).transpose(1, 3, 2, 0, 4)
        return value.reshape(capacity, HEADS * HEAD_DIM)

    def pair_from_heads(value):
        value = value.reshape(HEADS, group, share, 2, HEAD_DIM).transpose(3, 1, 2, 0, 4)
        value = value.reshape(2, capacity, HEADS * HEAD_DIM)
        return value[0], value[1]

    sent = jnp.concatenate([to_heads(queries, 2), pair_to_heads(keys, values), note(gate_sum)], axis=1)
    got = swap(sent)
    score_total = read_note(got[:, half + share :])
    chosen_total = jnp.sum(counts).astype(f32)
    ratio = chosen_total / score_total
    scaling = gate * ratio
    head_queries = got[:, :half].reshape(devices * half, LANES)
    kv = across_group(got[:, half : half + share].reshape(devices * share, LANES))
    mixed_packed, mixed_turned, lse = attend(factor, head_queries, kv, kpos, qpos, qlow)
    mixed = from_heads(swap(mixed_packed.reshape(devices, half, LANES)))

    attn_out = nn(mixed, w_out)
    middle = routed + attn_out
    normed_mlp = rms_scale(middle, mlp_gain).astype(bf16)
    dbranch = scaling[:, None] * upstream
    dmlp = dbranch.astype(bf16)
    gathered = lax.all_gather(
        jnp.concatenate([mixed, normed_mlp, dmlp], axis=1), "seq", axis=0, tiled=True
    )
    mixed_all = gathered[:, :width]
    normed_mlp_all = gathered[:, width : 2 * width]
    dmlp_all = gathered[:, 2 * width :]
    hidden = nn(normed_mlp, w_up)
    active = jax.nn.gelu(hidden, approximate=True).astype(bf16)
    branch = attn_out + nn(active, w_down)
    dweight = jnp.sum(upstream * branch, axis=1)

    def gelu_of(values):
        return jax.nn.gelu(values, approximate=True)

    dactive = nt(dmlp, w_down)
    dhidden = jax.vjp(gelu_of, hidden)[1](dactive)[0].astype(bf16)
    dnormed_mlp = nt(dhidden, w_up)
    dmiddle = jax.vjp(lambda v: rms_scale(v, mlp_gain), middle)[1](dnormed_mlp)[0]
    dattn = (dbranch + dmiddle).astype(bf16)
    dmixed = nt(dattn, w_out).astype(bf16)
    out_cols = width // devices
    dattn_split = dattn.reshape(capacity, devices, out_cols).swapaxes(0, 1)
    dattn_split = dattn_split.reshape(devices, capacity * out_cols // LANES, LANES)
    got = swap(
        jnp.concatenate(
            [to_heads(dmixed, 2), dattn_split, note(jnp.sum(jnp.where(live, dweight * gate, 0.0)))], axis=1
        )
    )
    dattn_own = got[:, half : half + capacity * out_cols // LANES].reshape(slots, out_cols)
    coefficient = read_note(got[:, half + capacity * out_cols // LANES :])
    dq_packed, dkv_parts = attend_back(
        factor,
        head_queries,
        got[:, :half].reshape(devices * half, LANES),
        kv,
        kpos,
        qpos,
        qlow,
        mixed_turned,
        lse,
    )
    dkv = sum_over_group(dkv_parts).astype(bf16)

    dscore = dweight * ratio - coefficient * chosen_total / (score_total * score_total)
    dlogit_router = jnp.where(live, dscore * gate * (1.0 - gate), 0.0)
    router_part = jnp.sum(dlogit_router[:, None] * routed, axis=0).reshape(devices, out_cols)
    router_parts = three_parts(router_part).swapaxes(0, 1).reshape(devices, 1, 3 * out_cols)
    router_note = jnp.pad(router_parts, ((0, 0), (0, 7), (0, LANES - 3 * out_cols)))
    got = swap(
        jnp.concatenate(
            [dq_packed.reshape(devices, half, LANES), dkv.reshape(devices, share, LANES), router_note], axis=1
        )
    )
    dquery = from_heads(got[:, :half])
    dkey, dvalue = pair_from_heads(got[:, half : half + share])
    grad_router = jnp.sum(got[:, half + share, : 3 * out_cols].astype(f32), axis=0)
    grad_router = jnp.sum(grad_router.reshape(3, out_cols), axis=0)

    normed_own = lax.dynamic_index_in_dim(normed_all.reshape(devices, group, share, width), member, 1, False)
    normed_own = normed_own.reshape(devices * share, width)
    dq_rows = dq_packed.reshape(devices, half, 2, HEAD_DIM).swapaxes(1, 2).reshape(devices * share, HEAD_DIM)
    dqkv = jnp.concatenate([dq_rows, dkv], axis=1)
    grad_qkv = lax.dot_general(normed_own, dqkv, (((0,), (0,)), ((), ())), preferred_element_type=f32)
    head_cols = 3 * HEAD_DIM // group
    grad_qkv = member_order(grad_qkv.reshape(width, group, head_cols).swapaxes(0, 1))
    grad_qkv = sum_over_group(grad_qkv).astype(bf16)
    grad_out = lax.dot_general(mixed_all, dattn_own, (((0,), (0,)), ((), ())), preferred_element_type=f32)

    hidden_cols = hidden_width // devices
    up_own = lax.dynamic_slice_in_dim(w_up, own * hidden_cols, hidden_cols, 1)
    down_own = lax.dynamic_slice_in_dim(w_down, own * hidden_cols, hidden_cols, 0)
    hidden_own = nn(normed_mlp_all, up_own)
    dactive_own = nt(dmlp_all, down_own)
    active_own, gelu_back = jax.vjp(gelu_of, hidden_own)
    dhidden_own = gelu_back(dactive_own)[0].astype(bf16)
    active_own = active_own.astype(bf16)
    grad_down = lax.dot_general(active_own, dmlp_all, (((0,), (0,)), ((), ())), preferred_element_type=f32)
    grad_up = lax.dot_general(
        normed_mlp_all, dhidden_own, (((0,), (0,)), ((), ())), preferred_element_type=f32
    )
    sent = jnp.concatenate([grad_up.astype(bf16), grad_qkv, grad_out.astype(bf16)], axis=1)
    got = swap(sent.reshape(devices, out_cols, sent.shape[1])).astype(f32)
    grad_up = got[:, :, :hidden_cols].swapaxes(0, 1).reshape(out_cols, hidden_width)
    grad_qkv = got[:, :, hidden_cols : hidden_cols + head_cols].reshape(HEADS, group, out_cols, head_cols)
    grad_qkv = grad_qkv.transpose(2, 0, 1, 3).reshape(out_cols, HEADS, 3, HEAD_DIM)
    grad_query = grad_qkv[:, :, 0].reshape(out_cols, width)
    grad_key = grad_qkv[:, :, 1].reshape(out_cols, width)
    grad_value = grad_qkv[:, :, 2].reshape(out_cols, width)
    grad_out = got[:, :, hidden_cols + head_cols :].swapaxes(0, 1).reshape(out_cols, width)

    def own_rows(value):
        return lax.dynamic_slice_in_dim(value, own * out_cols, out_cols, 0).astype(f32)

    grad_gain_attn = jnp.sum(
        own_rows(w_query) * grad_query + own_rows(w_key) * grad_key + own_rows(w_value) * grad_value, axis=1
    ) / own_rows(attn_gain)
    grad_gain_mlp = jnp.sum(own_rows(w_up) * grad_up, axis=1) / own_rows(mlp_gain)

    dnormed = nt(dquery, w_query) + nt(dkey, w_key) + nt(dvalue, w_value)
    drows = jax.vjp(lambda v: rms_scale(v, attn_gain), routed)[1](dnormed)[0]
    droutes = drows + dmiddle + dlogit_router[:, None] * w_router.astype(f32)[None, :]
    new_rows = (routed + scaling[:, None] * branch).astype(bf16)
    new_grads = (upstream + droutes).astype(bf16)
    put = (jnp.arange(tok_rows, dtype=jnp.int32)[:, None] == offsets[None, :]) & live[None, :]
    hit = jnp.any(put, axis=1, keepdims=True)
    put = put.astype(bf16)
    output = jnp.where(hit, nn(put, new_rows).astype(bf16), tokens_in)
    input_grad = jnp.where(hit, nn(put, new_grads).astype(bf16), out_grad)
    return (
        output,
        input_grad,
        grad_router,
        grad_gain_attn,
        grad_query,
        grad_key,
        grad_value,
        grad_out,
        grad_gain_mlp,
        grad_up,
        grad_down,
    )


SHARE = 64
HALF = 32
NOTE = 8
OUT_HALF = 16
OUT_ROWS = 32
TILES = 2
AT_OUT = TILES * OUT_ROWS
AT_QUERY = AT_OUT + OUT_HALF
AT_PAIR = AT_QUERY + OUT_HALF
AT_NOTE = AT_PAIR + OUT_ROWS
GRAD_ROWS = AT_NOTE + NOTE


def swapped(tile):
    return jnp.concatenate([tile[..., HEAD_DIM:], tile[..., :HEAD_DIM]], axis=-1)


def joined(left, right):
    return jnp.concatenate([left[..., :HEAD_DIM], right[..., HEAD_DIM:]], axis=-1)


def pack_rows(target, first, value):
    for pair in range(HEADS // 2):
        tile = value[:, pair * LANES : (pair + 1) * LANES]
        turned = swapped(tile)
        target[2 * pair, first : first + HALF, :] = joined(tile[:HALF], turned[HALF:])
        target[2 * pair + 1, first : first + HALF, :] = joined(turned[:HALF], tile[HALF:])


def pack_pairs(target, first, left, right):
    for pair in range(HEADS // 2):
        lanes = slice(pair * LANES, (pair + 1) * LANES)
        one, two = left[:, lanes], right[:, lanes]
        target[2 * pair, first : first + SHARE, :] = joined(one, swapped(two))
        target[2 * pair + 1, first : first + SHARE, :] = joined(swapped(one), two)


def unpack_rows(source, first, half):
    columns = []
    for pair in range(HEADS // 2):
        even = source[2 * pair, first : first + half, :]
        odd = source[2 * pair + 1, first : first + half, :]
        columns.append(jnp.concatenate([joined(even, swapped(odd)), joined(swapped(even), odd)], axis=0))
    return jnp.concatenate(columns, axis=1)


def unpack_pairs(source, first, rows):
    left, right = [], []
    for pair in range(HEADS // 2):
        even = source[2 * pair, first : first + rows, :]
        odd = source[2 * pair + 1, first : first + rows, :]
        left.append(joined(even, swapped(odd)))
        right.append(joined(swapped(even), odd))
    return jnp.concatenate(left, axis=1), jnp.concatenate(right, axis=1)


def in_parts(value):
    high = value.astype(bf16).astype(f32)
    rest = value - high
    middle = rest.astype(bf16).astype(f32)
    row = lax.broadcasted_iota(jnp.int32, value.shape, len(value.shape) - 2)
    parts = jnp.where(row == 0, high, jnp.where(row == 1, middle, jnp.where(row == 2, rest - middle, 0.0)))
    return parts.astype(bf16)


def write_note(target, first, value):
    rows = in_parts(jnp.broadcast_to(value, (NOTE, LANES)))
    for k in range(target.shape[0]):
        target[k, first : first + NOTE, :] = rows


def read_note(source, first):
    rows = source[:, first : first + NOTE, :].astype(f32)
    return jnp.sum(jnp.sum(rows, axis=0), axis=0, keepdims=True)[:, :1]


def one_hot(own_ref, counts_ref, chosen_ref, tok_rows, live_only):
    offsets = chosen_ref[pl.ds(own_ref[0], 1), :]
    capacity = offsets.shape[1]
    rows = lax.broadcasted_iota(jnp.int32, (tok_rows, capacity), 0)
    hot = rows == offsets
    if live_only:
        slot = lax.broadcasted_iota(jnp.int32, (tok_rows, capacity), 1)
        hot = hot & (slot < counts_ref[own_ref[0]])
    return jnp.where(hot, 1.0, 0.0)


def live_column(own_ref, counts_ref, capacity):
    return lax.broadcasted_iota(jnp.int32, (capacity, 1), 0) < counts_ref[own_ref[0]]


def gate_of(rows, vectors_ref):
    return jax.nn.sigmoid(jnp.sum(rows * vectors_ref[0:1, :], axis=1, keepdims=True))


def inverse_rms(values):
    return lax.rsqrt(jnp.mean(values * values, axis=-1, keepdims=True) + eps_norm)


def total_count(counts_ref):
    return lax.fori_loop(0, counts_ref.shape[0], lambda i, s: s + counts_ref[i], 0).astype(f32)


def gelu_pair(u):
    c = 0.7978845608028654
    square = u * u
    t = jnp.tanh(c * (u + 0.044715 * (square * u)))
    value = 0.5 * u * (1.0 + t)
    slope = 0.5 * (1.0 + t) + (0.5 * u) * ((1.0 - t * t) * (c + (3.0 * 0.044715 * c) * square))
    return value, slope


def chip_of(own_ref, k):
    return jnp.bitwise_xor(own_ref[0] // 2, (k // 4) ^ (4 * (k % 4)))


def row_of(column):
    wide = jnp.broadcast_to(column, (column.shape[0], LANES))
    filled = jnp.concatenate([wide, jnp.zeros((LANES - column.shape[0], LANES), f32)], axis=0)
    return jnp.transpose(filled)[:1, : column.shape[0]]


def fetch_kernel(own_ref, counts_ref, chosen_ref, tokens_ref, grads_ref, both_ref):
    hot = one_hot(own_ref, counts_ref, chosen_ref, tokens_ref.shape[0], False)
    capacity = hot.shape[1]
    pick = jnp.transpose(jnp.concatenate([hot, jnp.zeros_like(hot)], axis=1))[:capacity].astype(bf16)
    live = live_column(own_ref, counts_ref, capacity)
    both_ref[0, :capacity, :] = nn(pick, tokens_ref[...]).astype(bf16)
    both_ref[0, capacity:, :] = jnp.where(live, nn(pick, grads_ref[...]), 0.0).astype(bf16)


def prepare_kernel(own_ref, counts_ref, both_ref, vectors_ref, wq_ref, wk_ref, wv_ref, sent_ref, wq, wk, wv, sems):
    copies = [
        pltpu.make_async_copy(source, target, sems.at[i])
        for i, (source, target) in enumerate(((wq_ref, wq), (wk_ref, wk), (wv_ref, wv)))
    ]
    for copy in copies:
        copy.start()
    capacity = both_ref.shape[1] // 2
    rows = both_ref[0, :capacity, :].astype(f32)
    live = live_column(own_ref, counts_ref, capacity)
    gate_sum = jnp.sum(jnp.where(live, gate_of(rows, vectors_ref), 0.0), axis=0, keepdims=True)
    write_note(sent_ref, HALF + SHARE, gate_sum)
    normed = (rows * inverse_rms(rows) * vectors_ref[1:2, :]).astype(bf16)
    copies[0].wait()
    pack_rows(sent_ref, 0, nn(normed, wq[...]).astype(bf16))
    copies[1].wait()
    keys = nn(normed, wk[...]).astype(bf16)
    copies[2].wait()
    pack_pairs(sent_ref, HALF, keys, nn(normed, wv[...]).astype(bf16))


def unpack_kernel(got_ref, mixed_ref):
    mixed_ref[0] = unpack_rows(got_ref, 0, HALF)


CHUNKS = 4
PIECES = 1


def middle_kernel(
    own_ref, counts_ref, mixed_ref, total_ref, both_ref, vectors_ref, out_ref, up_ref, down_ref,
    sent_ref, new_ref, dmiddle_ref, dweight_ref, w_out, w_up, w_down, hidden_ref, active_ref, sems,
):
    width, total_cols = up_ref.shape
    cols = total_cols // CHUNKS
    copies = [pltpu.make_async_copy(out_ref, w_out, sems.at[0])]
    for c in range(CHUNKS):
        part = pl.ds(c * cols, cols)
        copies.append(pltpu.make_async_copy(up_ref.at[:, part], w_up.at[:, part], sems.at[1 + c]))
    for c in range(CHUNKS):
        part = pl.ds(c * cols, cols)
        copies.append(pltpu.make_async_copy(down_ref.at[part, :], w_down.at[part, :], sems.at[1 + CHUNKS + c]))
    for copy in copies:
        copy.start()
    capacity = mixed_ref.shape[1]
    rows = both_ref[0, :capacity, :].astype(f32)
    upstream = both_ref[0, capacity:, :].astype(f32)
    live = live_column(own_ref, counts_ref, capacity)
    gate = gate_of(rows, vectors_ref)
    ratio = total_count(counts_ref) / total_ref[:1, :1]
    scaling = gate * ratio
    gain = vectors_ref[2:3, :]
    dbranch = scaling * upstream
    dmlp = dbranch.astype(bf16)
    copies[0].wait()
    attn_out = nn(mixed_ref[0], w_out[...])
    middle = rows + attn_out
    scale = inverse_rms(middle)
    normed = (middle * scale * gain).astype(bf16)
    for c in range(CHUNKS):
        copies[1 + c].wait()
        hidden_ref[:, c * cols : (c + 1) * cols] = nn(normed, w_up[:, c * cols : (c + 1) * cols])
    dnormed = jnp.zeros((capacity, width), f32)
    for c in range(CHUNKS):
        part = slice(c * cols, (c + 1) * cols)
        copies[1 + CHUNKS + c].wait()
        hidden = hidden_ref[:, part]
        value, slope = gelu_pair(hidden)
        active_ref[:, part] = value.astype(bf16)
        dhidden = (nt(dmlp, w_down[part, :]) * slope).astype(bf16)
        dnormed = dnormed + nt(dhidden, w_up[:, part])
    branch = attn_out + nn(active_ref[...], w_down[...])
    new_ref[...] = (rows + scaling * branch).astype(bf16)
    dweight = jnp.sum(upstream * branch, axis=1, keepdims=True)
    dweight_ref[...] = jnp.broadcast_to(dweight, dweight_ref.shape)
    scaled = gain * dnormed
    dmiddle = scale * scaled - middle * (scale * scale * scale) * jnp.mean(scaled * middle, axis=-1, keepdims=True)
    dmiddle_ref[...] = dmiddle
    dattn = (dbranch + dmiddle).astype(bf16)
    pack_rows(sent_ref, 0, nt(dattn, w_out[...]).astype(bf16))
    pack_rows(sent_ref, HALF, dattn)
    write_note(sent_ref, 2 * HALF, jnp.sum(jnp.where(live, dweight * gate, 0.0), axis=0, keepdims=True))


def put_kernel(own_ref, counts_ref, chosen_ref, old_ref, new_ref, result_ref):
    put_rows(own_ref, counts_ref, chosen_ref, old_ref, new_ref[...], result_ref)


def put_rows(own_ref, counts_ref, chosen_ref, old_ref, new, result_ref):
    hot = one_hot(own_ref, counts_ref, chosen_ref, old_ref.shape[0], True)
    hit = jnp.sum(hot, axis=1, keepdims=True) > 0.5
    placed = nn(hot.astype(bf16), new)
    result_ref[...] = jnp.where(hit, placed, old_ref[...].astype(f32)).astype(bf16)


def router_slope(own_ref, counts_ref, rows, dweight_ref, total_ref, coef_ref, vectors_ref):
    gate = gate_of(rows, vectors_ref)
    live = live_column(own_ref, counts_ref, rows.shape[0])
    count = total_count(counts_ref)
    total = total_ref[:1, :1]
    dscore = dweight_ref[:, :1] * (count / total) - coef_ref[:1, :1] * count / (total * total)
    return jnp.where(live, dscore * gate * (1.0 - gate), 0.0)


def keys_kernel(dq_ref, dkv_ref, moved_ref, coef_ref, sent_ref, sum_ref):
    rows = dkv_ref.shape[0]
    sent_ref[:, :HALF, :] = dq_ref[...]
    dkv = dkv_ref[...] + moved_ref[:rows, :]
    sent_ref[:, HALF:, :] = dkv.astype(bf16).reshape(sent_ref.shape[0], SHARE, LANES)
    sum_ref[...] = coef_ref[...] + moved_ref[rows:, :]


def units_kernel(
    own_ref, counts_ref, got_ref, dqkv_ref, total_ref, coef_ref, vectors_ref, rows_ref, dweight_ref,
    out_ref, up_ref, down_ref, *rest,
):
    boths, mixeds, rest = rest[:PIECES], rest[PIECES : PIECES + 4], rest[PIECES + 4 :]
    down_keep_ref, down_give_ref, keep_ref, give_ref, rest = *rest[:4], rest[4:]
    both, mixed_slots, grad_up, grad_down, grad_out, grad_q, grad_kv, ratio_ref, both_sems, mixed_sems = rest
    step = pl.program_id(0)
    steps = pl.num_programs(0)
    _, sources, twice, width = both.shape
    capacity = twice // 2
    core = own_ref[0] % 2
    slot = step % 2

    def both_copies(k, at):
        if PIECES == 4:
            return [pltpu.make_async_copy(boths[k], both.at[at], both_sems.at[at, 0])]
        return [
            pltpu.make_async_copy(boths[0].at[chip_of(own_ref, 4 * k + j)], both.at[at, j], both_sems.at[at, j])
            for j in range(4)
        ]

    def copies(k):
        return both_copies(k, k % 2) + [
            pltpu.make_async_copy(mixeds[k], mixed_slots.at[k % 2], mixed_sems.at[k % 2])
        ]

    for k in range(4):

        @pl.when(step == max(k - 1, 0))
        def _(k=k):
            for copy in copies(k):
                copy.start()

    @pl.when(step == 0)
    def _():
        for ref in (grad_up, grad_down, grad_out, grad_q, grad_kv):
            ref[...] = jnp.zeros_like(ref)
        ratio_ref[...] = jnp.broadcast_to(total_count(counts_ref) / total_ref[:1, :1], ratio_ref.shape)

    for k in range(4):

        @pl.when(step == k)
        def _(k=k):
            for copy in copies(k):
                copy.wait()

    def halves(ref, first):
        blocks = [ref[chip_of(own_ref, 4 * step + j), first : first + HALF, :] for j in range(sources)]
        turned = jnp.transpose(jnp.concatenate(blocks, axis=0).astype(f32)).astype(bf16)
        return turned[:HEAD_DIM], turned[HEAD_DIM:]

    def low_high(value):
        value = value.reshape(sources, capacity, width)
        return value[:, :HALF, :].reshape(sources * HALF, width), value[:, HALF:, :].reshape(sources * HALF, width)

    rows = both[slot, :, :capacity, :].reshape(sources * capacity, width).astype(f32)
    upstream = both[slot, :, capacity:, :].reshape(sources * capacity, width).astype(f32)
    mixed = mixed_slots[slot].reshape(sources * capacity, width)
    normed_attn = (rows * inverse_rms(rows) * vectors_ref[1:2, :]).astype(bf16)
    low_query, high_query = halves(dqkv_ref, 0)
    low_rows, high_rows = low_high(normed_attn)
    grad_q[...] += nn(low_query, low_rows) + nn(high_query, high_rows)
    blocks = [dqkv_ref[chip_of(own_ref, 4 * step + j), HALF:, :] for j in range(sources)]
    pairs_turned = jnp.transpose(jnp.concatenate(blocks, axis=0).astype(f32)).astype(bf16)
    grad_kv[...] += nn(pairs_turned, normed_attn)
    low_attn, high_attn = halves(got_ref, HALF)
    low_mixed, high_mixed = low_high(mixed)
    grad_out[...] += nn(low_attn, low_mixed) + nn(high_attn, high_mixed)
    middle = rows + nn(mixed, out_ref[...])
    normed = (middle * inverse_rms(middle) * vectors_ref[2:3, :]).astype(bf16)
    dmlp = (gate_of(rows, vectors_ref) * ratio_ref[:1, :1] * upstream).astype(bf16)
    value, slope = gelu_pair(nn(normed, up_ref[...]))
    dhidden = nt(dmlp, down_ref[...]) * slope
    grad_down[...] += nn(jnp.transpose(value).astype(bf16), dmlp)
    grad_up[...] += nn(jnp.transpose(dhidden).astype(bf16), normed)

    @pl.when(step == steps - 1)
    def _():
        chips = keep_ref.shape[0]

        def split(value):
            value = value.reshape(chips, 2, OUT_ROWS, LANES)
            even, odd = value[:, 0], value[:, 1]
            return jnp.where(core == 0, even, odd), jnp.where(core == 0, odd, even)

        def store(first, kept, given):
            keep_ref[:, first : first + kept.shape[1], :] = kept
            give_ref[:, first : first + kept.shape[1], :] = given.astype(bf16)

        for t in range(TILES):
            store(t * OUT_ROWS, *split(jnp.transpose(grad_up[t * LANES : (t + 1) * LANES, :])))

        def two_in_one(value):
            return joined(value[:, :OUT_HALF], swapped(value[:, OUT_HALF:]))

        both_turned = jnp.transpose(jnp.concatenate([grad_out[...], grad_q[...]], axis=0))
        kept, given = split(both_turned)
        store(AT_OUT, two_in_one(kept), two_in_one(given))
        store(AT_QUERY, two_in_one(swapped(kept)), two_in_one(swapped(given)))
        store(AT_PAIR, *split(jnp.transpose(grad_kv[...])))
        own_rows = rows_ref[0, :capacity, :].astype(f32)
        dlogit = router_slope(own_ref, counts_ref, own_rows, dweight_ref, total_ref, coef_ref, vectors_ref)
        part = jnp.broadcast_to(jnp.sum(dlogit * own_rows, axis=0, keepdims=True), (NOTE, width))
        per_tile = LANES // OUT_ROWS
        for c in range(chips):
            tile = part[:, (2 * c) // per_tile * LANES : ((2 * c) // per_tile + 1) * LANES]
            shift = (2 * c) % per_tile * OUT_ROWS
            if shift:
                tile = jnp.concatenate([tile[:, shift:], tile[:, :shift]], axis=1)
            after = jnp.concatenate([tile[:, OUT_ROWS:], tile[:, :OUT_ROWS]], axis=1)
            keep_ref[c, AT_NOTE:, :] = jnp.where(core == 0, tile, after)
            give_ref[c, AT_NOTE:, :] = in_parts(jnp.where(core == 0, after, tile))
        down = grad_down[...]
        half = down.shape[0] // 2
        down_keep_ref[...] = jnp.where(core == 0, down[:half], down[half:])
        down_give_ref[...] = jnp.where(core == 0, down[half:], down[:half]).astype(bf16)


def merge_kernel(keep_ref, moved_ref, down_keep_ref, down_moved_ref, sent_ref, down_ref):
    sent_ref[:, :AT_NOTE, :] = (keep_ref[:, :AT_NOTE, :] + moved_ref[:, :AT_NOTE, :].astype(f32)).astype(bf16)
    note = keep_ref[:, AT_NOTE:, :] + jnp.sum(moved_ref[:, AT_NOTE:, :].astype(f32), axis=1, keepdims=True)
    sent_ref[:, AT_NOTE:, :] = in_parts(note)
    down_ref[...] = down_keep_ref[...] + down_moved_ref[...].astype(f32)


def rows_kernel(
    own_ref, counts_ref, chosen_ref, got_ref, both_ref, dmiddle_ref, dweight_ref, total_ref, coef_ref, vectors_ref,
    old_ref, wq_ref, wk_ref, wv_ref, grads_ref, wq, wk, wv, sems,
):
    copies = [
        pltpu.make_async_copy(source, target, sems.at[i])
        for i, (source, target) in enumerate(((wq_ref, wq), (wk_ref, wk), (wv_ref, wv)))
    ]
    for copy in copies:
        copy.start()
    capacity = dmiddle_ref.shape[0]
    rows = both_ref[0, :capacity, :].astype(f32)
    upstream = both_ref[0, capacity:, :].astype(f32)
    gain = vectors_ref[1:2, :]
    dlogit = router_slope(own_ref, counts_ref, rows, dweight_ref, total_ref, coef_ref, vectors_ref)
    partial = upstream + dmiddle_ref[...] + dlogit * vectors_ref[0:1, :]
    dquery = unpack_rows(got_ref, 0, HALF)
    dkey, dvalue = unpack_pairs(got_ref, HALF, SHARE)
    copies[0].wait()
    dnormed = jnp.zeros_like(partial) + nt(dquery, wq[...])
    copies[1].wait()
    dnormed = dnormed + nt(dkey, wk[...])
    copies[2].wait()
    dnormed = dnormed + nt(dvalue, wv[...])
    scale = inverse_rms(rows)
    scaled = gain * dnormed
    drows = scale * scaled - rows * (scale * scale * scale) * jnp.mean(scaled * rows, axis=-1, keepdims=True)
    put_rows(own_ref, counts_ref, chosen_ref, old_ref, (partial + drows).astype(bf16), grads_ref)


def finish_kernel(
    own_ref, got_ref, own_gain_ref, up_ref, wq_ref, wk_ref, wv_ref,
    grad_up_ref, grad_out_ref, grad_q_ref, grad_k_ref, grad_v_ref, router_ref, gain_attn_ref, gain_mlp_ref,
):
    total = jnp.zeros((OUT_ROWS, LANES), f32)
    for c in range(got_ref.shape[0]):
        for t in range(TILES):
            lanes = slice((TILES * c + t) * LANES, (TILES * c + t + 1) * LANES)
            part = got_ref[c, t * OUT_ROWS : (t + 1) * OUT_ROWS, :].astype(f32)
            grad_up_ref[:, lanes] = part
            total = total + part * up_ref[:, lanes].astype(f32)
    gain_mlp_ref[...] = row_of(jnp.sum(total, axis=1, keepdims=True)) / own_gain_ref[2:3, :]
    grad_out_ref[...] = unpack_rows(got_ref, AT_OUT, OUT_HALF).astype(f32)
    grad_q = unpack_rows(got_ref, AT_QUERY, OUT_HALF).astype(f32)
    grad_k, grad_v = (value.astype(f32) for value in unpack_pairs(got_ref, AT_PAIR, OUT_ROWS))
    grad_q_ref[...] = grad_q
    grad_k_ref[...] = grad_k
    grad_v_ref[...] = grad_v
    products = wq_ref[...].astype(f32) * grad_q + wk_ref[...].astype(f32) * grad_k + wv_ref[...].astype(f32) * grad_v
    gain_attn_ref[...] = row_of(jnp.sum(products, axis=1, keepdims=True)) / own_gain_ref[1:2, :]
    notes = jnp.sum(got_ref[:, AT_NOTE:, :].astype(f32), axis=0)
    router_ref[...] = jnp.sum(notes, axis=0, keepdims=True)[:, :OUT_ROWS]


def pair_attend_kernel(factor, got_ref, other_ref, kpos_ref, qpos_ref, qlow_ref, mixed_ref, turned_ref, lse_ref, total_ref):
    lists = (got_ref, other_ref)
    chips = got_ref.shape[0]
    blocks = chips * HALF // BLOCK
    sources = chips // blocks
    total = read_note(got_ref, HALF + SHARE) + read_note(other_ref, HALF + SHARE)
    total_ref[...] = jnp.broadcast_to(total, total_ref.shape)
    attend_core(
        factor,
        lambda b: got_ref[b * sources : (b + 1) * sources, :HALF, :].reshape(BLOCK, LANES),
        lambda m, extent: lists[m][: extent // SHARE, HALF : HALF + SHARE, :].reshape(extent, LANES),
        2, blocks, chips * SHARE, kpos_ref, qpos_ref, qlow_ref, mixed_ref, turned_ref, lse_ref,
    )


def pair_attend_back_kernel(
    factor, got_ref, other_ref, grad_ref, kpos_ref, qpos_ref, qlow_ref, turned_ref, lse_ref,
    dq_ref, own_ref, moved_ref, coef_ref,
):
    lists = (got_ref, other_ref)
    sums = (own_ref, moved_ref)
    chips = got_ref.shape[0]
    blocks = chips * HALF // BLOCK
    sources = chips // blocks
    coef = jnp.broadcast_to(read_note(grad_ref, 2 * HALF), coef_ref.shape)
    coef_ref[...] = coef
    moved_ref[chips * SHARE :, :] = coef

    def add_dkv(m, extent, first, update):
        if first:
            sums[m][:extent, :] = update
        else:
            sums[m][:extent, :] += update

    attend_back_core(
        factor,
        lambda b: got_ref[b * sources : (b + 1) * sources, :HALF, :].reshape(BLOCK, LANES),
        lambda b: grad_ref[b * sources : (b + 1) * sources, :HALF, :].reshape(BLOCK, LANES),
        lambda m, extent: lists[m][: extent // SHARE, HALF : HALF + SHARE, :].reshape(extent, LANES),
        2, blocks, chips * SHARE, kpos_ref, qpos_ref, qlow_ref, turned_ref, lse_ref, dq_ref, add_dkv,
    )


smem = pl.BlockSpec(memory_space=pltpu.SMEM)
hbm = pl.BlockSpec(memory_space=pl.ANY)
params = pltpu.CompilerParams(vmem_limit_bytes=vmem_limit)


def shaped(shape, dtype):
    return jax.ShapeDtypeStruct(shape, dtype)


def call(kernel, name, in_specs, out_shape, arguments, scratch=()):
    return pl.pallas_call(
        kernel,
        out_shape=out_shape,
        in_specs=in_specs,
        out_specs=jax.tree.map(lambda _: vmem, out_shape),
        scratch_shapes=list(scratch),
        compiler_params=params,
        name=name,
    )(*arguments)


def pairs(
    tokens_in,
    w_router,
    gain_attn,
    w_query,
    w_key,
    w_value,
    w_out,
    gain_mlp,
    w_up,
    w_down,
    out_grad,
    lengths,
    counts,
    chosen,
):
    devices = lax.axis_size("seq")
    chips = devices // 2
    own = lax.axis_index("seq")
    capacity = chosen.shape[0] // devices
    tok_rows, width = tokens_in.shape
    hidden_width = w_up.shape[1]
    out_rows = width // devices
    factor = HEAD_DIM ** (-0.5)
    core = own % 2
    own_id = own.astype(jnp.int32).reshape(1)
    chosen = chosen.reshape(devices, capacity)
    vectors = jnp.stack([w_router, gain_attn, gain_mlp]).astype(f32)
    own_gains = lax.dynamic_slice_in_dim(vectors, own * out_rows, out_rows, 1)
    cores = [[2 * c + k for c in range(chips)] for k in range(2)]

    def swap(value):
        return lax.all_to_all(value, "seq", split_axis=0, concat_axis=0, tiled=True, axis_index_groups=cores)

    def across(value, bits):
        return lax.ppermute(value, "seq", [(s, s ^ bits) for s in range(devices)])

    def gathered(block):
        line = jnp.concatenate([block] + [across(block, 8 * k) for k in (1, 2, 3)], axis=0)
        return [line] + [across(line, 2 * k) for k in (1, 2, 3)]

    slot_ids = jnp.arange(capacity, dtype=jnp.int32)
    places = jnp.arange(devices, dtype=jnp.int32)[:, None] * tok_rows + chosen
    live_all = slot_ids[None, :] < counts[:, None]
    seq_ends = jnp.cumsum(lengths)
    starts = jnp.max(jnp.where(places[..., None] >= seq_ends, seq_ends, 0), axis=-1)
    kpos = jnp.where(live_all, places.astype(f32), far_away).reshape(chips, 2, SHARE)
    kpos = jnp.where(core == 0, kpos, kpos[:, ::-1]).swapaxes(0, 1).reshape(2, chips * SHARE)
    blocks = chips * HALF // BLOCK

    def query_order(value):
        value = lax.dynamic_index_in_dim(value.reshape(chips, 2, SHARE), core, 1, False)
        return value.reshape(blocks, chips // blocks, 2, HALF).swapaxes(1, 2).reshape(blocks, 2 * BLOCK)

    qpos = query_order(jnp.where(live_all, places, -1).astype(f32))
    qlow = query_order(starts.astype(f32))

    square = pltpu.VMEM((width, width), bf16)
    both = call(
        fetch_kernel, "fetch", [smem, smem] + [vmem] * 3, shaped((1, 2 * capacity, width), bf16),
        (own_id, counts, chosen, tokens_in, out_grad),
    )
    both_all = [lax.all_gather(both[0], "seq", axis=0, axis_index_groups=cores)]
    sent = call(
        prepare_kernel, "prepare", [smem, smem] + [vmem] * 2 + [hbm] * 3,
        shaped((chips, HALF + SHARE + NOTE, LANES), bf16),
        (own_id, counts, both, vectors, w_query, w_key, w_value),
        [square] * 3 + [pltpu.SemaphoreType.DMA((3,))],
    )
    got = swap(sent)
    other = across(got, 1)
    mixed_packed, turned, lse, total = call(
        functools.partial(pair_attend_kernel, factor), "attend", [vmem] * 5,
        (
            shaped((chips * HALF, LANES), bf16),
            shaped((chips * HALF, LANES), f32),
            shaped((blocks, 2 * BLOCK), f32),
            shaped((8, LANES), f32),
        ),
        (got, other, kpos, qpos, qlow),
    )
    mixed_got = swap(mixed_packed.reshape(chips, HALF, LANES))
    mixed = call(unpack_kernel, "unpack", [vmem], shaped((1, capacity, width), bf16), (mixed_got,))
    mixed_all = gathered(mixed)
    sent, new_rows, dmiddle, dweight = call(
        middle_kernel, "middle", [smem, smem] + [vmem] * 4 + [hbm] * 3,
        (
            shaped((chips, 2 * HALF + NOTE, LANES), bf16),
            shaped((capacity, width), bf16),
            shaped((capacity, width), f32),
            shaped((capacity, LANES), f32),
        ),
        (own_id, counts, mixed, total, both, vectors, w_out, w_up, w_down),
        [
            square,
            pltpu.VMEM((width, hidden_width), bf16),
            pltpu.VMEM((hidden_width, width), bf16),
            pltpu.VMEM((capacity, hidden_width), f32),
            pltpu.VMEM((capacity, hidden_width), bf16),
            pltpu.SemaphoreType.DMA((1 + 2 * CHUNKS,)),
        ],
    )
    grads_got = swap(sent)
    output = call(
        put_kernel, "put", [smem, smem] + [vmem] * 3, shaped((tok_rows, width), bf16),
        (own_id, counts, chosen, tokens_in, new_rows),
    )
    dq, dkv_own, dkv_other, coef = call(
        functools.partial(pair_attend_back_kernel, factor), "attend_back", [vmem] * 8,
        (
            shaped((chips * HALF, LANES), bf16),
            shaped((chips * SHARE, LANES), f32),
            shaped((chips * SHARE + 8, LANES), f32),
            shaped((8, LANES), f32),
        ),
        (got, other, grads_got, kpos, qpos, qlow, turned, lse),
    )
    dqkv, coef = call(
        keys_kernel, "keys", [vmem] * 4,
        (shaped((chips, HALF + SHARE, LANES), bf16), shaped((8, LANES), f32)),
        (dq.reshape(chips, HALF, LANES), dkv_own, across(dkv_other, 1), coef),
    )
    got = swap(dqkv)
    sources = 4
    hidden_cols = hidden_width // chips
    whole = lambda *shape: pl.BlockSpec(shape, lambda i, o: (0,) * len(shape))
    down_keep, down_give, keep, give = pl.pallas_call(
        units_kernel,
        out_shape=(
            shaped((hidden_cols // 2, width), f32),
            shaped((hidden_cols // 2, width), bf16),
            shaped((chips, GRAD_ROWS, LANES), f32),
            shaped((chips, GRAD_ROWS, LANES), bf16),
        ),
        grid_spec=pltpu.PrefetchScalarGridSpec(
            num_scalar_prefetch=1,
            grid=(chips // sources,),
            in_specs=[
                smem,
                whole(chips, 2 * HALF + NOTE, LANES),
                whole(chips, HALF + SHARE, LANES),
                whole(8, LANES),
                whole(8, LANES),
                whole(3, width),
                whole(1, 2 * capacity, width),
                whole(capacity, LANES),
                whole(width, width),
                pl.BlockSpec((width, hidden_cols), lambda i, o: (0, o[0] // 2)),
                pl.BlockSpec((hidden_cols, width), lambda i, o: (o[0] // 2, 0)),
            ]
            + [hbm] * (PIECES + 4),
            out_specs=(
                whole(hidden_cols // 2, width),
                whole(hidden_cols // 2, width),
                whole(chips, GRAD_ROWS, LANES),
                whole(chips, GRAD_ROWS, LANES),
            ),
            scratch_shapes=[
                pltpu.VMEM((2, sources, 2 * capacity, width), bf16),
                pltpu.VMEM((2, sources, capacity, width), bf16),
                pltpu.VMEM((hidden_cols, width), f32),
                pltpu.VMEM((hidden_cols, width), f32),
                pltpu.VMEM((HEAD_DIM, width), f32),
                pltpu.VMEM((HEAD_DIM, width), f32),
                pltpu.VMEM((2 * HEAD_DIM, width), f32),
                pltpu.VMEM((8, LANES), f32),
                pltpu.SemaphoreType.DMA((2, 4)),
                pltpu.SemaphoreType.DMA((2,)),
            ],
        ),
        compiler_params=params,
        name="units",
    )(own_id, counts, grads_got, dqkv, total, coef, vectors, both, dweight, w_out, w_up, w_down, *both_all, *mixed_all)
    sent, grad_down = call(
        merge_kernel, "merge", [vmem] * 4,
        (shaped((chips, GRAD_ROWS, LANES), bf16), shaped((hidden_cols // 2, width), f32)),
        (keep, across(give, 1), down_keep, across(down_give, 1)),
    )
    last = swap(sent)
    input_grad = call(
        rows_kernel, "rows", [smem, smem] + [vmem] * 9 + [hbm] * 3, shaped((tok_rows, width), bf16),
        (
            own_id, counts, chosen, got, both, dmiddle, dweight, total, coef, vectors, out_grad,
            w_query, w_key, w_value,
        ),
        [square] * 3 + [pltpu.SemaphoreType.DMA((3,))],
    )
    block = shaped((out_rows, width), f32)
    row = shaped((1, out_rows), f32)
    own_rows = pl.BlockSpec((out_rows, width), lambda i, o: (o[0], 0))
    grad_up, grad_out, grad_query, grad_key, grad_value, grad_router, grad_gain_attn, grad_gain_mlp = pl.pallas_call(
        finish_kernel,
        out_shape=(shaped((out_rows, hidden_width), f32), block, block, block, block, row, row, row),
        grid_spec=pltpu.PrefetchScalarGridSpec(
            num_scalar_prefetch=1,
            grid=(1,),
            in_specs=[
                whole(chips, GRAD_ROWS, LANES),
                whole(3, out_rows),
                pl.BlockSpec((out_rows, hidden_width), lambda i, o: (o[0], 0)),
                own_rows,
                own_rows,
                own_rows,
            ],
            out_specs=(whole(out_rows, hidden_width),) + (whole(out_rows, width),) * 4 + (whole(1, out_rows),) * 3,
        ),
        compiler_params=params,
        name="finish",
    )(own_id, last, own_gains, w_up, w_query, w_key, w_value)
    return (
        output,
        input_grad,
        grad_router.reshape(out_rows),
        grad_gain_attn.reshape(out_rows),
        grad_query,
        grad_key,
        grad_value,
        grad_out,
        grad_gain_mlp.reshape(out_rows),
        grad_up,
        grad_down,
    )


def per_device(*arguments):
    w_up, chosen = arguments[8], arguments[13]
    devices = lax.axis_size("seq")
    width, hidden_width = w_up.shape
    paired = (
        devices == 2 * HEADS
        and chosen.shape[0] == devices * SHARE
        and width == devices * OUT_ROWS
        and width == HEADS * HEAD_DIM
        and hidden_width == devices // 2 * TILES * LANES
    )
    return (pairs if paired else general)(*arguments)


def solution(mesh):
    placed = (P("seq", None),) + (P(),) * 9 + (P("seq", None),) + (P(),) * 3
    rows = P("seq", None)
    return jax.shard_map(
        per_device,
        mesh=mesh,
        in_specs=placed,
        out_specs=(rows, rows, P("seq"), P("seq"), rows, rows, rows, rows, P("seq"), rows, rows),
        check_vma=False,
    )
```

```python
import functools
import jax
import jax.numpy as jnp
from jax import lax
from jax.experimental import pallas as pl
from jax.experimental.pallas import tpu as pltpu
from jax.sharding import PartitionSpec as P

HEADS = 16
HEAD_DIM = 64
LANES = 128
BLOCK = 128

masked_score = -1e30
eps_norm = 1e-05
far_away = 1e9

f32 = jnp.float32
bf16 = jnp.bfloat16


def nt(left, right):
    return lax.dot_general(left, right, (((1,), (1,)), ((), ())), preferred_element_type=f32)


def nn(left, right):
    return lax.dot_general(left, right, (((1,), (0,)), ((), ())), preferred_element_type=f32)


def rms_scale(values, gain):
    return values * lax.rsqrt(jnp.mean(values * values, axis=-1, keepdims=True) + eps_norm) * gain


def three_parts(value):
    high = lax.reduce_precision(value, 8, 7)
    rest = value - high
    middle = lax.reduce_precision(rest, 8, 7)
    return jnp.stack([high, middle, rest - middle]).astype(bf16)


def spread_rows(packed, upper):
    lanes = lax.broadcasted_iota(jnp.int32, packed.shape, 1)
    zero = jnp.zeros_like(packed)
    rolled = jnp.concatenate([packed[:, HEAD_DIM:], packed[:, :HEAD_DIM]], axis=1)
    if upper:
        return jnp.concatenate(
            [jnp.where(lanes >= HEAD_DIM, rolled, zero), jnp.where(lanes >= HEAD_DIM, packed, zero)], axis=0
        )
    return jnp.concatenate(
        [jnp.where(lanes < HEAD_DIM, packed, zero), jnp.where(lanes < HEAD_DIM, rolled, zero)], axis=0
    )


def pack_columns(turned):
    return jnp.concatenate([turned[:, :BLOCK], turned[:, BLOCK:]], axis=0)


def key_columns(kpos_ref, member, extent):
    row = kpos_ref[member : member + 1, :extent]
    column = jnp.transpose(jnp.broadcast_to(row, (LANES, extent)))
    return jnp.concatenate([column, column], axis=1)


def attend_core(factor, load_query, load_kv, members, blocks, key_rows, kpos_ref, qpos_ref, qlow_ref, mixed_ref, turned_ref, lse_ref):
    kv_turned = [jnp.transpose(load_kv(m, key_rows)) for m in range(members)]
    for b in range(blocks):
        extent = key_rows * (b + 1) // blocks
        packed = (load_query(b).astype(f32) * factor).astype(bf16)
        wide = spread_rows(packed, False)
        qpos = qpos_ref[b : b + 1, :]
        qlow = qlow_ref[b : b + 1, :]
        scores = []
        for m in range(members):
            score = nt(load_kv(m, extent), wide)
            kpos = key_columns(kpos_ref, m, extent)
            score = jnp.where((kpos <= qpos) & (kpos >= qlow), score, masked_score)
            scores.append(score)
        peak = jnp.max(scores[0], axis=0, keepdims=True)
        for score in scores[1:]:
            peak = jnp.maximum(peak, jnp.max(score, axis=0, keepdims=True))
        peak = jnp.maximum(peak, 0.1 * masked_score)
        total = jnp.zeros_like(peak)
        mixed = jnp.zeros((LANES, 2 * BLOCK), f32)
        for m in range(members):
            prob = jnp.exp(scores[m] - peak)
            total = total + jnp.sum(prob, axis=0, keepdims=True)
            mixed = mixed + nn(kv_turned[m][:, :extent], prob.astype(bf16))
        safe = jnp.where(total > 0, total, 1.0)
        lse_ref[b : b + 1, :] = peak + jnp.log(safe)
        turned = pack_columns(mixed[HEAD_DIM:, :] / safe)
        turned_ref[b * BLOCK : (b + 1) * BLOCK, :] = turned
        mixed_ref[b * BLOCK : (b + 1) * BLOCK, :] = jnp.transpose(turned).astype(bf16)


def attend_back_core(
    factor, load_query, load_grad, load_kv, members, blocks, key_rows, kpos_ref, qpos_ref, qlow_ref, turned_ref, lse_ref,
    dq_ref, add_dkv,
):
    kv_turned = [jnp.transpose(load_kv(m, key_rows)) for m in range(members)]
    for b in range(blocks - 1, -1, -1):
        extent = key_rows * (b + 1) // blocks
        rows = slice(b * BLOCK, (b + 1) * BLOCK)
        packed = (load_query(b).astype(f32) * factor).astype(bf16)
        grads = load_grad(b)
        wide = jnp.concatenate([spread_rows(packed, False), spread_rows(grads, True)], axis=0)
        product = jnp.transpose(grads.astype(f32)) * turned_ref[rows, :]
        delta = jnp.concatenate(
            [
                jnp.sum(product[:HEAD_DIM], axis=0, keepdims=True),
                jnp.sum(product[HEAD_DIM:], axis=0, keepdims=True),
            ],
            axis=1,
        )
        qpos = qpos_ref[b : b + 1, :]
        qlow = qlow_ref[b : b + 1, :]
        lse = lse_ref[b : b + 1, :]
        dquery = jnp.zeros((LANES, 2 * BLOCK), f32)
        for m in range(members):
            both = nt(load_kv(m, extent), wide)
            kpos = key_columns(kpos_ref, m, extent)
            prob = jnp.exp(
                jnp.where((kpos <= qpos) & (kpos >= qlow), both[:, : 2 * BLOCK] - lse, masked_score)
            )
            dlogit = (prob * (both[:, 2 * BLOCK :] - delta)).astype(bf16)
            dquery = dquery + nn(kv_turned[m][:, :extent], dlogit)
            add_dkv(m, extent, b == blocks - 1, nn(jnp.concatenate([dlogit, prob.astype(bf16)], axis=1), wide))
        dq_ref[rows, :] = jnp.transpose(pack_columns(dquery[:HEAD_DIM, :] * factor)).astype(bf16)


def attend_kernel(factor, q_ref, kv_ref, kpos_ref, qpos_ref, qlow_ref, mixed_ref, turned_ref, lse_ref):
    members, key_rows, _ = kv_ref.shape
    attend_core(
        factor,
        lambda b: q_ref[b * BLOCK : (b + 1) * BLOCK, :],
        lambda m, extent: kv_ref[m, :extent, :],
        members, q_ref.shape[0] // BLOCK, key_rows, kpos_ref, qpos_ref, qlow_ref, mixed_ref, turned_ref, lse_ref,
    )


def attend_back_kernel(
    factor, q_ref, do_ref, kv_ref, kpos_ref, qpos_ref, qlow_ref, turned_ref, lse_ref, dq_ref, dkv_ref
):
    members, key_rows, _ = kv_ref.shape

    def add_dkv(m, extent, first, update):
        if first:
            dkv_ref[m, :extent, :] = update
        else:
            dkv_ref[m, :extent, :] += update

    attend_back_core(
        factor,
        lambda b: q_ref[b * BLOCK : (b + 1) * BLOCK, :],
        lambda b: do_ref[b * BLOCK : (b + 1) * BLOCK, :],
        lambda m, extent: kv_ref[m, :extent, :],
        members, q_ref.shape[0] // BLOCK, key_rows, kpos_ref, qpos_ref, qlow_ref, turned_ref, lse_ref, dq_ref, add_dkv,
    )


vmem = pl.BlockSpec(memory_space=pltpu.VMEM)
vmem_limit = 56 * 1024 * 1024


def attend(factor, queries, kv, kpos, qpos, qlow):
    rows = queries.shape[0]
    return pl.pallas_call(
        functools.partial(attend_kernel, factor),
        out_shape=(
            jax.ShapeDtypeStruct((rows, LANES), bf16),
            jax.ShapeDtypeStruct((rows, LANES), f32),
            jax.ShapeDtypeStruct(qpos.shape, f32),
        ),
        in_specs=[vmem] * 5,
        out_specs=(vmem,) * 3,
        compiler_params=pltpu.CompilerParams(vmem_limit_bytes=vmem_limit),
        name="attend",
    )(queries, kv, kpos, qpos, qlow)


def attend_back(factor, queries, dmixed, kv, kpos, qpos, qlow, turned, lse):
    rows = queries.shape[0]
    return pl.pallas_call(
        functools.partial(attend_back_kernel, factor),
        out_shape=(
            jax.ShapeDtypeStruct((rows, LANES), bf16),
            jax.ShapeDtypeStruct(kv.shape, f32),
        ),
        in_specs=[vmem] * 8,
        out_specs=(vmem,) * 2,
        compiler_params=pltpu.CompilerParams(vmem_limit_bytes=vmem_limit),
        name="attend_back",
    )(queries, dmixed, kv, kpos, qpos, qlow, turned, lse)


def general(
    tokens_in,
    w_router,
    gain_attn,
    w_query,
    w_key,
    w_value,
    w_out,
    gain_mlp,
    w_up,
    w_down,
    out_grad,
    lengths,
    counts,
    chosen,
):
    devices = lax.axis_size("seq")
    own = lax.axis_index("seq")
    capacity = chosen.shape[0] // devices
    tok_rows, width = tokens_in.shape
    hidden_width = w_up.shape[1]
    group = devices // HEADS
    share = capacity // group
    half = share // 2
    member = own % group
    slots = devices * capacity
    factor = HEAD_DIM ** (-0.5)
    attn_gain = gain_attn.astype(f32)
    mlp_gain = gain_mlp.astype(f32)

    def swap(value):
        return lax.all_to_all(value, "seq", split_axis=0, concat_axis=0, tiled=True)

    groups = [[h * group + m for m in range(group)] for h in range(HEADS)]

    def across_group(value):
        if group == 2:
            other = lax.ppermute(value, "seq", [(s, s ^ 1) for s in range(devices)])
            return jnp.stack([value, other])
        return lax.all_gather(value, "seq", axis_index_groups=groups)

    def sum_over_group(value):
        if group == 2:
            return value[0] + lax.ppermute(value[1], "seq", [(s, s ^ 1) for s in range(devices)])
        return lax.psum_scatter(value, "seq", scatter_dimension=0, axis_index_groups=groups)

    def member_order(value):
        if group == 2:
            return jnp.where(member == 0, value, value[::-1])
        return value

    slot_ids = jnp.arange(capacity, dtype=jnp.int32)
    places = jnp.arange(devices, dtype=jnp.int32)[:, None] * tok_rows + chosen.reshape(devices, capacity)
    live_all = slot_ids[None, :] < counts[:, None]
    seq_ends = jnp.cumsum(lengths)
    starts = jnp.max(jnp.where(places[..., None] >= seq_ends, seq_ends, 0), axis=-1)
    kpos = jnp.where(live_all, places.astype(f32), far_away)
    kpos = member_order(kpos.reshape(devices, group, share).swapaxes(0, 1).reshape(group, devices * share))
    blocks = devices * half // BLOCK

    def query_order(value):
        value = lax.dynamic_index_in_dim(value.reshape(devices, group, share), member, 1, False)
        return value.reshape(blocks, devices // blocks, 2, half).swapaxes(1, 2).reshape(blocks, 2 * BLOCK)

    qpos = query_order(jnp.where(live_all, places, -1).astype(f32))
    qlow = query_order(starts.astype(f32))

    offsets = lax.dynamic_slice_in_dim(chosen, own * capacity, capacity)
    live = slot_ids < counts[own]
    pick = (offsets[:, None] == jnp.arange(tok_rows, dtype=jnp.int32)[None, :]).astype(bf16)
    routed = nn(pick, tokens_in)
    upstream = jnp.where(live[:, None], nn(pick, out_grad), 0.0)
    gate = jax.nn.sigmoid(jnp.sum(routed * w_router.astype(f32)[None, :], axis=1))
    gate_sum = jnp.sum(jnp.where(live, gate, 0.0))
    normed = rms_scale(routed, attn_gain).astype(bf16)
    normed_all = lax.all_gather(normed, "seq", axis=0, tiled=True)
    queries = nn(normed, w_query).astype(bf16)
    keys = nn(normed, w_key).astype(bf16)
    values = nn(normed, w_value).astype(bf16)

    def note(value):
        parts = jnp.pad(three_parts(value), (0, LANES - 3))
        return jnp.broadcast_to(parts, (devices, 8, LANES))

    def read_note(rows):
        return jnp.sum(rows[:, 0, :3].astype(f32))

    def to_heads(value, per_row):
        if per_row == 2:
            value = value.reshape(group, 2, half, HEADS, HEAD_DIM).transpose(3, 0, 2, 1, 4)
            return value.reshape(devices, half, LANES)
        return value

    def pair_to_heads(first, second):
        both = jnp.stack([first, second], axis=1).reshape(group, share, 2, HEADS, HEAD_DIM)
        return both.transpose(3, 0, 1, 2, 4).reshape(devices, share, LANES)

    def from_heads(value):
        value = value.reshape(HEADS, group, half, 2, HEAD_DIM).transpose(1, 3, 2, 0, 4)
        return value.reshape(capacity, HEADS * HEAD_DIM)

    def pair_from_heads(value):
        value = value.reshape(HEADS, group, share, 2, HEAD_DIM).transpose(3, 1, 2, 0, 4)
        value = value.reshape(2, capacity, HEADS * HEAD_DIM)
        return value[0], value[1]

    sent = jnp.concatenate([to_heads(queries, 2), pair_to_heads(keys, values), note(gate_sum)], axis=1)
    got = swap(sent)
    score_total = read_note(got[:, half + share :])
    chosen_total = jnp.sum(counts).astype(f32)
    ratio = chosen_total / score_total
    scaling = gate * ratio
    head_queries = got[:, :half].reshape(devices * half, LANES)
    kv = across_group(got[:, half : half + share].reshape(devices * share, LANES))
    mixed_packed, mixed_turned, lse = attend(factor, head_queries, kv, kpos, qpos, qlow)
    mixed = from_heads(swap(mixed_packed.reshape(devices, half, LANES)))

    attn_out = nn(mixed, w_out)
    middle = routed + attn_out
    normed_mlp = rms_scale(middle, mlp_gain).astype(bf16)
    dbranch = scaling[:, None] * upstream
    dmlp = dbranch.astype(bf16)
    gathered = lax.all_gather(
        jnp.concatenate([mixed, normed_mlp, dmlp], axis=1), "seq", axis=0, tiled=True
    )
    mixed_all = gathered[:, :width]
    normed_mlp_all = gathered[:, width : 2 * width]
    dmlp_all = gathered[:, 2 * width :]
    hidden = nn(normed_mlp, w_up)
    active = jax.nn.gelu(hidden, approximate=True).astype(bf16)
    branch = attn_out + nn(active, w_down)
    dweight = jnp.sum(upstream * branch, axis=1)

    def gelu_of(values):
        return jax.nn.gelu(values, approximate=True)

    dactive = nt(dmlp, w_down)
    dhidden = jax.vjp(gelu_of, hidden)[1](dactive)[0].astype(bf16)
    dnormed_mlp = nt(dhidden, w_up)
    dmiddle = jax.vjp(lambda v: rms_scale(v, mlp_gain), middle)[1](dnormed_mlp)[0]
    dattn = (dbranch + dmiddle).astype(bf16)
    dmixed = nt(dattn, w_out).astype(bf16)
    out_cols = width // devices
    dattn_split = dattn.reshape(capacity, devices, out_cols).swapaxes(0, 1)
    dattn_split = dattn_split.reshape(devices, capacity * out_cols // LANES, LANES)
    got = swap(
        jnp.concatenate(
            [to_heads(dmixed, 2), dattn_split, note(jnp.sum(jnp.where(live, dweight * gate, 0.0)))], axis=1
        )
    )
    dattn_own = got[:, half : half + capacity * out_cols // LANES].reshape(slots, out_cols)
    coefficient = read_note(got[:, half + capacity * out_cols // LANES :])
    dq_packed, dkv_parts = attend_back(
        factor,
        head_queries,
        got[:, :half].reshape(devices * half, LANES),
        kv,
        kpos,
        qpos,
        qlow,
        mixed_turned,
        lse,
    )
    dkv = sum_over_group(dkv_parts).astype(bf16)

    dscore = dweight * ratio - coefficient * chosen_total / (score_total * score_total)
    dlogit_router = jnp.where(live, dscore * gate * (1.0 - gate), 0.0)
    router_part = jnp.sum(dlogit_router[:, None] * routed, axis=0).reshape(devices, out_cols)
    router_parts = three_parts(router_part).swapaxes(0, 1).reshape(devices, 1, 3 * out_cols)
    router_note = jnp.pad(router_parts, ((0, 0), (0, 7), (0, LANES - 3 * out_cols)))
    got = swap(
        jnp.concatenate(
            [dq_packed.reshape(devices, half, LANES), dkv.reshape(devices, share, LANES), router_note], axis=1
        )
    )
    dquery = from_heads(got[:, :half])
    dkey, dvalue = pair_from_heads(got[:, half : half + share])
    grad_router = jnp.sum(got[:, half + share, : 3 * out_cols].astype(f32), axis=0)
    grad_router = jnp.sum(grad_router.reshape(3, out_cols), axis=0)

    normed_own = lax.dynamic_index_in_dim(normed_all.reshape(devices, group, share, width), member, 1, False)
    normed_own = normed_own.reshape(devices * share, width)
    dq_rows = dq_packed.reshape(devices, half, 2, HEAD_DIM).swapaxes(1, 2).reshape(devices * share, HEAD_DIM)
    dqkv = jnp.concatenate([dq_rows, dkv], axis=1)
    grad_qkv = lax.dot_general(normed_own, dqkv, (((0,), (0,)), ((), ())), preferred_element_type=f32)
    head_cols = 3 * HEAD_DIM // group
    grad_qkv = member_order(grad_qkv.reshape(width, group, head_cols).swapaxes(0, 1))
    grad_qkv = sum_over_group(grad_qkv).astype(bf16)
    grad_out = lax.dot_general(mixed_all, dattn_own, (((0,), (0,)), ((), ())), preferred_element_type=f32)

    hidden_cols = hidden_width // devices
    up_own = lax.dynamic_slice_in_dim(w_up, own * hidden_cols, hidden_cols, 1)
    down_own = lax.dynamic_slice_in_dim(w_down, own * hidden_cols, hidden_cols, 0)
    hidden_own = nn(normed_mlp_all, up_own)
    dactive_own = nt(dmlp_all, down_own)
    active_own, gelu_back = jax.vjp(gelu_of, hidden_own)
    dhidden_own = gelu_back(dactive_own)[0].astype(bf16)
    active_own = active_own.astype(bf16)
    grad_down = lax.dot_general(active_own, dmlp_all, (((0,), (0,)), ((), ())), preferred_element_type=f32)
    grad_up = lax.dot_general(
        normed_mlp_all, dhidden_own, (((0,), (0,)), ((), ())), preferred_element_type=f32
    )
    sent = jnp.concatenate([grad_up.astype(bf16), grad_qkv, grad_out.astype(bf16)], axis=1)
    got = swap(sent.reshape(devices, out_cols, sent.shape[1])).astype(f32)
    grad_up = got[:, :, :hidden_cols].swapaxes(0, 1).reshape(out_cols, hidden_width)
    grad_qkv = got[:, :, hidden_cols : hidden_cols + head_cols].reshape(HEADS, group, out_cols, head_cols)
    grad_qkv = grad_qkv.transpose(2, 0, 1, 3).reshape(out_cols, HEADS, 3, HEAD_DIM)
    grad_query = grad_qkv[:, :, 0].reshape(out_cols, width)
    grad_key = grad_qkv[:, :, 1].reshape(out_cols, width)
    grad_value = grad_qkv[:, :, 2].reshape(out_cols, width)
    grad_out = got[:, :, hidden_cols + head_cols :].swapaxes(0, 1).reshape(out_cols, width)

    def own_rows(value):
        return lax.dynamic_slice_in_dim(value, own * out_cols, out_cols, 0).astype(f32)

    grad_gain_attn = jnp.sum(
        own_rows(w_query) * grad_query + own_rows(w_key) * grad_key + own_rows(w_value) * grad_value, axis=1
    ) / own_rows(attn_gain)
    grad_gain_mlp = jnp.sum(own_rows(w_up) * grad_up, axis=1) / own_rows(mlp_gain)

    dnormed = nt(dquery, w_query) + nt(dkey, w_key) + nt(dvalue, w_value)
    drows = jax.vjp(lambda v: rms_scale(v, attn_gain), routed)[1](dnormed)[0]
    droutes = drows + dmiddle + dlogit_router[:, None] * w_router.astype(f32)[None, :]
    new_rows = (routed + scaling[:, None] * branch).astype(bf16)
    new_grads = (upstream + droutes).astype(bf16)
    put = (jnp.arange(tok_rows, dtype=jnp.int32)[:, None] == offsets[None, :]) & live[None, :]
    hit = jnp.any(put, axis=1, keepdims=True)
    put = put.astype(bf16)
    output = jnp.where(hit, nn(put, new_rows).astype(bf16), tokens_in)
    input_grad = jnp.where(hit, nn(put, new_grads).astype(bf16), out_grad)
    return (
        output,
        input_grad,
        grad_router,
        grad_gain_attn,
        grad_query,
        grad_key,
        grad_value,
        grad_out,
        grad_gain_mlp,
        grad_up,
        grad_down,
    )


SHARE = 64
HALF = 32
NOTE = 8
OUT_HALF = 16
OUT_ROWS = 32
TILES = 2
AT_OUT = TILES * OUT_ROWS
AT_QUERY = AT_OUT + OUT_HALF
AT_PAIR = AT_QUERY + OUT_HALF
AT_NOTE = AT_PAIR + OUT_ROWS
GRAD_ROWS = AT_NOTE + NOTE


def swapped(tile):
    return jnp.concatenate([tile[..., HEAD_DIM:], tile[..., :HEAD_DIM]], axis=-1)


def joined(left, right):
    return jnp.concatenate([left[..., :HEAD_DIM], right[..., HEAD_DIM:]], axis=-1)


def pack_rows(target, first, value):
    for pair in range(HEADS // 2):
        tile = value[:, pair * LANES : (pair + 1) * LANES]
        turned = swapped(tile)
        target[2 * pair, first : first + HALF, :] = joined(tile[:HALF], turned[HALF:])
        target[2 * pair + 1, first : first + HALF, :] = joined(turned[:HALF], tile[HALF:])


def pack_pairs(target, first, left, right):
    for pair in range(HEADS // 2):
        lanes = slice(pair * LANES, (pair + 1) * LANES)
        one, two = left[:, lanes], right[:, lanes]
        target[2 * pair, first : first + SHARE, :] = joined(one, swapped(two))
        target[2 * pair + 1, first : first + SHARE, :] = joined(swapped(one), two)


def unpack_rows(source, first, half):
    columns = []
    for pair in range(HEADS // 2):
        even = source[2 * pair, first : first + half, :]
        odd = source[2 * pair + 1, first : first + half, :]
        columns.append(jnp.concatenate([joined(even, swapped(odd)), joined(swapped(even), odd)], axis=0))
    return jnp.concatenate(columns, axis=1)


def unpack_pairs(source, first, rows):
    left, right = [], []
    for pair in range(HEADS // 2):
        even = source[2 * pair, first : first + rows, :]
        odd = source[2 * pair + 1, first : first + rows, :]
        left.append(joined(even, swapped(odd)))
        right.append(joined(swapped(even), odd))
    return jnp.concatenate(left, axis=1), jnp.concatenate(right, axis=1)


def in_parts(value):
    high = value.astype(bf16).astype(f32)
    rest = value - high
    middle = rest.astype(bf16).astype(f32)
    row = lax.broadcasted_iota(jnp.int32, value.shape, len(value.shape) - 2)
    parts = jnp.where(row == 0, high, jnp.where(row == 1, middle, jnp.where(row == 2, rest - middle, 0.0)))
    return parts.astype(bf16)


def write_note(target, first, value):
    rows = in_parts(jnp.broadcast_to(value, (NOTE, LANES)))
    for k in range(target.shape[0]):
        target[k, first : first + NOTE, :] = rows


def read_note(source, first):
    rows = source[:, first : first + NOTE, :].astype(f32)
    return jnp.sum(jnp.sum(rows, axis=0), axis=0, keepdims=True)[:, :1]


def one_hot(own_ref, counts_ref, chosen_ref, tok_rows, live_only):
    offsets = chosen_ref[pl.ds(own_ref[0], 1), :]
    capacity = offsets.shape[1]
    rows = lax.broadcasted_iota(jnp.int32, (tok_rows, capacity), 0)
    hot = rows == offsets
    if live_only:
        slot = lax.broadcasted_iota(jnp.int32, (tok_rows, capacity), 1)
        hot = hot & (slot < counts_ref[own_ref[0]])
    return jnp.where(hot, 1.0, 0.0)


def live_column(own_ref, counts_ref, capacity):
    return lax.broadcasted_iota(jnp.int32, (capacity, 1), 0) < counts_ref[own_ref[0]]


def gate_of(rows, vectors_ref):
    return jax.nn.sigmoid(jnp.sum(rows * vectors_ref[0:1, :], axis=1, keepdims=True))


def inverse_rms(values):
    return lax.rsqrt(jnp.mean(values * values, axis=-1, keepdims=True) + eps_norm)


def total_count(counts_ref):
    return lax.fori_loop(0, counts_ref.shape[0], lambda i, s: s + counts_ref[i], 0).astype(f32)


def gelu_pair(u):
    c = 0.7978845608028654
    square = u * u
    t = jnp.tanh(c * (u + 0.044715 * (square * u)))
    value = 0.5 * u * (1.0 + t)
    slope = 0.5 * (1.0 + t) + (0.5 * u) * ((1.0 - t * t) * (c + (3.0 * 0.044715 * c) * square))
    return value, slope


def chip_of(own_ref, k):
    return jnp.bitwise_xor(own_ref[0] // 2, (k // 4) ^ (4 * (k % 4)))


def row_of(column):
    wide = jnp.broadcast_to(column, (column.shape[0], LANES))
    filled = jnp.concatenate([wide, jnp.zeros((LANES - column.shape[0], LANES), f32)], axis=0)
    return jnp.transpose(filled)[:1, : column.shape[0]]


def places_kernel(own_ref, counts_ref, lengths_ref, chosen_ref, kpos_ref, qpos_ref, qlow_ref):
    core = own_ref[0] % 2
    devices, capacity = chosen_ref.shape
    tok_rows = lengths_ref[lengths_ref.shape[0] - 1]
    slot = lax.broadcasted_iota(jnp.int32, (1, capacity), 1)
    ends = []
    for k in range(lengths_ref.shape[0] - 1):
        ends.append(lengths_ref[k] + (ends[-1] if ends else 0))

    def place(device):
        value = device * tok_rows + chosen_ref[pl.ds(device, 1), :]
        return value, slot < counts_ref[device]

    def key_row(device):
        value, live = place(device)
        return jnp.where(live, value.astype(f32), far_away)

    for m in range(2):
        parity = jnp.bitwise_xor(core, m)
        for c in range(0, devices // 2, 2):
            tile = jnp.concatenate([key_row(2 * c + parity), key_row(2 * c + 2 + parity)], axis=1)
            kpos_ref[m : m + 1, c * capacity : (c + 2) * capacity] = tile
    blocks = qpos_ref.shape[0]
    sources = devices // 2 // blocks
    for b in range(blocks):
        lows, highs = [], []
        for c in range(b * sources, (b + 1) * sources):
            value, live = place(2 * c + core)
            low = jnp.zeros_like(value)
            for end in ends:
                low = jnp.maximum(low, jnp.where(value >= end, end, 0))
            both = jnp.concatenate([jnp.where(live, value, -1), low], axis=0).astype(f32)
            lows.append(both[:, :HALF])
            highs.append(both[:, HALF:])
        both = jnp.concatenate(lows + highs, axis=1)
        qpos_ref[b : b + 1, :] = both[:1]
        qlow_ref[b : b + 1, :] = both[1:]


def fetch_kernel(own_ref, counts_ref, chosen_ref, tokens_ref, grads_ref, both_ref):
    hot = one_hot(own_ref, counts_ref, chosen_ref, tokens_ref.shape[0], False)
    capacity = hot.shape[1]
    pick = jnp.transpose(jnp.concatenate([hot, jnp.zeros_like(hot)], axis=1))[:capacity].astype(bf16)
    live = live_column(own_ref, counts_ref, capacity)
    both_ref[0, :capacity, :] = nn(pick, tokens_ref[...]).astype(bf16)
    both_ref[0, capacity:, :] = jnp.where(live, nn(pick, grads_ref[...]), 0.0).astype(bf16)


def prepare_kernel(own_ref, counts_ref, both_ref, vectors_ref, wq_ref, wk_ref, wv_ref, sent_ref, wq, wk, wv, sems):
    copies = [
        pltpu.make_async_copy(source, target, sems.at[i])
        for i, (source, target) in enumerate(((wq_ref, wq), (wk_ref, wk), (wv_ref, wv)))
    ]
    for copy in copies:
        copy.start()
    capacity = both_ref.shape[1] // 2
    rows = both_ref[0, :capacity, :].astype(f32)
    live = live_column(own_ref, counts_ref, capacity)
    gate_sum = jnp.sum(jnp.where(live, gate_of(rows, vectors_ref), 0.0), axis=0, keepdims=True)
    write_note(sent_ref, HALF + SHARE, gate_sum)
    normed = (rows * inverse_rms(rows) * vectors_ref[1:2, :]).astype(bf16)
    copies[0].wait()
    pack_rows(sent_ref, 0, nn(normed, wq[...]).astype(bf16))
    copies[1].wait()
    keys = nn(normed, wk[...]).astype(bf16)
    copies[2].wait()
    pack_pairs(sent_ref, HALF, keys, nn(normed, wv[...]).astype(bf16))


def unpack_kernel(got_ref, mixed_ref):
    mixed_ref[0] = unpack_rows(got_ref, 0, HALF)


CHUNKS = 4
PIECES = 1


def middle_kernel(
    own_ref, counts_ref, mixed_ref, total_ref, both_ref, vectors_ref, out_ref, up_ref, down_ref,
    sent_ref, new_ref, dmiddle_ref, dweight_ref, w_out, w_up, w_down, hidden_ref, active_ref, sems,
):
    width, total_cols = up_ref.shape
    cols = total_cols // CHUNKS
    copies = [pltpu.make_async_copy(out_ref, w_out, sems.at[0])]
    for c in range(CHUNKS):
        part = pl.ds(c * cols, cols)
        copies.append(pltpu.make_async_copy(up_ref.at[:, part], w_up.at[:, part], sems.at[1 + c]))
    for c in range(CHUNKS):
        part = pl.ds(c * cols, cols)
        copies.append(pltpu.make_async_copy(down_ref.at[part, :], w_down.at[part, :], sems.at[1 + CHUNKS + c]))
    for copy in copies:
        copy.start()
    capacity = mixed_ref.shape[1]
    rows = both_ref[0, :capacity, :].astype(f32)
    upstream = both_ref[0, capacity:, :].astype(f32)
    live = live_column(own_ref, counts_ref, capacity)
    gate = gate_of(rows, vectors_ref)
    ratio = total_count(counts_ref) / total_ref[:1, :1]
    scaling = gate * ratio
    gain = vectors_ref[2:3, :]
    dbranch = scaling * upstream
    dmlp = dbranch.astype(bf16)
    copies[0].wait()
    attn_out = nn(mixed_ref[0], w_out[...])
    middle = rows + attn_out
    scale = inverse_rms(middle)
    normed = (middle * scale * gain).astype(bf16)
    for c in range(CHUNKS):
        copies[1 + c].wait()
        hidden_ref[:, c * cols : (c + 1) * cols] = nn(normed, w_up[:, c * cols : (c + 1) * cols])
    dnormed = jnp.zeros((capacity, width), f32)
    for c in range(CHUNKS):
        part = slice(c * cols, (c + 1) * cols)
        copies[1 + CHUNKS + c].wait()
        hidden = hidden_ref[:, part]
        value, slope = gelu_pair(hidden)
        active_ref[:, part] = value.astype(bf16)
        dhidden = (nt(dmlp, w_down[part, :]) * slope).astype(bf16)
        dnormed = dnormed + nt(dhidden, w_up[:, part])
    branch = attn_out + nn(active_ref[...], w_down[...])
    new_ref[...] = (rows + scaling * branch).astype(bf16)
    dweight = jnp.sum(upstream * branch, axis=1, keepdims=True)
    dweight_ref[...] = jnp.broadcast_to(dweight, dweight_ref.shape)
    scaled = gain * dnormed
    dmiddle = scale * scaled - middle * (scale * scale * scale) * jnp.mean(scaled * middle, axis=-1, keepdims=True)
    dmiddle_ref[...] = dmiddle
    dattn = (dbranch + dmiddle).astype(bf16)
    pack_rows(sent_ref, 0, nt(dattn, w_out[...]).astype(bf16))
    pack_rows(sent_ref, HALF, dattn)
    write_note(sent_ref, 2 * HALF, jnp.sum(jnp.where(live, dweight * gate, 0.0), axis=0, keepdims=True))


def put_kernel(own_ref, counts_ref, chosen_ref, old_ref, new_ref, result_ref):
    put_rows(own_ref, counts_ref, chosen_ref, old_ref, new_ref[...], result_ref)


def put_rows(own_ref, counts_ref, chosen_ref, old_ref, new, result_ref):
    hot = one_hot(own_ref, counts_ref, chosen_ref, old_ref.shape[0], True)
    hit = jnp.sum(hot, axis=1, keepdims=True) > 0.5
    placed = nn(hot.astype(bf16), new)
    result_ref[...] = jnp.where(hit, placed, old_ref[...].astype(f32)).astype(bf16)


def router_slope(own_ref, counts_ref, rows, dweight_ref, total_ref, coef_ref, vectors_ref):
    gate = gate_of(rows, vectors_ref)
    live = live_column(own_ref, counts_ref, rows.shape[0])
    count = total_count(counts_ref)
    total = total_ref[:1, :1]
    dscore = dweight_ref[:, :1] * (count / total) - coef_ref[:1, :1] * count / (total * total)
    return jnp.where(live, dscore * gate * (1.0 - gate), 0.0)


def keys_kernel(dq_ref, dkv_ref, moved_ref, coef_ref, sent_ref, sum_ref):
    rows = dkv_ref.shape[0]
    sent_ref[:, :HALF, :] = dq_ref[...]
    dkv = dkv_ref[...] + moved_ref[:rows, :]
    sent_ref[:, HALF:, :] = dkv.astype(bf16).reshape(sent_ref.shape[0], SHARE, LANES)
    sum_ref[...] = coef_ref[...] + moved_ref[rows:, :]


def units_kernel(
    own_ref, counts_ref, got_ref, dqkv_ref, total_ref, coef_ref, vectors_ref, rows_ref, dweight_ref,
    out_ref, up_ref, down_ref, *rest,
):
    boths, mixeds, rest = rest[:PIECES], rest[PIECES : PIECES + 5], rest[PIECES + 5 :]
    down_keep_ref, down_give_ref, keep_ref, give_ref, rest = *rest[:4], rest[4:]
    both, mixed_slots, grad_up, grad_down, grad_out, grad_q, grad_kv, ratio_ref, both_sems, mixed_sems = rest
    step = pl.program_id(0)
    steps = pl.num_programs(0)
    _, sources, twice, width = both.shape
    capacity = twice // 2
    core = own_ref[0] % 2
    slot = step % 2

    def both_copies(k, at):
        if PIECES == 5:
            return piece_copies(boths, both, both_sems, k)
        return [
            pltpu.make_async_copy(boths[0].at[chip_of(own_ref, 4 * k + j)], both.at[at, j], both_sems.at[at, j])
            for j in range(4)
        ]

    def piece_copies(pieces, slots, sems, k):
        at = k % 2
        if k < 3:
            return [pltpu.make_async_copy(pieces[k], slots.at[at], sems.at[at, 0])]
        return [
            pltpu.make_async_copy(pieces[k + half], slots.at[at, 2 * half : 2 * half + 2], sems.at[at, half])
            for half in range(2)
        ]

    def copies(k):
        return both_copies(k, k % 2) + piece_copies(mixeds, mixed_slots, mixed_sems, k)

    for k in range(4):

        @pl.when(step == max(k - 1, 0))
        def _(k=k):
            for copy in copies(k):
                copy.start()

    @pl.when(step == 0)
    def _():
        for ref in (grad_up, grad_down, grad_out, grad_q, grad_kv):
            ref[...] = jnp.zeros_like(ref)
        ratio_ref[...] = jnp.broadcast_to(total_count(counts_ref) / total_ref[:1, :1], ratio_ref.shape)

    for k in range(4):

        @pl.when(step == k)
        def _(k=k):
            for copy in copies(k):
                copy.wait()

    def halves(ref, first):
        blocks = [ref[chip_of(own_ref, 4 * step + j), first : first + HALF, :] for j in range(sources)]
        turned = jnp.transpose(jnp.concatenate(blocks, axis=0).astype(f32)).astype(bf16)
        return turned[:HEAD_DIM], turned[HEAD_DIM:]

    def low_high(value):
        value = value.reshape(sources, capacity, width)
        return value[:, :HALF, :].reshape(sources * HALF, width), value[:, HALF:, :].reshape(sources * HALF, width)

    rows = both[slot, :, :capacity, :].reshape(sources * capacity, width).astype(f32)
    upstream = both[slot, :, capacity:, :].reshape(sources * capacity, width).astype(f32)
    mixed = mixed_slots[slot].reshape(sources * capacity, width)
    normed_attn = (rows * inverse_rms(rows) * vectors_ref[1:2, :]).astype(bf16)
    low_query, high_query = halves(dqkv_ref, 0)
    low_rows, high_rows = low_high(normed_attn)
    grad_q[...] += nn(low_query, low_rows) + nn(high_query, high_rows)
    blocks = [dqkv_ref[chip_of(own_ref, 4 * step + j), HALF:, :] for j in range(sources)]
    pairs_turned = jnp.transpose(jnp.concatenate(blocks, axis=0).astype(f32)).astype(bf16)
    grad_kv[...] += nn(pairs_turned, normed_attn)
    low_attn, high_attn = halves(got_ref, HALF)
    low_mixed, high_mixed = low_high(mixed)
    grad_out[...] += nn(low_attn, low_mixed) + nn(high_attn, high_mixed)
    middle = rows + nn(mixed, out_ref[...])
    normed = (middle * inverse_rms(middle) * vectors_ref[2:3, :]).astype(bf16)
    dmlp = (gate_of(rows, vectors_ref) * ratio_ref[:1, :1] * upstream).astype(bf16)
    value, slope = gelu_pair(nn(normed, up_ref[...]))
    dhidden = nt(dmlp, down_ref[...]) * slope
    grad_down[...] += nn(jnp.transpose(value).astype(bf16), dmlp)
    grad_up[...] += nn(jnp.transpose(dhidden).astype(bf16), normed)

    @pl.when(step == steps - 1)
    def _():
        chips = keep_ref.shape[0]

        def split(value):
            value = value.reshape(chips, 2, OUT_ROWS, LANES)
            even, odd = value[:, 0], value[:, 1]
            return jnp.where(core == 0, even, odd), jnp.where(core == 0, odd, even)

        def store(first, kept, given):
            keep_ref[:, first : first + kept.shape[1], :] = kept
            give_ref[:, first : first + kept.shape[1], :] = given.astype(bf16)

        for t in range(TILES):
            store(t * OUT_ROWS, *split(jnp.transpose(grad_up[t * LANES : (t + 1) * LANES, :])))

        def two_in_one(value):
            return joined(value[:, :OUT_HALF], swapped(value[:, OUT_HALF:]))

        both_turned = jnp.transpose(jnp.concatenate([grad_out[...], grad_q[...]], axis=0))
        kept, given = split(both_turned)
        store(AT_OUT, two_in_one(kept), two_in_one(given))
        store(AT_QUERY, two_in_one(swapped(kept)), two_in_one(swapped(given)))
        store(AT_PAIR, *split(jnp.transpose(grad_kv[...])))
        own_rows = rows_ref[0, :capacity, :].astype(f32)
        dlogit = router_slope(own_ref, counts_ref, own_rows, dweight_ref, total_ref, coef_ref, vectors_ref)
        part = jnp.broadcast_to(jnp.sum(dlogit * own_rows, axis=0, keepdims=True), (NOTE, width))
        per_tile = LANES // OUT_ROWS
        for c in range(chips):
            tile = part[:, (2 * c) // per_tile * LANES : ((2 * c) // per_tile + 1) * LANES]
            shift = (2 * c) % per_tile * OUT_ROWS
            if shift:
                tile = jnp.concatenate([tile[:, shift:], tile[:, :shift]], axis=1)
            after = jnp.concatenate([tile[:, OUT_ROWS:], tile[:, :OUT_ROWS]], axis=1)
            keep_ref[c, AT_NOTE:, :] = jnp.where(core == 0, tile, after)
            give_ref[c, AT_NOTE:, :] = in_parts(jnp.where(core == 0, after, tile))
        down = grad_down[...]
        half = down.shape[0] // 2
        down_keep_ref[...] = jnp.where(core == 0, down[:half], down[half:])
        down_give_ref[...] = jnp.where(core == 0, down[half:], down[:half]).astype(bf16)


def merge_kernel(keep_ref, moved_ref, down_keep_ref, down_moved_ref, sent_ref, down_ref):
    sent_ref[:, :AT_NOTE, :] = (keep_ref[:, :AT_NOTE, :] + moved_ref[:, :AT_NOTE, :].astype(f32)).astype(bf16)
    note = keep_ref[:, AT_NOTE:, :] + jnp.sum(moved_ref[:, AT_NOTE:, :].astype(f32), axis=1, keepdims=True)
    sent_ref[:, AT_NOTE:, :] = in_parts(note)
    down_ref[...] = down_keep_ref[...] + down_moved_ref[...].astype(f32)


def rows_kernel(
    own_ref, counts_ref, chosen_ref, got_ref, both_ref, dmiddle_ref, dweight_ref, total_ref, coef_ref, vectors_ref,
    old_ref, wq_ref, wk_ref, wv_ref, grads_ref, wq, wk, wv, sems,
):
    copies = [
        pltpu.make_async_copy(source, target, sems.at[i])
        for i, (source, target) in enumerate(((wq_ref, wq), (wk_ref, wk), (wv_ref, wv)))
    ]
    for copy in copies:
        copy.start()
    capacity = dmiddle_ref.shape[0]
    rows = both_ref[0, :capacity, :].astype(f32)
    upstream = both_ref[0, capacity:, :].astype(f32)
    gain = vectors_ref[1:2, :]
    dlogit = router_slope(own_ref, counts_ref, rows, dweight_ref, total_ref, coef_ref, vectors_ref)
    partial = upstream + dmiddle_ref[...] + dlogit * vectors_ref[0:1, :]
    dquery = unpack_rows(got_ref, 0, HALF)
    dkey, dvalue = unpack_pairs(got_ref, HALF, SHARE)
    copies[0].wait()
    dnormed = jnp.zeros_like(partial) + nt(dquery, wq[...])
    copies[1].wait()
    dnormed = dnormed + nt(dkey, wk[...])
    copies[2].wait()
    dnormed = dnormed + nt(dvalue, wv[...])
    scale = inverse_rms(rows)
    scaled = gain * dnormed
    drows = scale * scaled - rows * (scale * scale * scale) * jnp.mean(scaled * rows, axis=-1, keepdims=True)
    put_rows(own_ref, counts_ref, chosen_ref, old_ref, (partial + drows).astype(bf16), grads_ref)


def finish_kernel(
    got_ref, own_gain_ref, up_ref, wq_ref, wk_ref, wv_ref,
    grad_up_ref, grad_out_ref, grad_q_ref, grad_k_ref, grad_v_ref, router_ref, gain_attn_ref, gain_mlp_ref,
):
    total = jnp.zeros((OUT_ROWS, LANES), f32)
    for c in range(got_ref.shape[0]):
        for t in range(TILES):
            lanes = slice((TILES * c + t) * LANES, (TILES * c + t + 1) * LANES)
            part = got_ref[c, t * OUT_ROWS : (t + 1) * OUT_ROWS, :].astype(f32)
            grad_up_ref[:, lanes] = part
            total = total + part * up_ref[:, lanes].astype(f32)
    gain_mlp_ref[...] = row_of(jnp.sum(total, axis=1, keepdims=True)) / own_gain_ref[2:3, :]
    grad_out_ref[...] = unpack_rows(got_ref, AT_OUT, OUT_HALF).astype(f32)
    grad_q = unpack_rows(got_ref, AT_QUERY, OUT_HALF).astype(f32)
    grad_k, grad_v = (value.astype(f32) for value in unpack_pairs(got_ref, AT_PAIR, OUT_ROWS))
    grad_q_ref[...] = grad_q
    grad_k_ref[...] = grad_k
    grad_v_ref[...] = grad_v
    products = wq_ref[...].astype(f32) * grad_q + wk_ref[...].astype(f32) * grad_k + wv_ref[...].astype(f32) * grad_v
    gain_attn_ref[...] = row_of(jnp.sum(products, axis=1, keepdims=True)) / own_gain_ref[1:2, :]
    notes = jnp.sum(got_ref[:, AT_NOTE:, :].astype(f32), axis=0)
    router_ref[...] = jnp.sum(notes, axis=0, keepdims=True)[:, :OUT_ROWS]


def pair_attend_kernel(factor, got_ref, other_ref, kpos_ref, qpos_ref, qlow_ref, mixed_ref, turned_ref, lse_ref, total_ref):
    lists = (got_ref, other_ref)
    chips = got_ref.shape[0]
    blocks = chips * HALF // BLOCK
    sources = chips // blocks
    total = read_note(got_ref, HALF + SHARE) + read_note(other_ref, HALF + SHARE)
    total_ref[...] = jnp.broadcast_to(total, total_ref.shape)
    attend_core(
        factor,
        lambda b: got_ref[b * sources : (b + 1) * sources, :HALF, :].reshape(BLOCK, LANES),
        lambda m, extent: lists[m][: extent // SHARE, HALF : HALF + SHARE, :].reshape(extent, LANES),
        2, blocks, chips * SHARE, kpos_ref, qpos_ref, qlow_ref, mixed_ref, turned_ref, lse_ref,
    )


def pair_attend_back_kernel(
    factor, got_ref, other_ref, grad_ref, kpos_ref, qpos_ref, qlow_ref, turned_ref, lse_ref,
    dq_ref, own_ref, moved_ref, coef_ref,
):
    lists = (got_ref, other_ref)
    sums = (own_ref, moved_ref)
    chips = got_ref.shape[0]
    blocks = chips * HALF // BLOCK
    sources = chips // blocks
    coef = jnp.broadcast_to(read_note(grad_ref, 2 * HALF), coef_ref.shape)
    coef_ref[...] = coef
    moved_ref[chips * SHARE :, :] = coef

    def add_dkv(m, extent, first, update):
        if first:
            sums[m][:extent, :] = update
        else:
            sums[m][:extent, :] += update

    attend_back_core(
        factor,
        lambda b: got_ref[b * sources : (b + 1) * sources, :HALF, :].reshape(BLOCK, LANES),
        lambda b: grad_ref[b * sources : (b + 1) * sources, :HALF, :].reshape(BLOCK, LANES),
        lambda m, extent: lists[m][: extent // SHARE, HALF : HALF + SHARE, :].reshape(extent, LANES),
        2, blocks, chips * SHARE, kpos_ref, qpos_ref, qlow_ref, turned_ref, lse_ref, dq_ref, add_dkv,
    )


smem = pl.BlockSpec(memory_space=pltpu.SMEM)
hbm = pl.BlockSpec(memory_space=pl.ANY)
megabytes = {
    "places": 4, "fetch": 56, "prepare": 56, "attend": 20, "unpack": 4, "middle": 56, "put": 56, "attend_back": 24,
    "keys": 8, "units": 56, "merge": 10, "rows": 56, "finish": 12,
}


def params_of(name):
    return pltpu.CompilerParams(vmem_limit_bytes=megabytes[name] * 1024 * 1024)


def shaped(shape, dtype):
    return jax.ShapeDtypeStruct(shape, dtype)


microseconds = {
    "places": 1, "fetch": 3, "prepare": 5, "attend": 5, "unpack": 2, "middle": 15, "put": 3, "attend_back": 6, "keys": 2,
    "units": 16, "merge": 3, "rows": 7, "finish": 2,
}


def cost_of(name):
    return pl.CostEstimate(flops=0, transcendentals=0, bytes_accessed=microseconds[name] * 3_300_000)


def call(kernel, name, in_specs, out_shape, arguments, scratch=()):
    return pl.pallas_call(
        kernel,
        out_shape=out_shape,
        in_specs=in_specs,
        out_specs=jax.tree.map(lambda _: vmem, out_shape),
        scratch_shapes=list(scratch),
        compiler_params=params_of(name),
        cost_estimate=cost_of(name),
        name=name,
    )(*arguments)


def pairs(
    tokens_in,
    w_router,
    gain_attn,
    w_query,
    w_key,
    w_value,
    w_out,
    gain_mlp,
    w_up,
    w_down,
    out_grad,
    lengths,
    counts,
    chosen,
):
    devices = lax.axis_size("seq")
    chips = devices // 2
    own = lax.axis_index("seq")
    capacity = chosen.shape[0] // devices
    tok_rows, width = tokens_in.shape
    hidden_width = w_up.shape[1]
    out_rows = width // devices
    factor = HEAD_DIM ** (-0.5)
    core = own % 2
    own_id = own.astype(jnp.int32).reshape(1)
    chosen = chosen.reshape(devices, capacity)
    vectors = jnp.stack([w_router, gain_attn, gain_mlp]).astype(f32)
    own_gains = lax.dynamic_slice_in_dim(vectors, own * out_rows, out_rows, 1)
    cores = [[2 * c + k for c in range(chips)] for k in range(2)]

    def swap(value):
        return lax.all_to_all(value, "seq", split_axis=0, concat_axis=0, tiled=True, axis_index_groups=cores)

    def across(value, bits):
        return lax.ppermute(value, "seq", [(s, s ^ bits) for s in range(devices)])

    def line_of(block):
        return jnp.concatenate([block] + [across(block, 8 * k) for k in (1, 2, 3)], axis=0)

    def sides_of(line):
        return [line, across(line, 2), across(line, 4)]

    def gathered(sides):
        return sides + [across(sides[2][:2], 2), across(sides[1][2:], 4)]

    blocks = chips * HALF // BLOCK
    square = pltpu.VMEM((width, width), bf16)
    both = call(
        fetch_kernel, "fetch", [smem, smem] + [vmem] * 3, shaped((1, 2 * capacity, width), bf16),
        (own_id, counts, chosen, tokens_in, out_grad),
    )
    both_all = [lax.all_gather(both[0], "seq", axis=0, axis_index_groups=cores)]
    sent = call(
        prepare_kernel, "prepare", [smem, smem] + [vmem] * 2 + [hbm] * 3,
        shaped((chips, HALF + SHARE + NOTE, LANES), bf16),
        (own_id, counts, both, vectors, w_query, w_key, w_value),
        [square] * 3 + [pltpu.SemaphoreType.DMA((3,))],
    )
    chosen_after, _ = lax.optimization_barrier((chosen, sent))
    kpos, qpos, qlow = call(
        places_kernel, "places", [smem] * 3 + [vmem],
        (
            shaped((2, chips * SHARE), f32),
            shaped((blocks, 2 * BLOCK), f32),
            shaped((blocks, 2 * BLOCK), f32),
        ),
        (own_id, counts, jnp.append(lengths, tok_rows), chosen_after),
    )
    got = swap(sent)
    other = across(got, 1)
    mixed_packed, turned, lse, total = call(
        functools.partial(pair_attend_kernel, factor), "attend", [vmem] * 5,
        (
            shaped((chips * HALF, LANES), bf16),
            shaped((chips * HALF, LANES), f32),
            shaped((blocks, 2 * BLOCK), f32),
            shaped((8, LANES), f32),
        ),
        (got, other, kpos, qpos, qlow),
    )
    mixed_got = swap(mixed_packed.reshape(chips, HALF, LANES))
    mixed = call(unpack_kernel, "unpack", [vmem], shaped((1, capacity, width), bf16), (mixed_got,))
    mixed_line = line_of(mixed)
    sent, new_rows, dmiddle, dweight = call(
        middle_kernel, "middle", [smem, smem] + [vmem] * 4 + [hbm] * 3,
        (
            shaped((chips, 2 * HALF + NOTE, LANES), bf16),
            shaped((capacity, width), bf16),
            shaped((capacity, width), f32),
            shaped((capacity, LANES), f32),
        ),
        (own_id, counts, mixed, total, both, vectors, w_out, w_up, w_down),
        [
            square,
            pltpu.VMEM((width, hidden_width), bf16),
            pltpu.VMEM((hidden_width, width), bf16),
            pltpu.VMEM((capacity, hidden_width), f32),
            pltpu.VMEM((capacity, hidden_width), bf16),
            pltpu.SemaphoreType.DMA((1 + 2 * CHUNKS,)),
        ],
    )
    mixed_line, sent = lax.optimization_barrier((mixed_line, sent))
    mixed_sides = sides_of(mixed_line)
    grads_got = swap(sent)
    mixed_all = gathered(mixed_sides)
    output = call(
        put_kernel, "put", [smem, smem] + [vmem] * 3, shaped((tok_rows, width), bf16),
        (own_id, counts, chosen, tokens_in, new_rows),
    )
    dq, dkv_own, dkv_other, coef = call(
        functools.partial(pair_attend_back_kernel, factor), "attend_back", [vmem] * 8,
        (
            shaped((chips * HALF, LANES), bf16),
            shaped((chips * SHARE, LANES), f32),
            shaped((chips * SHARE + 8, LANES), f32),
            shaped((8, LANES), f32),
        ),
        (got, other, grads_got, kpos, qpos, qlow, turned, lse),
    )
    moved = across(dkv_other, 1)
    dqkv, coef = call(
        keys_kernel, "keys", [vmem] * 4,
        (shaped((chips, HALF + SHARE, LANES), bf16), shaped((8, LANES), f32)),
        (dq.reshape(chips, HALF, LANES), dkv_own, moved, coef),
    )
    got = swap(dqkv)
    sources = 4
    hidden_cols = hidden_width // chips
    whole = lambda *shape: pl.BlockSpec(shape, lambda i, o: (0,) * len(shape))
    down_keep, down_give, keep, give = pl.pallas_call(
        units_kernel,
        out_shape=(
            shaped((hidden_cols // 2, width), f32),
            shaped((hidden_cols // 2, width), bf16),
            shaped((chips, GRAD_ROWS, LANES), f32),
            shaped((chips, GRAD_ROWS, LANES), bf16),
        ),
        grid_spec=pltpu.PrefetchScalarGridSpec(
            num_scalar_prefetch=1,
            grid=(chips // sources,),
            in_specs=[
                smem,
                whole(chips, 2 * HALF + NOTE, LANES),
                whole(chips, HALF + SHARE, LANES),
                whole(8, LANES),
                whole(8, LANES),
                whole(3, width),
                whole(1, 2 * capacity, width),
                whole(capacity, LANES),
                whole(width, width),
                pl.BlockSpec((width, hidden_cols), lambda i, o: (0, o[0] // 2)),
                pl.BlockSpec((hidden_cols, width), lambda i, o: (o[0] // 2, 0)),
            ]
            + [hbm] * (PIECES + 5),
            out_specs=(
                whole(hidden_cols // 2, width),
                whole(hidden_cols // 2, width),
                whole(chips, GRAD_ROWS, LANES),
                whole(chips, GRAD_ROWS, LANES),
            ),
            scratch_shapes=[
                pltpu.VMEM((2, sources, 2 * capacity, width), bf16),
                pltpu.VMEM((2, sources, capacity, width), bf16),
                pltpu.VMEM((hidden_cols, width), f32),
                pltpu.VMEM((hidden_cols, width), f32),
                pltpu.VMEM((HEAD_DIM, width), f32),
                pltpu.VMEM((HEAD_DIM, width), f32),
                pltpu.VMEM((2 * HEAD_DIM, width), f32),
                pltpu.VMEM((8, LANES), f32),
                pltpu.SemaphoreType.DMA((2, 4)),
                pltpu.SemaphoreType.DMA((2, 2)),
            ],
        ),
        compiler_params=params_of("units"),
        cost_estimate=cost_of("units"),
        name="units",
    )(own_id, counts, grads_got, dqkv, total, coef, vectors, both, dweight, w_out, w_up, w_down, *both_all, *mixed_all)
    sent, grad_down = call(
        merge_kernel, "merge", [vmem] * 4,
        (shaped((chips, GRAD_ROWS, LANES), bf16), shaped((hidden_cols // 2, width), f32)),
        (keep, across(give, 1), down_keep, across(down_give, 1)),
    )
    last = swap(sent)
    input_grad = call(
        rows_kernel, "rows", [smem, smem] + [vmem] * 9 + [hbm] * 3, shaped((tok_rows, width), bf16),
        (
            own_id, counts, chosen, got, both, dmiddle, dweight, total, coef, vectors, out_grad,
            w_query, w_key, w_value,
        ),
        [square] * 3 + [pltpu.SemaphoreType.DMA((3,))],
    )
    block = shaped((out_rows, width), f32)
    row = shaped((1, out_rows), f32)
    first_row = own * out_rows
    grad_up, grad_out, grad_query, grad_key, grad_value, grad_router, grad_gain_attn, grad_gain_mlp = call(
        finish_kernel, "finish", [vmem] * 6,
        (shaped((out_rows, hidden_width), f32), block, block, block, block, row, row, row),
        (last, own_gains, *(lax.dynamic_slice_in_dim(w, first_row, out_rows) for w in (w_up, w_query, w_key, w_value))),
    )
    return (
        output,
        input_grad,
        grad_router.reshape(out_rows),
        grad_gain_attn.reshape(out_rows),
        grad_query,
        grad_key,
        grad_value,
        grad_out,
        grad_gain_mlp.reshape(out_rows),
        grad_up,
        grad_down,
    )


def per_device(*arguments):
    w_up, chosen = arguments[8], arguments[13]
    devices = lax.axis_size("seq")
    width, hidden_width = w_up.shape
    paired = (
        devices == 2 * HEADS
        and chosen.shape[0] == devices * SHARE
        and width == devices * OUT_ROWS
        and width == HEADS * HEAD_DIM
        and hidden_width == devices // 2 * TILES * LANES
    )
    return (pairs if paired else general)(*arguments)


def solution(mesh):
    placed = (P("seq", None),) + (P(),) * 9 + (P("seq", None),) + (P(),) * 3
    rows = P("seq", None)
    return jax.shard_map(
        per_device,
        mesh=mesh,
        in_specs=placed,
        out_specs=(rows, rows, P("seq"), P("seq"), rows, rows, rows, rows, P("seq"), rows, rows),
        check_vma=False,
    )
```

```python
import functools
import jax
import jax.numpy as jnp
from jax import lax
from jax.experimental import pallas as pl
from jax.experimental.pallas import tpu as pltpu
from jax.sharding import PartitionSpec as P

HEADS = 16
HEAD_DIM = 64
LANES = 128
BLOCK = 128

masked_score = -1e30
eps_norm = 1e-05
far_away = 1e9

f32 = jnp.float32
bf16 = jnp.bfloat16


def nt(left, right):
    return lax.dot_general(left, right, (((1,), (1,)), ((), ())), preferred_element_type=f32)


def nn(left, right):
    return lax.dot_general(left, right, (((1,), (0,)), ((), ())), preferred_element_type=f32)


def rms_scale(values, gain):
    return values * lax.rsqrt(jnp.mean(values * values, axis=-1, keepdims=True) + eps_norm) * gain


def three_parts(value):
    high = lax.reduce_precision(value, 8, 7)
    rest = value - high
    middle = lax.reduce_precision(rest, 8, 7)
    return jnp.stack([high, middle, rest - middle]).astype(bf16)


def spread_rows(packed, upper):
    lanes = lax.broadcasted_iota(jnp.int32, packed.shape, 1)
    zero = jnp.zeros_like(packed)
    rolled = jnp.concatenate([packed[:, HEAD_DIM:], packed[:, :HEAD_DIM]], axis=1)
    if upper:
        return jnp.concatenate(
            [jnp.where(lanes >= HEAD_DIM, rolled, zero), jnp.where(lanes >= HEAD_DIM, packed, zero)], axis=0
        )
    return jnp.concatenate(
        [jnp.where(lanes < HEAD_DIM, packed, zero), jnp.where(lanes < HEAD_DIM, rolled, zero)], axis=0
    )


def pack_columns(turned):
    return jnp.concatenate([turned[:, :BLOCK], turned[:, BLOCK:]], axis=0)


def key_columns(kpos_ref, member, extent):
    row = kpos_ref[member : member + 1, :extent]
    column = jnp.transpose(jnp.broadcast_to(row, (LANES, extent)))
    return jnp.concatenate([column, column], axis=1)


def attend_core(factor, load_query, load_kv, members, blocks, key_rows, kpos_ref, qpos_ref, qlow_ref, mixed_ref, turned_ref, lse_ref):
    kv_turned = [jnp.transpose(load_kv(m, key_rows)) for m in range(members)]
    for b in range(blocks):
        extent = key_rows * (b + 1) // blocks
        packed = (load_query(b).astype(f32) * factor).astype(bf16)
        wide = spread_rows(packed, False)
        qpos = qpos_ref[b : b + 1, :]
        qlow = qlow_ref[b : b + 1, :]
        scores = []
        for m in range(members):
            score = nt(load_kv(m, extent), wide)
            kpos = key_columns(kpos_ref, m, extent)
            score = jnp.where((kpos <= qpos) & (kpos >= qlow), score, masked_score)
            scores.append(score)
        peak = jnp.max(scores[0], axis=0, keepdims=True)
        for score in scores[1:]:
            peak = jnp.maximum(peak, jnp.max(score, axis=0, keepdims=True))
        peak = jnp.maximum(peak, 0.1 * masked_score)
        total = jnp.zeros_like(peak)
        mixed = jnp.zeros((LANES, 2 * BLOCK), f32)
        for m in range(members):
            prob = jnp.exp(scores[m] - peak)
            total = total + jnp.sum(prob, axis=0, keepdims=True)
            mixed = mixed + nn(kv_turned[m][:, :extent], prob.astype(bf16))
        safe = jnp.where(total > 0, total, 1.0)
        lse_ref[b : b + 1, :] = peak + jnp.log(safe)
        turned = pack_columns(mixed[HEAD_DIM:, :] / safe)
        turned_ref[b * BLOCK : (b + 1) * BLOCK, :] = turned
        mixed_ref[b * BLOCK : (b + 1) * BLOCK, :] = jnp.transpose(turned).astype(bf16)


def attend_back_core(
    factor, load_query, load_grad, load_kv, members, blocks, key_rows, kpos_ref, qpos_ref, qlow_ref, turned_ref, lse_ref,
    dq_ref, add_dkv,
):
    kv_turned = [jnp.transpose(load_kv(m, key_rows)) for m in range(members)]
    for b in range(blocks - 1, -1, -1):
        extent = key_rows * (b + 1) // blocks
        rows = slice(b * BLOCK, (b + 1) * BLOCK)
        packed = (load_query(b).astype(f32) * factor).astype(bf16)
        grads = load_grad(b)
        wide = jnp.concatenate([spread_rows(packed, False), spread_rows(grads, True)], axis=0)
        product = jnp.transpose(grads.astype(f32)) * turned_ref[rows, :]
        delta = jnp.concatenate(
            [
                jnp.sum(product[:HEAD_DIM], axis=0, keepdims=True),
                jnp.sum(product[HEAD_DIM:], axis=0, keepdims=True),
            ],
            axis=1,
        )
        qpos = qpos_ref[b : b + 1, :]
        qlow = qlow_ref[b : b + 1, :]
        lse = lse_ref[b : b + 1, :]
        dquery = jnp.zeros((LANES, 2 * BLOCK), f32)
        for m in range(members):
            both = nt(load_kv(m, extent), wide)
            kpos = key_columns(kpos_ref, m, extent)
            prob = jnp.exp(
                jnp.where((kpos <= qpos) & (kpos >= qlow), both[:, : 2 * BLOCK] - lse, masked_score)
            )
            dlogit = (prob * (both[:, 2 * BLOCK :] - delta)).astype(bf16)
            dquery = dquery + nn(kv_turned[m][:, :extent], dlogit)
            add_dkv(m, extent, b == blocks - 1, nn(jnp.concatenate([dlogit, prob.astype(bf16)], axis=1), wide))
        dq_ref[rows, :] = jnp.transpose(pack_columns(dquery[:HEAD_DIM, :] * factor)).astype(bf16)


def attend_kernel(factor, q_ref, kv_ref, kpos_ref, qpos_ref, qlow_ref, mixed_ref, turned_ref, lse_ref):
    members, key_rows, _ = kv_ref.shape
    attend_core(
        factor,
        lambda b: q_ref[b * BLOCK : (b + 1) * BLOCK, :],
        lambda m, extent: kv_ref[m, :extent, :],
        members, q_ref.shape[0] // BLOCK, key_rows, kpos_ref, qpos_ref, qlow_ref, mixed_ref, turned_ref, lse_ref,
    )


def attend_back_kernel(
    factor, q_ref, do_ref, kv_ref, kpos_ref, qpos_ref, qlow_ref, turned_ref, lse_ref, dq_ref, dkv_ref
):
    members, key_rows, _ = kv_ref.shape

    def add_dkv(m, extent, first, update):
        if first:
            dkv_ref[m, :extent, :] = update
        else:
            dkv_ref[m, :extent, :] += update

    attend_back_core(
        factor,
        lambda b: q_ref[b * BLOCK : (b + 1) * BLOCK, :],
        lambda b: do_ref[b * BLOCK : (b + 1) * BLOCK, :],
        lambda m, extent: kv_ref[m, :extent, :],
        members, q_ref.shape[0] // BLOCK, key_rows, kpos_ref, qpos_ref, qlow_ref, turned_ref, lse_ref, dq_ref, add_dkv,
    )


vmem = pl.BlockSpec(memory_space=pltpu.VMEM)
vmem_limit = 56 * 1024 * 1024


def attend(factor, queries, kv, kpos, qpos, qlow):
    rows = queries.shape[0]
    return pl.pallas_call(
        functools.partial(attend_kernel, factor),
        out_shape=(
            jax.ShapeDtypeStruct((rows, LANES), bf16),
            jax.ShapeDtypeStruct((rows, LANES), f32),
            jax.ShapeDtypeStruct(qpos.shape, f32),
        ),
        in_specs=[vmem] * 5,
        out_specs=(vmem,) * 3,
        compiler_params=pltpu.CompilerParams(vmem_limit_bytes=vmem_limit),
        name="attend",
    )(queries, kv, kpos, qpos, qlow)


def attend_back(factor, queries, dmixed, kv, kpos, qpos, qlow, turned, lse):
    rows = queries.shape[0]
    return pl.pallas_call(
        functools.partial(attend_back_kernel, factor),
        out_shape=(
            jax.ShapeDtypeStruct((rows, LANES), bf16),
            jax.ShapeDtypeStruct(kv.shape, f32),
        ),
        in_specs=[vmem] * 8,
        out_specs=(vmem,) * 2,
        compiler_params=pltpu.CompilerParams(vmem_limit_bytes=vmem_limit),
        name="attend_back",
    )(queries, dmixed, kv, kpos, qpos, qlow, turned, lse)


def general(
    tokens_in,
    w_router,
    gain_attn,
    w_query,
    w_key,
    w_value,
    w_out,
    gain_mlp,
    w_up,
    w_down,
    out_grad,
    lengths,
    counts,
    chosen,
):
    devices = lax.axis_size("seq")
    own = lax.axis_index("seq")
    capacity = chosen.shape[0] // devices
    tok_rows, width = tokens_in.shape
    hidden_width = w_up.shape[1]
    group = devices // HEADS
    share = capacity // group
    half = share // 2
    member = own % group
    slots = devices * capacity
    factor = HEAD_DIM ** (-0.5)
    attn_gain = gain_attn.astype(f32)
    mlp_gain = gain_mlp.astype(f32)

    def swap(value):
        return lax.all_to_all(value, "seq", split_axis=0, concat_axis=0, tiled=True)

    groups = [[h * group + m for m in range(group)] for h in range(HEADS)]

    def across_group(value):
        if group == 2:
            other = lax.ppermute(value, "seq", [(s, s ^ 1) for s in range(devices)])
            return jnp.stack([value, other])
        return lax.all_gather(value, "seq", axis_index_groups=groups)

    def sum_over_group(value):
        if group == 2:
            return value[0] + lax.ppermute(value[1], "seq", [(s, s ^ 1) for s in range(devices)])
        return lax.psum_scatter(value, "seq", scatter_dimension=0, axis_index_groups=groups)

    def member_order(value):
        if group == 2:
            return jnp.where(member == 0, value, value[::-1])
        return value

    slot_ids = jnp.arange(capacity, dtype=jnp.int32)
    places = jnp.arange(devices, dtype=jnp.int32)[:, None] * tok_rows + chosen.reshape(devices, capacity)
    live_all = slot_ids[None, :] < counts[:, None]
    seq_ends = jnp.cumsum(lengths)
    starts = jnp.max(jnp.where(places[..., None] >= seq_ends, seq_ends, 0), axis=-1)
    kpos = jnp.where(live_all, places.astype(f32), far_away)
    kpos = member_order(kpos.reshape(devices, group, share).swapaxes(0, 1).reshape(group, devices * share))
    blocks = devices * half // BLOCK

    def query_order(value):
        value = lax.dynamic_index_in_dim(value.reshape(devices, group, share), member, 1, False)
        return value.reshape(blocks, devices // blocks, 2, half).swapaxes(1, 2).reshape(blocks, 2 * BLOCK)

    qpos = query_order(jnp.where(live_all, places, -1).astype(f32))
    qlow = query_order(starts.astype(f32))

    offsets = lax.dynamic_slice_in_dim(chosen, own * capacity, capacity)
    live = slot_ids < counts[own]
    pick = (offsets[:, None] == jnp.arange(tok_rows, dtype=jnp.int32)[None, :]).astype(bf16)
    routed = nn(pick, tokens_in)
    upstream = jnp.where(live[:, None], nn(pick, out_grad), 0.0)
    gate = jax.nn.sigmoid(jnp.sum(routed * w_router.astype(f32)[None, :], axis=1))
    gate_sum = jnp.sum(jnp.where(live, gate, 0.0))
    normed = rms_scale(routed, attn_gain).astype(bf16)
    normed_all = lax.all_gather(normed, "seq", axis=0, tiled=True)
    queries = nn(normed, w_query).astype(bf16)
    keys = nn(normed, w_key).astype(bf16)
    values = nn(normed, w_value).astype(bf16)

    def note(value):
        parts = jnp.pad(three_parts(value), (0, LANES - 3))
        return jnp.broadcast_to(parts, (devices, 8, LANES))

    def read_note(rows):
        return jnp.sum(rows[:, 0, :3].astype(f32))

    def to_heads(value, per_row):
        if per_row == 2:
            value = value.reshape(group, 2, half, HEADS, HEAD_DIM).transpose(3, 0, 2, 1, 4)
            return value.reshape(devices, half, LANES)
        return value

    def pair_to_heads(first, second):
        both = jnp.stack([first, second], axis=1).reshape(group, share, 2, HEADS, HEAD_DIM)
        return both.transpose(3, 0, 1, 2, 4).reshape(devices, share, LANES)

    def from_heads(value):
        value = value.reshape(HEADS, group, half, 2, HEAD_DIM).transpose(1, 3, 2, 0, 4)
        return value.reshape(capacity, HEADS * HEAD_DIM)

    def pair_from_heads(value):
        value = value.reshape(HEADS, group, share, 2, HEAD_DIM).transpose(3, 1, 2, 0, 4)
        value = value.reshape(2, capacity, HEADS * HEAD_DIM)
        return value[0], value[1]

    sent = jnp.concatenate([to_heads(queries, 2), pair_to_heads(keys, values), note(gate_sum)], axis=1)
    got = swap(sent)
    score_total = read_note(got[:, half + share :])
    chosen_total = jnp.sum(counts).astype(f32)
    ratio = chosen_total / score_total
    scaling = gate * ratio
    head_queries = got[:, :half].reshape(devices * half, LANES)
    kv = across_group(got[:, half : half + share].reshape(devices * share, LANES))
    mixed_packed, mixed_turned, lse = attend(factor, head_queries, kv, kpos, qpos, qlow)
    mixed = from_heads(swap(mixed_packed.reshape(devices, half, LANES)))

    attn_out = nn(mixed, w_out)
    middle = routed + attn_out
    normed_mlp = rms_scale(middle, mlp_gain).astype(bf16)
    dbranch = scaling[:, None] * upstream
    dmlp = dbranch.astype(bf16)
    gathered = lax.all_gather(
        jnp.concatenate([mixed, normed_mlp, dmlp], axis=1), "seq", axis=0, tiled=True
    )
    mixed_all = gathered[:, :width]
    normed_mlp_all = gathered[:, width : 2 * width]
    dmlp_all = gathered[:, 2 * width :]
    hidden = nn(normed_mlp, w_up)
    active = jax.nn.gelu(hidden, approximate=True).astype(bf16)
    branch = attn_out + nn(active, w_down)
    dweight = jnp.sum(upstream * branch, axis=1)

    def gelu_of(values):
        return jax.nn.gelu(values, approximate=True)

    dactive = nt(dmlp, w_down)
    dhidden = jax.vjp(gelu_of, hidden)[1](dactive)[0].astype(bf16)
    dnormed_mlp = nt(dhidden, w_up)
    dmiddle = jax.vjp(lambda v: rms_scale(v, mlp_gain), middle)[1](dnormed_mlp)[0]
    dattn = (dbranch + dmiddle).astype(bf16)
    dmixed = nt(dattn, w_out).astype(bf16)
    out_cols = width // devices
    dattn_split = dattn.reshape(capacity, devices, out_cols).swapaxes(0, 1)
    dattn_split = dattn_split.reshape(devices, capacity * out_cols // LANES, LANES)
    got = swap(
        jnp.concatenate(
            [to_heads(dmixed, 2), dattn_split, note(jnp.sum(jnp.where(live, dweight * gate, 0.0)))], axis=1
        )
    )
    dattn_own = got[:, half : half + capacity * out_cols // LANES].reshape(slots, out_cols)
    coefficient = read_note(got[:, half + capacity * out_cols // LANES :])
    dq_packed, dkv_parts = attend_back(
        factor,
        head_queries,
        got[:, :half].reshape(devices * half, LANES),
        kv,
        kpos,
        qpos,
        qlow,
        mixed_turned,
        lse,
    )
    dkv = sum_over_group(dkv_parts).astype(bf16)

    dscore = dweight * ratio - coefficient * chosen_total / (score_total * score_total)
    dlogit_router = jnp.where(live, dscore * gate * (1.0 - gate), 0.0)
    router_part = jnp.sum(dlogit_router[:, None] * routed, axis=0).reshape(devices, out_cols)
    router_parts = three_parts(router_part).swapaxes(0, 1).reshape(devices, 1, 3 * out_cols)
    router_note = jnp.pad(router_parts, ((0, 0), (0, 7), (0, LANES - 3 * out_cols)))
    got = swap(
        jnp.concatenate(
            [dq_packed.reshape(devices, half, LANES), dkv.reshape(devices, share, LANES), router_note], axis=1
        )
    )
    dquery = from_heads(got[:, :half])
    dkey, dvalue = pair_from_heads(got[:, half : half + share])
    grad_router = jnp.sum(got[:, half + share, : 3 * out_cols].astype(f32), axis=0)
    grad_router = jnp.sum(grad_router.reshape(3, out_cols), axis=0)

    normed_own = lax.dynamic_index_in_dim(normed_all.reshape(devices, group, share, width), member, 1, False)
    normed_own = normed_own.reshape(devices * share, width)
    dq_rows = dq_packed.reshape(devices, half, 2, HEAD_DIM).swapaxes(1, 2).reshape(devices * share, HEAD_DIM)
    dqkv = jnp.concatenate([dq_rows, dkv], axis=1)
    grad_qkv = lax.dot_general(normed_own, dqkv, (((0,), (0,)), ((), ())), preferred_element_type=f32)
    head_cols = 3 * HEAD_DIM // group
    grad_qkv = member_order(grad_qkv.reshape(width, group, head_cols).swapaxes(0, 1))
    grad_qkv = sum_over_group(grad_qkv).astype(bf16)
    grad_out = lax.dot_general(mixed_all, dattn_own, (((0,), (0,)), ((), ())), preferred_element_type=f32)

    hidden_cols = hidden_width // devices
    up_own = lax.dynamic_slice_in_dim(w_up, own * hidden_cols, hidden_cols, 1)
    down_own = lax.dynamic_slice_in_dim(w_down, own * hidden_cols, hidden_cols, 0)
    hidden_own = nn(normed_mlp_all, up_own)
    dactive_own = nt(dmlp_all, down_own)
    active_own, gelu_back = jax.vjp(gelu_of, hidden_own)
    dhidden_own = gelu_back(dactive_own)[0].astype(bf16)
    active_own = active_own.astype(bf16)
    grad_down = lax.dot_general(active_own, dmlp_all, (((0,), (0,)), ((), ())), preferred_element_type=f32)
    grad_up = lax.dot_general(
        normed_mlp_all, dhidden_own, (((0,), (0,)), ((), ())), preferred_element_type=f32
    )
    sent = jnp.concatenate([grad_up.astype(bf16), grad_qkv, grad_out.astype(bf16)], axis=1)
    got = swap(sent.reshape(devices, out_cols, sent.shape[1])).astype(f32)
    grad_up = got[:, :, :hidden_cols].swapaxes(0, 1).reshape(out_cols, hidden_width)
    grad_qkv = got[:, :, hidden_cols : hidden_cols + head_cols].reshape(HEADS, group, out_cols, head_cols)
    grad_qkv = grad_qkv.transpose(2, 0, 1, 3).reshape(out_cols, HEADS, 3, HEAD_DIM)
    grad_query = grad_qkv[:, :, 0].reshape(out_cols, width)
    grad_key = grad_qkv[:, :, 1].reshape(out_cols, width)
    grad_value = grad_qkv[:, :, 2].reshape(out_cols, width)
    grad_out = got[:, :, hidden_cols + head_cols :].swapaxes(0, 1).reshape(out_cols, width)

    def own_rows(value):
        return lax.dynamic_slice_in_dim(value, own * out_cols, out_cols, 0).astype(f32)

    grad_gain_attn = jnp.sum(
        own_rows(w_query) * grad_query + own_rows(w_key) * grad_key + own_rows(w_value) * grad_value, axis=1
    ) / own_rows(attn_gain)
    grad_gain_mlp = jnp.sum(own_rows(w_up) * grad_up, axis=1) / own_rows(mlp_gain)

    dnormed = nt(dquery, w_query) + nt(dkey, w_key) + nt(dvalue, w_value)
    drows = jax.vjp(lambda v: rms_scale(v, attn_gain), routed)[1](dnormed)[0]
    droutes = drows + dmiddle + dlogit_router[:, None] * w_router.astype(f32)[None, :]
    new_rows = (routed + scaling[:, None] * branch).astype(bf16)
    new_grads = (upstream + droutes).astype(bf16)
    put = (jnp.arange(tok_rows, dtype=jnp.int32)[:, None] == offsets[None, :]) & live[None, :]
    hit = jnp.any(put, axis=1, keepdims=True)
    put = put.astype(bf16)
    output = jnp.where(hit, nn(put, new_rows).astype(bf16), tokens_in)
    input_grad = jnp.where(hit, nn(put, new_grads).astype(bf16), out_grad)
    return (
        output,
        input_grad,
        grad_router,
        grad_gain_attn,
        grad_query,
        grad_key,
        grad_value,
        grad_out,
        grad_gain_mlp,
        grad_up,
        grad_down,
    )


SHARE = 64
HALF = 32
NOTE = 8
OUT_HALF = 16
OUT_ROWS = 32
TILES = 2
AT_OUT = TILES * OUT_ROWS
AT_QUERY = AT_OUT + OUT_HALF
AT_PAIR = AT_QUERY + OUT_HALF
AT_NOTE = AT_PAIR + OUT_ROWS
GRAD_ROWS = AT_NOTE + NOTE


def swapped(tile):
    return jnp.concatenate([tile[..., HEAD_DIM:], tile[..., :HEAD_DIM]], axis=-1)


def joined(left, right):
    return jnp.concatenate([left[..., :HEAD_DIM], right[..., HEAD_DIM:]], axis=-1)


def pack_rows(target, first, value):
    for pair in range(HEADS // 2):
        tile = value[:, pair * LANES : (pair + 1) * LANES]
        turned = swapped(tile)
        target[2 * pair, first : first + HALF, :] = joined(tile[:HALF], turned[HALF:])
        target[2 * pair + 1, first : first + HALF, :] = joined(turned[:HALF], tile[HALF:])


def pack_pairs(target, first, left, right):
    for pair in range(HEADS // 2):
        lanes = slice(pair * LANES, (pair + 1) * LANES)
        one, two = left[:, lanes], right[:, lanes]
        target[2 * pair, first : first + SHARE, :] = joined(one, swapped(two))
        target[2 * pair + 1, first : first + SHARE, :] = joined(swapped(one), two)


def unpack_rows(source, first, half):
    columns = []
    for pair in range(HEADS // 2):
        even = source[2 * pair, first : first + half, :]
        odd = source[2 * pair + 1, first : first + half, :]
        columns.append(jnp.concatenate([joined(even, swapped(odd)), joined(swapped(even), odd)], axis=0))
    return jnp.concatenate(columns, axis=1)


def unpack_pairs(source, first, rows):
    left, right = [], []
    for pair in range(HEADS // 2):
        even = source[2 * pair, first : first + rows, :]
        odd = source[2 * pair + 1, first : first + rows, :]
        left.append(joined(even, swapped(odd)))
        right.append(joined(swapped(even), odd))
    return jnp.concatenate(left, axis=1), jnp.concatenate(right, axis=1)


def in_parts(value):
    high = value.astype(bf16).astype(f32)
    rest = value - high
    middle = rest.astype(bf16).astype(f32)
    row = lax.broadcasted_iota(jnp.int32, value.shape, len(value.shape) - 2)
    parts = jnp.where(row == 0, high, jnp.where(row == 1, middle, jnp.where(row == 2, rest - middle, 0.0)))
    return parts.astype(bf16)


def write_note(target, first, value):
    rows = in_parts(jnp.broadcast_to(value, (NOTE, LANES)))
    for k in range(target.shape[0]):
        target[k, first : first + NOTE, :] = rows


def read_note(source, first):
    rows = source[:, first : first + NOTE, :].astype(f32)
    return jnp.sum(jnp.sum(rows, axis=0), axis=0, keepdims=True)[:, :1]


def one_hot(own_ref, counts_ref, chosen_ref, tok_rows, live_only):
    offsets = chosen_ref[pl.ds(own_ref[0], 1), :]
    capacity = offsets.shape[1]
    rows = lax.broadcasted_iota(jnp.int32, (tok_rows, capacity), 0)
    hot = rows == offsets
    if live_only:
        slot = lax.broadcasted_iota(jnp.int32, (tok_rows, capacity), 1)
        hot = hot & (slot < counts_ref[own_ref[0]])
    return jnp.where(hot, 1.0, 0.0)


def live_column(own_ref, counts_ref, capacity):
    return lax.broadcasted_iota(jnp.int32, (capacity, 1), 0) < counts_ref[own_ref[0]]


def gate_of(rows, vectors_ref):
    return jax.nn.sigmoid(jnp.sum(rows * vectors_ref[0:1, :], axis=1, keepdims=True))


def inverse_rms(values):
    return lax.rsqrt(jnp.mean(values * values, axis=-1, keepdims=True) + eps_norm)


def total_count(counts_ref):
    return lax.fori_loop(0, counts_ref.shape[0], lambda i, s: s + counts_ref[i], 0).astype(f32)


def gelu_pair(u):
    c = 0.7978845608028654
    square = u * u
    t = jnp.tanh(c * (u + 0.044715 * (square * u)))
    value = 0.5 * u * (1.0 + t)
    slope = 0.5 * (1.0 + t) + (0.5 * u) * ((1.0 - t * t) * (c + (3.0 * 0.044715 * c) * square))
    return value, slope


def chip_of(own_ref, k):
    return jnp.bitwise_xor(own_ref[0] // 2, (k // 4) ^ (4 * (k % 4)))


def row_of(column):
    wide = jnp.broadcast_to(column, (column.shape[0], LANES))
    filled = jnp.concatenate([wide, jnp.zeros((LANES - column.shape[0], LANES), f32)], axis=0)
    return jnp.transpose(filled)[:1, : column.shape[0]]


def places_kernel(own_ref, counts_ref, lengths_ref, chosen_ref, kpos_ref, qpos_ref, qlow_ref):
    core = own_ref[0] % 2
    devices, capacity = chosen_ref.shape
    tok_rows = lengths_ref[lengths_ref.shape[0] - 1]
    slot = lax.broadcasted_iota(jnp.int32, (1, capacity), 1)
    ends = []
    for k in range(lengths_ref.shape[0] - 1):
        ends.append(lengths_ref[k] + (ends[-1] if ends else 0))

    def place(device):
        value = device * tok_rows + chosen_ref[pl.ds(device, 1), :]
        return value, slot < counts_ref[device]

    def key_row(device):
        value, live = place(device)
        return jnp.where(live, value.astype(f32), far_away)

    for m in range(2):
        parity = jnp.bitwise_xor(core, m)
        for c in range(0, devices // 2, 2):
            tile = jnp.concatenate([key_row(2 * c + parity), key_row(2 * c + 2 + parity)], axis=1)
            kpos_ref[m : m + 1, c * capacity : (c + 2) * capacity] = tile
    blocks = qpos_ref.shape[0]
    sources = devices // 2 // blocks
    for b in range(blocks):
        lows, highs = [], []
        for c in range(b * sources, (b + 1) * sources):
            value, live = place(2 * c + core)
            low = jnp.zeros_like(value)
            for end in ends:
                low = jnp.maximum(low, jnp.where(value >= end, end, 0))
            both = jnp.concatenate([jnp.where(live, value, -1), low], axis=0).astype(f32)
            lows.append(both[:, :HALF])
            highs.append(both[:, HALF:])
        both = jnp.concatenate(lows + highs, axis=1)
        qpos_ref[b : b + 1, :] = both[:1]
        qlow_ref[b : b + 1, :] = both[1:]


def fetch_kernel(own_ref, counts_ref, chosen_ref, tokens_ref, grads_ref, both_ref, rows_ref, upstream_ref):
    hot = one_hot(own_ref, counts_ref, chosen_ref, tokens_ref.shape[0], False)
    capacity = hot.shape[1]
    pick = jnp.transpose(jnp.concatenate([hot, jnp.zeros_like(hot)], axis=1))[:capacity].astype(bf16)
    live = live_column(own_ref, counts_ref, capacity)
    rows = nn(pick, tokens_ref[...]).astype(bf16)
    upstream = jnp.where(live, nn(pick, grads_ref[...]), 0.0).astype(bf16)
    both_ref[0, :capacity, :] = rows
    both_ref[0, capacity:, :] = upstream
    rows_ref[0] = rows
    upstream_ref[0] = upstream


def project_kernel(own_ref, counts_ref, vectors_ref, wq, wk, wv, *rest):
    pieces, sent_ref = rest[:-1], rest[-1]
    head = own_ref[0] // 2
    core = own_ref[0] % 2
    even = head % 2 == 0
    k = 0
    weights = None
    for piece in pieces:
        blocks, capacity, width = piece.shape
        rows = piece[...].reshape(blocks * capacity, width).astype(f32)
        gate = gate_of(rows, vectors_ref)
        normed = (rows * inverse_rms(rows) * vectors_ref[1:2, :]).astype(bf16)
        if weights is None:
            w_pair = jnp.where(even, joined(wk[...], swapped(wv[...])), joined(swapped(wk[...]), wv[...]))
            weights = jnp.concatenate([w_pair, jnp.where(even, wq[...], swapped(wq[...]))], axis=1)
        product = nn(normed, weights)
        for j in range(blocks):
            chip = chip_of(own_ref, k)
            block = product[j * capacity : (j + 1) * capacity]
            query = block[:, LANES:]
            sent_ref[chip, :HALF, :] = joined(query[:HALF], swapped(query[HALF:])).astype(bf16)
            sent_ref[chip, HALF : HALF + SHARE, :] = block[:, :LANES].astype(bf16)
            slot = lax.broadcasted_iota(jnp.int32, (capacity, 1), 0)
            live = slot < counts_ref[2 * chip + core]
            part = jnp.where(live, gate[j * capacity : (j + 1) * capacity], 0.0)
            part = jnp.sum(part, axis=0, keepdims=True)
            sent_ref[chip, HALF + SHARE :, :] = in_parts(jnp.broadcast_to(part, (NOTE, LANES)))
            k += 1


def unpack_kernel(got_ref, mixed_ref):
    mixed_ref[0] = unpack_rows(got_ref, 0, HALF)


CHUNKS = 4
PIECES = (5, 4, 5)


def middle_kernel(
    own_ref, counts_ref, mixed_ref, total_ref, both_ref, vectors_ref, out_ref, up_ref, down_ref,
    sent_ref, new_ref, dmiddle_ref, dweight_ref, w_out, w_up, w_down, hidden_ref, active_ref, sems,
):
    width, total_cols = up_ref.shape
    cols = total_cols // CHUNKS
    copies = [pltpu.make_async_copy(out_ref, w_out, sems.at[0])]
    for c in range(CHUNKS):
        part = pl.ds(c * cols, cols)
        copies.append(pltpu.make_async_copy(up_ref.at[:, part], w_up.at[:, part], sems.at[1 + c]))
    for c in range(CHUNKS):
        part = pl.ds(c * cols, cols)
        copies.append(pltpu.make_async_copy(down_ref.at[part, :], w_down.at[part, :], sems.at[1 + CHUNKS + c]))
    for copy in copies:
        copy.start()
    capacity = mixed_ref.shape[1]
    rows = both_ref[0, :capacity, :].astype(f32)
    upstream = both_ref[0, capacity:, :].astype(f32)
    live = live_column(own_ref, counts_ref, capacity)
    gate = gate_of(rows, vectors_ref)
    ratio = total_count(counts_ref) / total_ref[:1, :1]
    scaling = gate * ratio
    gain = vectors_ref[2:3, :]
    dbranch = scaling * upstream
    dmlp = dbranch.astype(bf16)
    copies[0].wait()
    attn_out = nn(mixed_ref[0], w_out[...])
    middle = rows + attn_out
    scale = inverse_rms(middle)
    normed = (middle * scale * gain).astype(bf16)
    for c in range(CHUNKS):
        copies[1 + c].wait()
        hidden_ref[:, c * cols : (c + 1) * cols] = nn(normed, w_up[:, c * cols : (c + 1) * cols])
    dnormed = jnp.zeros((capacity, width), f32)
    for c in range(CHUNKS):
        part = slice(c * cols, (c + 1) * cols)
        copies[1 + CHUNKS + c].wait()
        hidden = hidden_ref[:, part]
        value, slope = gelu_pair(hidden)
        active_ref[:, part] = value.astype(bf16)
        dhidden = (nt(dmlp, w_down[part, :]) * slope).astype(bf16)
        dnormed = dnormed + nt(dhidden, w_up[:, part])
    branch = attn_out + nn(active_ref[...], w_down[...])
    new_ref[...] = (rows + scaling * branch).astype(bf16)
    dweight = jnp.sum(upstream * branch, axis=1, keepdims=True)
    dweight_ref[...] = jnp.broadcast_to(dweight, dweight_ref.shape)
    scaled = gain * dnormed
    dmiddle = scale * scaled - middle * (scale * scale * scale) * jnp.mean(scaled * middle, axis=-1, keepdims=True)
    dmiddle_ref[...] = dmiddle
    dattn = (dbranch + dmiddle).astype(bf16)
    pack_rows(sent_ref, 0, nt(dattn, w_out[...]).astype(bf16))
    pack_rows(sent_ref, HALF, dattn)
    write_note(sent_ref, 2 * HALF, jnp.sum(jnp.where(live, dweight * gate, 0.0), axis=0, keepdims=True))


def put_kernel(own_ref, counts_ref, chosen_ref, old_ref, new_ref, result_ref):
    put_rows(own_ref, counts_ref, chosen_ref, old_ref, new_ref[...], result_ref)


def put_rows(own_ref, counts_ref, chosen_ref, old_ref, new, result_ref):
    hot = one_hot(own_ref, counts_ref, chosen_ref, old_ref.shape[0], True)
    hit = jnp.sum(hot, axis=1, keepdims=True) > 0.5
    placed = nn(hot.astype(bf16), new)
    result_ref[...] = jnp.where(hit, placed, old_ref[...].astype(f32)).astype(bf16)


def router_slope(own_ref, counts_ref, rows, dweight_ref, total_ref, coef_ref, vectors_ref):
    gate = gate_of(rows, vectors_ref)
    live = live_column(own_ref, counts_ref, rows.shape[0])
    count = total_count(counts_ref)
    total = total_ref[:1, :1]
    dscore = dweight_ref[:, :1] * (count / total) - coef_ref[:1, :1] * count / (total * total)
    return jnp.where(live, dscore * gate * (1.0 - gate), 0.0)


def keys_kernel(dq_ref, dkv_ref, moved_ref, coef_ref, sent_ref, sum_ref):
    rows = dkv_ref.shape[0]
    sent_ref[:, :HALF, :] = dq_ref[...]
    dkv = dkv_ref[...] + moved_ref[:rows, :]
    sent_ref[:, HALF:, :] = dkv.astype(bf16).reshape(sent_ref.shape[0], SHARE, LANES)
    sum_ref[...] = coef_ref[...] + moved_ref[rows:, :]


def units_kernel(
    own_ref, counts_ref, got_ref, dqkv_ref, total_ref, coef_ref, vectors_ref, rows_ref, dweight_ref,
    out_ref, up_ref, down_ref, *rest,
):
    gathers = []
    for count in PIECES:
        gathers.append(rest[:count])
        rest = rest[count:]
    down_keep_ref, down_give_ref, keep_ref, give_ref, rest = *rest[:4], rest[4:]
    *slots, grad_up, grad_down, grad_out, grad_q, grad_kv, ratio_ref, sems = rest
    rows_slots, upstream_slots, mixed_slots = slots
    step = pl.program_id(0)
    steps = pl.num_programs(0)
    _, sources, capacity, width = mixed_slots.shape
    core = own_ref[0] % 2
    slot = step % 2

    def copies(k):
        at = k % 2
        result = []
        for i, pieces in enumerate(gathers):
            if k < 3 or len(pieces) == 4:
                result.append(pltpu.make_async_copy(pieces[k], slots[i].at[at], sems.at[at, i, 0]))
                continue
            for half in range(2):
                target = slots[i].at[at, 2 * half : 2 * half + 2]
                result.append(pltpu.make_async_copy(pieces[k + half], target, sems.at[at, i, half]))
        return result

    for k in range(4):

        @pl.when(step == max(k - 1, 0))
        def _(k=k):
            for copy in copies(k):
                copy.start()

    @pl.when(step == 0)
    def _():
        for ref in (grad_up, grad_down, grad_out, grad_q, grad_kv):
            ref[...] = jnp.zeros_like(ref)
        ratio_ref[...] = jnp.broadcast_to(total_count(counts_ref) / total_ref[:1, :1], ratio_ref.shape)

    for k in range(4):

        @pl.when(step == k)
        def _(k=k):
            for copy in copies(k):
                copy.wait()

    def halves(ref, first):
        blocks = [ref[chip_of(own_ref, 4 * step + j), first : first + HALF, :] for j in range(sources)]
        turned = jnp.transpose(jnp.concatenate(blocks, axis=0).astype(f32)).astype(bf16)
        return turned[:HEAD_DIM], turned[HEAD_DIM:]

    def low_high(value):
        value = value.reshape(sources, capacity, width)
        return value[:, :HALF, :].reshape(sources * HALF, width), value[:, HALF:, :].reshape(sources * HALF, width)

    rows = rows_slots[slot].reshape(sources * capacity, width).astype(f32)
    upstream = upstream_slots[slot].reshape(sources * capacity, width).astype(f32)
    mixed = mixed_slots[slot].reshape(sources * capacity, width)
    normed_attn = (rows * inverse_rms(rows) * vectors_ref[1:2, :]).astype(bf16)
    low_query, high_query = halves(dqkv_ref, 0)
    low_rows, high_rows = low_high(normed_attn)
    grad_q[...] += nn(low_query, low_rows) + nn(high_query, high_rows)
    blocks = [dqkv_ref[chip_of(own_ref, 4 * step + j), HALF:, :] for j in range(sources)]
    pairs_turned = jnp.transpose(jnp.concatenate(blocks, axis=0).astype(f32)).astype(bf16)
    grad_kv[...] += nn(pairs_turned, normed_attn)
    low_attn, high_attn = halves(got_ref, HALF)
    low_mixed, high_mixed = low_high(mixed)
    grad_out[...] += nn(low_attn, low_mixed) + nn(high_attn, high_mixed)
    middle = rows + nn(mixed, out_ref[...])
    normed = (middle * inverse_rms(middle) * vectors_ref[2:3, :]).astype(bf16)
    dmlp = (gate_of(rows, vectors_ref) * ratio_ref[:1, :1] * upstream).astype(bf16)
    value, slope = gelu_pair(nn(normed, up_ref[...]))
    dhidden = nt(dmlp, down_ref[...]) * slope
    grad_down[...] += nn(jnp.transpose(value).astype(bf16), dmlp)
    grad_up[...] += nn(jnp.transpose(dhidden).astype(bf16), normed)

    @pl.when(step == steps - 1)
    def _():
        chips = keep_ref.shape[0]

        def split(value):
            value = value.reshape(chips, 2, OUT_ROWS, LANES)
            even, odd = value[:, 0], value[:, 1]
            return jnp.where(core == 0, even, odd), jnp.where(core == 0, odd, even)

        def store(first, kept, given):
            keep_ref[:, first : first + kept.shape[1], :] = kept
            give_ref[:, first : first + kept.shape[1], :] = given.astype(bf16)

        for t in range(TILES):
            store(t * OUT_ROWS, *split(jnp.transpose(grad_up[t * LANES : (t + 1) * LANES, :])))

        def two_in_one(value):
            return joined(value[:, :OUT_HALF], swapped(value[:, OUT_HALF:]))

        both_turned = jnp.transpose(jnp.concatenate([grad_out[...], grad_q[...]], axis=0))
        kept, given = split(both_turned)
        store(AT_OUT, two_in_one(kept), two_in_one(given))
        store(AT_QUERY, two_in_one(swapped(kept)), two_in_one(swapped(given)))
        store(AT_PAIR, *split(jnp.transpose(grad_kv[...])))
        own_rows = rows_ref[0, :capacity, :].astype(f32)
        dlogit = router_slope(own_ref, counts_ref, own_rows, dweight_ref, total_ref, coef_ref, vectors_ref)
        part = jnp.broadcast_to(jnp.sum(dlogit * own_rows, axis=0, keepdims=True), (NOTE, width))
        per_tile = LANES // OUT_ROWS
        for c in range(chips):
            tile = part[:, (2 * c) // per_tile * LANES : ((2 * c) // per_tile + 1) * LANES]
            shift = (2 * c) % per_tile * OUT_ROWS
            if shift:
                tile = jnp.concatenate([tile[:, shift:], tile[:, :shift]], axis=1)
            after = jnp.concatenate([tile[:, OUT_ROWS:], tile[:, :OUT_ROWS]], axis=1)
            keep_ref[c, AT_NOTE:, :] = jnp.where(core == 0, tile, after)
            give_ref[c, AT_NOTE:, :] = in_parts(jnp.where(core == 0, after, tile))
        down = grad_down[...]
        half = down.shape[0] // 2
        down_keep_ref[...] = jnp.where(core == 0, down[:half], down[half:])
        down_give_ref[...] = jnp.where(core == 0, down[half:], down[:half]).astype(bf16)


def merge_kernel(keep_ref, moved_ref, down_keep_ref, down_moved_ref, sent_ref, down_ref):
    sent_ref[:, :AT_NOTE, :] = (keep_ref[:, :AT_NOTE, :] + moved_ref[:, :AT_NOTE, :].astype(f32)).astype(bf16)
    note = keep_ref[:, AT_NOTE:, :] + jnp.sum(moved_ref[:, AT_NOTE:, :].astype(f32), axis=1, keepdims=True)
    sent_ref[:, AT_NOTE:, :] = in_parts(note)
    down_ref[...] = down_keep_ref[...] + down_moved_ref[...].astype(f32)


def rows_kernel(
    own_ref, counts_ref, chosen_ref, got_ref, both_ref, dmiddle_ref, dweight_ref, total_ref, coef_ref, vectors_ref,
    old_ref, wq_ref, wk_ref, wv_ref, grads_ref, wq, wk, wv, sems,
):
    copies = [
        pltpu.make_async_copy(source, target, sems.at[i])
        for i, (source, target) in enumerate(((wq_ref, wq), (wk_ref, wk), (wv_ref, wv)))
    ]
    for copy in copies:
        copy.start()
    capacity = dmiddle_ref.shape[0]
    rows = both_ref[0, :capacity, :].astype(f32)
    upstream = both_ref[0, capacity:, :].astype(f32)
    gain = vectors_ref[1:2, :]
    dlogit = router_slope(own_ref, counts_ref, rows, dweight_ref, total_ref, coef_ref, vectors_ref)
    partial = upstream + dmiddle_ref[...] + dlogit * vectors_ref[0:1, :]
    dquery = unpack_rows(got_ref, 0, HALF)
    dkey, dvalue = unpack_pairs(got_ref, HALF, SHARE)
    copies[0].wait()
    dnormed = jnp.zeros_like(partial) + nt(dquery, wq[...])
    copies[1].wait()
    dnormed = dnormed + nt(dkey, wk[...])
    copies[2].wait()
    dnormed = dnormed + nt(dvalue, wv[...])
    scale = inverse_rms(rows)
    scaled = gain * dnormed
    drows = scale * scaled - rows * (scale * scale * scale) * jnp.mean(scaled * rows, axis=-1, keepdims=True)
    put_rows(own_ref, counts_ref, chosen_ref, old_ref, (partial + drows).astype(bf16), grads_ref)


def finish_kernel(
    got_ref, own_gain_ref, up_ref, wq_ref, wk_ref, wv_ref,
    grad_up_ref, grad_out_ref, grad_q_ref, grad_k_ref, grad_v_ref, router_ref, gain_attn_ref, gain_mlp_ref,
):
    total = jnp.zeros((OUT_ROWS, LANES), f32)
    for c in range(got_ref.shape[0]):
        for t in range(TILES):
            lanes = slice((TILES * c + t) * LANES, (TILES * c + t + 1) * LANES)
            part = got_ref[c, t * OUT_ROWS : (t + 1) * OUT_ROWS, :].astype(f32)
            grad_up_ref[:, lanes] = part
            total = total + part * up_ref[:, lanes].astype(f32)
    gain_mlp_ref[...] = row_of(jnp.sum(total, axis=1, keepdims=True)) / own_gain_ref[2:3, :]
    grad_out_ref[...] = unpack_rows(got_ref, AT_OUT, OUT_HALF).astype(f32)
    grad_q = unpack_rows(got_ref, AT_QUERY, OUT_HALF).astype(f32)
    grad_k, grad_v = (value.astype(f32) for value in unpack_pairs(got_ref, AT_PAIR, OUT_ROWS))
    grad_q_ref[...] = grad_q
    grad_k_ref[...] = grad_k
    grad_v_ref[...] = grad_v
    products = wq_ref[...].astype(f32) * grad_q + wk_ref[...].astype(f32) * grad_k + wv_ref[...].astype(f32) * grad_v
    gain_attn_ref[...] = row_of(jnp.sum(products, axis=1, keepdims=True)) / own_gain_ref[1:2, :]
    notes = jnp.sum(got_ref[:, AT_NOTE:, :].astype(f32), axis=0)
    router_ref[...] = jnp.sum(notes, axis=0, keepdims=True)[:, :OUT_ROWS]


def pair_attend_kernel(factor, got_ref, other_ref, kpos_ref, qpos_ref, qlow_ref, mixed_ref, turned_ref, lse_ref, total_ref):
    lists = (got_ref, other_ref)
    chips = got_ref.shape[0]
    blocks = chips * HALF // BLOCK
    sources = chips // blocks
    total = read_note(got_ref, HALF + SHARE) + read_note(other_ref, HALF + SHARE)
    total_ref[...] = jnp.broadcast_to(total, total_ref.shape)
    attend_core(
        factor,
        lambda b: got_ref[b * sources : (b + 1) * sources, :HALF, :].reshape(BLOCK, LANES),
        lambda m, extent: lists[m][: extent // SHARE, HALF : HALF + SHARE, :].reshape(extent, LANES),
        2, blocks, chips * SHARE, kpos_ref, qpos_ref, qlow_ref, mixed_ref, turned_ref, lse_ref,
    )


def pair_attend_back_kernel(
    factor, got_ref, other_ref, grad_ref, kpos_ref, qpos_ref, qlow_ref, turned_ref, lse_ref,
    dq_ref, own_ref, moved_ref, coef_ref,
):
    lists = (got_ref, other_ref)
    sums = (own_ref, moved_ref)
    chips = got_ref.shape[0]
    blocks = chips * HALF // BLOCK
    sources = chips // blocks
    coef = jnp.broadcast_to(read_note(grad_ref, 2 * HALF), coef_ref.shape)
    coef_ref[...] = coef
    moved_ref[chips * SHARE :, :] = coef

    def add_dkv(m, extent, first, update):
        if first:
            sums[m][:extent, :] = update
        else:
            sums[m][:extent, :] += update

    attend_back_core(
        factor,
        lambda b: got_ref[b * sources : (b + 1) * sources, :HALF, :].reshape(BLOCK, LANES),
        lambda b: grad_ref[b * sources : (b + 1) * sources, :HALF, :].reshape(BLOCK, LANES),
        lambda m, extent: lists[m][: extent // SHARE, HALF : HALF + SHARE, :].reshape(extent, LANES),
        2, blocks, chips * SHARE, kpos_ref, qpos_ref, qlow_ref, turned_ref, lse_ref, dq_ref, add_dkv,
    )


smem = pl.BlockSpec(memory_space=pltpu.SMEM)
hbm = pl.BlockSpec(memory_space=pl.ANY)
megabytes = {
    "places": 4, "fetch": 56, "project": 16, "attend": 20, "unpack": 4, "middle": 56, "put": 56, "attend_back": 24,
    "keys": 8, "units": 56, "merge": 10, "rows": 56, "finish": 12,
}


def params_of(name):
    return pltpu.CompilerParams(vmem_limit_bytes=megabytes[name] * 1024 * 1024)


def shaped(shape, dtype):
    return jax.ShapeDtypeStruct(shape, dtype)


microseconds = {
    "places": 1, "fetch": 3, "project": 4, "attend": 5, "unpack": 2, "middle": 15, "put": 3, "attend_back": 6, "keys": 2,
    "units": 16, "merge": 3, "rows": 7, "finish": 2,
}


def cost_of(name):
    return pl.CostEstimate(flops=0, transcendentals=0, bytes_accessed=microseconds[name] * 3_300_000)


def call(kernel, name, in_specs, out_shape, arguments, scratch=()):
    return pl.pallas_call(
        kernel,
        out_shape=out_shape,
        in_specs=in_specs,
        out_specs=jax.tree.map(lambda _: vmem, out_shape),
        scratch_shapes=list(scratch),
        compiler_params=params_of(name),
        cost_estimate=cost_of(name),
        name=name,
    )(*arguments)


def pairs(
    tokens_in,
    w_router,
    gain_attn,
    w_query,
    w_key,
    w_value,
    w_out,
    gain_mlp,
    w_up,
    w_down,
    out_grad,
    lengths,
    counts,
    chosen,
):
    devices = lax.axis_size("seq")
    chips = devices // 2
    own = lax.axis_index("seq")
    capacity = chosen.shape[0] // devices
    tok_rows, width = tokens_in.shape
    hidden_width = w_up.shape[1]
    out_rows = width // devices
    factor = HEAD_DIM ** (-0.5)
    core = own % 2
    own_id = own.astype(jnp.int32).reshape(1)
    chosen = chosen.reshape(devices, capacity)
    vectors = jnp.stack([w_router, gain_attn, gain_mlp]).astype(f32)
    own_gains = lax.dynamic_slice_in_dim(vectors, own * out_rows, out_rows, 1)
    cores = [[2 * c + k for c in range(chips)] for k in range(2)]

    def swap(value):
        return lax.all_to_all(value, "seq", split_axis=0, concat_axis=0, tiled=True, axis_index_groups=cores)

    def across(value, bits):
        return lax.ppermute(value, "seq", [(s, s ^ bits) for s in range(devices)])

    def line_of(block):
        return jnp.concatenate([block] + [across(block, 8 * k) for k in (1, 2, 3)], axis=0)

    def sides_of(line):
        return [line, across(line, 2), across(line, 4)]

    def gathered(sides):
        return sides + [across(sides[2][:2], 2), across(sides[1][2:], 4)]

    def gathered_whole(sides):
        return sides + [across(sides[2], 2)]

    blocks = chips * HALF // BLOCK
    square = pltpu.VMEM((width, width), bf16)
    block = shaped((1, capacity, width), bf16)
    both, own_rows, own_upstream = call(
        fetch_kernel, "fetch", [smem, smem] + [vmem] * 3, (shaped((1, 2 * capacity, width), bf16), block, block),
        (own_id, counts, chosen, tokens_in, out_grad),
    )
    rows_line = line_of(own_rows)
    chosen_after, rows_line = lax.optimization_barrier((chosen, rows_line))
    kpos, qpos, qlow = call(
        places_kernel, "places", [smem] * 3 + [vmem],
        (
            shaped((2, chips * SHARE), f32),
            shaped((blocks, 2 * BLOCK), f32),
            shaped((blocks, 2 * BLOCK), f32),
        ),
        (own_id, counts, jnp.append(lengths, tok_rows), chosen_after),
    )
    rows_all = gathered(sides_of(rows_line))
    column = own // 4 * LANES
    columns = [lax.dynamic_slice_in_dim(w, column, LANES, 1) for w in (w_query, w_key, w_value)]
    upstream_line = line_of(own_upstream)
    rows_all, upstream_line = lax.optimization_barrier((rows_all, upstream_line))
    kpos, qpos, qlow, columns, rows_all = lax.optimization_barrier((kpos, qpos, qlow, columns, rows_all))
    got = call(
        project_kernel, "project", [smem, smem] + [vmem] * 9,
        shaped((chips, HALF + SHARE + NOTE, LANES), bf16),
        (own_id, counts, vectors, *columns, *rows_all),
    )
    other = across(got, 1)
    upstream_sides = sides_of(upstream_line)
    mixed_packed, turned, lse, total = call(
        functools.partial(pair_attend_kernel, factor), "attend", [vmem] * 5,
        (
            shaped((chips * HALF, LANES), bf16),
            shaped((chips * HALF, LANES), f32),
            shaped((blocks, 2 * BLOCK), f32),
            shaped((8, LANES), f32),
        ),
        (got, other, kpos, qpos, qlow),
    )
    mixed_got = swap(mixed_packed.reshape(chips, HALF, LANES))
    upstream_sides, mixed_got = lax.optimization_barrier((upstream_sides, mixed_got))
    upstream_all = gathered_whole(upstream_sides)
    mixed = call(unpack_kernel, "unpack", [vmem], shaped((1, capacity, width), bf16), (mixed_got,))
    mixed_line = line_of(mixed)
    sent, new_rows, dmiddle, dweight = call(
        middle_kernel, "middle", [smem, smem] + [vmem] * 4 + [hbm] * 3,
        (
            shaped((chips, 2 * HALF + NOTE, LANES), bf16),
            shaped((capacity, width), bf16),
            shaped((capacity, width), f32),
            shaped((capacity, LANES), f32),
        ),
        (own_id, counts, mixed, total, both, vectors, w_out, w_up, w_down),
        [
            square,
            pltpu.VMEM((width, hidden_width), bf16),
            pltpu.VMEM((hidden_width, width), bf16),
            pltpu.VMEM((capacity, hidden_width), f32),
            pltpu.VMEM((capacity, hidden_width), bf16),
            pltpu.SemaphoreType.DMA((1 + 2 * CHUNKS,)),
        ],
    )
    mixed_line, sent = lax.optimization_barrier((mixed_line, sent))
    mixed_sides = sides_of(mixed_line)
    upstream_all, sent = lax.optimization_barrier((upstream_all, sent))
    grads_got = swap(sent)
    mixed_all = gathered(mixed_sides)
    output = call(
        put_kernel, "put", [smem, smem] + [vmem] * 3, shaped((tok_rows, width), bf16),
        (own_id, counts, chosen, tokens_in, new_rows),
    )
    dq, dkv_own, dkv_other, coef = call(
        functools.partial(pair_attend_back_kernel, factor), "attend_back", [vmem] * 8,
        (
            shaped((chips * HALF, LANES), bf16),
            shaped((chips * SHARE, LANES), f32),
            shaped((chips * SHARE + 8, LANES), f32),
            shaped((8, LANES), f32),
        ),
        (got, other, grads_got, kpos, qpos, qlow, turned, lse),
    )
    moved = across(dkv_other, 1)
    dqkv, coef = call(
        keys_kernel, "keys", [vmem] * 4,
        (shaped((chips, HALF + SHARE, LANES), bf16), shaped((8, LANES), f32)),
        (dq.reshape(chips, HALF, LANES), dkv_own, moved, coef),
    )
    got = swap(dqkv)
    sources = 4
    hidden_cols = hidden_width // chips
    whole = lambda *shape: pl.BlockSpec(shape, lambda i, o: (0,) * len(shape))
    down_keep, down_give, keep, give = pl.pallas_call(
        units_kernel,
        out_shape=(
            shaped((hidden_cols // 2, width), f32),
            shaped((hidden_cols // 2, width), bf16),
            shaped((chips, GRAD_ROWS, LANES), f32),
            shaped((chips, GRAD_ROWS, LANES), bf16),
        ),
        grid_spec=pltpu.PrefetchScalarGridSpec(
            num_scalar_prefetch=1,
            grid=(chips // sources,),
            in_specs=[
                smem,
                whole(chips, 2 * HALF + NOTE, LANES),
                whole(chips, HALF + SHARE, LANES),
                whole(8, LANES),
                whole(8, LANES),
                whole(3, width),
                whole(1, 2 * capacity, width),
                whole(capacity, LANES),
                whole(width, width),
                pl.BlockSpec((width, hidden_cols), lambda i, o: (0, o[0] // 2)),
                pl.BlockSpec((hidden_cols, width), lambda i, o: (o[0] // 2, 0)),
            ]
            + [hbm] * sum(PIECES),
            out_specs=(
                whole(hidden_cols // 2, width),
                whole(hidden_cols // 2, width),
                whole(chips, GRAD_ROWS, LANES),
                whole(chips, GRAD_ROWS, LANES),
            ),
            scratch_shapes=[
                pltpu.VMEM((2, sources, capacity, width), bf16),
                pltpu.VMEM((2, sources, capacity, width), bf16),
                pltpu.VMEM((2, sources, capacity, width), bf16),
                pltpu.VMEM((hidden_cols, width), f32),
                pltpu.VMEM((hidden_cols, width), f32),
                pltpu.VMEM((HEAD_DIM, width), f32),
                pltpu.VMEM((HEAD_DIM, width), f32),
                pltpu.VMEM((2 * HEAD_DIM, width), f32),
                pltpu.VMEM((8, LANES), f32),
                pltpu.SemaphoreType.DMA((2, 3, 2)),
            ],
        ),
        compiler_params=params_of("units"),
        cost_estimate=cost_of("units"),
        name="units",
    )(own_id, counts, grads_got, dqkv, total, coef, vectors, both, dweight, w_out, w_up, w_down, *rows_all, *upstream_all, *mixed_all)
    sent, grad_down = call(
        merge_kernel, "merge", [vmem] * 4,
        (shaped((chips, GRAD_ROWS, LANES), bf16), shaped((hidden_cols // 2, width), f32)),
        (keep, across(give, 1), down_keep, across(down_give, 1)),
    )
    last = swap(sent)
    input_grad = call(
        rows_kernel, "rows", [smem, smem] + [vmem] * 9 + [hbm] * 3, shaped((tok_rows, width), bf16),
        (
            own_id, counts, chosen, got, both, dmiddle, dweight, total, coef, vectors, out_grad,
            w_query, w_key, w_value,
        ),
        [square] * 3 + [pltpu.SemaphoreType.DMA((3,))],
    )
    block = shaped((out_rows, width), f32)
    row = shaped((1, out_rows), f32)
    first_row = own * out_rows
    grad_up, grad_out, grad_query, grad_key, grad_value, grad_router, grad_gain_attn, grad_gain_mlp = call(
        finish_kernel, "finish", [vmem] * 6,
        (shaped((out_rows, hidden_width), f32), block, block, block, block, row, row, row),
        (last, own_gains, *(lax.dynamic_slice_in_dim(w, first_row, out_rows) for w in (w_up, w_query, w_key, w_value))),
    )
    return (
        output,
        input_grad,
        grad_router.reshape(out_rows),
        grad_gain_attn.reshape(out_rows),
        grad_query,
        grad_key,
        grad_value,
        grad_out,
        grad_gain_mlp.reshape(out_rows),
        grad_up,
        grad_down,
    )


def per_device(*arguments):
    w_up, chosen = arguments[8], arguments[13]
    devices = lax.axis_size("seq")
    width, hidden_width = w_up.shape
    paired = (
        devices == 2 * HEADS
        and chosen.shape[0] == devices * SHARE
        and width == devices * OUT_ROWS
        and width == HEADS * HEAD_DIM
        and hidden_width == devices // 2 * TILES * LANES
    )
    return (pairs if paired else general)(*arguments)


def solution(mesh):
    placed = (P("seq", None),) + (P(),) * 9 + (P("seq", None),) + (P(),) * 3
    rows = P("seq", None)
    return jax.shard_map(
        per_device,
        mesh=mesh,
        in_specs=placed,
        out_specs=(rows, rows, P("seq"), P("seq"), rows, rows, rows, rows, P("seq"), rows, rows),
        check_vma=False,
    )
```

```python
import functools
import jax
import jax.numpy as jnp
from jax import lax
from jax.experimental import pallas as pl
from jax.experimental.pallas import tpu as pltpu
from jax.sharding import PartitionSpec as P

HEADS = 16
HEAD_DIM = 64
LANES = 128
BLOCK = 128

masked_score = -1e30
eps_norm = 1e-05
far_away = 1e9

f32 = jnp.float32
bf16 = jnp.bfloat16


def nt(left, right):
    return lax.dot_general(left, right, (((1,), (1,)), ((), ())), preferred_element_type=f32)


def nn(left, right):
    return lax.dot_general(left, right, (((1,), (0,)), ((), ())), preferred_element_type=f32)


def rms_scale(values, gain):
    return values * lax.rsqrt(jnp.mean(values * values, axis=-1, keepdims=True) + eps_norm) * gain


def three_parts(value):
    high = lax.reduce_precision(value, 8, 7)
    rest = value - high
    middle = lax.reduce_precision(rest, 8, 7)
    return jnp.stack([high, middle, rest - middle]).astype(bf16)


def spread_rows(packed, upper):
    lanes = lax.broadcasted_iota(jnp.int32, packed.shape, 1)
    zero = jnp.zeros_like(packed)
    rolled = jnp.concatenate([packed[:, HEAD_DIM:], packed[:, :HEAD_DIM]], axis=1)
    if upper:
        return jnp.concatenate(
            [jnp.where(lanes >= HEAD_DIM, rolled, zero), jnp.where(lanes >= HEAD_DIM, packed, zero)], axis=0
        )
    return jnp.concatenate(
        [jnp.where(lanes < HEAD_DIM, packed, zero), jnp.where(lanes < HEAD_DIM, rolled, zero)], axis=0
    )


def pack_columns(turned):
    return jnp.concatenate([turned[:, :BLOCK], turned[:, BLOCK:]], axis=0)


def key_columns(kpos_ref, member, extent):
    row = kpos_ref[member : member + 1, :extent]
    column = jnp.transpose(jnp.broadcast_to(row, (LANES, extent)))
    return jnp.concatenate([column, column], axis=1)


def attend_core(factor, load_query, load_kv, members, blocks, key_rows, kpos_ref, qpos_ref, qlow_ref, mixed_ref, turned_ref, lse_ref):
    kv_turned = [jnp.transpose(load_kv(m, key_rows)) for m in range(members)]
    for b in range(blocks):
        extent = key_rows * (b + 1) // blocks
        packed = (load_query(b).astype(f32) * factor).astype(bf16)
        wide = spread_rows(packed, False)
        qpos = qpos_ref[b : b + 1, :]
        qlow = qlow_ref[b : b + 1, :]
        scores = []
        for m in range(members):
            score = nt(load_kv(m, extent), wide)
            kpos = key_columns(kpos_ref, m, extent)
            score = jnp.where((kpos <= qpos) & (kpos >= qlow), score, masked_score)
            scores.append(score)
        peak = jnp.max(scores[0], axis=0, keepdims=True)
        for score in scores[1:]:
            peak = jnp.maximum(peak, jnp.max(score, axis=0, keepdims=True))
        peak = jnp.maximum(peak, 0.1 * masked_score)
        total = jnp.zeros_like(peak)
        mixed = jnp.zeros((LANES, 2 * BLOCK), f32)
        for m in range(members):
            prob = jnp.exp(scores[m] - peak)
            total = total + jnp.sum(prob, axis=0, keepdims=True)
            mixed = mixed + nn(kv_turned[m][:, :extent], prob.astype(bf16))
        safe = jnp.where(total > 0, total, 1.0)
        lse_ref[b : b + 1, :] = peak + jnp.log(safe)
        turned = pack_columns(mixed[HEAD_DIM:, :] / safe)
        turned_ref[b * BLOCK : (b + 1) * BLOCK, :] = turned
        mixed_ref[b * BLOCK : (b + 1) * BLOCK, :] = jnp.transpose(turned).astype(bf16)


def attend_back_core(
    factor, load_query, load_grad, load_kv, members, blocks, key_rows, kpos_ref, qpos_ref, qlow_ref, turned_ref, lse_ref,
    dq_ref, add_dkv,
):
    kv_turned = [jnp.transpose(load_kv(m, key_rows)) for m in range(members)]
    for b in range(blocks - 1, -1, -1):
        extent = key_rows * (b + 1) // blocks
        rows = slice(b * BLOCK, (b + 1) * BLOCK)
        packed = (load_query(b).astype(f32) * factor).astype(bf16)
        grads = load_grad(b)
        wide = jnp.concatenate([spread_rows(packed, False), spread_rows(grads, True)], axis=0)
        product = jnp.transpose(grads.astype(f32)) * turned_ref[rows, :]
        delta = jnp.concatenate(
            [
                jnp.sum(product[:HEAD_DIM], axis=0, keepdims=True),
                jnp.sum(product[HEAD_DIM:], axis=0, keepdims=True),
            ],
            axis=1,
        )
        qpos = qpos_ref[b : b + 1, :]
        qlow = qlow_ref[b : b + 1, :]
        lse = lse_ref[b : b + 1, :]
        dquery = jnp.zeros((LANES, 2 * BLOCK), f32)
        for m in range(members):
            both = nt(load_kv(m, extent), wide)
            kpos = key_columns(kpos_ref, m, extent)
            prob = jnp.exp(
                jnp.where((kpos <= qpos) & (kpos >= qlow), both[:, : 2 * BLOCK] - lse, masked_score)
            )
            dlogit = (prob * (both[:, 2 * BLOCK :] - delta)).astype(bf16)
            dquery = dquery + nn(kv_turned[m][:, :extent], dlogit)
            add_dkv(m, extent, b == blocks - 1, nn(jnp.concatenate([dlogit, prob.astype(bf16)], axis=1), wide))
        dq_ref[rows, :] = jnp.transpose(pack_columns(dquery[:HEAD_DIM, :] * factor)).astype(bf16)


def attend_kernel(factor, q_ref, kv_ref, kpos_ref, qpos_ref, qlow_ref, mixed_ref, turned_ref, lse_ref):
    members, key_rows, _ = kv_ref.shape
    attend_core(
        factor,
        lambda b: q_ref[b * BLOCK : (b + 1) * BLOCK, :],
        lambda m, extent: kv_ref[m, :extent, :],
        members, q_ref.shape[0] // BLOCK, key_rows, kpos_ref, qpos_ref, qlow_ref, mixed_ref, turned_ref, lse_ref,
    )


def attend_back_kernel(
    factor, q_ref, do_ref, kv_ref, kpos_ref, qpos_ref, qlow_ref, turned_ref, lse_ref, dq_ref, dkv_ref
):
    members, key_rows, _ = kv_ref.shape

    def add_dkv(m, extent, first, update):
        if first:
            dkv_ref[m, :extent, :] = update
        else:
            dkv_ref[m, :extent, :] += update

    attend_back_core(
        factor,
        lambda b: q_ref[b * BLOCK : (b + 1) * BLOCK, :],
        lambda b: do_ref[b * BLOCK : (b + 1) * BLOCK, :],
        lambda m, extent: kv_ref[m, :extent, :],
        members, q_ref.shape[0] // BLOCK, key_rows, kpos_ref, qpos_ref, qlow_ref, turned_ref, lse_ref, dq_ref, add_dkv,
    )


vmem = pl.BlockSpec(memory_space=pltpu.VMEM)
vmem_limit = 56 * 1024 * 1024


def attend(factor, queries, kv, kpos, qpos, qlow):
    rows = queries.shape[0]
    return pl.pallas_call(
        functools.partial(attend_kernel, factor),
        out_shape=(
            jax.ShapeDtypeStruct((rows, LANES), bf16),
            jax.ShapeDtypeStruct((rows, LANES), f32),
            jax.ShapeDtypeStruct(qpos.shape, f32),
        ),
        in_specs=[vmem] * 5,
        out_specs=(vmem,) * 3,
        compiler_params=pltpu.CompilerParams(vmem_limit_bytes=vmem_limit),
        name="attend",
    )(queries, kv, kpos, qpos, qlow)


def attend_back(factor, queries, dmixed, kv, kpos, qpos, qlow, turned, lse):
    rows = queries.shape[0]
    return pl.pallas_call(
        functools.partial(attend_back_kernel, factor),
        out_shape=(
            jax.ShapeDtypeStruct((rows, LANES), bf16),
            jax.ShapeDtypeStruct(kv.shape, f32),
        ),
        in_specs=[vmem] * 8,
        out_specs=(vmem,) * 2,
        compiler_params=pltpu.CompilerParams(vmem_limit_bytes=vmem_limit),
        name="attend_back",
    )(queries, dmixed, kv, kpos, qpos, qlow, turned, lse)


def general(
    tokens_in,
    w_router,
    gain_attn,
    w_query,
    w_key,
    w_value,
    w_out,
    gain_mlp,
    w_up,
    w_down,
    out_grad,
    lengths,
    counts,
    chosen,
):
    devices = lax.axis_size("seq")
    own = lax.axis_index("seq")
    capacity = chosen.shape[0] // devices
    tok_rows, width = tokens_in.shape
    hidden_width = w_up.shape[1]
    group = devices // HEADS
    share = capacity // group
    half = share // 2
    member = own % group
    slots = devices * capacity
    factor = HEAD_DIM ** (-0.5)
    attn_gain = gain_attn.astype(f32)
    mlp_gain = gain_mlp.astype(f32)

    def swap(value):
        return lax.all_to_all(value, "seq", split_axis=0, concat_axis=0, tiled=True)

    groups = [[h * group + m for m in range(group)] for h in range(HEADS)]

    def across_group(value):
        if group == 2:
            other = lax.ppermute(value, "seq", [(s, s ^ 1) for s in range(devices)])
            return jnp.stack([value, other])
        return lax.all_gather(value, "seq", axis_index_groups=groups)

    def sum_over_group(value):
        if group == 2:
            return value[0] + lax.ppermute(value[1], "seq", [(s, s ^ 1) for s in range(devices)])
        return lax.psum_scatter(value, "seq", scatter_dimension=0, axis_index_groups=groups)

    def member_order(value):
        if group == 2:
            return jnp.where(member == 0, value, value[::-1])
        return value

    slot_ids = jnp.arange(capacity, dtype=jnp.int32)
    places = jnp.arange(devices, dtype=jnp.int32)[:, None] * tok_rows + chosen.reshape(devices, capacity)
    live_all = slot_ids[None, :] < counts[:, None]
    seq_ends = jnp.cumsum(lengths)
    starts = jnp.max(jnp.where(places[..., None] >= seq_ends, seq_ends, 0), axis=-1)
    kpos = jnp.where(live_all, places.astype(f32), far_away)
    kpos = member_order(kpos.reshape(devices, group, share).swapaxes(0, 1).reshape(group, devices * share))
    blocks = devices * half // BLOCK

    def query_order(value):
        value = lax.dynamic_index_in_dim(value.reshape(devices, group, share), member, 1, False)
        return value.reshape(blocks, devices // blocks, 2, half).swapaxes(1, 2).reshape(blocks, 2 * BLOCK)

    qpos = query_order(jnp.where(live_all, places, -1).astype(f32))
    qlow = query_order(starts.astype(f32))

    offsets = lax.dynamic_slice_in_dim(chosen, own * capacity, capacity)
    live = slot_ids < counts[own]
    pick = (offsets[:, None] == jnp.arange(tok_rows, dtype=jnp.int32)[None, :]).astype(bf16)
    routed = nn(pick, tokens_in)
    upstream = jnp.where(live[:, None], nn(pick, out_grad), 0.0)
    gate = jax.nn.sigmoid(jnp.sum(routed * w_router.astype(f32)[None, :], axis=1))
    gate_sum = jnp.sum(jnp.where(live, gate, 0.0))
    normed = rms_scale(routed, attn_gain).astype(bf16)
    normed_all = lax.all_gather(normed, "seq", axis=0, tiled=True)
    queries = nn(normed, w_query).astype(bf16)
    keys = nn(normed, w_key).astype(bf16)
    values = nn(normed, w_value).astype(bf16)

    def note(value):
        parts = jnp.pad(three_parts(value), (0, LANES - 3))
        return jnp.broadcast_to(parts, (devices, 8, LANES))

    def read_note(rows):
        return jnp.sum(rows[:, 0, :3].astype(f32))

    def to_heads(value, per_row):
        if per_row == 2:
            value = value.reshape(group, 2, half, HEADS, HEAD_DIM).transpose(3, 0, 2, 1, 4)
            return value.reshape(devices, half, LANES)
        return value

    def pair_to_heads(first, second):
        both = jnp.stack([first, second], axis=1).reshape(group, share, 2, HEADS, HEAD_DIM)
        return both.transpose(3, 0, 1, 2, 4).reshape(devices, share, LANES)

    def from_heads(value):
        value = value.reshape(HEADS, group, half, 2, HEAD_DIM).transpose(1, 3, 2, 0, 4)
        return value.reshape(capacity, HEADS * HEAD_DIM)

    def pair_from_heads(value):
        value = value.reshape(HEADS, group, share, 2, HEAD_DIM).transpose(3, 1, 2, 0, 4)
        value = value.reshape(2, capacity, HEADS * HEAD_DIM)
        return value[0], value[1]

    sent = jnp.concatenate([to_heads(queries, 2), pair_to_heads(keys, values), note(gate_sum)], axis=1)
    got = swap(sent)
    score_total = read_note(got[:, half + share :])
    chosen_total = jnp.sum(counts).astype(f32)
    ratio = chosen_total / score_total
    scaling = gate * ratio
    head_queries = got[:, :half].reshape(devices * half, LANES)
    kv = across_group(got[:, half : half + share].reshape(devices * share, LANES))
    mixed_packed, mixed_turned, lse = attend(factor, head_queries, kv, kpos, qpos, qlow)
    mixed = from_heads(swap(mixed_packed.reshape(devices, half, LANES)))

    attn_out = nn(mixed, w_out)
    middle = routed + attn_out
    normed_mlp = rms_scale(middle, mlp_gain).astype(bf16)
    dbranch = scaling[:, None] * upstream
    dmlp = dbranch.astype(bf16)
    gathered = lax.all_gather(
        jnp.concatenate([mixed, normed_mlp, dmlp], axis=1), "seq", axis=0, tiled=True
    )
    mixed_all = gathered[:, :width]
    normed_mlp_all = gathered[:, width : 2 * width]
    dmlp_all = gathered[:, 2 * width :]
    hidden = nn(normed_mlp, w_up)
    active = jax.nn.gelu(hidden, approximate=True).astype(bf16)
    branch = attn_out + nn(active, w_down)
    dweight = jnp.sum(upstream * branch, axis=1)

    def gelu_of(values):
        return jax.nn.gelu(values, approximate=True)

    dactive = nt(dmlp, w_down)
    dhidden = jax.vjp(gelu_of, hidden)[1](dactive)[0].astype(bf16)
    dnormed_mlp = nt(dhidden, w_up)
    dmiddle = jax.vjp(lambda v: rms_scale(v, mlp_gain), middle)[1](dnormed_mlp)[0]
    dattn = (dbranch + dmiddle).astype(bf16)
    dmixed = nt(dattn, w_out).astype(bf16)
    out_cols = width // devices
    dattn_split = dattn.reshape(capacity, devices, out_cols).swapaxes(0, 1)
    dattn_split = dattn_split.reshape(devices, capacity * out_cols // LANES, LANES)
    got = swap(
        jnp.concatenate(
            [to_heads(dmixed, 2), dattn_split, note(jnp.sum(jnp.where(live, dweight * gate, 0.0)))], axis=1
        )
    )
    dattn_own = got[:, half : half + capacity * out_cols // LANES].reshape(slots, out_cols)
    coefficient = read_note(got[:, half + capacity * out_cols // LANES :])
    dq_packed, dkv_parts = attend_back(
        factor,
        head_queries,
        got[:, :half].reshape(devices * half, LANES),
        kv,
        kpos,
        qpos,
        qlow,
        mixed_turned,
        lse,
    )
    dkv = sum_over_group(dkv_parts).astype(bf16)

    dscore = dweight * ratio - coefficient * chosen_total / (score_total * score_total)
    dlogit_router = jnp.where(live, dscore * gate * (1.0 - gate), 0.0)
    router_part = jnp.sum(dlogit_router[:, None] * routed, axis=0).reshape(devices, out_cols)
    router_parts = three_parts(router_part).swapaxes(0, 1).reshape(devices, 1, 3 * out_cols)
    router_note = jnp.pad(router_parts, ((0, 0), (0, 7), (0, LANES - 3 * out_cols)))
    got = swap(
        jnp.concatenate(
            [dq_packed.reshape(devices, half, LANES), dkv.reshape(devices, share, LANES), router_note], axis=1
        )
    )
    dquery = from_heads(got[:, :half])
    dkey, dvalue = pair_from_heads(got[:, half : half + share])
    grad_router = jnp.sum(got[:, half + share, : 3 * out_cols].astype(f32), axis=0)
    grad_router = jnp.sum(grad_router.reshape(3, out_cols), axis=0)

    normed_own = lax.dynamic_index_in_dim(normed_all.reshape(devices, group, share, width), member, 1, False)
    normed_own = normed_own.reshape(devices * share, width)
    dq_rows = dq_packed.reshape(devices, half, 2, HEAD_DIM).swapaxes(1, 2).reshape(devices * share, HEAD_DIM)
    dqkv = jnp.concatenate([dq_rows, dkv], axis=1)
    grad_qkv = lax.dot_general(normed_own, dqkv, (((0,), (0,)), ((), ())), preferred_element_type=f32)
    head_cols = 3 * HEAD_DIM // group
    grad_qkv = member_order(grad_qkv.reshape(width, group, head_cols).swapaxes(0, 1))
    grad_qkv = sum_over_group(grad_qkv).astype(bf16)
    grad_out = lax.dot_general(mixed_all, dattn_own, (((0,), (0,)), ((), ())), preferred_element_type=f32)

    hidden_cols = hidden_width // devices
    up_own = lax.dynamic_slice_in_dim(w_up, own * hidden_cols, hidden_cols, 1)
    down_own = lax.dynamic_slice_in_dim(w_down, own * hidden_cols, hidden_cols, 0)
    hidden_own = nn(normed_mlp_all, up_own)
    dactive_own = nt(dmlp_all, down_own)
    active_own, gelu_back = jax.vjp(gelu_of, hidden_own)
    dhidden_own = gelu_back(dactive_own)[0].astype(bf16)
    active_own = active_own.astype(bf16)
    grad_down = lax.dot_general(active_own, dmlp_all, (((0,), (0,)), ((), ())), preferred_element_type=f32)
    grad_up = lax.dot_general(
        normed_mlp_all, dhidden_own, (((0,), (0,)), ((), ())), preferred_element_type=f32
    )
    sent = jnp.concatenate([grad_up.astype(bf16), grad_qkv, grad_out.astype(bf16)], axis=1)
    got = swap(sent.reshape(devices, out_cols, sent.shape[1])).astype(f32)
    grad_up = got[:, :, :hidden_cols].swapaxes(0, 1).reshape(out_cols, hidden_width)
    grad_qkv = got[:, :, hidden_cols : hidden_cols + head_cols].reshape(HEADS, group, out_cols, head_cols)
    grad_qkv = grad_qkv.transpose(2, 0, 1, 3).reshape(out_cols, HEADS, 3, HEAD_DIM)
    grad_query = grad_qkv[:, :, 0].reshape(out_cols, width)
    grad_key = grad_qkv[:, :, 1].reshape(out_cols, width)
    grad_value = grad_qkv[:, :, 2].reshape(out_cols, width)
    grad_out = got[:, :, hidden_cols + head_cols :].swapaxes(0, 1).reshape(out_cols, width)

    def own_rows(value):
        return lax.dynamic_slice_in_dim(value, own * out_cols, out_cols, 0).astype(f32)

    grad_gain_attn = jnp.sum(
        own_rows(w_query) * grad_query + own_rows(w_key) * grad_key + own_rows(w_value) * grad_value, axis=1
    ) / own_rows(attn_gain)
    grad_gain_mlp = jnp.sum(own_rows(w_up) * grad_up, axis=1) / own_rows(mlp_gain)

    dnormed = nt(dquery, w_query) + nt(dkey, w_key) + nt(dvalue, w_value)
    drows = jax.vjp(lambda v: rms_scale(v, attn_gain), routed)[1](dnormed)[0]
    droutes = drows + dmiddle + dlogit_router[:, None] * w_router.astype(f32)[None, :]
    new_rows = (routed + scaling[:, None] * branch).astype(bf16)
    new_grads = (upstream + droutes).astype(bf16)
    put = (jnp.arange(tok_rows, dtype=jnp.int32)[:, None] == offsets[None, :]) & live[None, :]
    hit = jnp.any(put, axis=1, keepdims=True)
    put = put.astype(bf16)
    output = jnp.where(hit, nn(put, new_rows).astype(bf16), tokens_in)
    input_grad = jnp.where(hit, nn(put, new_grads).astype(bf16), out_grad)
    return (
        output,
        input_grad,
        grad_router,
        grad_gain_attn,
        grad_query,
        grad_key,
        grad_value,
        grad_out,
        grad_gain_mlp,
        grad_up,
        grad_down,
    )


SHARE = 64
HALF = 32
NOTE = 8
OUT_HALF = 16
OUT_ROWS = 32
TILES = 2
AT_OUT = TILES * OUT_ROWS
AT_QUERY = AT_OUT + OUT_HALF
AT_PAIR = AT_QUERY + OUT_HALF
AT_NOTE = AT_PAIR + OUT_ROWS
GRAD_ROWS = AT_NOTE + NOTE


def swapped(tile):
    return jnp.concatenate([tile[..., HEAD_DIM:], tile[..., :HEAD_DIM]], axis=-1)


def joined(left, right):
    return jnp.concatenate([left[..., :HEAD_DIM], right[..., HEAD_DIM:]], axis=-1)


def pack_rows(target, first, value):
    for pair in range(HEADS // 2):
        tile = value[:, pair * LANES : (pair + 1) * LANES]
        turned = swapped(tile)
        target[2 * pair, first : first + HALF, :] = joined(tile[:HALF], turned[HALF:])
        target[2 * pair + 1, first : first + HALF, :] = joined(turned[:HALF], tile[HALF:])


def pack_pairs(target, first, left, right):
    for pair in range(HEADS // 2):
        lanes = slice(pair * LANES, (pair + 1) * LANES)
        one, two = left[:, lanes], right[:, lanes]
        target[2 * pair, first : first + SHARE, :] = joined(one, swapped(two))
        target[2 * pair + 1, first : first + SHARE, :] = joined(swapped(one), two)


def unpack_rows(source, first, half):
    columns = []
    for pair in range(HEADS // 2):
        even = source[2 * pair, first : first + half, :]
        odd = source[2 * pair + 1, first : first + half, :]
        columns.append(jnp.concatenate([joined(even, swapped(odd)), joined(swapped(even), odd)], axis=0))
    return jnp.concatenate(columns, axis=1)


def unpack_pairs(source, first, rows):
    left, right = [], []
    for pair in range(HEADS // 2):
        even = source[2 * pair, first : first + rows, :]
        odd = source[2 * pair + 1, first : first + rows, :]
        left.append(joined(even, swapped(odd)))
        right.append(joined(swapped(even), odd))
    return jnp.concatenate(left, axis=1), jnp.concatenate(right, axis=1)


def in_parts(value):
    high = value.astype(bf16).astype(f32)
    rest = value - high
    middle = rest.astype(bf16).astype(f32)
    row = lax.broadcasted_iota(jnp.int32, value.shape, len(value.shape) - 2)
    parts = jnp.where(row == 0, high, jnp.where(row == 1, middle, jnp.where(row == 2, rest - middle, 0.0)))
    return parts.astype(bf16)


def write_note(target, first, value):
    rows = in_parts(jnp.broadcast_to(value, (NOTE, LANES)))
    for k in range(target.shape[0]):
        target[k, first : first + NOTE, :] = rows


def read_note(source, first):
    rows = source[:, first : first + NOTE, :].astype(f32)
    return jnp.sum(jnp.sum(rows, axis=0), axis=0, keepdims=True)[:, :1]


def slots_of(chosen_ref, device):
    row = chosen_ref[pl.ds(device // 2, 1), :]
    return jnp.where(device % 2 == 0, row[:, :SHARE], row[:, SHARE:])


def one_hot(own_ref, counts_ref, chosen_ref, tok_rows, live_only):
    offsets = slots_of(chosen_ref, own_ref[0])
    capacity = offsets.shape[1]
    rows = lax.broadcasted_iota(jnp.int32, (tok_rows, capacity), 0)
    hot = rows == offsets
    if live_only:
        slot = lax.broadcasted_iota(jnp.int32, (tok_rows, capacity), 1)
        hot = hot & (slot < counts_ref[own_ref[0]])
    return jnp.where(hot, 1.0, 0.0)


def live_column(own_ref, counts_ref, capacity):
    return lax.broadcasted_iota(jnp.int32, (capacity, 1), 0) < counts_ref[own_ref[0]]


def gate_of(rows, vectors_ref):
    return jax.nn.sigmoid(jnp.sum(rows * vectors_ref[0:1, :], axis=1, keepdims=True))


def inverse_rms(values):
    return lax.rsqrt(jnp.mean(values * values, axis=-1, keepdims=True) + eps_norm)


def total_count(counts_ref):
    return lax.fori_loop(0, counts_ref.shape[0], lambda i, s: s + counts_ref[i], 0).astype(f32)


def gelu_pair(u):
    c = 0.7978845608028654
    square = u * u
    t = jnp.tanh(c * (u + 0.044715 * (square * u)))
    value = 0.5 * u * (1.0 + t)
    slope = 0.5 * (1.0 + t) + (0.5 * u) * ((1.0 - t * t) * (c + (3.0 * 0.044715 * c) * square))
    return value, slope


def chip_of(own_ref, k):
    return jnp.bitwise_xor(own_ref[0] // 2, (k // 4) ^ (4 * (k % 4)))


def row_of(column):
    wide = jnp.broadcast_to(column, (column.shape[0], LANES))
    filled = jnp.concatenate([wide, jnp.zeros((LANES - column.shape[0], LANES), f32)], axis=0)
    return jnp.transpose(filled)[:1, : column.shape[0]]


def places_kernel(own_ref, counts_ref, lengths_ref, chosen_ref, kpos_ref, qpos_ref, qlow_ref):
    core = own_ref[0] % 2
    devices, capacity = 2 * chosen_ref.shape[0], SHARE
    tok_rows = lengths_ref[lengths_ref.shape[0] - 1]
    slot = lax.broadcasted_iota(jnp.int32, (1, capacity), 1)
    ends = []
    for k in range(lengths_ref.shape[0] - 1):
        ends.append(lengths_ref[k] + (ends[-1] if ends else 0))

    def place(device):
        value = device * tok_rows + slots_of(chosen_ref, device)
        return value, slot < counts_ref[device]

    def key_row(device):
        value, live = place(device)
        return jnp.where(live, value.astype(f32), far_away)

    for m in range(2):
        parity = jnp.bitwise_xor(core, m)
        for c in range(0, devices // 2, 2):
            tile = jnp.concatenate([key_row(2 * c + parity), key_row(2 * c + 2 + parity)], axis=1)
            kpos_ref[m : m + 1, c * capacity : (c + 2) * capacity] = tile
    blocks = qpos_ref.shape[0]
    sources = devices // 2 // blocks
    for b in range(blocks):
        lows, highs = [], []
        for c in range(b * sources, (b + 1) * sources):
            value, live = place(2 * c + core)
            low = jnp.zeros_like(value)
            for end in ends:
                low = jnp.maximum(low, jnp.where(value >= end, end, 0))
            both = jnp.concatenate([jnp.where(live, value, -1), low], axis=0).astype(f32)
            lows.append(both[:, :HALF])
            highs.append(both[:, HALF:])
        both = jnp.concatenate(lows + highs, axis=1)
        qpos_ref[b : b + 1, :] = both[:1]
        qlow_ref[b : b + 1, :] = both[1:]


def fetch_kernel(own_ref, counts_ref, chosen_ref, tokens_ref, grads_ref, both_ref, rows_ref, upstream_ref):
    hot = one_hot(own_ref, counts_ref, chosen_ref, tokens_ref.shape[0], False)
    capacity = hot.shape[1]
    pick = jnp.transpose(jnp.concatenate([hot, jnp.zeros_like(hot)], axis=1))[:capacity].astype(bf16)
    live = live_column(own_ref, counts_ref, capacity)
    rows = nn(pick, tokens_ref[...]).astype(bf16)
    upstream = jnp.where(live, nn(pick, grads_ref[...]), 0.0).astype(bf16)
    both_ref[0, :capacity, :] = rows
    both_ref[0, capacity:, :] = upstream
    rows_ref[0] = rows
    upstream_ref[0] = upstream


def project_kernel(own_ref, counts_ref, vectors_ref, wq, wk, wv, *rest):
    pieces, sent_ref = rest[:-1], rest[-1]
    head = own_ref[0] // 2
    core = own_ref[0] % 2
    even = head % 2 == 0
    k = 0
    weights = None
    for piece in pieces:
        blocks, capacity, width = piece.shape
        rows = piece[...].reshape(blocks * capacity, width).astype(f32)
        gate = gate_of(rows, vectors_ref)
        normed = (rows * inverse_rms(rows) * vectors_ref[1:2, :]).astype(bf16)
        if weights is None:
            w_pair = jnp.where(even, joined(wk[...], swapped(wv[...])), joined(swapped(wk[...]), wv[...]))
            weights = jnp.concatenate([w_pair, jnp.where(even, wq[...], swapped(wq[...]))], axis=1)
        product = nn(normed, weights)
        for j in range(blocks):
            chip = chip_of(own_ref, k)
            block = product[j * capacity : (j + 1) * capacity]
            query = block[:, LANES:]
            sent_ref[chip, :HALF, :] = joined(query[:HALF], swapped(query[HALF:])).astype(bf16)
            sent_ref[chip, HALF : HALF + SHARE, :] = block[:, :LANES].astype(bf16)
            slot = lax.broadcasted_iota(jnp.int32, (capacity, 1), 0)
            live = slot < counts_ref[2 * chip + core]
            part = jnp.where(live, gate[j * capacity : (j + 1) * capacity], 0.0)
            part = jnp.sum(part, axis=0, keepdims=True)
            sent_ref[chip, HALF + SHARE :, :] = in_parts(jnp.broadcast_to(part, (NOTE, LANES)))
            k += 1


def unpack_kernel(got_ref, mixed_ref):
    mixed_ref[0] = unpack_rows(got_ref, 0, HALF)


CHUNKS = 4
PIECES = (5, 4, 5)


def middle_kernel(
    own_ref, counts_ref, mixed_ref, total_ref, both_ref, vectors_ref, out_ref, up_ref, down_ref,
    sent_ref, active_ref, attn_ref, dmiddle_ref, dweight_ref, w_out, w_up, w_down, hidden_ref, sems,
):
    width, total_cols = up_ref.shape
    cols = total_cols // CHUNKS
    copies = [pltpu.make_async_copy(out_ref, w_out, sems.at[0])]
    for c in range(CHUNKS):
        part = pl.ds(c * cols, cols)
        copies.append(pltpu.make_async_copy(up_ref.at[:, part], w_up.at[:, part], sems.at[1 + c]))
    for c in range(CHUNKS):
        part = pl.ds(c * cols, cols)
        copies.append(pltpu.make_async_copy(down_ref.at[part, :], w_down.at[part, :], sems.at[1 + CHUNKS + c]))
    for copy in copies:
        copy.start()
    capacity = mixed_ref.shape[1]
    rows = both_ref[0, :capacity, :].astype(f32)
    upstream = both_ref[0, capacity:, :].astype(f32)
    live = live_column(own_ref, counts_ref, capacity)
    gate = gate_of(rows, vectors_ref)
    ratio = total_count(counts_ref) / total_ref[:1, :1]
    scaling = gate * ratio
    gain = vectors_ref[2:3, :]
    dbranch = scaling * upstream
    upstream_low = both_ref[0, capacity:, :]
    copies[0].wait()
    attn_out = nn(mixed_ref[0], w_out[...])
    attn_ref[...] = attn_out
    dweight = jnp.sum(upstream * attn_out, axis=1, keepdims=True)
    middle = rows + attn_out
    scale = inverse_rms(middle)
    normed = (middle * scale * gain).astype(bf16)
    for c in range(CHUNKS):
        copies[1 + c].wait()
        hidden_ref[:, c * cols : (c + 1) * cols] = nn(normed, w_up[:, c * cols : (c + 1) * cols])
    dnormed = jnp.zeros((capacity, width), f32)
    for c in range(CHUNKS):
        part = slice(c * cols, (c + 1) * cols)
        copies[1 + CHUNKS + c].wait()
        hidden = hidden_ref[:, part]
        value, slope = gelu_pair(hidden)
        active = value.astype(bf16)
        active_ref[:, part] = active
        product = nt(upstream_low, w_down[part, :])
        dweight = dweight + jnp.sum(active.astype(f32) * product, axis=1, keepdims=True)
        dhidden = (scaling * product * slope).astype(bf16)
        dnormed = dnormed + nt(dhidden, w_up[:, part])
    dweight_ref[...] = jnp.broadcast_to(dweight, dweight_ref.shape)
    scaled = gain * dnormed
    dmiddle = scale * scaled - middle * (scale * scale * scale) * jnp.mean(scaled * middle, axis=-1, keepdims=True)
    dmiddle_ref[...] = dmiddle
    dattn = (dbranch + dmiddle).astype(bf16)
    pack_rows(sent_ref, 0, nt(dattn, w_out[...]).astype(bf16))
    pack_rows(sent_ref, HALF, dattn)
    write_note(sent_ref, 2 * HALF, jnp.sum(jnp.where(live, dweight * gate, 0.0), axis=0, keepdims=True))


def put_kernel(
    own_ref, counts_ref, chosen_ref, total_ref, both_ref, vectors_ref, active_ref, attn_ref, old_ref, down_ref,
    result_ref, w_down, sems,
):
    rows_of_chunk = down_ref.shape[0] // CHUNKS
    parts = [pl.ds(c * rows_of_chunk, rows_of_chunk) for c in range(CHUNKS)]
    copies = [pltpu.make_async_copy(down_ref.at[p, :], w_down.at[p, :], sems.at[c]) for c, p in enumerate(parts)]
    for copy in copies:
        copy.start()
    rows = both_ref[0, : both_ref.shape[1] // 2, :].astype(f32)
    scaling = gate_of(rows, vectors_ref) * (total_count(counts_ref) / total_ref[:1, :1])
    mlp_out = jnp.zeros_like(rows)
    for c, copy in enumerate(copies):
        part = slice(c * rows_of_chunk, (c + 1) * rows_of_chunk)
        copy.wait()
        mlp_out = mlp_out + nn(active_ref[:, part], w_down[part, :])
    new = (rows + scaling * (attn_ref[...] + mlp_out)).astype(bf16)
    put_rows(own_ref, counts_ref, chosen_ref, old_ref, new, result_ref)


def put_rows(own_ref, counts_ref, chosen_ref, old_ref, new, result_ref):
    hot = one_hot(own_ref, counts_ref, chosen_ref, old_ref.shape[0], True)
    hit = jnp.sum(hot, axis=1, keepdims=True) > 0.5
    placed = nn(hot.astype(bf16), new)
    result_ref[...] = jnp.where(hit, placed, old_ref[...].astype(f32)).astype(bf16)


def router_slope(own_ref, counts_ref, rows, dweight_ref, total_ref, coef_ref, vectors_ref):
    gate = gate_of(rows, vectors_ref)
    live = live_column(own_ref, counts_ref, rows.shape[0])
    count = total_count(counts_ref)
    total = total_ref[:1, :1]
    dscore = dweight_ref[:, :1] * (count / total) - coef_ref[:1, :1] * count / (total * total)
    return jnp.where(live, dscore * gate * (1.0 - gate), 0.0)


def keys_kernel(dq_ref, dkv_ref, moved_ref, coef_ref, sent_ref, sum_ref):
    rows = dkv_ref.shape[0]
    sent_ref[:, :HALF, :] = dq_ref[...]
    dkv = dkv_ref[...] + moved_ref[:rows, :]
    sent_ref[:, HALF:, :] = dkv.astype(bf16).reshape(sent_ref.shape[0], SHARE, LANES)
    sum_ref[...] = coef_ref[...] + moved_ref[rows:, :]


def units_kernel(
    own_ref, counts_ref, got_ref, dqkv_ref, total_ref, coef_ref, vectors_ref, rows_ref, dweight_ref,
    out_ref, up_ref, down_ref, *rest,
):
    gathers = []
    for count in PIECES:
        gathers.append(rest[:count])
        rest = rest[count:]
    down_keep_ref, down_give_ref, keep_ref, give_ref, rest = *rest[:4], rest[4:]
    *slots, grad_up, grad_down, grad_out, grad_q, grad_kv, ratio_ref, sems = rest
    rows_slots, upstream_slots, mixed_slots = slots
    step = pl.program_id(0)
    steps = pl.num_programs(0)
    _, sources, capacity, width = mixed_slots.shape
    core = own_ref[0] % 2
    slot = step % 2

    def copies(k):
        at = k % 2
        result = []
        for i, pieces in enumerate(gathers):
            if k < 3 or len(pieces) == 4:
                result.append(pltpu.make_async_copy(pieces[k], slots[i].at[at], sems.at[at, i, 0]))
                continue
            for half in range(2):
                target = slots[i].at[at, 2 * half : 2 * half + 2]
                result.append(pltpu.make_async_copy(pieces[k + half], target, sems.at[at, i, half]))
        return result

    for k in range(4):

        @pl.when(step == max(k - 1, 0))
        def _(k=k):
            for copy in copies(k):
                copy.start()

    @pl.when(step == 0)
    def _():
        for ref in (grad_up, grad_down, grad_out, grad_q, grad_kv):
            ref[...] = jnp.zeros_like(ref)
        ratio_ref[...] = jnp.broadcast_to(total_count(counts_ref) / total_ref[:1, :1], ratio_ref.shape)

    for k in range(4):

        @pl.when(step == k)
        def _(k=k):
            for copy in copies(k):
                copy.wait()

    def halves(ref, first):
        blocks = [ref[chip_of(own_ref, 4 * step + j), first : first + HALF, :] for j in range(sources)]
        turned = jnp.transpose(jnp.concatenate(blocks, axis=0).astype(f32)).astype(bf16)
        return turned[:HEAD_DIM], turned[HEAD_DIM:]

    def low_high(value):
        value = value.reshape(sources, capacity, width)
        return value[:, :HALF, :].reshape(sources * HALF, width), value[:, HALF:, :].reshape(sources * HALF, width)

    rows = rows_slots[slot].reshape(sources * capacity, width).astype(f32)
    upstream = upstream_slots[slot].reshape(sources * capacity, width).astype(f32)
    mixed = mixed_slots[slot].reshape(sources * capacity, width)
    normed_attn = (rows * inverse_rms(rows) * vectors_ref[1:2, :]).astype(bf16)
    low_query, high_query = halves(dqkv_ref, 0)
    low_rows, high_rows = low_high(normed_attn)
    grad_q[...] += nn(low_query, low_rows) + nn(high_query, high_rows)
    blocks = [dqkv_ref[chip_of(own_ref, 4 * step + j), HALF:, :] for j in range(sources)]
    pairs_turned = jnp.transpose(jnp.concatenate(blocks, axis=0).astype(f32)).astype(bf16)
    grad_kv[...] += nn(pairs_turned, normed_attn)
    low_attn, high_attn = halves(got_ref, HALF)
    low_mixed, high_mixed = low_high(mixed)
    grad_out[...] += nn(low_attn, low_mixed) + nn(high_attn, high_mixed)
    middle = rows + nn(mixed, out_ref[...])
    normed = (middle * inverse_rms(middle) * vectors_ref[2:3, :]).astype(bf16)
    dmlp = (gate_of(rows, vectors_ref) * ratio_ref[:1, :1] * upstream).astype(bf16)
    value, slope = gelu_pair(nn(normed, up_ref[...]))
    dhidden = nt(dmlp, down_ref[...]) * slope
    grad_down[...] += nn(jnp.transpose(value).astype(bf16), dmlp)
    grad_up[...] += nn(jnp.transpose(dhidden).astype(bf16), normed)

    @pl.when(step == steps - 1)
    def _():
        chips = keep_ref.shape[0]

        def split(value):
            value = value.reshape(chips, 2, OUT_ROWS, LANES)
            even, odd = value[:, 0], value[:, 1]
            return jnp.where(core == 0, even, odd), jnp.where(core == 0, odd, even)

        def store(first, kept, given):
            keep_ref[:, first : first + kept.shape[1], :] = kept.astype(bf16)
            give_ref[:, first : first + kept.shape[1], :] = given.astype(bf16)

        for t in range(TILES):
            store(t * OUT_ROWS, *split(jnp.transpose(grad_up[t * LANES : (t + 1) * LANES, :])))

        def two_in_one(value):
            return joined(value[:, :OUT_HALF], swapped(value[:, OUT_HALF:]))

        both_turned = jnp.transpose(jnp.concatenate([grad_out[...], grad_q[...]], axis=0))
        kept, given = split(both_turned)
        store(AT_OUT, two_in_one(kept), two_in_one(given))
        store(AT_QUERY, two_in_one(swapped(kept)), two_in_one(swapped(given)))
        store(AT_PAIR, *split(jnp.transpose(grad_kv[...])))
        own_rows = rows_ref[0, :capacity, :].astype(f32)
        dlogit = router_slope(own_ref, counts_ref, own_rows, dweight_ref, total_ref, coef_ref, vectors_ref)
        part = jnp.broadcast_to(jnp.sum(dlogit * own_rows, axis=0, keepdims=True), (NOTE, width))
        per_tile = LANES // OUT_ROWS
        for c in range(chips):
            tile = part[:, (2 * c) // per_tile * LANES : ((2 * c) // per_tile + 1) * LANES]
            shift = (2 * c) % per_tile * OUT_ROWS
            if shift:
                tile = jnp.concatenate([tile[:, shift:], tile[:, :shift]], axis=1)
            after = jnp.concatenate([tile[:, OUT_ROWS:], tile[:, :OUT_ROWS]], axis=1)
            keep_ref[c, AT_NOTE:, :] = in_parts(jnp.where(core == 0, tile, after))
            give_ref[c, AT_NOTE:, :] = in_parts(jnp.where(core == 0, after, tile))
        down = grad_down[...]
        half = down.shape[0] // 2
        down_keep_ref[...] = jnp.where(core == 0, down[:half], down[half:])
        down_give_ref[...] = jnp.where(core == 0, down[half:], down[:half]).astype(bf16)


def merge_kernel(keep_ref, moved_ref, sent_ref):
    total = keep_ref[...].astype(f32) + moved_ref[...].astype(f32)
    sent_ref[:, :AT_NOTE, :] = total[:, :AT_NOTE].astype(bf16)
    note = jnp.sum(total[:, AT_NOTE:], axis=1, keepdims=True)
    sent_ref[:, AT_NOTE:, :] = in_parts(jnp.broadcast_to(note, (note.shape[0], NOTE, LANES)))


def rows_kernel(
    own_ref, counts_ref, chosen_ref, got_ref, both_ref, dmiddle_ref, dweight_ref, total_ref, coef_ref, vectors_ref,
    old_ref, wq_ref, wk_ref, wv_ref, grads_ref, wq, wk, wv, sems,
):
    copies = [
        pltpu.make_async_copy(source, target, sems.at[i])
        for i, (source, target) in enumerate(((wq_ref, wq), (wk_ref, wk), (wv_ref, wv)))
    ]
    for copy in copies:
        copy.start()
    capacity = dmiddle_ref.shape[0]
    rows = both_ref[0, :capacity, :].astype(f32)
    upstream = both_ref[0, capacity:, :].astype(f32)
    gain = vectors_ref[1:2, :]
    dlogit = router_slope(own_ref, counts_ref, rows, dweight_ref, total_ref, coef_ref, vectors_ref)
    partial = upstream + dmiddle_ref[...] + dlogit * vectors_ref[0:1, :]
    dquery = unpack_rows(got_ref, 0, HALF)
    dkey, dvalue = unpack_pairs(got_ref, HALF, SHARE)
    copies[0].wait()
    dnormed = jnp.zeros_like(partial) + nt(dquery, wq[...])
    copies[1].wait()
    dnormed = dnormed + nt(dkey, wk[...])
    copies[2].wait()
    dnormed = dnormed + nt(dvalue, wv[...])
    scale = inverse_rms(rows)
    scaled = gain * dnormed
    drows = scale * scaled - rows * (scale * scale * scale) * jnp.mean(scaled * rows, axis=-1, keepdims=True)
    put_rows(own_ref, counts_ref, chosen_ref, old_ref, (partial + drows).astype(bf16), grads_ref)


def finish_kernel(
    got_ref, own_gain_ref, up_ref, wq_ref, wk_ref, wv_ref,
    grad_up_ref, grad_out_ref, grad_q_ref, grad_k_ref, grad_v_ref, router_ref, gain_attn_ref, gain_mlp_ref,
):
    total = jnp.zeros((OUT_ROWS, LANES), f32)
    for c in range(got_ref.shape[0]):
        for t in range(TILES):
            lanes = slice((TILES * c + t) * LANES, (TILES * c + t + 1) * LANES)
            part = got_ref[c, t * OUT_ROWS : (t + 1) * OUT_ROWS, :].astype(f32)
            grad_up_ref[:, lanes] = part
            total = total + part * up_ref[:, lanes].astype(f32)
    gain_mlp_ref[...] = row_of(jnp.sum(total, axis=1, keepdims=True)) / own_gain_ref[2:3, :]
    grad_out_ref[...] = unpack_rows(got_ref, AT_OUT, OUT_HALF).astype(f32)
    grad_q = unpack_rows(got_ref, AT_QUERY, OUT_HALF).astype(f32)
    grad_k, grad_v = (value.astype(f32) for value in unpack_pairs(got_ref, AT_PAIR, OUT_ROWS))
    grad_q_ref[...] = grad_q
    grad_k_ref[...] = grad_k
    grad_v_ref[...] = grad_v
    products = wq_ref[...].astype(f32) * grad_q + wk_ref[...].astype(f32) * grad_k + wv_ref[...].astype(f32) * grad_v
    gain_attn_ref[...] = row_of(jnp.sum(products, axis=1, keepdims=True)) / own_gain_ref[1:2, :]
    notes = jnp.sum(got_ref[:, AT_NOTE:, :].astype(f32), axis=0)
    router_ref[...] = jnp.sum(notes, axis=0, keepdims=True)[:, :OUT_ROWS]


def pair_attend_kernel(factor, got_ref, other_ref, kpos_ref, qpos_ref, qlow_ref, mixed_ref, turned_ref, lse_ref, total_ref):
    lists = (got_ref, other_ref)
    chips = got_ref.shape[0]
    blocks = chips * HALF // BLOCK
    sources = chips // blocks
    total = read_note(got_ref, HALF + SHARE) + read_note(other_ref, HALF + SHARE)
    total_ref[...] = jnp.broadcast_to(total, total_ref.shape)
    attend_core(
        factor,
        lambda b: got_ref[b * sources : (b + 1) * sources, :HALF, :].reshape(BLOCK, LANES),
        lambda m, extent: lists[m][: extent // SHARE, HALF : HALF + SHARE, :].reshape(extent, LANES),
        2, blocks, chips * SHARE, kpos_ref, qpos_ref, qlow_ref, mixed_ref, turned_ref, lse_ref,
    )


def pair_attend_back_kernel(
    factor, got_ref, other_ref, grad_ref, kpos_ref, qpos_ref, qlow_ref, turned_ref, lse_ref,
    dq_ref, own_ref, moved_ref, coef_ref,
):
    lists = (got_ref, other_ref)
    sums = (own_ref, moved_ref)
    chips = got_ref.shape[0]
    blocks = chips * HALF // BLOCK
    sources = chips // blocks
    coef = jnp.broadcast_to(read_note(grad_ref, 2 * HALF), coef_ref.shape)
    coef_ref[...] = coef
    moved_ref[chips * SHARE :, :] = coef

    def add_dkv(m, extent, first, update):
        if first:
            sums[m][:extent, :] = update
        else:
            sums[m][:extent, :] += update

    attend_back_core(
        factor,
        lambda b: got_ref[b * sources : (b + 1) * sources, :HALF, :].reshape(BLOCK, LANES),
        lambda b: grad_ref[b * sources : (b + 1) * sources, :HALF, :].reshape(BLOCK, LANES),
        lambda m, extent: lists[m][: extent // SHARE, HALF : HALF + SHARE, :].reshape(extent, LANES),
        2, blocks, chips * SHARE, kpos_ref, qpos_ref, qlow_ref, turned_ref, lse_ref, dq_ref, add_dkv,
    )


smem = pl.BlockSpec(memory_space=pltpu.SMEM)
hbm = pl.BlockSpec(memory_space=pl.ANY)
megabytes = {
    "places": 4, "fetch": 56, "project": 16, "attend": 20, "unpack": 4, "middle": 56, "put": 56, "attend_back": 24,
    "keys": 8, "units": 56, "merge": 10, "rows": 56, "finish": 12,
}


def params_of(name):
    return pltpu.CompilerParams(vmem_limit_bytes=megabytes[name] * 1024 * 1024)


def shaped(shape, dtype):
    return jax.ShapeDtypeStruct(shape, dtype)


microseconds = {
    "places": 1, "fetch": 3, "project": 4, "attend": 5, "unpack": 2, "middle": 15, "put": 6, "attend_back": 6, "keys": 2,
    "units": 16, "merge": 3, "rows": 7, "finish": 2,
}


def cost_of(name):
    return pl.CostEstimate(flops=0, transcendentals=0, bytes_accessed=microseconds[name] * 3_300_000)


def call(kernel, name, in_specs, out_shape, arguments, scratch=()):
    return pl.pallas_call(
        kernel,
        out_shape=out_shape,
        in_specs=in_specs,
        out_specs=jax.tree.map(lambda _: vmem, out_shape),
        scratch_shapes=list(scratch),
        compiler_params=params_of(name),
        cost_estimate=cost_of(name),
        name=name,
    )(*arguments)


def pairs(
    tokens_in,
    w_router,
    gain_attn,
    w_query,
    w_key,
    w_value,
    w_out,
    gain_mlp,
    w_up,
    w_down,
    out_grad,
    lengths,
    counts,
    chosen,
):
    devices = lax.axis_size("seq")
    chips = devices // 2
    own = lax.axis_index("seq")
    capacity = chosen.shape[0] // devices
    tok_rows, width = tokens_in.shape
    hidden_width = w_up.shape[1]
    out_rows = width // devices
    factor = HEAD_DIM ** (-0.5)
    core = own % 2
    own_id = own.astype(jnp.int32).reshape(1)
    chosen = chosen.reshape(chips, 2 * capacity)
    vectors = jnp.stack([w_router, gain_attn, gain_mlp]).astype(f32)
    own_gains = lax.dynamic_slice_in_dim(vectors, own * out_rows, out_rows, 1)
    cores = [[2 * c + k for c in range(chips)] for k in range(2)]

    def swap(value):
        return lax.all_to_all(value, "seq", split_axis=0, concat_axis=0, tiled=True, axis_index_groups=cores)

    def across(value, bits):
        return lax.ppermute(value, "seq", [(s, s ^ bits) for s in range(devices)])

    def line_of(block):
        return jnp.concatenate([block] + [across(block, 8 * k) for k in (1, 2, 3)], axis=0)

    def sides_of(line):
        return [line, across(line, 2), across(line, 4)]

    def gathered(sides):
        return sides + [across(sides[2][:2], 2), across(sides[1][2:], 4)]

    def gathered_whole(sides):
        return sides + [across(sides[2], 2)]

    blocks = chips * HALF // BLOCK
    square = pltpu.VMEM((width, width), bf16)
    block = shaped((1, capacity, width), bf16)
    both, own_rows, own_upstream = call(
        fetch_kernel, "fetch", [smem, smem] + [vmem] * 3, (shaped((1, 2 * capacity, width), bf16), block, block),
        (own_id, counts, chosen, tokens_in, out_grad),
    )
    rows_line = line_of(own_rows)
    chosen_after, rows_line = lax.optimization_barrier((chosen, rows_line))
    kpos, qpos, qlow = call(
        places_kernel, "places", [smem] * 3 + [vmem],
        (
            shaped((2, chips * SHARE), f32),
            shaped((blocks, 2 * BLOCK), f32),
            shaped((blocks, 2 * BLOCK), f32),
        ),
        (own_id, counts, jnp.append(lengths, tok_rows), chosen_after),
    )
    rows_all = gathered(sides_of(rows_line))
    column = own // 4 * LANES
    columns = [lax.dynamic_slice_in_dim(w, column, LANES, 1) for w in (w_query, w_key, w_value)]
    upstream_line = line_of(own_upstream)
    rows_all, upstream_line = lax.optimization_barrier((rows_all, upstream_line))
    kpos, qpos, qlow, columns, rows_all = lax.optimization_barrier((kpos, qpos, qlow, columns, rows_all))
    got = call(
        project_kernel, "project", [smem, smem] + [vmem] * 9,
        shaped((chips, HALF + SHARE + NOTE, LANES), bf16),
        (own_id, counts, vectors, *columns, *rows_all),
    )
    other = across(got, 1)
    upstream_sides = sides_of(upstream_line)
    mixed_packed, turned, lse, total = call(
        functools.partial(pair_attend_kernel, factor), "attend", [vmem] * 5,
        (
            shaped((chips * HALF, LANES), bf16),
            shaped((chips * HALF, LANES), f32),
            shaped((blocks, 2 * BLOCK), f32),
            shaped((8, LANES), f32),
        ),
        (got, other, kpos, qpos, qlow),
    )
    mixed_got = swap(mixed_packed.reshape(chips, HALF, LANES))
    upstream_sides, mixed_got = lax.optimization_barrier((upstream_sides, mixed_got))
    upstream_all = gathered_whole(upstream_sides)
    mixed = call(unpack_kernel, "unpack", [vmem], shaped((1, capacity, width), bf16), (mixed_got,))
    mixed_line = line_of(mixed)
    sent, active, attn_out, dmiddle, dweight = call(
        middle_kernel, "middle", [smem, smem] + [vmem] * 4 + [hbm] * 3,
        (
            shaped((chips, 2 * HALF + NOTE, LANES), bf16),
            shaped((capacity, hidden_width), bf16),
            shaped((capacity, width), f32),
            shaped((capacity, width), f32),
            shaped((capacity, LANES), f32),
        ),
        (own_id, counts, mixed, total, both, vectors, w_out, w_up, w_down),
        [
            square,
            pltpu.VMEM((width, hidden_width), bf16),
            pltpu.VMEM((hidden_width, width), bf16),
            pltpu.VMEM((capacity, hidden_width), f32),
            pltpu.SemaphoreType.DMA((1 + 2 * CHUNKS,)),
        ],
    )
    mixed_line, sent = lax.optimization_barrier((mixed_line, sent))
    mixed_sides = sides_of(mixed_line)
    upstream_all, sent = lax.optimization_barrier((upstream_all, sent))
    grads_got = swap(sent)
    output = call(
        put_kernel, "put", [smem, smem] + [vmem] * 7 + [hbm], shaped((tok_rows, width), bf16),
        (own_id, counts, chosen, total, both, vectors, active, attn_out, tokens_in, w_down),
        [pltpu.VMEM((hidden_width, width), bf16), pltpu.SemaphoreType.DMA((CHUNKS,))],
    )
    mixed_all = gathered(mixed_sides)
    output, grads_got = lax.optimization_barrier((output, grads_got))
    dq, dkv_own, dkv_other, coef = call(
        functools.partial(pair_attend_back_kernel, factor), "attend_back", [vmem] * 8,
        (
            shaped((chips * HALF, LANES), bf16),
            shaped((chips * SHARE, LANES), f32),
            shaped((chips * SHARE + 8, LANES), f32),
            shaped((8, LANES), f32),
        ),
        (got, other, grads_got, kpos, qpos, qlow, turned, lse),
    )
    moved = across(dkv_other, 1)
    dqkv, coef = call(
        keys_kernel, "keys", [vmem] * 4,
        (shaped((chips, HALF + SHARE, LANES), bf16), shaped((8, LANES), f32)),
        (dq.reshape(chips, HALF, LANES), dkv_own, moved, coef),
    )
    got = swap(dqkv)
    sources = 4
    hidden_cols = hidden_width // chips
    whole = lambda *shape: pl.BlockSpec(shape, lambda i, o: (0,) * len(shape))
    down_keep, down_give, keep, give = pl.pallas_call(
        units_kernel,
        out_shape=(
            shaped((hidden_cols // 2, width), f32),
            shaped((hidden_cols // 2, width), bf16),
            shaped((chips, GRAD_ROWS, LANES), bf16),
            shaped((chips, GRAD_ROWS, LANES), bf16),
        ),
        grid_spec=pltpu.PrefetchScalarGridSpec(
            num_scalar_prefetch=1,
            grid=(chips // sources,),
            in_specs=[
                smem,
                whole(chips, 2 * HALF + NOTE, LANES),
                whole(chips, HALF + SHARE, LANES),
                whole(8, LANES),
                whole(8, LANES),
                whole(3, width),
                whole(1, 2 * capacity, width),
                whole(capacity, LANES),
                whole(width, width),
                pl.BlockSpec((width, hidden_cols), lambda i, o: (0, o[0] // 2)),
                pl.BlockSpec((hidden_cols, width), lambda i, o: (o[0] // 2, 0)),
            ]
            + [hbm] * sum(PIECES),
            out_specs=(
                whole(hidden_cols // 2, width),
                whole(hidden_cols // 2, width),
                whole(chips, GRAD_ROWS, LANES),
                whole(chips, GRAD_ROWS, LANES),
            ),
            scratch_shapes=[
                pltpu.VMEM((2, sources, capacity, width), bf16),
                pltpu.VMEM((2, sources, capacity, width), bf16),
                pltpu.VMEM((2, sources, capacity, width), bf16),
                pltpu.VMEM((hidden_cols, width), f32),
                pltpu.VMEM((hidden_cols, width), f32),
                pltpu.VMEM((HEAD_DIM, width), f32),
                pltpu.VMEM((HEAD_DIM, width), f32),
                pltpu.VMEM((2 * HEAD_DIM, width), f32),
                pltpu.VMEM((8, LANES), f32),
                pltpu.SemaphoreType.DMA((2, 3, 2)),
            ],
        ),
        compiler_params=params_of("units"),
        cost_estimate=cost_of("units"),
        name="units",
    )(own_id, counts, grads_got, dqkv, total, coef, vectors, both, dweight, w_out, w_up, w_down, *rows_all, *upstream_all, *mixed_all)
    sent = call(
        merge_kernel, "merge", [vmem] * 2, shaped((chips, GRAD_ROWS, LANES), bf16), (keep, across(give, 1))
    )
    grad_down = down_keep + across(down_give, 1).astype(f32)
    last = swap(sent)
    input_grad = call(
        rows_kernel, "rows", [smem, smem] + [vmem] * 9 + [hbm] * 3, shaped((tok_rows, width), bf16),
        (
            own_id, counts, chosen, got, both, dmiddle, dweight, total, coef, vectors, out_grad,
            w_query, w_key, w_value,
        ),
        [square] * 3 + [pltpu.SemaphoreType.DMA((3,))],
    )
    block = shaped((out_rows, width), f32)
    row = shaped((1, out_rows), f32)
    first_row = own * out_rows
    grad_up, grad_out, grad_query, grad_key, grad_value, grad_router, grad_gain_attn, grad_gain_mlp = call(
        finish_kernel, "finish", [vmem] * 6,
        (shaped((out_rows, hidden_width), f32), block, block, block, block, row, row, row),
        (last, own_gains, *(lax.dynamic_slice_in_dim(w, first_row, out_rows) for w in (w_up, w_query, w_key, w_value))),
    )
    return (
        output,
        input_grad,
        grad_router.reshape(out_rows),
        grad_gain_attn.reshape(out_rows),
        grad_query,
        grad_key,
        grad_value,
        grad_out,
        grad_gain_mlp.reshape(out_rows),
        grad_up,
        grad_down,
    )


def per_device(*arguments):
    w_up, chosen = arguments[8], arguments[13]
    devices = lax.axis_size("seq")
    width, hidden_width = w_up.shape
    paired = (
        devices == 2 * HEADS
        and chosen.shape[0] == devices * SHARE
        and width == devices * OUT_ROWS
        and width == HEADS * HEAD_DIM
        and hidden_width == devices // 2 * TILES * LANES
    )
    return (pairs if paired else general)(*arguments)


def solution(mesh):
    placed = (P("seq", None),) + (P(),) * 9 + (P("seq", None),) + (P(),) * 3
    rows = P("seq", None)
    return jax.shard_map(
        per_device,
        mesh=mesh,
        in_specs=placed,
        out_specs=(rows, rows, P("seq"), P("seq"), rows, rows, rows, rows, P("seq"), rows, rows),
        check_vma=False,
    )
```

```python
import functools
import jax
import jax.numpy as jnp
from jax import lax
from jax.experimental import pallas as pl
from jax.experimental.pallas import tpu as pltpu
from jax.sharding import PartitionSpec as P

HEADS = 16
HEAD_DIM = 64
LANES = 128
BLOCK = 128

masked_score = -1e30
eps_norm = 1e-05
far_away = 1e9

f32 = jnp.float32
bf16 = jnp.bfloat16


def nt(left, right):
    return lax.dot_general(left, right, (((1,), (1,)), ((), ())), preferred_element_type=f32)


def nn(left, right):
    return lax.dot_general(left, right, (((1,), (0,)), ((), ())), preferred_element_type=f32)


def rms_scale(values, gain):
    return values * lax.rsqrt(jnp.mean(values * values, axis=-1, keepdims=True) + eps_norm) * gain


def three_parts(value):
    high = lax.reduce_precision(value, 8, 7)
    rest = value - high
    middle = lax.reduce_precision(rest, 8, 7)
    return jnp.stack([high, middle, rest - middle]).astype(bf16)


def spread_rows(packed, upper):
    lanes = lax.broadcasted_iota(jnp.int32, packed.shape, 1)
    zero = jnp.zeros_like(packed)
    rolled = jnp.concatenate([packed[:, HEAD_DIM:], packed[:, :HEAD_DIM]], axis=1)
    if upper:
        return jnp.concatenate(
            [jnp.where(lanes >= HEAD_DIM, rolled, zero), jnp.where(lanes >= HEAD_DIM, packed, zero)], axis=0
        )
    return jnp.concatenate(
        [jnp.where(lanes < HEAD_DIM, packed, zero), jnp.where(lanes < HEAD_DIM, rolled, zero)], axis=0
    )


def pack_columns(turned):
    return jnp.concatenate([turned[:, :BLOCK], turned[:, BLOCK:]], axis=0)


def key_columns(kpos_ref, member, extent):
    row = kpos_ref[member : member + 1, :extent]
    column = jnp.transpose(jnp.broadcast_to(row, (LANES, extent)))
    return jnp.concatenate([column, column], axis=1)


def attend_core(factor, load_query, load_kv, members, blocks, key_rows, kpos_ref, qpos_ref, qlow_ref, mixed_ref, turned_ref, lse_ref):
    kv_turned = [jnp.transpose(load_kv(m, key_rows)) for m in range(members)]
    for b in range(blocks):
        extent = key_rows * (b + 1) // blocks
        packed = (load_query(b).astype(f32) * factor).astype(bf16)
        wide = spread_rows(packed, False)
        qpos = qpos_ref[b : b + 1, :]
        qlow = qlow_ref[b : b + 1, :]
        scores = []
        for m in range(members):
            score = nt(load_kv(m, extent), wide)
            kpos = key_columns(kpos_ref, m, extent)
            score = jnp.where((kpos <= qpos) & (kpos >= qlow), score, masked_score)
            scores.append(score)
        peak = jnp.max(scores[0], axis=0, keepdims=True)
        for score in scores[1:]:
            peak = jnp.maximum(peak, jnp.max(score, axis=0, keepdims=True))
        peak = jnp.maximum(peak, 0.1 * masked_score)
        total = jnp.zeros_like(peak)
        mixed = jnp.zeros((LANES, 2 * BLOCK), f32)
        for m in range(members):
            prob = jnp.exp(scores[m] - peak)
            total = total + jnp.sum(prob, axis=0, keepdims=True)
            mixed = mixed + nn(kv_turned[m][:, :extent], prob.astype(bf16))
        safe = jnp.where(total > 0, total, 1.0)
        lse_ref[b : b + 1, :] = peak + jnp.log(safe)
        turned = pack_columns(mixed[HEAD_DIM:, :] / safe)
        turned_ref[b * BLOCK : (b + 1) * BLOCK, :] = turned
        mixed_ref[b * BLOCK : (b + 1) * BLOCK, :] = jnp.transpose(turned).astype(bf16)


def attend_back_core(
    factor, load_query, load_grad, load_kv, members, blocks, key_rows, kpos_ref, qpos_ref, qlow_ref, turned_ref, lse_ref,
    dq_ref, add_dkv,
):
    kv_turned = [jnp.transpose(load_kv(m, key_rows)) for m in range(members)]
    for b in range(blocks - 1, -1, -1):
        extent = key_rows * (b + 1) // blocks
        rows = slice(b * BLOCK, (b + 1) * BLOCK)
        packed = (load_query(b).astype(f32) * factor).astype(bf16)
        grads = load_grad(b)
        wide = jnp.concatenate([spread_rows(packed, False), spread_rows(grads, True)], axis=0)
        product = jnp.transpose(grads.astype(f32)) * turned_ref[rows, :]
        delta = jnp.concatenate(
            [
                jnp.sum(product[:HEAD_DIM], axis=0, keepdims=True),
                jnp.sum(product[HEAD_DIM:], axis=0, keepdims=True),
            ],
            axis=1,
        )
        qpos = qpos_ref[b : b + 1, :]
        qlow = qlow_ref[b : b + 1, :]
        lse = lse_ref[b : b + 1, :]
        dquery = jnp.zeros((LANES, 2 * BLOCK), f32)
        for m in range(members):
            both = nt(load_kv(m, extent), wide)
            kpos = key_columns(kpos_ref, m, extent)
            prob = jnp.exp(
                jnp.where((kpos <= qpos) & (kpos >= qlow), both[:, : 2 * BLOCK] - lse, masked_score)
            )
            dlogit = (prob * (both[:, 2 * BLOCK :] - delta)).astype(bf16)
            dquery = dquery + nn(kv_turned[m][:, :extent], dlogit)
            add_dkv(m, extent, b == blocks - 1, nn(jnp.concatenate([dlogit, prob.astype(bf16)], axis=1), wide))
        dq_ref[rows, :] = jnp.transpose(pack_columns(dquery[:HEAD_DIM, :] * factor)).astype(bf16)


def attend_kernel(factor, q_ref, kv_ref, kpos_ref, qpos_ref, qlow_ref, mixed_ref, turned_ref, lse_ref):
    members, key_rows, _ = kv_ref.shape
    attend_core(
        factor,
        lambda b: q_ref[b * BLOCK : (b + 1) * BLOCK, :],
        lambda m, extent: kv_ref[m, :extent, :],
        members, q_ref.shape[0] // BLOCK, key_rows, kpos_ref, qpos_ref, qlow_ref, mixed_ref, turned_ref, lse_ref,
    )


def attend_back_kernel(
    factor, q_ref, do_ref, kv_ref, kpos_ref, qpos_ref, qlow_ref, turned_ref, lse_ref, dq_ref, dkv_ref
):
    members, key_rows, _ = kv_ref.shape

    def add_dkv(m, extent, first, update):
        if first:
            dkv_ref[m, :extent, :] = update
        else:
            dkv_ref[m, :extent, :] += update

    attend_back_core(
        factor,
        lambda b: q_ref[b * BLOCK : (b + 1) * BLOCK, :],
        lambda b: do_ref[b * BLOCK : (b + 1) * BLOCK, :],
        lambda m, extent: kv_ref[m, :extent, :],
        members, q_ref.shape[0] // BLOCK, key_rows, kpos_ref, qpos_ref, qlow_ref, turned_ref, lse_ref, dq_ref, add_dkv,
    )


vmem = pl.BlockSpec(memory_space=pltpu.VMEM)
vmem_limit = 56 * 1024 * 1024


def attend(factor, queries, kv, kpos, qpos, qlow):
    rows = queries.shape[0]
    return pl.pallas_call(
        functools.partial(attend_kernel, factor),
        out_shape=(
            jax.ShapeDtypeStruct((rows, LANES), bf16),
            jax.ShapeDtypeStruct((rows, LANES), f32),
            jax.ShapeDtypeStruct(qpos.shape, f32),
        ),
        in_specs=[vmem] * 5,
        out_specs=(vmem,) * 3,
        compiler_params=pltpu.CompilerParams(vmem_limit_bytes=vmem_limit),
        name="attend",
    )(queries, kv, kpos, qpos, qlow)


def attend_back(factor, queries, dmixed, kv, kpos, qpos, qlow, turned, lse):
    rows = queries.shape[0]
    return pl.pallas_call(
        functools.partial(attend_back_kernel, factor),
        out_shape=(
            jax.ShapeDtypeStruct((rows, LANES), bf16),
            jax.ShapeDtypeStruct(kv.shape, f32),
        ),
        in_specs=[vmem] * 8,
        out_specs=(vmem,) * 2,
        compiler_params=pltpu.CompilerParams(vmem_limit_bytes=vmem_limit),
        name="attend_back",
    )(queries, dmixed, kv, kpos, qpos, qlow, turned, lse)


def general(
    tokens_in,
    w_router,
    gain_attn,
    w_query,
    w_key,
    w_value,
    w_out,
    gain_mlp,
    w_up,
    w_down,
    out_grad,
    lengths,
    counts,
    chosen,
):
    devices = lax.axis_size("seq")
    own = lax.axis_index("seq")
    capacity = chosen.shape[0] // devices
    tok_rows, width = tokens_in.shape
    hidden_width = w_up.shape[1]
    group = devices // HEADS
    share = capacity // group
    half = share // 2
    member = own % group
    slots = devices * capacity
    factor = HEAD_DIM ** (-0.5)
    attn_gain = gain_attn.astype(f32)
    mlp_gain = gain_mlp.astype(f32)

    def swap(value):
        return lax.all_to_all(value, "seq", split_axis=0, concat_axis=0, tiled=True)

    groups = [[h * group + m for m in range(group)] for h in range(HEADS)]

    def across_group(value):
        if group == 2:
            other = lax.ppermute(value, "seq", [(s, s ^ 1) for s in range(devices)])
            return jnp.stack([value, other])
        return lax.all_gather(value, "seq", axis_index_groups=groups)

    def sum_over_group(value):
        if group == 2:
            return value[0] + lax.ppermute(value[1], "seq", [(s, s ^ 1) for s in range(devices)])
        return lax.psum_scatter(value, "seq", scatter_dimension=0, axis_index_groups=groups)

    def member_order(value):
        if group == 2:
            return jnp.where(member == 0, value, value[::-1])
        return value

    slot_ids = jnp.arange(capacity, dtype=jnp.int32)
    places = jnp.arange(devices, dtype=jnp.int32)[:, None] * tok_rows + chosen.reshape(devices, capacity)
    live_all = slot_ids[None, :] < counts[:, None]
    seq_ends = jnp.cumsum(lengths)
    starts = jnp.max(jnp.where(places[..., None] >= seq_ends, seq_ends, 0), axis=-1)
    kpos = jnp.where(live_all, places.astype(f32), far_away)
    kpos = member_order(kpos.reshape(devices, group, share).swapaxes(0, 1).reshape(group, devices * share))
    blocks = devices * half // BLOCK

    def query_order(value):
        value = lax.dynamic_index_in_dim(value.reshape(devices, group, share), member, 1, False)
        return value.reshape(blocks, devices // blocks, 2, half).swapaxes(1, 2).reshape(blocks, 2 * BLOCK)

    qpos = query_order(jnp.where(live_all, places, -1).astype(f32))
    qlow = query_order(starts.astype(f32))

    offsets = lax.dynamic_slice_in_dim(chosen, own * capacity, capacity)
    live = slot_ids < counts[own]
    pick = (offsets[:, None] == jnp.arange(tok_rows, dtype=jnp.int32)[None, :]).astype(bf16)
    routed = nn(pick, tokens_in)
    upstream = jnp.where(live[:, None], nn(pick, out_grad), 0.0)
    gate = jax.nn.sigmoid(jnp.sum(routed * w_router.astype(f32)[None, :], axis=1))
    gate_sum = jnp.sum(jnp.where(live, gate, 0.0))
    normed = rms_scale(routed, attn_gain).astype(bf16)
    normed_all = lax.all_gather(normed, "seq", axis=0, tiled=True)
    queries = nn(normed, w_query).astype(bf16)
    keys = nn(normed, w_key).astype(bf16)
    values = nn(normed, w_value).astype(bf16)

    def note(value):
        parts = jnp.pad(three_parts(value), (0, LANES - 3))
        return jnp.broadcast_to(parts, (devices, 8, LANES))

    def read_note(rows):
        return jnp.sum(rows[:, 0, :3].astype(f32))

    def to_heads(value, per_row):
        if per_row == 2:
            value = value.reshape(group, 2, half, HEADS, HEAD_DIM).transpose(3, 0, 2, 1, 4)
            return value.reshape(devices, half, LANES)
        return value

    def pair_to_heads(first, second):
        both = jnp.stack([first, second], axis=1).reshape(group, share, 2, HEADS, HEAD_DIM)
        return both.transpose(3, 0, 1, 2, 4).reshape(devices, share, LANES)

    def from_heads(value):
        value = value.reshape(HEADS, group, half, 2, HEAD_DIM).transpose(1, 3, 2, 0, 4)
        return value.reshape(capacity, HEADS * HEAD_DIM)

    def pair_from_heads(value):
        value = value.reshape(HEADS, group, share, 2, HEAD_DIM).transpose(3, 1, 2, 0, 4)
        value = value.reshape(2, capacity, HEADS * HEAD_DIM)
        return value[0], value[1]

    sent = jnp.concatenate([to_heads(queries, 2), pair_to_heads(keys, values), note(gate_sum)], axis=1)
    got = swap(sent)
    score_total = read_note(got[:, half + share :])
    chosen_total = jnp.sum(counts).astype(f32)
    ratio = chosen_total / score_total
    scaling = gate * ratio
    head_queries = got[:, :half].reshape(devices * half, LANES)
    kv = across_group(got[:, half : half + share].reshape(devices * share, LANES))
    mixed_packed, mixed_turned, lse = attend(factor, head_queries, kv, kpos, qpos, qlow)
    mixed = from_heads(swap(mixed_packed.reshape(devices, half, LANES)))

    attn_out = nn(mixed, w_out)
    middle = routed + attn_out
    normed_mlp = rms_scale(middle, mlp_gain).astype(bf16)
    dbranch = scaling[:, None] * upstream
    dmlp = dbranch.astype(bf16)
    gathered = lax.all_gather(
        jnp.concatenate([mixed, normed_mlp, dmlp], axis=1), "seq", axis=0, tiled=True
    )
    mixed_all = gathered[:, :width]
    normed_mlp_all = gathered[:, width : 2 * width]
    dmlp_all = gathered[:, 2 * width :]
    hidden = nn(normed_mlp, w_up)
    active = jax.nn.gelu(hidden, approximate=True).astype(bf16)
    branch = attn_out + nn(active, w_down)
    dweight = jnp.sum(upstream * branch, axis=1)

    def gelu_of(values):
        return jax.nn.gelu(values, approximate=True)

    dactive = nt(dmlp, w_down)
    dhidden = jax.vjp(gelu_of, hidden)[1](dactive)[0].astype(bf16)
    dnormed_mlp = nt(dhidden, w_up)
    dmiddle = jax.vjp(lambda v: rms_scale(v, mlp_gain), middle)[1](dnormed_mlp)[0]
    dattn = (dbranch + dmiddle).astype(bf16)
    dmixed = nt(dattn, w_out).astype(bf16)
    out_cols = width // devices
    dattn_split = dattn.reshape(capacity, devices, out_cols).swapaxes(0, 1)
    dattn_split = dattn_split.reshape(devices, capacity * out_cols // LANES, LANES)
    got = swap(
        jnp.concatenate(
            [to_heads(dmixed, 2), dattn_split, note(jnp.sum(jnp.where(live, dweight * gate, 0.0)))], axis=1
        )
    )
    dattn_own = got[:, half : half + capacity * out_cols // LANES].reshape(slots, out_cols)
    coefficient = read_note(got[:, half + capacity * out_cols // LANES :])
    dq_packed, dkv_parts = attend_back(
        factor,
        head_queries,
        got[:, :half].reshape(devices * half, LANES),
        kv,
        kpos,
        qpos,
        qlow,
        mixed_turned,
        lse,
    )
    dkv = sum_over_group(dkv_parts).astype(bf16)

    dscore = dweight * ratio - coefficient * chosen_total / (score_total * score_total)
    dlogit_router = jnp.where(live, dscore * gate * (1.0 - gate), 0.0)
    router_part = jnp.sum(dlogit_router[:, None] * routed, axis=0).reshape(devices, out_cols)
    router_parts = three_parts(router_part).swapaxes(0, 1).reshape(devices, 1, 3 * out_cols)
    router_note = jnp.pad(router_parts, ((0, 0), (0, 7), (0, LANES - 3 * out_cols)))
    got = swap(
        jnp.concatenate(
            [dq_packed.reshape(devices, half, LANES), dkv.reshape(devices, share, LANES), router_note], axis=1
        )
    )
    dquery = from_heads(got[:, :half])
    dkey, dvalue = pair_from_heads(got[:, half : half + share])
    grad_router = jnp.sum(got[:, half + share, : 3 * out_cols].astype(f32), axis=0)
    grad_router = jnp.sum(grad_router.reshape(3, out_cols), axis=0)

    normed_own = lax.dynamic_index_in_dim(normed_all.reshape(devices, group, share, width), member, 1, False)
    normed_own = normed_own.reshape(devices * share, width)
    dq_rows = dq_packed.reshape(devices, half, 2, HEAD_DIM).swapaxes(1, 2).reshape(devices * share, HEAD_DIM)
    dqkv = jnp.concatenate([dq_rows, dkv], axis=1)
    grad_qkv = lax.dot_general(normed_own, dqkv, (((0,), (0,)), ((), ())), preferred_element_type=f32)
    head_cols = 3 * HEAD_DIM // group
    grad_qkv = member_order(grad_qkv.reshape(width, group, head_cols).swapaxes(0, 1))
    grad_qkv = sum_over_group(grad_qkv).astype(bf16)
    grad_out = lax.dot_general(mixed_all, dattn_own, (((0,), (0,)), ((), ())), preferred_element_type=f32)

    hidden_cols = hidden_width // devices
    up_own = lax.dynamic_slice_in_dim(w_up, own * hidden_cols, hidden_cols, 1)
    down_own = lax.dynamic_slice_in_dim(w_down, own * hidden_cols, hidden_cols, 0)
    hidden_own = nn(normed_mlp_all, up_own)
    dactive_own = nt(dmlp_all, down_own)
    active_own, gelu_back = jax.vjp(gelu_of, hidden_own)
    dhidden_own = gelu_back(dactive_own)[0].astype(bf16)
    active_own = active_own.astype(bf16)
    grad_down = lax.dot_general(active_own, dmlp_all, (((0,), (0,)), ((), ())), preferred_element_type=f32)
    grad_up = lax.dot_general(
        normed_mlp_all, dhidden_own, (((0,), (0,)), ((), ())), preferred_element_type=f32
    )
    sent = jnp.concatenate([grad_up.astype(bf16), grad_qkv, grad_out.astype(bf16)], axis=1)
    got = swap(sent.reshape(devices, out_cols, sent.shape[1])).astype(f32)
    grad_up = got[:, :, :hidden_cols].swapaxes(0, 1).reshape(out_cols, hidden_width)
    grad_qkv = got[:, :, hidden_cols : hidden_cols + head_cols].reshape(HEADS, group, out_cols, head_cols)
    grad_qkv = grad_qkv.transpose(2, 0, 1, 3).reshape(out_cols, HEADS, 3, HEAD_DIM)
    grad_query = grad_qkv[:, :, 0].reshape(out_cols, width)
    grad_key = grad_qkv[:, :, 1].reshape(out_cols, width)
    grad_value = grad_qkv[:, :, 2].reshape(out_cols, width)
    grad_out = got[:, :, hidden_cols + head_cols :].swapaxes(0, 1).reshape(out_cols, width)

    def own_rows(value):
        return lax.dynamic_slice_in_dim(value, own * out_cols, out_cols, 0).astype(f32)

    grad_gain_attn = jnp.sum(
        own_rows(w_query) * grad_query + own_rows(w_key) * grad_key + own_rows(w_value) * grad_value, axis=1
    ) / own_rows(attn_gain)
    grad_gain_mlp = jnp.sum(own_rows(w_up) * grad_up, axis=1) / own_rows(mlp_gain)

    dnormed = nt(dquery, w_query) + nt(dkey, w_key) + nt(dvalue, w_value)
    drows = jax.vjp(lambda v: rms_scale(v, attn_gain), routed)[1](dnormed)[0]
    droutes = drows + dmiddle + dlogit_router[:, None] * w_router.astype(f32)[None, :]
    new_rows = (routed + scaling[:, None] * branch).astype(bf16)
    new_grads = (upstream + droutes).astype(bf16)
    put = (jnp.arange(tok_rows, dtype=jnp.int32)[:, None] == offsets[None, :]) & live[None, :]
    hit = jnp.any(put, axis=1, keepdims=True)
    put = put.astype(bf16)
    output = jnp.where(hit, nn(put, new_rows).astype(bf16), tokens_in)
    input_grad = jnp.where(hit, nn(put, new_grads).astype(bf16), out_grad)
    return (
        output,
        input_grad,
        grad_router,
        grad_gain_attn,
        grad_query,
        grad_key,
        grad_value,
        grad_out,
        grad_gain_mlp,
        grad_up,
        grad_down,
    )


SHARE = 64
HALF = 32
NOTE = 8
OUT_HALF = 16
OUT_ROWS = 32
TILES = 2
AT_OUT = TILES * OUT_ROWS
AT_QUERY = AT_OUT + OUT_HALF
AT_PAIR = AT_QUERY + OUT_HALF
AT_NOTE = AT_PAIR + OUT_ROWS
GRAD_ROWS = AT_NOTE + NOTE


def swapped(tile):
    return jnp.concatenate([tile[..., HEAD_DIM:], tile[..., :HEAD_DIM]], axis=-1)


def joined(left, right):
    return jnp.concatenate([left[..., :HEAD_DIM], right[..., HEAD_DIM:]], axis=-1)


def pack_rows(target, first, value):
    for pair in range(HEADS // 2):
        tile = value[:, pair * LANES : (pair + 1) * LANES]
        turned = swapped(tile)
        target[2 * pair, first : first + HALF, :] = joined(tile[:HALF], turned[HALF:])
        target[2 * pair + 1, first : first + HALF, :] = joined(turned[:HALF], tile[HALF:])


def pack_pairs(target, first, left, right):
    for pair in range(HEADS // 2):
        lanes = slice(pair * LANES, (pair + 1) * LANES)
        one, two = left[:, lanes], right[:, lanes]
        target[2 * pair, first : first + SHARE, :] = joined(one, swapped(two))
        target[2 * pair + 1, first : first + SHARE, :] = joined(swapped(one), two)


def unpack_rows(source, first, half):
    columns = []
    for pair in range(HEADS // 2):
        even = source[2 * pair, first : first + half, :]
        odd = source[2 * pair + 1, first : first + half, :]
        columns.append(jnp.concatenate([joined(even, swapped(odd)), joined(swapped(even), odd)], axis=0))
    return jnp.concatenate(columns, axis=1)


def unpack_pairs(source, first, rows):
    left, right = [], []
    for pair in range(HEADS // 2):
        even = source[2 * pair, first : first + rows, :]
        odd = source[2 * pair + 1, first : first + rows, :]
        left.append(joined(even, swapped(odd)))
        right.append(joined(swapped(even), odd))
    return jnp.concatenate(left, axis=1), jnp.concatenate(right, axis=1)


def in_parts(value):
    high = value.astype(bf16).astype(f32)
    rest = value - high
    middle = rest.astype(bf16).astype(f32)
    row = lax.broadcasted_iota(jnp.int32, value.shape, len(value.shape) - 2)
    parts = jnp.where(row == 0, high, jnp.where(row == 1, middle, jnp.where(row == 2, rest - middle, 0.0)))
    return parts.astype(bf16)


def write_note(target, first, value):
    rows = in_parts(jnp.broadcast_to(value, (NOTE, LANES)))
    for k in range(target.shape[0]):
        target[k, first : first + NOTE, :] = rows


def read_note(source, first):
    rows = source[:, first : first + NOTE, :].astype(f32)
    return jnp.sum(jnp.sum(rows, axis=0), axis=0, keepdims=True)[:, :1]


def slots_of(chosen_ref, device):
    row = chosen_ref[pl.ds(device // 2, 1), :]
    return jnp.where(device % 2 == 0, row[:, :SHARE], row[:, SHARE:])


def one_hot(own_ref, counts_ref, chosen_ref, tok_rows, live_only):
    offsets = slots_of(chosen_ref, own_ref[0])
    capacity = offsets.shape[1]
    rows = lax.broadcasted_iota(jnp.int32, (tok_rows, capacity), 0)
    hot = rows == offsets
    if live_only:
        slot = lax.broadcasted_iota(jnp.int32, (tok_rows, capacity), 1)
        hot = hot & (slot < counts_ref[own_ref[0]])
    return jnp.where(hot, 1.0, 0.0)


def live_column(own_ref, counts_ref, capacity):
    return lax.broadcasted_iota(jnp.int32, (capacity, 1), 0) < counts_ref[own_ref[0]]


def gate_of(rows, vectors_ref):
    return jax.nn.sigmoid(jnp.sum(rows * vectors_ref[0:1, :], axis=1, keepdims=True))


def inverse_rms(values):
    return lax.rsqrt(jnp.mean(values * values, axis=-1, keepdims=True) + eps_norm)


def total_count(counts_ref):
    return lax.fori_loop(0, counts_ref.shape[0], lambda i, s: s + counts_ref[i], 0).astype(f32)


def gelu_pair(u):
    c = 0.7978845608028654
    square = u * u
    t = jnp.tanh(c * (u + 0.044715 * (square * u)))
    value = 0.5 * u * (1.0 + t)
    slope = 0.5 * (1.0 + t) + (0.5 * u) * ((1.0 - t * t) * (c + (3.0 * 0.044715 * c) * square))
    return value, slope


def chip_of(own_ref, k):
    return jnp.bitwise_xor(own_ref[0] // 2, (k // 4) ^ (4 * (k % 4)))


def row_of(column):
    wide = jnp.broadcast_to(column, (column.shape[0], LANES))
    filled = jnp.concatenate([wide, jnp.zeros((LANES - column.shape[0], LANES), f32)], axis=0)
    return jnp.transpose(filled)[:1, : column.shape[0]]


def places_kernel(own_ref, counts_ref, lengths_ref, chosen_ref, kpos_ref, qpos_ref, qlow_ref):
    core = own_ref[0] % 2
    devices, capacity = 2 * chosen_ref.shape[0], SHARE
    tok_rows = lengths_ref[lengths_ref.shape[0] - 1]
    slot = lax.broadcasted_iota(jnp.int32, (1, capacity), 1)
    ends = []
    for k in range(lengths_ref.shape[0] - 1):
        ends.append(lengths_ref[k] + (ends[-1] if ends else 0))

    def place(device):
        value = device * tok_rows + slots_of(chosen_ref, device)
        return value, slot < counts_ref[device]

    def key_row(device):
        value, live = place(device)
        return jnp.where(live, value.astype(f32), far_away)

    for m in range(2):
        parity = jnp.bitwise_xor(core, m)
        for c in range(0, devices // 2, 2):
            tile = jnp.concatenate([key_row(2 * c + parity), key_row(2 * c + 2 + parity)], axis=1)
            kpos_ref[m : m + 1, c * capacity : (c + 2) * capacity] = tile
    blocks = qpos_ref.shape[0]
    sources = devices // 2 // blocks
    for b in range(blocks):
        lows, highs = [], []
        for c in range(b * sources, (b + 1) * sources):
            value, live = place(2 * c + core)
            low = jnp.zeros_like(value)
            for end in ends:
                low = jnp.maximum(low, jnp.where(value >= end, end, 0))
            both = jnp.concatenate([jnp.where(live, value, -1), low], axis=0).astype(f32)
            lows.append(both[:, :HALF])
            highs.append(both[:, HALF:])
        both = jnp.concatenate(lows + highs, axis=1)
        qpos_ref[b : b + 1, :] = both[:1]
        qlow_ref[b : b + 1, :] = both[1:]


def fetch_kernel(own_ref, counts_ref, chosen_ref, tokens_ref, grads_ref, both_ref, rows_ref, upstream_ref):
    hot = one_hot(own_ref, counts_ref, chosen_ref, tokens_ref.shape[0], False)
    capacity = hot.shape[1]
    pick = jnp.transpose(jnp.concatenate([hot, jnp.zeros_like(hot)], axis=1))[:capacity].astype(bf16)
    live = live_column(own_ref, counts_ref, capacity)
    rows = nn(pick, tokens_ref[...]).astype(bf16)
    upstream = jnp.where(live, nn(pick, grads_ref[...]), 0.0).astype(bf16)
    both_ref[0, :capacity, :] = rows
    both_ref[0, capacity:, :] = upstream
    rows_ref[0] = rows
    upstream_ref[0] = upstream


def project_kernel(own_ref, counts_ref, vectors_ref, wq, wk, wv, *rest):
    pieces, sent_ref = rest[:-1], rest[-1]
    head = own_ref[0] // 2
    core = own_ref[0] % 2
    even = head % 2 == 0
    k = 0
    weights = None
    for piece in pieces:
        blocks, capacity, width = piece.shape
        rows = piece[...].reshape(blocks * capacity, width).astype(f32)
        gate = gate_of(rows, vectors_ref)
        normed = (rows * inverse_rms(rows) * vectors_ref[1:2, :]).astype(bf16)
        if weights is None:
            w_pair = jnp.where(even, joined(wk[...], swapped(wv[...])), joined(swapped(wk[...]), wv[...]))
            weights = jnp.concatenate([w_pair, jnp.where(even, wq[...], swapped(wq[...]))], axis=1)
        product = nn(normed, weights)
        for j in range(blocks):
            chip = chip_of(own_ref, k)
            block = product[j * capacity : (j + 1) * capacity]
            query = block[:, LANES:]
            sent_ref[chip, :HALF, :] = joined(query[:HALF], swapped(query[HALF:])).astype(bf16)
            sent_ref[chip, HALF : HALF + SHARE, :] = block[:, :LANES].astype(bf16)
            slot = lax.broadcasted_iota(jnp.int32, (capacity, 1), 0)
            live = slot < counts_ref[2 * chip + core]
            part = jnp.where(live, gate[j * capacity : (j + 1) * capacity], 0.0)
            part = jnp.sum(part, axis=0, keepdims=True)
            sent_ref[chip, HALF + SHARE :, :] = in_parts(jnp.broadcast_to(part, (NOTE, LANES)))
            k += 1


def unpack_kernel(got_ref, mixed_ref):
    mixed_ref[0] = unpack_rows(got_ref, 0, HALF)


CHUNKS = 4
PIECES = (5, 4, 5)


def early_kernel(both_ref, down_ref, product_ref, w_down, sems):
    cols = down_ref.shape[0] // CHUNKS
    parts = [pl.ds(c * cols, cols) for c in range(CHUNKS)]
    copies = [pltpu.make_async_copy(down_ref.at[p, :], w_down.at[p, :], sems.at[c]) for c, p in enumerate(parts)]
    for copy in copies:
        copy.start()
    upstream = both_ref[0, both_ref.shape[1] // 2 :, :]
    for c, copy in enumerate(copies):
        copy.wait()
        part = slice(c * cols, (c + 1) * cols)
        product_ref[:, part] = nt(upstream, w_down[part, :])


def middle_kernel(
    own_ref, counts_ref, mixed_ref, total_ref, both_ref, vectors_ref, product_ref, out_ref, up_ref,
    sent_ref, active_ref, attn_ref, dmiddle_ref, dweight_ref, w_out, w_up, sems,
):
    width, total_cols = up_ref.shape
    cols = total_cols // CHUNKS
    copies = [pltpu.make_async_copy(out_ref, w_out, sems.at[0])]
    for c in range(CHUNKS):
        part = pl.ds(c * cols, cols)
        copies.append(pltpu.make_async_copy(up_ref.at[:, part], w_up.at[:, part], sems.at[1 + c]))
    for copy in copies:
        copy.start()
    capacity = mixed_ref.shape[1]
    rows = both_ref[0, :capacity, :].astype(f32)
    upstream = both_ref[0, capacity:, :].astype(f32)
    live = live_column(own_ref, counts_ref, capacity)
    gate = gate_of(rows, vectors_ref)
    ratio = total_count(counts_ref) / total_ref[:1, :1]
    scaling = gate * ratio
    gain = vectors_ref[2:3, :]
    dbranch = scaling * upstream
    copies[0].wait()
    attn_out = nn(mixed_ref[0], w_out[...])
    attn_ref[...] = attn_out
    dweight = jnp.sum(upstream * attn_out, axis=1, keepdims=True)
    middle = rows + attn_out
    scale = inverse_rms(middle)
    normed = (middle * scale * gain).astype(bf16)
    dnormed = jnp.zeros((capacity, width), f32)
    for c in range(CHUNKS):
        part = slice(c * cols, (c + 1) * cols)
        copies[1 + c].wait()
        value, slope = gelu_pair(nn(normed, w_up[:, part]))
        active = value.astype(bf16)
        active_ref[:, part] = active
        product = product_ref[:, part]
        dweight = dweight + jnp.sum(active.astype(f32) * product, axis=1, keepdims=True)
        dnormed = dnormed + nt((scaling * product * slope).astype(bf16), w_up[:, part])
    dweight_ref[...] = jnp.broadcast_to(dweight, dweight_ref.shape)
    scaled = gain * dnormed
    dmiddle = scale * scaled - middle * (scale * scale * scale) * jnp.mean(scaled * middle, axis=-1, keepdims=True)
    dmiddle_ref[...] = dmiddle
    dattn = (dbranch + dmiddle).astype(bf16)
    pack_rows(sent_ref, 0, nt(dattn, w_out[...]).astype(bf16))
    pack_rows(sent_ref, HALF, dattn)
    write_note(sent_ref, 2 * HALF, jnp.sum(jnp.where(live, dweight * gate, 0.0), axis=0, keepdims=True))


def put_kernel(
    own_ref, counts_ref, chosen_ref, total_ref, both_ref, vectors_ref, active_ref, attn_ref, old_ref, down_ref,
    result_ref, w_down, sems,
):
    rows_of_chunk = down_ref.shape[0] // CHUNKS
    parts = [pl.ds(c * rows_of_chunk, rows_of_chunk) for c in range(CHUNKS)]
    copies = [pltpu.make_async_copy(down_ref.at[p, :], w_down.at[p, :], sems.at[c]) for c, p in enumerate(parts)]
    for copy in copies:
        copy.start()
    rows = both_ref[0, : both_ref.shape[1] // 2, :].astype(f32)
    scaling = gate_of(rows, vectors_ref) * (total_count(counts_ref) / total_ref[:1, :1])
    mlp_out = jnp.zeros_like(rows)
    for c, copy in enumerate(copies):
        part = slice(c * rows_of_chunk, (c + 1) * rows_of_chunk)
        copy.wait()
        mlp_out = mlp_out + nn(active_ref[:, part], w_down[part, :])
    new = (rows + scaling * (attn_ref[...] + mlp_out)).astype(bf16)
    put_rows(own_ref, counts_ref, chosen_ref, old_ref, new, result_ref)


def put_rows(own_ref, counts_ref, chosen_ref, old_ref, new, result_ref):
    hot = one_hot(own_ref, counts_ref, chosen_ref, old_ref.shape[0], True)
    hit = jnp.sum(hot, axis=1, keepdims=True) > 0.5
    placed = nn(hot.astype(bf16), new)
    result_ref[...] = jnp.where(hit, placed, old_ref[...].astype(f32)).astype(bf16)


def router_slope(own_ref, counts_ref, rows, dweight_ref, total_ref, coef_ref, vectors_ref):
    gate = gate_of(rows, vectors_ref)
    live = live_column(own_ref, counts_ref, rows.shape[0])
    count = total_count(counts_ref)
    total = total_ref[:1, :1]
    dscore = dweight_ref[:, :1] * (count / total) - coef_ref[:1, :1] * count / (total * total)
    return jnp.where(live, dscore * gate * (1.0 - gate), 0.0)


def keys_kernel(dq_ref, dkv_ref, moved_ref, coef_ref, sent_ref, sum_ref):
    rows = dkv_ref.shape[0]
    sent_ref[:, :HALF, :] = dq_ref[...]
    dkv = dkv_ref[...] + moved_ref[:rows, :]
    sent_ref[:, HALF:, :] = dkv.astype(bf16).reshape(sent_ref.shape[0], SHARE, LANES)
    sum_ref[...] = coef_ref[...] + moved_ref[rows:, :]


def units_kernel(
    own_ref, counts_ref, got_ref, dqkv_ref, total_ref, coef_ref, vectors_ref, rows_ref, dweight_ref,
    out_ref, up_ref, down_ref, *rest,
):
    gathers = []
    for count in PIECES:
        gathers.append(rest[:count])
        rest = rest[count:]
    down_keep_ref, down_give_ref, keep_ref, give_ref, rest = *rest[:4], rest[4:]
    *slots, grad_up, grad_down, grad_out, grad_q, grad_kv, ratio_ref, sems = rest
    rows_slots, upstream_slots, mixed_slots = slots
    step = pl.program_id(0)
    steps = pl.num_programs(0)
    _, sources, capacity, width = mixed_slots.shape
    core = own_ref[0] % 2
    slot = step % 2

    def copies(k):
        at = k % 2
        result = []
        for i, pieces in enumerate(gathers):
            if k < 3 or len(pieces) == 4:
                result.append(pltpu.make_async_copy(pieces[k], slots[i].at[at], sems.at[at, i, 0]))
                continue
            for half in range(2):
                target = slots[i].at[at, 2 * half : 2 * half + 2]
                result.append(pltpu.make_async_copy(pieces[k + half], target, sems.at[at, i, half]))
        return result

    for k in range(4):

        @pl.when(step == max(k - 1, 0))
        def _(k=k):
            for copy in copies(k):
                copy.start()

    @pl.when(step == 0)
    def _():
        for ref in (grad_up, grad_down, grad_out, grad_q, grad_kv):
            ref[...] = jnp.zeros_like(ref)
        ratio_ref[...] = jnp.broadcast_to(total_count(counts_ref) / total_ref[:1, :1], ratio_ref.shape)

    for k in range(4):

        @pl.when(step == k)
        def _(k=k):
            for copy in copies(k):
                copy.wait()

    def halves(ref, first):
        blocks = [ref[chip_of(own_ref, 4 * step + j), first : first + HALF, :] for j in range(sources)]
        turned = jnp.transpose(jnp.concatenate(blocks, axis=0).astype(f32)).astype(bf16)
        return turned[:HEAD_DIM], turned[HEAD_DIM:]

    def low_high(value):
        value = value.reshape(sources, capacity, width)
        return value[:, :HALF, :].reshape(sources * HALF, width), value[:, HALF:, :].reshape(sources * HALF, width)

    rows = rows_slots[slot].reshape(sources * capacity, width).astype(f32)
    upstream = upstream_slots[slot].reshape(sources * capacity, width).astype(f32)
    mixed = mixed_slots[slot].reshape(sources * capacity, width)
    normed_attn = (rows * inverse_rms(rows) * vectors_ref[1:2, :]).astype(bf16)
    low_query, high_query = halves(dqkv_ref, 0)
    low_rows, high_rows = low_high(normed_attn)
    grad_q[...] += nn(low_query, low_rows) + nn(high_query, high_rows)
    blocks = [dqkv_ref[chip_of(own_ref, 4 * step + j), HALF:, :] for j in range(sources)]
    pairs_turned = jnp.transpose(jnp.concatenate(blocks, axis=0).astype(f32)).astype(bf16)
    grad_kv[...] += nn(pairs_turned, normed_attn)
    low_attn, high_attn = halves(got_ref, HALF)
    low_mixed, high_mixed = low_high(mixed)
    grad_out[...] += nn(low_attn, low_mixed) + nn(high_attn, high_mixed)
    middle = rows + nn(mixed, out_ref[...])
    normed = (middle * inverse_rms(middle) * vectors_ref[2:3, :]).astype(bf16)
    dmlp = (gate_of(rows, vectors_ref) * ratio_ref[:1, :1] * upstream).astype(bf16)
    value, slope = gelu_pair(nn(normed, up_ref[...]))
    dhidden = nt(dmlp, down_ref[...]) * slope
    grad_down[...] += nn(jnp.transpose(value).astype(bf16), dmlp)
    grad_up[...] += nn(jnp.transpose(dhidden).astype(bf16), normed)

    @pl.when(step == steps - 1)
    def _():
        chips = keep_ref.shape[0]

        def split(value):
            value = value.reshape(chips, 2, OUT_ROWS, LANES)
            even, odd = value[:, 0], value[:, 1]
            return jnp.where(core == 0, even, odd), jnp.where(core == 0, odd, even)

        def store(first, kept, given):
            keep_ref[:, first : first + kept.shape[1], :] = kept.astype(bf16)
            give_ref[:, first : first + kept.shape[1], :] = given.astype(bf16)

        for t in range(TILES):
            store(t * OUT_ROWS, *split(jnp.transpose(grad_up[t * LANES : (t + 1) * LANES, :])))

        def two_in_one(value):
            return joined(value[:, :OUT_HALF], swapped(value[:, OUT_HALF:]))

        both_turned = jnp.transpose(jnp.concatenate([grad_out[...], grad_q[...]], axis=0))
        kept, given = split(both_turned)
        store(AT_OUT, two_in_one(kept), two_in_one(given))
        store(AT_QUERY, two_in_one(swapped(kept)), two_in_one(swapped(given)))
        store(AT_PAIR, *split(jnp.transpose(grad_kv[...])))
        own_rows = rows_ref[0, :capacity, :].astype(f32)
        dlogit = router_slope(own_ref, counts_ref, own_rows, dweight_ref, total_ref, coef_ref, vectors_ref)
        part = jnp.broadcast_to(jnp.sum(dlogit * own_rows, axis=0, keepdims=True), (NOTE, width))
        per_tile = LANES // OUT_ROWS
        for c in range(chips):
            tile = part[:, (2 * c) // per_tile * LANES : ((2 * c) // per_tile + 1) * LANES]
            shift = (2 * c) % per_tile * OUT_ROWS
            if shift:
                tile = jnp.concatenate([tile[:, shift:], tile[:, :shift]], axis=1)
            after = jnp.concatenate([tile[:, OUT_ROWS:], tile[:, :OUT_ROWS]], axis=1)
            keep_ref[c, AT_NOTE:, :] = in_parts(jnp.where(core == 0, tile, after))
            give_ref[c, AT_NOTE:, :] = in_parts(jnp.where(core == 0, after, tile))
        down = grad_down[...]
        half = down.shape[0] // 2
        down_keep_ref[...] = jnp.where(core == 0, down[:half], down[half:])
        down_give_ref[...] = jnp.where(core == 0, down[half:], down[:half]).astype(bf16)


def merge_kernel(keep_ref, moved_ref, sent_ref):
    total = keep_ref[...].astype(f32) + moved_ref[...].astype(f32)
    sent_ref[:, :AT_NOTE, :] = total[:, :AT_NOTE].astype(bf16)
    note = jnp.sum(total[:, AT_NOTE:], axis=1, keepdims=True)
    sent_ref[:, AT_NOTE:, :] = in_parts(jnp.broadcast_to(note, (note.shape[0], NOTE, LANES)))


def rows_kernel(
    own_ref, counts_ref, chosen_ref, got_ref, both_ref, dmiddle_ref, dweight_ref, total_ref, coef_ref, vectors_ref,
    old_ref, wq_ref, wk_ref, wv_ref, grads_ref, wq, wk, wv, sems,
):
    copies = [
        pltpu.make_async_copy(source, target, sems.at[i])
        for i, (source, target) in enumerate(((wq_ref, wq), (wk_ref, wk), (wv_ref, wv)))
    ]
    for copy in copies:
        copy.start()
    capacity = dmiddle_ref.shape[0]
    rows = both_ref[0, :capacity, :].astype(f32)
    upstream = both_ref[0, capacity:, :].astype(f32)
    gain = vectors_ref[1:2, :]
    dlogit = router_slope(own_ref, counts_ref, rows, dweight_ref, total_ref, coef_ref, vectors_ref)
    partial = upstream + dmiddle_ref[...] + dlogit * vectors_ref[0:1, :]
    dquery = unpack_rows(got_ref, 0, HALF)
    dkey, dvalue = unpack_pairs(got_ref, HALF, SHARE)
    copies[0].wait()
    dnormed = jnp.zeros_like(partial) + nt(dquery, wq[...])
    copies[1].wait()
    dnormed = dnormed + nt(dkey, wk[...])
    copies[2].wait()
    dnormed = dnormed + nt(dvalue, wv[...])
    scale = inverse_rms(rows)
    scaled = gain * dnormed
    drows = scale * scaled - rows * (scale * scale * scale) * jnp.mean(scaled * rows, axis=-1, keepdims=True)
    put_rows(own_ref, counts_ref, chosen_ref, old_ref, (partial + drows).astype(bf16), grads_ref)


def finish_kernel(
    got_ref, own_gain_ref, up_ref, wq_ref, wk_ref, wv_ref,
    grad_up_ref, grad_out_ref, grad_q_ref, grad_k_ref, grad_v_ref, router_ref, gain_attn_ref, gain_mlp_ref,
):
    total = jnp.zeros((OUT_ROWS, LANES), f32)
    for c in range(got_ref.shape[0]):
        for t in range(TILES):
            lanes = slice((TILES * c + t) * LANES, (TILES * c + t + 1) * LANES)
            part = got_ref[c, t * OUT_ROWS : (t + 1) * OUT_ROWS, :].astype(f32)
            grad_up_ref[:, lanes] = part
            total = total + part * up_ref[:, lanes].astype(f32)
    gain_mlp_ref[...] = row_of(jnp.sum(total, axis=1, keepdims=True)) / own_gain_ref[2:3, :]
    grad_out_ref[...] = unpack_rows(got_ref, AT_OUT, OUT_HALF).astype(f32)
    grad_q = unpack_rows(got_ref, AT_QUERY, OUT_HALF).astype(f32)
    grad_k, grad_v = (value.astype(f32) for value in unpack_pairs(got_ref, AT_PAIR, OUT_ROWS))
    grad_q_ref[...] = grad_q
    grad_k_ref[...] = grad_k
    grad_v_ref[...] = grad_v
    products = wq_ref[...].astype(f32) * grad_q + wk_ref[...].astype(f32) * grad_k + wv_ref[...].astype(f32) * grad_v
    gain_attn_ref[...] = row_of(jnp.sum(products, axis=1, keepdims=True)) / own_gain_ref[1:2, :]
    notes = jnp.sum(got_ref[:, AT_NOTE:, :].astype(f32), axis=0)
    router_ref[...] = jnp.sum(notes, axis=0, keepdims=True)[:, :OUT_ROWS]


def pair_attend_kernel(factor, got_ref, other_ref, kpos_ref, qpos_ref, qlow_ref, mixed_ref, turned_ref, lse_ref, total_ref):
    lists = (got_ref, other_ref)
    chips = got_ref.shape[0]
    blocks = chips * HALF // BLOCK
    sources = chips // blocks
    total = read_note(got_ref, HALF + SHARE) + read_note(other_ref, HALF + SHARE)
    total_ref[...] = jnp.broadcast_to(total, total_ref.shape)
    attend_core(
        factor,
        lambda b: got_ref[b * sources : (b + 1) * sources, :HALF, :].reshape(BLOCK, LANES),
        lambda m, extent: lists[m][: extent // SHARE, HALF : HALF + SHARE, :].reshape(extent, LANES),
        2, blocks, chips * SHARE, kpos_ref, qpos_ref, qlow_ref, mixed_ref, turned_ref, lse_ref,
    )


def pair_attend_back_kernel(
    factor, got_ref, other_ref, grad_ref, kpos_ref, qpos_ref, qlow_ref, turned_ref, lse_ref,
    dq_ref, own_ref, moved_ref, coef_ref,
):
    lists = (got_ref, other_ref)
    sums = (own_ref, moved_ref)
    chips = got_ref.shape[0]
    blocks = chips * HALF // BLOCK
    sources = chips // blocks
    coef = jnp.broadcast_to(read_note(grad_ref, 2 * HALF), coef_ref.shape)
    coef_ref[...] = coef
    moved_ref[chips * SHARE :, :] = coef

    def add_dkv(m, extent, first, update):
        if first:
            sums[m][:extent, :] = update
        else:
            sums[m][:extent, :] += update

    attend_back_core(
        factor,
        lambda b: got_ref[b * sources : (b + 1) * sources, :HALF, :].reshape(BLOCK, LANES),
        lambda b: grad_ref[b * sources : (b + 1) * sources, :HALF, :].reshape(BLOCK, LANES),
        lambda m, extent: lists[m][: extent // SHARE, HALF : HALF + SHARE, :].reshape(extent, LANES),
        2, blocks, chips * SHARE, kpos_ref, qpos_ref, qlow_ref, turned_ref, lse_ref, dq_ref, add_dkv,
    )


smem = pl.BlockSpec(memory_space=pltpu.SMEM)
hbm = pl.BlockSpec(memory_space=pl.ANY)
megabytes = {
    "places": 4, "early": 56, "fetch": 56, "project": 16, "attend": 20, "unpack": 4, "middle": 56, "put": 56, "attend_back": 24,
    "keys": 8, "units": 56, "merge": 10, "rows": 56, "finish": 12,
}


def params_of(name):
    return pltpu.CompilerParams(vmem_limit_bytes=megabytes[name] * 1024 * 1024)


def shaped(shape, dtype):
    return jax.ShapeDtypeStruct(shape, dtype)


microseconds = {
    "places": 1, "early": 5, "fetch": 3, "project": 4, "attend": 5, "unpack": 2, "middle": 11, "put": 6, "attend_back": 6, "keys": 2,
    "units": 16, "merge": 3, "rows": 7, "finish": 2,
}


def cost_of(name):
    return pl.CostEstimate(flops=0, transcendentals=0, bytes_accessed=microseconds[name] * 3_300_000)


def call(kernel, name, in_specs, out_shape, arguments, scratch=()):
    return pl.pallas_call(
        kernel,
        out_shape=out_shape,
        in_specs=in_specs,
        out_specs=jax.tree.map(lambda _: vmem, out_shape),
        scratch_shapes=list(scratch),
        compiler_params=params_of(name),
        cost_estimate=cost_of(name),
        name=name,
    )(*arguments)


def pairs(
    tokens_in,
    w_router,
    gain_attn,
    w_query,
    w_key,
    w_value,
    w_out,
    gain_mlp,
    w_up,
    w_down,
    out_grad,
    lengths,
    counts,
    chosen,
):
    devices = lax.axis_size("seq")
    chips = devices // 2
    own = lax.axis_index("seq")
    capacity = chosen.shape[0] // devices
    tok_rows, width = tokens_in.shape
    hidden_width = w_up.shape[1]
    out_rows = width // devices
    factor = HEAD_DIM ** (-0.5)
    core = own % 2
    own_id = own.astype(jnp.int32).reshape(1)
    chosen = chosen.reshape(chips, 2 * capacity)
    vectors = jnp.stack([w_router, gain_attn, gain_mlp]).astype(f32)
    own_gains = lax.dynamic_slice_in_dim(vectors, own * out_rows, out_rows, 1)
    cores = [[2 * c + k for c in range(chips)] for k in range(2)]

    def swap(value):
        return lax.all_to_all(value, "seq", split_axis=0, concat_axis=0, tiled=True, axis_index_groups=cores)

    def across(value, bits):
        return lax.ppermute(value, "seq", [(s, s ^ bits) for s in range(devices)])

    def line_of(block):
        return jnp.concatenate([block] + [across(block, 8 * k) for k in (1, 2, 3)], axis=0)

    def sides_of(line):
        return [line, across(line, 2), across(line, 4)]

    def gathered(sides):
        return sides + [across(sides[2][:2], 2), across(sides[1][2:], 4)]

    def gathered_whole(sides):
        return sides + [across(sides[2], 2)]

    blocks = chips * HALF // BLOCK
    square = pltpu.VMEM((width, width), bf16)
    block = shaped((1, capacity, width), bf16)
    both, own_rows, own_upstream = call(
        fetch_kernel, "fetch", [smem, smem] + [vmem] * 3, (shaped((1, 2 * capacity, width), bf16), block, block),
        (own_id, counts, chosen, tokens_in, out_grad),
    )
    rows_line = line_of(own_rows)
    product = call(
        early_kernel, "early", [vmem, hbm], shaped((capacity, hidden_width), f32), (both, w_down),
        [pltpu.VMEM((hidden_width, width), bf16), pltpu.SemaphoreType.DMA((CHUNKS,))],
    )
    chosen_after, product, rows_line = lax.optimization_barrier((chosen, product, rows_line))
    kpos, qpos, qlow = call(
        places_kernel, "places", [smem] * 3 + [vmem],
        (
            shaped((2, chips * SHARE), f32),
            shaped((blocks, 2 * BLOCK), f32),
            shaped((blocks, 2 * BLOCK), f32),
        ),
        (own_id, counts, jnp.append(lengths, tok_rows), chosen_after),
    )
    rows_all = gathered(sides_of(rows_line))
    column = own // 4 * LANES
    columns = [lax.dynamic_slice_in_dim(w, column, LANES, 1) for w in (w_query, w_key, w_value)]
    upstream_line = line_of(own_upstream)
    rows_all, upstream_line = lax.optimization_barrier((rows_all, upstream_line))
    kpos, qpos, qlow, columns, rows_all = lax.optimization_barrier((kpos, qpos, qlow, columns, rows_all))
    got = call(
        project_kernel, "project", [smem, smem] + [vmem] * 9,
        shaped((chips, HALF + SHARE + NOTE, LANES), bf16),
        (own_id, counts, vectors, *columns, *rows_all),
    )
    other = across(got, 1)
    upstream_sides = sides_of(upstream_line)
    mixed_packed, turned, lse, total = call(
        functools.partial(pair_attend_kernel, factor), "attend", [vmem] * 5,
        (
            shaped((chips * HALF, LANES), bf16),
            shaped((chips * HALF, LANES), f32),
            shaped((blocks, 2 * BLOCK), f32),
            shaped((8, LANES), f32),
        ),
        (got, other, kpos, qpos, qlow),
    )
    mixed_got = swap(mixed_packed.reshape(chips, HALF, LANES))
    upstream_sides, mixed_got = lax.optimization_barrier((upstream_sides, mixed_got))
    upstream_all = gathered_whole(upstream_sides)
    mixed = call(unpack_kernel, "unpack", [vmem], shaped((1, capacity, width), bf16), (mixed_got,))
    mixed_line = line_of(mixed)
    sent, active, attn_out, dmiddle, dweight = call(
        middle_kernel, "middle", [smem, smem] + [vmem] * 5 + [hbm] * 2,
        (
            shaped((chips, 2 * HALF + NOTE, LANES), bf16),
            shaped((capacity, hidden_width), bf16),
            shaped((capacity, width), f32),
            shaped((capacity, width), f32),
            shaped((capacity, LANES), f32),
        ),
        (own_id, counts, mixed, total, both, vectors, product, w_out, w_up),
        [
            square,
            pltpu.VMEM((width, hidden_width), bf16),
            pltpu.SemaphoreType.DMA((1 + CHUNKS,)),
        ],
    )
    mixed_line, sent = lax.optimization_barrier((mixed_line, sent))
    mixed_sides = sides_of(mixed_line)
    upstream_all, sent = lax.optimization_barrier((upstream_all, sent))
    grads_got = swap(sent)
    output = call(
        put_kernel, "put", [smem, smem] + [vmem] * 7 + [hbm], shaped((tok_rows, width), bf16),
        (own_id, counts, chosen, total, both, vectors, active, attn_out, tokens_in, w_down),
        [pltpu.VMEM((hidden_width, width), bf16), pltpu.SemaphoreType.DMA((CHUNKS,))],
    )
    mixed_all = gathered(mixed_sides)
    output, grads_got = lax.optimization_barrier((output, grads_got))
    dq, dkv_own, dkv_other, coef = call(
        functools.partial(pair_attend_back_kernel, factor), "attend_back", [vmem] * 8,
        (
            shaped((chips * HALF, LANES), bf16),
            shaped((chips * SHARE, LANES), f32),
            shaped((chips * SHARE + 8, LANES), f32),
            shaped((8, LANES), f32),
        ),
        (got, other, grads_got, kpos, qpos, qlow, turned, lse),
    )
    moved = across(dkv_other, 1)
    dqkv, coef = call(
        keys_kernel, "keys", [vmem] * 4,
        (shaped((chips, HALF + SHARE, LANES), bf16), shaped((8, LANES), f32)),
        (dq.reshape(chips, HALF, LANES), dkv_own, moved, coef),
    )
    got = swap(dqkv)
    sources = 4
    hidden_cols = hidden_width // chips
    whole = lambda *shape: pl.BlockSpec(shape, lambda i, o: (0,) * len(shape))
    down_keep, down_give, keep, give = pl.pallas_call(
        units_kernel,
        out_shape=(
            shaped((hidden_cols // 2, width), f32),
            shaped((hidden_cols // 2, width), bf16),
            shaped((chips, GRAD_ROWS, LANES), bf16),
            shaped((chips, GRAD_ROWS, LANES), bf16),
        ),
        grid_spec=pltpu.PrefetchScalarGridSpec(
            num_scalar_prefetch=1,
            grid=(chips // sources,),
            in_specs=[
                smem,
                whole(chips, 2 * HALF + NOTE, LANES),
                whole(chips, HALF + SHARE, LANES),
                whole(8, LANES),
                whole(8, LANES),
                whole(3, width),
                whole(1, 2 * capacity, width),
                whole(capacity, LANES),
                whole(width, width),
                pl.BlockSpec((width, hidden_cols), lambda i, o: (0, o[0] // 2)),
                pl.BlockSpec((hidden_cols, width), lambda i, o: (o[0] // 2, 0)),
            ]
            + [hbm] * sum(PIECES),
            out_specs=(
                whole(hidden_cols // 2, width),
                whole(hidden_cols // 2, width),
                whole(chips, GRAD_ROWS, LANES),
                whole(chips, GRAD_ROWS, LANES),
            ),
            scratch_shapes=[
                pltpu.VMEM((2, sources, capacity, width), bf16),
                pltpu.VMEM((2, sources, capacity, width), bf16),
                pltpu.VMEM((2, sources, capacity, width), bf16),
                pltpu.VMEM((hidden_cols, width), f32),
                pltpu.VMEM((hidden_cols, width), f32),
                pltpu.VMEM((HEAD_DIM, width), f32),
                pltpu.VMEM((HEAD_DIM, width), f32),
                pltpu.VMEM((2 * HEAD_DIM, width), f32),
                pltpu.VMEM((8, LANES), f32),
                pltpu.SemaphoreType.DMA((2, 3, 2)),
            ],
        ),
        compiler_params=params_of("units"),
        cost_estimate=cost_of("units"),
        name="units",
    )(own_id, counts, grads_got, dqkv, total, coef, vectors, both, dweight, w_out, w_up, w_down, *rows_all, *upstream_all, *mixed_all)
    sent = call(
        merge_kernel, "merge", [vmem] * 2, shaped((chips, GRAD_ROWS, LANES), bf16), (keep, across(give, 1))
    )
    grad_down = down_keep + across(down_give, 1).astype(f32)
    last = swap(sent)
    input_grad = call(
        rows_kernel, "rows", [smem, smem] + [vmem] * 9 + [hbm] * 3, shaped((tok_rows, width), bf16),
        (
            own_id, counts, chosen, got, both, dmiddle, dweight, total, coef, vectors, out_grad,
            w_query, w_key, w_value,
        ),
        [square] * 3 + [pltpu.SemaphoreType.DMA((3,))],
    )
    block = shaped((out_rows, width), f32)
    row = shaped((1, out_rows), f32)
    first_row = own * out_rows
    grad_up, grad_out, grad_query, grad_key, grad_value, grad_router, grad_gain_attn, grad_gain_mlp = call(
        finish_kernel, "finish", [vmem] * 6,
        (shaped((out_rows, hidden_width), f32), block, block, block, block, row, row, row),
        (last, own_gains, *(lax.dynamic_slice_in_dim(w, first_row, out_rows) for w in (w_up, w_query, w_key, w_value))),
    )
    return (
        output,
        input_grad,
        grad_router.reshape(out_rows),
        grad_gain_attn.reshape(out_rows),
        grad_query,
        grad_key,
        grad_value,
        grad_out,
        grad_gain_mlp.reshape(out_rows),
        grad_up,
        grad_down,
    )


def per_device(*arguments):
    w_up, chosen = arguments[8], arguments[13]
    devices = lax.axis_size("seq")
    width, hidden_width = w_up.shape
    paired = (
        devices == 2 * HEADS
        and chosen.shape[0] == devices * SHARE
        and width == devices * OUT_ROWS
        and width == HEADS * HEAD_DIM
        and hidden_width == devices // 2 * TILES * LANES
    )
    return (pairs if paired else general)(*arguments)


def solution(mesh):
    placed = (P("seq", None),) + (P(),) * 9 + (P("seq", None),) + (P(),) * 3
    rows = P("seq", None)
    return jax.shard_map(
        per_device,
        mesh=mesh,
        in_specs=placed,
        out_specs=(rows, rows, P("seq"), P("seq"), rows, rows, rows, rows, P("seq"), rows, rows),
        check_vma=False,
    )
```

```python
import functools
import jax
import jax.numpy as jnp
from jax import lax
from jax.experimental import pallas as pl
from jax.experimental.pallas import tpu as pltpu
from jax.sharding import PartitionSpec as P

HEADS = 16
HEAD_DIM = 64
LANES = 128
BLOCK = 128

masked_score = -1e30
eps_norm = 1e-05
far_away = 1e9

f32 = jnp.float32
bf16 = jnp.bfloat16


def nt(left, right):
    return lax.dot_general(left, right, (((1,), (1,)), ((), ())), preferred_element_type=f32)


def nn(left, right):
    return lax.dot_general(left, right, (((1,), (0,)), ((), ())), preferred_element_type=f32)


def rms_scale(values, gain):
    return values * lax.rsqrt(jnp.mean(values * values, axis=-1, keepdims=True) + eps_norm) * gain


def three_parts(value):
    high = lax.reduce_precision(value, 8, 7)
    rest = value - high
    middle = lax.reduce_precision(rest, 8, 7)
    return jnp.stack([high, middle, rest - middle]).astype(bf16)


def spread_rows(packed, upper):
    lanes = lax.broadcasted_iota(jnp.int32, packed.shape, 1)
    zero = jnp.zeros_like(packed)
    rolled = jnp.concatenate([packed[:, HEAD_DIM:], packed[:, :HEAD_DIM]], axis=1)
    if upper:
        return jnp.concatenate(
            [jnp.where(lanes >= HEAD_DIM, rolled, zero), jnp.where(lanes >= HEAD_DIM, packed, zero)], axis=0
        )
    return jnp.concatenate(
        [jnp.where(lanes < HEAD_DIM, packed, zero), jnp.where(lanes < HEAD_DIM, rolled, zero)], axis=0
    )


def pack_columns(turned):
    return jnp.concatenate([turned[:, :BLOCK], turned[:, BLOCK:]], axis=0)


def key_columns(kpos_ref, member, extent):
    row = kpos_ref[member : member + 1, :extent]
    column = jnp.transpose(jnp.broadcast_to(row, (LANES, extent)))
    return jnp.concatenate([column, column], axis=1)


def attend_core(factor, load_query, load_kv, members, blocks, key_rows, kpos_ref, qpos_ref, qlow_ref, mixed_ref, turned_ref, lse_ref):
    kv_turned = [jnp.transpose(load_kv(m, key_rows)) for m in range(members)]
    for b in range(blocks):
        extent = key_rows * (b + 1) // blocks
        packed = (load_query(b).astype(f32) * factor).astype(bf16)
        wide = spread_rows(packed, False)
        qpos = qpos_ref[b : b + 1, :]
        qlow = qlow_ref[b : b + 1, :]
        scores = []
        for m in range(members):
            score = nt(load_kv(m, extent), wide)
            kpos = key_columns(kpos_ref, m, extent)
            score = jnp.where((kpos <= qpos) & (kpos >= qlow), score, masked_score)
            scores.append(score)
        peak = jnp.max(scores[0], axis=0, keepdims=True)
        for score in scores[1:]:
            peak = jnp.maximum(peak, jnp.max(score, axis=0, keepdims=True))
        peak = jnp.maximum(peak, 0.1 * masked_score)
        total = jnp.zeros_like(peak)
        mixed = jnp.zeros((LANES, 2 * BLOCK), f32)
        for m in range(members):
            prob = jnp.exp(scores[m] - peak)
            total = total + jnp.sum(prob, axis=0, keepdims=True)
            mixed = mixed + nn(kv_turned[m][:, :extent], prob.astype(bf16))
        safe = jnp.where(total > 0, total, 1.0)
        lse_ref[b : b + 1, :] = peak + jnp.log(safe)
        turned = pack_columns(mixed[HEAD_DIM:, :] / safe)
        turned_ref[b * BLOCK : (b + 1) * BLOCK, :] = turned
        mixed_ref[b * BLOCK : (b + 1) * BLOCK, :] = jnp.transpose(turned).astype(bf16)


def attend_back_core(
    factor, load_query, load_grad, load_kv, members, blocks, key_rows, kpos_ref, qpos_ref, qlow_ref, turned_ref, lse_ref,
    dq_ref, add_dkv,
):
    kv_turned = [jnp.transpose(load_kv(m, key_rows)) for m in range(members)]
    for b in range(blocks - 1, -1, -1):
        extent = key_rows * (b + 1) // blocks
        rows = slice(b * BLOCK, (b + 1) * BLOCK)
        packed = (load_query(b).astype(f32) * factor).astype(bf16)
        grads = load_grad(b)
        wide = jnp.concatenate([spread_rows(packed, False), spread_rows(grads, True)], axis=0)
        product = jnp.transpose(grads.astype(f32)) * turned_ref[rows, :]
        delta = jnp.concatenate(
            [
                jnp.sum(product[:HEAD_DIM], axis=0, keepdims=True),
                jnp.sum(product[HEAD_DIM:], axis=0, keepdims=True),
            ],
            axis=1,
        )
        qpos = qpos_ref[b : b + 1, :]
        qlow = qlow_ref[b : b + 1, :]
        lse = lse_ref[b : b + 1, :]
        dquery = jnp.zeros((LANES, 2 * BLOCK), f32)
        for m in range(members):
            both = nt(load_kv(m, extent), wide)
            kpos = key_columns(kpos_ref, m, extent)
            prob = jnp.exp(
                jnp.where((kpos <= qpos) & (kpos >= qlow), both[:, : 2 * BLOCK] - lse, masked_score)
            )
            dlogit = (prob * (both[:, 2 * BLOCK :] - delta)).astype(bf16)
            dquery = dquery + nn(kv_turned[m][:, :extent], dlogit)
            add_dkv(m, extent, b == blocks - 1, nn(jnp.concatenate([dlogit, prob.astype(bf16)], axis=1), wide))
        dq_ref[rows, :] = jnp.transpose(pack_columns(dquery[:HEAD_DIM, :] * factor)).astype(bf16)


def attend_kernel(factor, q_ref, kv_ref, kpos_ref, qpos_ref, qlow_ref, mixed_ref, turned_ref, lse_ref):
    members, key_rows, _ = kv_ref.shape
    attend_core(
        factor,
        lambda b: q_ref[b * BLOCK : (b + 1) * BLOCK, :],
        lambda m, extent: kv_ref[m, :extent, :],
        members, q_ref.shape[0] // BLOCK, key_rows, kpos_ref, qpos_ref, qlow_ref, mixed_ref, turned_ref, lse_ref,
    )


def attend_back_kernel(
    factor, q_ref, do_ref, kv_ref, kpos_ref, qpos_ref, qlow_ref, turned_ref, lse_ref, dq_ref, dkv_ref
):
    members, key_rows, _ = kv_ref.shape

    def add_dkv(m, extent, first, update):
        if first:
            dkv_ref[m, :extent, :] = update
        else:
            dkv_ref[m, :extent, :] += update

    attend_back_core(
        factor,
        lambda b: q_ref[b * BLOCK : (b + 1) * BLOCK, :],
        lambda b: do_ref[b * BLOCK : (b + 1) * BLOCK, :],
        lambda m, extent: kv_ref[m, :extent, :],
        members, q_ref.shape[0] // BLOCK, key_rows, kpos_ref, qpos_ref, qlow_ref, turned_ref, lse_ref, dq_ref, add_dkv,
    )


vmem = pl.BlockSpec(memory_space=pltpu.VMEM)
vmem_limit = 56 * 1024 * 1024


def attend(factor, queries, kv, kpos, qpos, qlow):
    rows = queries.shape[0]
    return pl.pallas_call(
        functools.partial(attend_kernel, factor),
        out_shape=(
            jax.ShapeDtypeStruct((rows, LANES), bf16),
            jax.ShapeDtypeStruct((rows, LANES), f32),
            jax.ShapeDtypeStruct(qpos.shape, f32),
        ),
        in_specs=[vmem] * 5,
        out_specs=(vmem,) * 3,
        compiler_params=pltpu.CompilerParams(vmem_limit_bytes=vmem_limit),
        name="attend",
    )(queries, kv, kpos, qpos, qlow)


def attend_back(factor, queries, dmixed, kv, kpos, qpos, qlow, turned, lse):
    rows = queries.shape[0]
    return pl.pallas_call(
        functools.partial(attend_back_kernel, factor),
        out_shape=(
            jax.ShapeDtypeStruct((rows, LANES), bf16),
            jax.ShapeDtypeStruct(kv.shape, f32),
        ),
        in_specs=[vmem] * 8,
        out_specs=(vmem,) * 2,
        compiler_params=pltpu.CompilerParams(vmem_limit_bytes=vmem_limit),
        name="attend_back",
    )(queries, dmixed, kv, kpos, qpos, qlow, turned, lse)


def general(
    tokens_in,
    w_router,
    gain_attn,
    w_query,
    w_key,
    w_value,
    w_out,
    gain_mlp,
    w_up,
    w_down,
    out_grad,
    lengths,
    counts,
    chosen,
):
    devices = lax.axis_size("seq")
    own = lax.axis_index("seq")
    capacity = chosen.shape[0] // devices
    tok_rows, width = tokens_in.shape
    hidden_width = w_up.shape[1]
    group = devices // HEADS
    share = capacity // group
    half = share // 2
    member = own % group
    slots = devices * capacity
    factor = HEAD_DIM ** (-0.5)
    attn_gain = gain_attn.astype(f32)
    mlp_gain = gain_mlp.astype(f32)

    def swap(value):
        return lax.all_to_all(value, "seq", split_axis=0, concat_axis=0, tiled=True)

    groups = [[h * group + m for m in range(group)] for h in range(HEADS)]

    def across_group(value):
        if group == 2:
            other = lax.ppermute(value, "seq", [(s, s ^ 1) for s in range(devices)])
            return jnp.stack([value, other])
        return lax.all_gather(value, "seq", axis_index_groups=groups)

    def sum_over_group(value):
        if group == 2:
            return value[0] + lax.ppermute(value[1], "seq", [(s, s ^ 1) for s in range(devices)])
        return lax.psum_scatter(value, "seq", scatter_dimension=0, axis_index_groups=groups)

    def member_order(value):
        if group == 2:
            return jnp.where(member == 0, value, value[::-1])
        return value

    slot_ids = jnp.arange(capacity, dtype=jnp.int32)
    places = jnp.arange(devices, dtype=jnp.int32)[:, None] * tok_rows + chosen.reshape(devices, capacity)
    live_all = slot_ids[None, :] < counts[:, None]
    seq_ends = jnp.cumsum(lengths)
    starts = jnp.max(jnp.where(places[..., None] >= seq_ends, seq_ends, 0), axis=-1)
    kpos = jnp.where(live_all, places.astype(f32), far_away)
    kpos = member_order(kpos.reshape(devices, group, share).swapaxes(0, 1).reshape(group, devices * share))
    blocks = devices * half // BLOCK

    def query_order(value):
        value = lax.dynamic_index_in_dim(value.reshape(devices, group, share), member, 1, False)
        return value.reshape(blocks, devices // blocks, 2, half).swapaxes(1, 2).reshape(blocks, 2 * BLOCK)

    qpos = query_order(jnp.where(live_all, places, -1).astype(f32))
    qlow = query_order(starts.astype(f32))

    offsets = lax.dynamic_slice_in_dim(chosen, own * capacity, capacity)
    live = slot_ids < counts[own]
    pick = (offsets[:, None] == jnp.arange(tok_rows, dtype=jnp.int32)[None, :]).astype(bf16)
    routed = nn(pick, tokens_in)
    upstream = jnp.where(live[:, None], nn(pick, out_grad), 0.0)
    gate = jax.nn.sigmoid(jnp.sum(routed * w_router.astype(f32)[None, :], axis=1))
    gate_sum = jnp.sum(jnp.where(live, gate, 0.0))
    normed = rms_scale(routed, attn_gain).astype(bf16)
    normed_all = lax.all_gather(normed, "seq", axis=0, tiled=True)
    queries = nn(normed, w_query).astype(bf16)
    keys = nn(normed, w_key).astype(bf16)
    values = nn(normed, w_value).astype(bf16)

    def note(value):
        parts = jnp.pad(three_parts(value), (0, LANES - 3))
        return jnp.broadcast_to(parts, (devices, 8, LANES))

    def read_note(rows):
        return jnp.sum(rows[:, 0, :3].astype(f32))

    def to_heads(value, per_row):
        if per_row == 2:
            value = value.reshape(group, 2, half, HEADS, HEAD_DIM).transpose(3, 0, 2, 1, 4)
            return value.reshape(devices, half, LANES)
        return value

    def pair_to_heads(first, second):
        both = jnp.stack([first, second], axis=1).reshape(group, share, 2, HEADS, HEAD_DIM)
        return both.transpose(3, 0, 1, 2, 4).reshape(devices, share, LANES)

    def from_heads(value):
        value = value.reshape(HEADS, group, half, 2, HEAD_DIM).transpose(1, 3, 2, 0, 4)
        return value.reshape(capacity, HEADS * HEAD_DIM)

    def pair_from_heads(value):
        value = value.reshape(HEADS, group, share, 2, HEAD_DIM).transpose(3, 1, 2, 0, 4)
        value = value.reshape(2, capacity, HEADS * HEAD_DIM)
        return value[0], value[1]

    sent = jnp.concatenate([to_heads(queries, 2), pair_to_heads(keys, values), note(gate_sum)], axis=1)
    got = swap(sent)
    score_total = read_note(got[:, half + share :])
    chosen_total = jnp.sum(counts).astype(f32)
    ratio = chosen_total / score_total
    scaling = gate * ratio
    head_queries = got[:, :half].reshape(devices * half, LANES)
    kv = across_group(got[:, half : half + share].reshape(devices * share, LANES))
    mixed_packed, mixed_turned, lse = attend(factor, head_queries, kv, kpos, qpos, qlow)
    mixed = from_heads(swap(mixed_packed.reshape(devices, half, LANES)))

    attn_out = nn(mixed, w_out)
    middle = routed + attn_out
    normed_mlp = rms_scale(middle, mlp_gain).astype(bf16)
    dbranch = scaling[:, None] * upstream
    dmlp = dbranch.astype(bf16)
    gathered = lax.all_gather(
        jnp.concatenate([mixed, normed_mlp, dmlp], axis=1), "seq", axis=0, tiled=True
    )
    mixed_all = gathered[:, :width]
    normed_mlp_all = gathered[:, width : 2 * width]
    dmlp_all = gathered[:, 2 * width :]
    hidden = nn(normed_mlp, w_up)
    active = jax.nn.gelu(hidden, approximate=True).astype(bf16)
    branch = attn_out + nn(active, w_down)
    dweight = jnp.sum(upstream * branch, axis=1)

    def gelu_of(values):
        return jax.nn.gelu(values, approximate=True)

    dactive = nt(dmlp, w_down)
    dhidden = jax.vjp(gelu_of, hidden)[1](dactive)[0].astype(bf16)
    dnormed_mlp = nt(dhidden, w_up)
    dmiddle = jax.vjp(lambda v: rms_scale(v, mlp_gain), middle)[1](dnormed_mlp)[0]
    dattn = (dbranch + dmiddle).astype(bf16)
    dmixed = nt(dattn, w_out).astype(bf16)
    out_cols = width // devices
    dattn_split = dattn.reshape(capacity, devices, out_cols).swapaxes(0, 1)
    dattn_split = dattn_split.reshape(devices, capacity * out_cols // LANES, LANES)
    got = swap(
        jnp.concatenate(
            [to_heads(dmixed, 2), dattn_split, note(jnp.sum(jnp.where(live, dweight * gate, 0.0)))], axis=1
        )
    )
    dattn_own = got[:, half : half + capacity * out_cols // LANES].reshape(slots, out_cols)
    coefficient = read_note(got[:, half + capacity * out_cols // LANES :])
    dq_packed, dkv_parts = attend_back(
        factor,
        head_queries,
        got[:, :half].reshape(devices * half, LANES),
        kv,
        kpos,
        qpos,
        qlow,
        mixed_turned,
        lse,
    )
    dkv = sum_over_group(dkv_parts).astype(bf16)

    dscore = dweight * ratio - coefficient * chosen_total / (score_total * score_total)
    dlogit_router = jnp.where(live, dscore * gate * (1.0 - gate), 0.0)
    router_part = jnp.sum(dlogit_router[:, None] * routed, axis=0).reshape(devices, out_cols)
    router_parts = three_parts(router_part).swapaxes(0, 1).reshape(devices, 1, 3 * out_cols)
    router_note = jnp.pad(router_parts, ((0, 0), (0, 7), (0, LANES - 3 * out_cols)))
    got = swap(
        jnp.concatenate(
            [dq_packed.reshape(devices, half, LANES), dkv.reshape(devices, share, LANES), router_note], axis=1
        )
    )
    dquery = from_heads(got[:, :half])
    dkey, dvalue = pair_from_heads(got[:, half : half + share])
    grad_router = jnp.sum(got[:, half + share, : 3 * out_cols].astype(f32), axis=0)
    grad_router = jnp.sum(grad_router.reshape(3, out_cols), axis=0)

    normed_own = lax.dynamic_index_in_dim(normed_all.reshape(devices, group, share, width), member, 1, False)
    normed_own = normed_own.reshape(devices * share, width)
    dq_rows = dq_packed.reshape(devices, half, 2, HEAD_DIM).swapaxes(1, 2).reshape(devices * share, HEAD_DIM)
    dqkv = jnp.concatenate([dq_rows, dkv], axis=1)
    grad_qkv = lax.dot_general(normed_own, dqkv, (((0,), (0,)), ((), ())), preferred_element_type=f32)
    head_cols = 3 * HEAD_DIM // group
    grad_qkv = member_order(grad_qkv.reshape(width, group, head_cols).swapaxes(0, 1))
    grad_qkv = sum_over_group(grad_qkv).astype(bf16)
    grad_out = lax.dot_general(mixed_all, dattn_own, (((0,), (0,)), ((), ())), preferred_element_type=f32)

    hidden_cols = hidden_width // devices
    up_own = lax.dynamic_slice_in_dim(w_up, own * hidden_cols, hidden_cols, 1)
    down_own = lax.dynamic_slice_in_dim(w_down, own * hidden_cols, hidden_cols, 0)
    hidden_own = nn(normed_mlp_all, up_own)
    dactive_own = nt(dmlp_all, down_own)
    active_own, gelu_back = jax.vjp(gelu_of, hidden_own)
    dhidden_own = gelu_back(dactive_own)[0].astype(bf16)
    active_own = active_own.astype(bf16)
    grad_down = lax.dot_general(active_own, dmlp_all, (((0,), (0,)), ((), ())), preferred_element_type=f32)
    grad_up = lax.dot_general(
        normed_mlp_all, dhidden_own, (((0,), (0,)), ((), ())), preferred_element_type=f32
    )
    sent = jnp.concatenate([grad_up.astype(bf16), grad_qkv, grad_out.astype(bf16)], axis=1)
    got = swap(sent.reshape(devices, out_cols, sent.shape[1])).astype(f32)
    grad_up = got[:, :, :hidden_cols].swapaxes(0, 1).reshape(out_cols, hidden_width)
    grad_qkv = got[:, :, hidden_cols : hidden_cols + head_cols].reshape(HEADS, group, out_cols, head_cols)
    grad_qkv = grad_qkv.transpose(2, 0, 1, 3).reshape(out_cols, HEADS, 3, HEAD_DIM)
    grad_query = grad_qkv[:, :, 0].reshape(out_cols, width)
    grad_key = grad_qkv[:, :, 1].reshape(out_cols, width)
    grad_value = grad_qkv[:, :, 2].reshape(out_cols, width)
    grad_out = got[:, :, hidden_cols + head_cols :].swapaxes(0, 1).reshape(out_cols, width)

    def own_rows(value):
        return lax.dynamic_slice_in_dim(value, own * out_cols, out_cols, 0).astype(f32)

    grad_gain_attn = jnp.sum(
        own_rows(w_query) * grad_query + own_rows(w_key) * grad_key + own_rows(w_value) * grad_value, axis=1
    ) / own_rows(attn_gain)
    grad_gain_mlp = jnp.sum(own_rows(w_up) * grad_up, axis=1) / own_rows(mlp_gain)

    dnormed = nt(dquery, w_query) + nt(dkey, w_key) + nt(dvalue, w_value)
    drows = jax.vjp(lambda v: rms_scale(v, attn_gain), routed)[1](dnormed)[0]
    droutes = drows + dmiddle + dlogit_router[:, None] * w_router.astype(f32)[None, :]
    new_rows = (routed + scaling[:, None] * branch).astype(bf16)
    new_grads = (upstream + droutes).astype(bf16)
    put = (jnp.arange(tok_rows, dtype=jnp.int32)[:, None] == offsets[None, :]) & live[None, :]
    hit = jnp.any(put, axis=1, keepdims=True)
    put = put.astype(bf16)
    output = jnp.where(hit, nn(put, new_rows).astype(bf16), tokens_in)
    input_grad = jnp.where(hit, nn(put, new_grads).astype(bf16), out_grad)
    return (
        output,
        input_grad,
        grad_router,
        grad_gain_attn,
        grad_query,
        grad_key,
        grad_value,
        grad_out,
        grad_gain_mlp,
        grad_up,
        grad_down,
    )


SHARE = 64
HALF = 32
NOTE = 8
OUT_HALF = 16
OUT_ROWS = 32
TILES = 2
AT_OUT = TILES * OUT_ROWS
AT_QUERY = AT_OUT + OUT_HALF
AT_PAIR = AT_QUERY + OUT_HALF
AT_NOTE = AT_PAIR + OUT_ROWS
GRAD_ROWS = AT_NOTE + NOTE


def swapped(tile):
    return jnp.concatenate([tile[..., HEAD_DIM:], tile[..., :HEAD_DIM]], axis=-1)


def joined(left, right):
    return jnp.concatenate([left[..., :HEAD_DIM], right[..., HEAD_DIM:]], axis=-1)


def pack_rows(target, first, value):
    for pair in range(HEADS // 2):
        tile = value[:, pair * LANES : (pair + 1) * LANES]
        turned = swapped(tile)
        target[2 * pair, first : first + HALF, :] = joined(tile[:HALF], turned[HALF:])
        target[2 * pair + 1, first : first + HALF, :] = joined(turned[:HALF], tile[HALF:])


def pack_pairs(target, first, left, right):
    for pair in range(HEADS // 2):
        lanes = slice(pair * LANES, (pair + 1) * LANES)
        one, two = left[:, lanes], right[:, lanes]
        target[2 * pair, first : first + SHARE, :] = joined(one, swapped(two))
        target[2 * pair + 1, first : first + SHARE, :] = joined(swapped(one), two)


def unpack_rows(source, first, half):
    columns = []
    for pair in range(HEADS // 2):
        even = source[2 * pair, first : first + half, :]
        odd = source[2 * pair + 1, first : first + half, :]
        columns.append(jnp.concatenate([joined(even, swapped(odd)), joined(swapped(even), odd)], axis=0))
    return jnp.concatenate(columns, axis=1)


def unpack_pairs(source, first, rows):
    left, right = [], []
    for pair in range(HEADS // 2):
        even = source[2 * pair, first : first + rows, :]
        odd = source[2 * pair + 1, first : first + rows, :]
        left.append(joined(even, swapped(odd)))
        right.append(joined(swapped(even), odd))
    return jnp.concatenate(left, axis=1), jnp.concatenate(right, axis=1)


def in_parts(value):
    high = value.astype(bf16).astype(f32)
    rest = value - high
    middle = rest.astype(bf16).astype(f32)
    row = lax.broadcasted_iota(jnp.int32, value.shape, len(value.shape) - 2)
    parts = jnp.where(row == 0, high, jnp.where(row == 1, middle, jnp.where(row == 2, rest - middle, 0.0)))
    return parts.astype(bf16)


def write_note(target, first, value):
    rows = in_parts(jnp.broadcast_to(value, (NOTE, LANES)))
    for k in range(target.shape[0]):
        target[k, first : first + NOTE, :] = rows


def read_note(source, first):
    rows = source[:, first : first + NOTE, :].astype(f32)
    return jnp.sum(jnp.sum(rows, axis=0), axis=0, keepdims=True)[:, :1]


def slots_of(chosen_ref, device):
    row = chosen_ref[pl.ds(device // 2, 1), :]
    return jnp.where(device % 2 == 0, row[:, :SHARE], row[:, SHARE:])


def one_hot(own_ref, counts_ref, chosen_ref, tok_rows, live_only):
    offsets = slots_of(chosen_ref, own_ref[0])
    capacity = offsets.shape[1]
    rows = lax.broadcasted_iota(jnp.int32, (tok_rows, capacity), 0)
    hot = rows == offsets
    if live_only:
        slot = lax.broadcasted_iota(jnp.int32, (tok_rows, capacity), 1)
        hot = hot & (slot < counts_ref[own_ref[0]])
    return jnp.where(hot, 1.0, 0.0)


def live_column(own_ref, counts_ref, capacity):
    return lax.broadcasted_iota(jnp.int32, (capacity, 1), 0) < counts_ref[own_ref[0]]


def gate_of(rows, vectors_ref):
    return jax.nn.sigmoid(jnp.sum(rows * vectors_ref[0:1, :], axis=1, keepdims=True))


def inverse_rms(values):
    return lax.rsqrt(jnp.mean(values * values, axis=-1, keepdims=True) + eps_norm)


def total_count(counts_ref):
    return lax.fori_loop(0, counts_ref.shape[0], lambda i, s: s + counts_ref[i], 0).astype(f32)


def gelu_pair(u):
    c = 0.7978845608028654
    square = u * u
    t = jnp.tanh(c * (u + 0.044715 * (square * u)))
    value = 0.5 * u * (1.0 + t)
    slope = 0.5 * (1.0 + t) + (0.5 * u) * ((1.0 - t * t) * (c + (3.0 * 0.044715 * c) * square))
    return value, slope


def chip_of(own_ref, k):
    return jnp.bitwise_xor(own_ref[0] // 2, (k // 4) ^ (4 * (k % 4)))


def row_of(column):
    wide = jnp.broadcast_to(column, (column.shape[0], LANES))
    filled = jnp.concatenate([wide, jnp.zeros((LANES - column.shape[0], LANES), f32)], axis=0)
    return jnp.transpose(filled)[:1, : column.shape[0]]


def places_kernel(own_ref, counts_ref, lengths_ref, chosen_ref, kpos_ref, qpos_ref, qlow_ref):
    core = own_ref[0] % 2
    devices, capacity = 2 * chosen_ref.shape[0], SHARE
    tok_rows = lengths_ref[lengths_ref.shape[0] - 1]
    slot = lax.broadcasted_iota(jnp.int32, (1, capacity), 1)
    ends = []
    for k in range(lengths_ref.shape[0] - 1):
        ends.append(lengths_ref[k] + (ends[-1] if ends else 0))

    def place(device):
        value = device * tok_rows + slots_of(chosen_ref, device)
        return value, slot < counts_ref[device]

    def key_row(device):
        value, live = place(device)
        return jnp.where(live, value.astype(f32), far_away)

    for m in range(2):
        parity = jnp.bitwise_xor(core, m)
        for c in range(0, devices // 2, 2):
            tile = jnp.concatenate([key_row(2 * c + parity), key_row(2 * c + 2 + parity)], axis=1)
            kpos_ref[m : m + 1, c * capacity : (c + 2) * capacity] = tile
    blocks = qpos_ref.shape[0]
    sources = devices // 2 // blocks
    for b in range(blocks):
        lows, highs = [], []
        for c in range(b * sources, (b + 1) * sources):
            value, live = place(2 * c + core)
            low = jnp.zeros_like(value)
            for end in ends:
                low = jnp.maximum(low, jnp.where(value >= end, end, 0))
            both = jnp.concatenate([jnp.where(live, value, -1), low], axis=0).astype(f32)
            lows.append(both[:, :HALF])
            highs.append(both[:, HALF:])
        both = jnp.concatenate(lows + highs, axis=1)
        qpos_ref[b : b + 1, :] = both[:1]
        qlow_ref[b : b + 1, :] = both[1:]


def fetch_kernel(own_ref, counts_ref, chosen_ref, tokens_ref, grads_ref, both_ref, rows_ref, upstream_ref):
    hot = one_hot(own_ref, counts_ref, chosen_ref, tokens_ref.shape[0], False)
    capacity = hot.shape[1]
    pick = jnp.transpose(jnp.concatenate([hot, jnp.zeros_like(hot)], axis=1))[:capacity].astype(bf16)
    live = live_column(own_ref, counts_ref, capacity)
    rows = nn(pick, tokens_ref[...]).astype(bf16)
    upstream = jnp.where(live, nn(pick, grads_ref[...]), 0.0).astype(bf16)
    both_ref[0, :capacity, :] = rows
    both_ref[0, capacity:, :] = upstream
    rows_ref[0] = rows
    upstream_ref[0] = upstream


def project_kernel(own_ref, counts_ref, vectors_ref, wq, wk, wv, *rest):
    pieces, sent_ref = rest[:-1], rest[-1]
    head = own_ref[0] // 2
    core = own_ref[0] % 2
    even = head % 2 == 0
    k = 0
    weights = None
    for piece in pieces:
        blocks, capacity, width = piece.shape
        rows = piece[...].reshape(blocks * capacity, width).astype(f32)
        gate = gate_of(rows, vectors_ref)
        normed = (rows * inverse_rms(rows) * vectors_ref[1:2, :]).astype(bf16)
        if weights is None:
            w_pair = jnp.where(even, joined(wk[...], swapped(wv[...])), joined(swapped(wk[...]), wv[...]))
            weights = jnp.concatenate([w_pair, jnp.where(even, wq[...], swapped(wq[...]))], axis=1)
        product = nn(normed, weights)
        for j in range(blocks):
            chip = chip_of(own_ref, k)
            block = product[j * capacity : (j + 1) * capacity]
            query = block[:, LANES:]
            sent_ref[chip, :HALF, :] = joined(query[:HALF], swapped(query[HALF:])).astype(bf16)
            sent_ref[chip, HALF : HALF + SHARE, :] = block[:, :LANES].astype(bf16)
            slot = lax.broadcasted_iota(jnp.int32, (capacity, 1), 0)
            live = slot < counts_ref[2 * chip + core]
            part = jnp.where(live, gate[j * capacity : (j + 1) * capacity], 0.0)
            part = jnp.sum(part, axis=0, keepdims=True)
            sent_ref[chip, HALF + SHARE :, :] = in_parts(jnp.broadcast_to(part, (NOTE, LANES)))
            k += 1


def unpack_kernel(got_ref, mixed_ref):
    mixed_ref[0] = unpack_rows(got_ref, 0, HALF)


CHUNKS = 4
PIECES = (5, 4, 5)


def early_kernel(both_ref, down_ref, product_ref, w_down, sems):
    cols = down_ref.shape[0] // CHUNKS
    parts = [pl.ds(c * cols, cols) for c in range(CHUNKS)]
    copies = [pltpu.make_async_copy(down_ref.at[p, :], w_down.at[p, :], sems.at[c]) for c, p in enumerate(parts)]
    for copy in copies:
        copy.start()
    upstream = both_ref[0, both_ref.shape[1] // 2 :, :]
    for c, copy in enumerate(copies):
        copy.wait()
        part = slice(c * cols, (c + 1) * cols)
        product_ref[:, part] = nt(upstream, w_down[part, :])


def middle_kernel(
    own_ref, counts_ref, mixed_ref, total_ref, both_ref, vectors_ref, product_ref, out_ref, up_ref,
    sent_ref, active_ref, attn_ref, dmiddle_ref, dweight_ref, w_out, w_up, sems,
):
    width, total_cols = up_ref.shape
    cols = total_cols // CHUNKS
    copies = [pltpu.make_async_copy(out_ref, w_out, sems.at[0])]
    for c in range(CHUNKS):
        part = pl.ds(c * cols, cols)
        copies.append(pltpu.make_async_copy(up_ref.at[:, part], w_up.at[:, part], sems.at[1 + c]))
    for copy in copies:
        copy.start()
    capacity = mixed_ref.shape[1]
    rows = both_ref[0, :capacity, :].astype(f32)
    upstream = both_ref[0, capacity:, :].astype(f32)
    live = live_column(own_ref, counts_ref, capacity)
    gate = gate_of(rows, vectors_ref)
    ratio = total_count(counts_ref) / total_ref[:1, :1]
    scaling = gate * ratio
    gain = vectors_ref[2:3, :]
    dbranch = scaling * upstream
    copies[0].wait()
    attn_out = nn(mixed_ref[0], w_out[...])
    attn_ref[...] = attn_out
    dweight = jnp.sum(upstream * attn_out, axis=1, keepdims=True)
    middle = rows + attn_out
    scale = inverse_rms(middle)
    normed = (middle * scale * gain).astype(bf16)
    dnormed = jnp.zeros((capacity, width), f32)
    for c in range(CHUNKS):
        part = slice(c * cols, (c + 1) * cols)
        copies[1 + c].wait()
        value, slope = gelu_pair(nn(normed, w_up[:, part]))
        active = value.astype(bf16)
        active_ref[:, part] = active
        product = product_ref[:, part]
        dweight = dweight + jnp.sum(active.astype(f32) * product, axis=1, keepdims=True)
        dnormed = dnormed + nt((scaling * product * slope).astype(bf16), w_up[:, part])
    dweight_ref[...] = jnp.broadcast_to(dweight, dweight_ref.shape)
    scaled = gain * dnormed
    dmiddle = scale * scaled - middle * (scale * scale * scale) * jnp.mean(scaled * middle, axis=-1, keepdims=True)
    dmiddle_ref[...] = dmiddle
    dattn = (dbranch + dmiddle).astype(bf16)
    pack_rows(sent_ref, 0, nt(dattn, w_out[...]).astype(bf16))
    pack_rows(sent_ref, HALF, dattn)
    write_note(sent_ref, 2 * HALF, jnp.sum(jnp.where(live, dweight * gate, 0.0), axis=0, keepdims=True))


def put_kernel(
    own_ref, counts_ref, chosen_ref, total_ref, both_ref, vectors_ref, active_ref, attn_ref, old_ref, down_ref,
    result_ref, w_down, sems,
):
    rows_of_chunk = down_ref.shape[0] // CHUNKS
    parts = [pl.ds(c * rows_of_chunk, rows_of_chunk) for c in range(CHUNKS)]
    copies = [pltpu.make_async_copy(down_ref.at[p, :], w_down.at[p, :], sems.at[c]) for c, p in enumerate(parts)]
    for copy in copies:
        copy.start()
    rows = both_ref[0, : both_ref.shape[1] // 2, :].astype(f32)
    scaling = gate_of(rows, vectors_ref) * (total_count(counts_ref) / total_ref[:1, :1])
    mlp_out = jnp.zeros_like(rows)
    for c, copy in enumerate(copies):
        part = slice(c * rows_of_chunk, (c + 1) * rows_of_chunk)
        copy.wait()
        mlp_out = mlp_out + nn(active_ref[:, part], w_down[part, :])
    new = (rows + scaling * (attn_ref[...] + mlp_out)).astype(bf16)
    put_rows(own_ref, counts_ref, chosen_ref, old_ref, new, result_ref)


def put_rows(own_ref, counts_ref, chosen_ref, old_ref, new, result_ref):
    hot = one_hot(own_ref, counts_ref, chosen_ref, old_ref.shape[0], True)
    hit = jnp.sum(hot, axis=1, keepdims=True) > 0.5
    placed = nn(hot.astype(bf16), new)
    result_ref[...] = jnp.where(hit, placed, old_ref[...].astype(f32)).astype(bf16)


def router_slope(own_ref, counts_ref, rows, dweight_ref, total_ref, coef_ref, vectors_ref):
    gate = gate_of(rows, vectors_ref)
    live = live_column(own_ref, counts_ref, rows.shape[0])
    count = total_count(counts_ref)
    total = total_ref[:1, :1]
    dscore = dweight_ref[:, :1] * (count / total) - coef_ref[:1, :1] * count / (total * total)
    return jnp.where(live, dscore * gate * (1.0 - gate), 0.0)


def keys_kernel(dq_ref, dkv_ref, moved_ref, coef_ref, sent_ref, sum_ref):
    rows = dkv_ref.shape[0]
    sent_ref[:, :HALF, :] = dq_ref[...]
    dkv = dkv_ref[...] + moved_ref[:rows, :]
    sent_ref[:, HALF:, :] = dkv.astype(bf16).reshape(sent_ref.shape[0], SHARE, LANES)
    sum_ref[...] = coef_ref[...] + moved_ref[rows:, :]


def units_kernel(
    own_ref, counts_ref, got_ref, dqkv_ref, total_ref, coef_ref, vectors_ref, rows_ref, dweight_ref,
    out_ref, up_ref, down_ref, *rest,
):
    gathers = []
    for count in PIECES:
        gathers.append(rest[:count])
        rest = rest[count:]
    down_keep_ref, down_give_ref, keep_ref, give_ref, rest = *rest[:4], rest[4:]
    *slots, grad_up, grad_down, grad_out, grad_q, grad_kv, ratio_ref, sems = rest
    rows_slots, upstream_slots, mixed_slots = slots
    step = pl.program_id(0)
    steps = pl.num_programs(0)
    _, sources, capacity, width = mixed_slots.shape
    core = own_ref[0] % 2
    slot = step % 2

    def copies(k):
        result = []
        for i, pieces in enumerate(gathers):
            for side in range(2):
                piece = 2 * k + side
                if piece < 3 or len(pieces) == 4:
                    target = slots[i].at[k, 4 * side : 4 * side + 4]
                    result.append(pltpu.make_async_copy(pieces[piece], target, sems.at[k, i, side, 0]))
                    continue
                for half in range(2):
                    first = 4 * side + 2 * half
                    target = slots[i].at[k, first : first + 2]
                    result.append(pltpu.make_async_copy(pieces[piece + half], target, sems.at[k, i, side, half]))
        return result

    @pl.when(step == 0)
    def _():
        for k in range(2):
            for copy in copies(k):
                copy.start()

    @pl.when(step == 0)
    def _():
        for ref in (grad_up, grad_down, grad_out, grad_q, grad_kv):
            ref[...] = jnp.zeros_like(ref)
        ratio_ref[...] = jnp.broadcast_to(total_count(counts_ref) / total_ref[:1, :1], ratio_ref.shape)

    for k in range(2):

        @pl.when(step == k)
        def _(k=k):
            for copy in copies(k):
                copy.wait()

    def halves(ref, first):
        blocks = [ref[chip_of(own_ref, sources * step + j), first : first + HALF, :] for j in range(sources)]
        turned = jnp.transpose(jnp.concatenate(blocks, axis=0).astype(f32)).astype(bf16)
        return turned[:HEAD_DIM], turned[HEAD_DIM:]

    def low_high(value):
        value = value.reshape(sources, capacity, width)
        return value[:, :HALF, :].reshape(sources * HALF, width), value[:, HALF:, :].reshape(sources * HALF, width)

    rows = rows_slots[slot].reshape(sources * capacity, width).astype(f32)
    upstream = upstream_slots[slot].reshape(sources * capacity, width).astype(f32)
    mixed = mixed_slots[slot].reshape(sources * capacity, width)
    normed_attn = (rows * inverse_rms(rows) * vectors_ref[1:2, :]).astype(bf16)
    low_query, high_query = halves(dqkv_ref, 0)
    low_rows, high_rows = low_high(normed_attn)
    grad_q[...] += nn(low_query, low_rows) + nn(high_query, high_rows)
    blocks = [dqkv_ref[chip_of(own_ref, sources * step + j), HALF:, :] for j in range(sources)]
    pairs_turned = jnp.transpose(jnp.concatenate(blocks, axis=0).astype(f32)).astype(bf16)
    grad_kv[...] += nn(pairs_turned, normed_attn)
    low_attn, high_attn = halves(got_ref, HALF)
    low_mixed, high_mixed = low_high(mixed)
    grad_out[...] += nn(low_attn, low_mixed) + nn(high_attn, high_mixed)
    middle = rows + nn(mixed, out_ref[...])
    normed = (middle * inverse_rms(middle) * vectors_ref[2:3, :]).astype(bf16)
    dmlp = (gate_of(rows, vectors_ref) * ratio_ref[:1, :1] * upstream).astype(bf16)
    value, slope = gelu_pair(nn(normed, up_ref[...]))
    dhidden = nt(dmlp, down_ref[...]) * slope
    grad_down[...] += nn(jnp.transpose(value).astype(bf16), dmlp)
    grad_up[...] += nn(jnp.transpose(dhidden).astype(bf16), normed)

    @pl.when(step == steps - 1)
    def _():
        chips = keep_ref.shape[0]

        def split(value):
            value = value.reshape(chips, 2, OUT_ROWS, LANES)
            even, odd = value[:, 0], value[:, 1]
            return jnp.where(core == 0, even, odd), jnp.where(core == 0, odd, even)

        def store(first, kept, given):
            keep_ref[:, first : first + kept.shape[1], :] = kept.astype(bf16)
            give_ref[:, first : first + kept.shape[1], :] = given.astype(bf16)

        for t in range(TILES):
            store(t * OUT_ROWS, *split(jnp.transpose(grad_up[t * LANES : (t + 1) * LANES, :])))

        def two_in_one(value):
            return joined(value[:, :OUT_HALF], swapped(value[:, OUT_HALF:]))

        both_turned = jnp.transpose(jnp.concatenate([grad_out[...], grad_q[...]], axis=0))
        kept, given = split(both_turned)
        store(AT_OUT, two_in_one(kept), two_in_one(given))
        store(AT_QUERY, two_in_one(swapped(kept)), two_in_one(swapped(given)))
        store(AT_PAIR, *split(jnp.transpose(grad_kv[...])))
        own_rows = rows_ref[0, :capacity, :].astype(f32)
        dlogit = router_slope(own_ref, counts_ref, own_rows, dweight_ref, total_ref, coef_ref, vectors_ref)
        part = jnp.broadcast_to(jnp.sum(dlogit * own_rows, axis=0, keepdims=True), (NOTE, width))
        per_tile = LANES // OUT_ROWS
        for c in range(chips):
            tile = part[:, (2 * c) // per_tile * LANES : ((2 * c) // per_tile + 1) * LANES]
            shift = (2 * c) % per_tile * OUT_ROWS
            if shift:
                tile = jnp.concatenate([tile[:, shift:], tile[:, :shift]], axis=1)
            after = jnp.concatenate([tile[:, OUT_ROWS:], tile[:, :OUT_ROWS]], axis=1)
            keep_ref[c, AT_NOTE:, :] = in_parts(jnp.where(core == 0, tile, after))
            give_ref[c, AT_NOTE:, :] = in_parts(jnp.where(core == 0, after, tile))
        down = grad_down[...]
        half = down.shape[0] // 2
        down_keep_ref[...] = jnp.where(core == 0, down[:half], down[half:])
        down_give_ref[...] = jnp.where(core == 0, down[half:], down[:half]).astype(bf16)


def merge_kernel(keep_ref, moved_ref, sent_ref):
    total = keep_ref[...].astype(f32) + moved_ref[...].astype(f32)
    sent_ref[:, :AT_NOTE, :] = total[:, :AT_NOTE].astype(bf16)
    note = jnp.sum(total[:, AT_NOTE:], axis=1, keepdims=True)
    sent_ref[:, AT_NOTE:, :] = in_parts(jnp.broadcast_to(note, (note.shape[0], NOTE, LANES)))


def rows_kernel(
    own_ref, counts_ref, chosen_ref, got_ref, both_ref, dmiddle_ref, dweight_ref, total_ref, coef_ref, vectors_ref,
    old_ref, wq_ref, wk_ref, wv_ref, grads_ref, wq, wk, wv, sems,
):
    copies = [
        pltpu.make_async_copy(source, target, sems.at[i])
        for i, (source, target) in enumerate(((wq_ref, wq), (wk_ref, wk), (wv_ref, wv)))
    ]
    for copy in copies:
        copy.start()
    capacity = dmiddle_ref.shape[0]
    rows = both_ref[0, :capacity, :].astype(f32)
    upstream = both_ref[0, capacity:, :].astype(f32)
    gain = vectors_ref[1:2, :]
    dlogit = router_slope(own_ref, counts_ref, rows, dweight_ref, total_ref, coef_ref, vectors_ref)
    partial = upstream + dmiddle_ref[...] + dlogit * vectors_ref[0:1, :]
    dquery = unpack_rows(got_ref, 0, HALF)
    dkey, dvalue = unpack_pairs(got_ref, HALF, SHARE)
    copies[0].wait()
    dnormed = jnp.zeros_like(partial) + nt(dquery, wq[...])
    copies[1].wait()
    dnormed = dnormed + nt(dkey, wk[...])
    copies[2].wait()
    dnormed = dnormed + nt(dvalue, wv[...])
    scale = inverse_rms(rows)
    scaled = gain * dnormed
    drows = scale * scaled - rows * (scale * scale * scale) * jnp.mean(scaled * rows, axis=-1, keepdims=True)
    put_rows(own_ref, counts_ref, chosen_ref, old_ref, (partial + drows).astype(bf16), grads_ref)


def finish_kernel(
    got_ref, own_gain_ref, up_ref, wq_ref, wk_ref, wv_ref,
    grad_up_ref, grad_out_ref, grad_q_ref, grad_k_ref, grad_v_ref, router_ref, gain_attn_ref, gain_mlp_ref,
):
    total = jnp.zeros((OUT_ROWS, LANES), f32)
    for c in range(got_ref.shape[0]):
        for t in range(TILES):
            lanes = slice((TILES * c + t) * LANES, (TILES * c + t + 1) * LANES)
            part = got_ref[c, t * OUT_ROWS : (t + 1) * OUT_ROWS, :].astype(f32)
            grad_up_ref[:, lanes] = part
            total = total + part * up_ref[:, lanes].astype(f32)
    gain_mlp_ref[...] = row_of(jnp.sum(total, axis=1, keepdims=True)) / own_gain_ref[2:3, :]
    grad_out_ref[...] = unpack_rows(got_ref, AT_OUT, OUT_HALF).astype(f32)
    grad_q = unpack_rows(got_ref, AT_QUERY, OUT_HALF).astype(f32)
    grad_k, grad_v = (value.astype(f32) for value in unpack_pairs(got_ref, AT_PAIR, OUT_ROWS))
    grad_q_ref[...] = grad_q
    grad_k_ref[...] = grad_k
    grad_v_ref[...] = grad_v
    products = wq_ref[...].astype(f32) * grad_q + wk_ref[...].astype(f32) * grad_k + wv_ref[...].astype(f32) * grad_v
    gain_attn_ref[...] = row_of(jnp.sum(products, axis=1, keepdims=True)) / own_gain_ref[1:2, :]
    notes = jnp.sum(got_ref[:, AT_NOTE:, :].astype(f32), axis=0)
    router_ref[...] = jnp.sum(notes, axis=0, keepdims=True)[:, :OUT_ROWS]


def pair_attend_kernel(factor, got_ref, other_ref, kpos_ref, qpos_ref, qlow_ref, mixed_ref, turned_ref, lse_ref, total_ref):
    lists = (got_ref, other_ref)
    chips = got_ref.shape[0]
    blocks = chips * HALF // BLOCK
    sources = chips // blocks
    total = read_note(got_ref, HALF + SHARE) + read_note(other_ref, HALF + SHARE)
    total_ref[...] = jnp.broadcast_to(total, total_ref.shape)
    attend_core(
        factor,
        lambda b: got_ref[b * sources : (b + 1) * sources, :HALF, :].reshape(BLOCK, LANES),
        lambda m, extent: lists[m][: extent // SHARE, HALF : HALF + SHARE, :].reshape(extent, LANES),
        2, blocks, chips * SHARE, kpos_ref, qpos_ref, qlow_ref, mixed_ref, turned_ref, lse_ref,
    )


def pair_attend_back_kernel(
    factor, got_ref, other_ref, grad_ref, kpos_ref, qpos_ref, qlow_ref, turned_ref, lse_ref,
    dq_ref, own_ref, moved_ref, coef_ref,
):
    lists = (got_ref, other_ref)
    sums = (own_ref, moved_ref)
    chips = got_ref.shape[0]
    blocks = chips * HALF // BLOCK
    sources = chips // blocks
    coef = jnp.broadcast_to(read_note(grad_ref, 2 * HALF), coef_ref.shape)
    coef_ref[...] = coef
    moved_ref[chips * SHARE :, :] = coef

    def add_dkv(m, extent, first, update):
        if first:
            sums[m][:extent, :] = update
        else:
            sums[m][:extent, :] += update

    attend_back_core(
        factor,
        lambda b: got_ref[b * sources : (b + 1) * sources, :HALF, :].reshape(BLOCK, LANES),
        lambda b: grad_ref[b * sources : (b + 1) * sources, :HALF, :].reshape(BLOCK, LANES),
        lambda m, extent: lists[m][: extent // SHARE, HALF : HALF + SHARE, :].reshape(extent, LANES),
        2, blocks, chips * SHARE, kpos_ref, qpos_ref, qlow_ref, turned_ref, lse_ref, dq_ref, add_dkv,
    )


smem = pl.BlockSpec(memory_space=pltpu.SMEM)
hbm = pl.BlockSpec(memory_space=pl.ANY)
megabytes = {
    "places": 4, "early": 56, "fetch": 56, "project": 16, "attend": 20, "unpack": 4, "middle": 56, "put": 56, "attend_back": 24,
    "keys": 8, "units": 56, "merge": 10, "rows": 56, "finish": 12,
}


def params_of(name):
    return pltpu.CompilerParams(vmem_limit_bytes=megabytes[name] * 1024 * 1024)


def shaped(shape, dtype):
    return jax.ShapeDtypeStruct(shape, dtype)


microseconds = {
    "places": 1, "early": 5, "fetch": 3, "project": 4, "attend": 5, "unpack": 2, "middle": 11, "put": 6, "attend_back": 6, "keys": 2,
    "units": 16, "merge": 3, "rows": 7, "finish": 2,
}


def cost_of(name):
    return pl.CostEstimate(flops=0, transcendentals=0, bytes_accessed=microseconds[name] * 3_300_000)


def call(kernel, name, in_specs, out_shape, arguments, scratch=()):
    return pl.pallas_call(
        kernel,
        out_shape=out_shape,
        in_specs=in_specs,
        out_specs=jax.tree.map(lambda _: vmem, out_shape),
        scratch_shapes=list(scratch),
        compiler_params=params_of(name),
        cost_estimate=cost_of(name),
        name=name,
    )(*arguments)


def pairs(
    tokens_in,
    w_router,
    gain_attn,
    w_query,
    w_key,
    w_value,
    w_out,
    gain_mlp,
    w_up,
    w_down,
    out_grad,
    lengths,
    counts,
    chosen,
):
    devices = lax.axis_size("seq")
    chips = devices // 2
    own = lax.axis_index("seq")
    capacity = chosen.shape[0] // devices
    tok_rows, width = tokens_in.shape
    hidden_width = w_up.shape[1]
    out_rows = width // devices
    factor = HEAD_DIM ** (-0.5)
    core = own % 2
    own_id = own.astype(jnp.int32).reshape(1)
    chosen = chosen.reshape(chips, 2 * capacity)
    vectors = jnp.stack([w_router, gain_attn, gain_mlp]).astype(f32)
    own_gains = lax.dynamic_slice_in_dim(vectors, own * out_rows, out_rows, 1)
    cores = [[2 * c + k for c in range(chips)] for k in range(2)]

    def swap(value):
        return lax.all_to_all(value, "seq", split_axis=0, concat_axis=0, tiled=True, axis_index_groups=cores)

    def across(value, bits):
        return lax.ppermute(value, "seq", [(s, s ^ bits) for s in range(devices)])

    def line_of(block):
        return jnp.concatenate([block] + [across(block, 8 * k) for k in (1, 2, 3)], axis=0)

    def sides_of(line):
        return [line, across(line, 2), across(line, 4)]

    def gathered(sides):
        return sides + [across(sides[2][:2], 2), across(sides[1][2:], 4)]

    def gathered_whole(sides):
        return sides + [across(sides[2], 2)]

    blocks = chips * HALF // BLOCK
    square = pltpu.VMEM((width, width), bf16)
    block = shaped((1, capacity, width), bf16)
    both, own_rows, own_upstream = call(
        fetch_kernel, "fetch", [smem, smem] + [vmem] * 3, (shaped((1, 2 * capacity, width), bf16), block, block),
        (own_id, counts, chosen, tokens_in, out_grad),
    )
    rows_line = line_of(own_rows)
    product = call(
        early_kernel, "early", [vmem, hbm], shaped((capacity, hidden_width), f32), (both, w_down),
        [pltpu.VMEM((hidden_width, width), bf16), pltpu.SemaphoreType.DMA((CHUNKS,))],
    )
    chosen_after, product, rows_line = lax.optimization_barrier((chosen, product, rows_line))
    kpos, qpos, qlow = call(
        places_kernel, "places", [smem] * 3 + [vmem],
        (
            shaped((2, chips * SHARE), f32),
            shaped((blocks, 2 * BLOCK), f32),
            shaped((blocks, 2 * BLOCK), f32),
        ),
        (own_id, counts, jnp.append(lengths, tok_rows), chosen_after),
    )
    rows_all = gathered(sides_of(rows_line))
    column = own // 4 * LANES
    columns = [lax.dynamic_slice_in_dim(w, column, LANES, 1) for w in (w_query, w_key, w_value)]
    upstream_line = line_of(own_upstream)
    rows_all, upstream_line = lax.optimization_barrier((rows_all, upstream_line))
    kpos, qpos, qlow, columns, rows_all = lax.optimization_barrier((kpos, qpos, qlow, columns, rows_all))
    got = call(
        project_kernel, "project", [smem, smem] + [vmem] * 9,
        shaped((chips, HALF + SHARE + NOTE, LANES), bf16),
        (own_id, counts, vectors, *columns, *rows_all),
    )
    other = across(got, 1)
    upstream_sides = sides_of(upstream_line)
    mixed_packed, turned, lse, total = call(
        functools.partial(pair_attend_kernel, factor), "attend", [vmem] * 5,
        (
            shaped((chips * HALF, LANES), bf16),
            shaped((chips * HALF, LANES), f32),
            shaped((blocks, 2 * BLOCK), f32),
            shaped((8, LANES), f32),
        ),
        (got, other, kpos, qpos, qlow),
    )
    mixed_got = swap(mixed_packed.reshape(chips, HALF, LANES))
    upstream_sides, mixed_got = lax.optimization_barrier((upstream_sides, mixed_got))
    upstream_all = gathered_whole(upstream_sides)
    mixed = call(unpack_kernel, "unpack", [vmem], shaped((1, capacity, width), bf16), (mixed_got,))
    mixed_line = line_of(mixed)
    sent, active, attn_out, dmiddle, dweight = call(
        middle_kernel, "middle", [smem, smem] + [vmem] * 5 + [hbm] * 2,
        (
            shaped((chips, 2 * HALF + NOTE, LANES), bf16),
            shaped((capacity, hidden_width), bf16),
            shaped((capacity, width), f32),
            shaped((capacity, width), f32),
            shaped((capacity, LANES), f32),
        ),
        (own_id, counts, mixed, total, both, vectors, product, w_out, w_up),
        [
            square,
            pltpu.VMEM((width, hidden_width), bf16),
            pltpu.SemaphoreType.DMA((1 + CHUNKS,)),
        ],
    )
    mixed_line, sent = lax.optimization_barrier((mixed_line, sent))
    mixed_sides = sides_of(mixed_line)
    upstream_all, sent = lax.optimization_barrier((upstream_all, sent))
    grads_got = swap(sent)
    output = call(
        put_kernel, "put", [smem, smem] + [vmem] * 7 + [hbm], shaped((tok_rows, width), bf16),
        (own_id, counts, chosen, total, both, vectors, active, attn_out, tokens_in, w_down),
        [pltpu.VMEM((hidden_width, width), bf16), pltpu.SemaphoreType.DMA((CHUNKS,))],
    )
    mixed_all = gathered(mixed_sides)
    output, grads_got = lax.optimization_barrier((output, grads_got))
    dq, dkv_own, dkv_other, coef = call(
        functools.partial(pair_attend_back_kernel, factor), "attend_back", [vmem] * 8,
        (
            shaped((chips * HALF, LANES), bf16),
            shaped((chips * SHARE, LANES), f32),
            shaped((chips * SHARE + 8, LANES), f32),
            shaped((8, LANES), f32),
        ),
        (got, other, grads_got, kpos, qpos, qlow, turned, lse),
    )
    moved = across(dkv_other, 1)
    dqkv, coef = call(
        keys_kernel, "keys", [vmem] * 4,
        (shaped((chips, HALF + SHARE, LANES), bf16), shaped((8, LANES), f32)),
        (dq.reshape(chips, HALF, LANES), dkv_own, moved, coef),
    )
    got = swap(dqkv)
    sources = 8
    hidden_cols = hidden_width // chips
    whole = lambda *shape: pl.BlockSpec(shape, lambda i, o: (0,) * len(shape))
    down_keep, down_give, keep, give = pl.pallas_call(
        units_kernel,
        out_shape=(
            shaped((hidden_cols // 2, width), f32),
            shaped((hidden_cols // 2, width), bf16),
            shaped((chips, GRAD_ROWS, LANES), bf16),
            shaped((chips, GRAD_ROWS, LANES), bf16),
        ),
        grid_spec=pltpu.PrefetchScalarGridSpec(
            num_scalar_prefetch=1,
            grid=(chips // sources,),
            in_specs=[
                smem,
                whole(chips, 2 * HALF + NOTE, LANES),
                whole(chips, HALF + SHARE, LANES),
                whole(8, LANES),
                whole(8, LANES),
                whole(3, width),
                whole(1, 2 * capacity, width),
                whole(capacity, LANES),
                whole(width, width),
                pl.BlockSpec((width, hidden_cols), lambda i, o: (0, o[0] // 2)),
                pl.BlockSpec((hidden_cols, width), lambda i, o: (o[0] // 2, 0)),
            ]
            + [hbm] * sum(PIECES),
            out_specs=(
                whole(hidden_cols // 2, width),
                whole(hidden_cols // 2, width),
                whole(chips, GRAD_ROWS, LANES),
                whole(chips, GRAD_ROWS, LANES),
            ),
            scratch_shapes=[
                pltpu.VMEM((2, sources, capacity, width), bf16),
                pltpu.VMEM((2, sources, capacity, width), bf16),
                pltpu.VMEM((2, sources, capacity, width), bf16),
                pltpu.VMEM((hidden_cols, width), f32),
                pltpu.VMEM((hidden_cols, width), f32),
                pltpu.VMEM((HEAD_DIM, width), f32),
                pltpu.VMEM((HEAD_DIM, width), f32),
                pltpu.VMEM((2 * HEAD_DIM, width), f32),
                pltpu.VMEM((8, LANES), f32),
                pltpu.SemaphoreType.DMA((2, 3, 2, 2)),
            ],
        ),
        compiler_params=params_of("units"),
        cost_estimate=cost_of("units"),
        name="units",
    )(own_id, counts, grads_got, dqkv, total, coef, vectors, both, dweight, w_out, w_up, w_down, *rows_all, *upstream_all, *mixed_all)
    sent = call(
        merge_kernel, "merge", [vmem] * 2, shaped((chips, GRAD_ROWS, LANES), bf16), (keep, across(give, 1))
    )
    grad_down = down_keep + across(down_give, 1).astype(f32)
    last = swap(sent)
    input_grad = call(
        rows_kernel, "rows", [smem, smem] + [vmem] * 9 + [hbm] * 3, shaped((tok_rows, width), bf16),
        (
            own_id, counts, chosen, got, both, dmiddle, dweight, total, coef, vectors, out_grad,
            w_query, w_key, w_value,
        ),
        [square] * 3 + [pltpu.SemaphoreType.DMA((3,))],
    )
    block = shaped((out_rows, width), f32)
    row = shaped((1, out_rows), f32)
    first_row = own * out_rows
    grad_up, grad_out, grad_query, grad_key, grad_value, grad_router, grad_gain_attn, grad_gain_mlp = call(
        finish_kernel, "finish", [vmem] * 6,
        (shaped((out_rows, hidden_width), f32), block, block, block, block, row, row, row),
        (last, own_gains, *(lax.dynamic_slice_in_dim(w, first_row, out_rows) for w in (w_up, w_query, w_key, w_value))),
    )
    return (
        output,
        input_grad,
        grad_router.reshape(out_rows),
        grad_gain_attn.reshape(out_rows),
        grad_query,
        grad_key,
        grad_value,
        grad_out,
        grad_gain_mlp.reshape(out_rows),
        grad_up,
        grad_down,
    )


def per_device(*arguments):
    w_up, chosen = arguments[8], arguments[13]
    devices = lax.axis_size("seq")
    width, hidden_width = w_up.shape
    paired = (
        devices == 2 * HEADS
        and chosen.shape[0] == devices * SHARE
        and width == devices * OUT_ROWS
        and width == HEADS * HEAD_DIM
        and hidden_width == devices // 2 * TILES * LANES
    )
    return (pairs if paired else general)(*arguments)


def solution(mesh):
    placed = (P("seq", None),) + (P(),) * 9 + (P("seq", None),) + (P(),) * 3
    rows = P("seq", None)
    return jax.shard_map(
        per_device,
        mesh=mesh,
        in_specs=placed,
        out_specs=(rows, rows, P("seq"), P("seq"), rows, rows, rows, rows, P("seq"), rows, rows),
        check_vma=False,
    )
```

```python
import functools
import jax
import jax.numpy as jnp
from jax import lax
from jax.experimental import pallas as pl
from jax.experimental.pallas import tpu as pltpu
from jax.sharding import PartitionSpec as P

HEADS = 16
HEAD_DIM = 64
LANES = 128
BLOCK = 128

masked_score = -1e30
eps_norm = 1e-05
far_away = 1e9

f32 = jnp.float32
bf16 = jnp.bfloat16


def nt(left, right):
    return lax.dot_general(left, right, (((1,), (1,)), ((), ())), preferred_element_type=f32)


def nn(left, right):
    return lax.dot_general(left, right, (((1,), (0,)), ((), ())), preferred_element_type=f32)


def rms_scale(values, gain):
    return values * lax.rsqrt(jnp.mean(values * values, axis=-1, keepdims=True) + eps_norm) * gain


def three_parts(value):
    high = lax.reduce_precision(value, 8, 7)
    rest = value - high
    middle = lax.reduce_precision(rest, 8, 7)
    return jnp.stack([high, middle, rest - middle]).astype(bf16)


def spread_rows(packed, upper):
    lanes = lax.broadcasted_iota(jnp.int32, packed.shape, 1)
    zero = jnp.zeros_like(packed)
    rolled = jnp.concatenate([packed[:, HEAD_DIM:], packed[:, :HEAD_DIM]], axis=1)
    if upper:
        return jnp.concatenate(
            [jnp.where(lanes >= HEAD_DIM, rolled, zero), jnp.where(lanes >= HEAD_DIM, packed, zero)], axis=0
        )
    return jnp.concatenate(
        [jnp.where(lanes < HEAD_DIM, packed, zero), jnp.where(lanes < HEAD_DIM, rolled, zero)], axis=0
    )


def pack_columns(turned):
    return jnp.concatenate([turned[:, :BLOCK], turned[:, BLOCK:]], axis=0)


def key_columns(kpos_ref, member, extent):
    row = kpos_ref[member : member + 1, :extent]
    column = jnp.transpose(jnp.broadcast_to(row, (LANES, extent)))
    return jnp.concatenate([column, column], axis=1)


def attend_core(factor, load_query, load_kv, members, blocks, key_rows, kpos_ref, qpos_ref, qlow_ref, mixed_ref, turned_ref, lse_ref):
    kv_turned = [jnp.transpose(load_kv(m, key_rows)) for m in range(members)]
    columns = [key_columns(kpos_ref, m, key_rows) for m in range(members)]
    for b in range(blocks):
        extent = key_rows * (b + 1) // blocks
        packed = (load_query(b).astype(f32) * factor).astype(bf16)
        wide = spread_rows(packed, False)
        qpos = qpos_ref[b : b + 1, :]
        qlow = qlow_ref[b : b + 1, :]
        scores = []
        for m in range(members):
            score = nt(load_kv(m, extent), wide)
            kpos = columns[m][:extent]
            score = jnp.where((kpos <= qpos) & (kpos >= qlow), score, masked_score)
            scores.append(score)
        peak = jnp.max(scores[0], axis=0, keepdims=True)
        for score in scores[1:]:
            peak = jnp.maximum(peak, jnp.max(score, axis=0, keepdims=True))
        peak = jnp.maximum(peak, 0.1 * masked_score)
        total = jnp.zeros_like(peak)
        mixed = jnp.zeros((LANES, 2 * BLOCK), f32)
        for m in range(members):
            prob = jnp.exp(scores[m] - peak)
            total = total + jnp.sum(prob, axis=0, keepdims=True)
            mixed = mixed + nn(kv_turned[m][:, :extent], prob.astype(bf16))
        safe = jnp.where(total > 0, total, 1.0)
        lse_ref[b : b + 1, :] = peak + jnp.log(safe)
        turned = pack_columns(mixed[HEAD_DIM:, :] / safe)
        turned_ref[b * BLOCK : (b + 1) * BLOCK, :] = turned
        mixed_ref[b * BLOCK : (b + 1) * BLOCK, :] = jnp.transpose(turned).astype(bf16)


def attend_back_core(
    factor, load_query, load_grad, load_kv, members, blocks, key_rows, kpos_ref, qpos_ref, qlow_ref, turned_ref, lse_ref,
    dq_ref, add_dkv,
):
    kv_turned = [jnp.transpose(load_kv(m, key_rows)) for m in range(members)]
    columns = [key_columns(kpos_ref, m, key_rows) for m in range(members)]
    for b in range(blocks - 1, -1, -1):
        extent = key_rows * (b + 1) // blocks
        rows = slice(b * BLOCK, (b + 1) * BLOCK)
        packed = (load_query(b).astype(f32) * factor).astype(bf16)
        grads = load_grad(b)
        wide = jnp.concatenate([spread_rows(packed, False), spread_rows(grads, True)], axis=0)
        product = jnp.transpose(grads.astype(f32)) * turned_ref[rows, :]
        delta = jnp.concatenate(
            [
                jnp.sum(product[:HEAD_DIM], axis=0, keepdims=True),
                jnp.sum(product[HEAD_DIM:], axis=0, keepdims=True),
            ],
            axis=1,
        )
        qpos = qpos_ref[b : b + 1, :]
        qlow = qlow_ref[b : b + 1, :]
        lse = lse_ref[b : b + 1, :]
        dquery = jnp.zeros((LANES, 2 * BLOCK), f32)
        for m in range(members):
            both = nt(load_kv(m, extent), wide)
            kpos = columns[m][:extent]
            prob = jnp.exp(
                jnp.where((kpos <= qpos) & (kpos >= qlow), both[:, : 2 * BLOCK] - lse, masked_score)
            )
            dlogit = (prob * (both[:, 2 * BLOCK :] - delta)).astype(bf16)
            dquery = dquery + nn(kv_turned[m][:, :extent], dlogit)
            add_dkv(m, extent, b == blocks - 1, nn(jnp.concatenate([dlogit, prob.astype(bf16)], axis=1), wide))
        dq_ref[rows, :] = jnp.transpose(pack_columns(dquery[:HEAD_DIM, :] * factor)).astype(bf16)


def attend_kernel(factor, q_ref, kv_ref, kpos_ref, qpos_ref, qlow_ref, mixed_ref, turned_ref, lse_ref):
    members, key_rows, _ = kv_ref.shape
    attend_core(
        factor,
        lambda b: q_ref[b * BLOCK : (b + 1) * BLOCK, :],
        lambda m, extent: kv_ref[m, :extent, :],
        members, q_ref.shape[0] // BLOCK, key_rows, kpos_ref, qpos_ref, qlow_ref, mixed_ref, turned_ref, lse_ref,
    )


def attend_back_kernel(
    factor, q_ref, do_ref, kv_ref, kpos_ref, qpos_ref, qlow_ref, turned_ref, lse_ref, dq_ref, dkv_ref
):
    members, key_rows, _ = kv_ref.shape

    def add_dkv(m, extent, first, update):
        if first:
            dkv_ref[m, :extent, :] = update
        else:
            dkv_ref[m, :extent, :] += update

    attend_back_core(
        factor,
        lambda b: q_ref[b * BLOCK : (b + 1) * BLOCK, :],
        lambda b: do_ref[b * BLOCK : (b + 1) * BLOCK, :],
        lambda m, extent: kv_ref[m, :extent, :],
        members, q_ref.shape[0] // BLOCK, key_rows, kpos_ref, qpos_ref, qlow_ref, turned_ref, lse_ref, dq_ref, add_dkv,
    )


vmem = pl.BlockSpec(memory_space=pltpu.VMEM)
vmem_limit = 56 * 1024 * 1024


def attend(factor, queries, kv, kpos, qpos, qlow):
    rows = queries.shape[0]
    return pl.pallas_call(
        functools.partial(attend_kernel, factor),
        out_shape=(
            jax.ShapeDtypeStruct((rows, LANES), bf16),
            jax.ShapeDtypeStruct((rows, LANES), f32),
            jax.ShapeDtypeStruct(qpos.shape, f32),
        ),
        in_specs=[vmem] * 5,
        out_specs=(vmem,) * 3,
        compiler_params=pltpu.CompilerParams(vmem_limit_bytes=vmem_limit),
        name="attend",
    )(queries, kv, kpos, qpos, qlow)


def attend_back(factor, queries, dmixed, kv, kpos, qpos, qlow, turned, lse):
    rows = queries.shape[0]
    return pl.pallas_call(
        functools.partial(attend_back_kernel, factor),
        out_shape=(
            jax.ShapeDtypeStruct((rows, LANES), bf16),
            jax.ShapeDtypeStruct(kv.shape, f32),
        ),
        in_specs=[vmem] * 8,
        out_specs=(vmem,) * 2,
        compiler_params=pltpu.CompilerParams(vmem_limit_bytes=vmem_limit),
        name="attend_back",
    )(queries, dmixed, kv, kpos, qpos, qlow, turned, lse)


def general(
    tokens_in,
    w_router,
    gain_attn,
    w_query,
    w_key,
    w_value,
    w_out,
    gain_mlp,
    w_up,
    w_down,
    out_grad,
    lengths,
    counts,
    chosen,
):
    devices = lax.axis_size("seq")
    own = lax.axis_index("seq")
    capacity = chosen.shape[0] // devices
    tok_rows, width = tokens_in.shape
    hidden_width = w_up.shape[1]
    group = devices // HEADS
    share = capacity // group
    half = share // 2
    member = own % group
    slots = devices * capacity
    factor = HEAD_DIM ** (-0.5)
    attn_gain = gain_attn.astype(f32)
    mlp_gain = gain_mlp.astype(f32)

    def swap(value):
        return lax.all_to_all(value, "seq", split_axis=0, concat_axis=0, tiled=True)

    groups = [[h * group + m for m in range(group)] for h in range(HEADS)]

    def across_group(value):
        if group == 2:
            other = lax.ppermute(value, "seq", [(s, s ^ 1) for s in range(devices)])
            return jnp.stack([value, other])
        return lax.all_gather(value, "seq", axis_index_groups=groups)

    def sum_over_group(value):
        if group == 2:
            return value[0] + lax.ppermute(value[1], "seq", [(s, s ^ 1) for s in range(devices)])
        return lax.psum_scatter(value, "seq", scatter_dimension=0, axis_index_groups=groups)

    def member_order(value):
        if group == 2:
            return jnp.where(member == 0, value, value[::-1])
        return value

    slot_ids = jnp.arange(capacity, dtype=jnp.int32)
    places = jnp.arange(devices, dtype=jnp.int32)[:, None] * tok_rows + chosen.reshape(devices, capacity)
    live_all = slot_ids[None, :] < counts[:, None]
    seq_ends = jnp.cumsum(lengths)
    starts = jnp.max(jnp.where(places[..., None] >= seq_ends, seq_ends, 0), axis=-1)
    kpos = jnp.where(live_all, places.astype(f32), far_away)
    kpos = member_order(kpos.reshape(devices, group, share).swapaxes(0, 1).reshape(group, devices * share))
    blocks = devices * half // BLOCK

    def query_order(value):
        value = lax.dynamic_index_in_dim(value.reshape(devices, group, share), member, 1, False)
        return value.reshape(blocks, devices // blocks, 2, half).swapaxes(1, 2).reshape(blocks, 2 * BLOCK)

    qpos = query_order(jnp.where(live_all, places, -1).astype(f32))
    qlow = query_order(starts.astype(f32))

    offsets = lax.dynamic_slice_in_dim(chosen, own * capacity, capacity)
    live = slot_ids < counts[own]
    pick = (offsets[:, None] == jnp.arange(tok_rows, dtype=jnp.int32)[None, :]).astype(bf16)
    routed = nn(pick, tokens_in)
    upstream = jnp.where(live[:, None], nn(pick, out_grad), 0.0)
    gate = jax.nn.sigmoid(jnp.sum(routed * w_router.astype(f32)[None, :], axis=1))
    gate_sum = jnp.sum(jnp.where(live, gate, 0.0))
    normed = rms_scale(routed, attn_gain).astype(bf16)
    normed_all = lax.all_gather(normed, "seq", axis=0, tiled=True)
    queries = nn(normed, w_query).astype(bf16)
    keys = nn(normed, w_key).astype(bf16)
    values = nn(normed, w_value).astype(bf16)

    def note(value):
        parts = jnp.pad(three_parts(value), (0, LANES - 3))
        return jnp.broadcast_to(parts, (devices, 8, LANES))

    def read_note(rows):
        return jnp.sum(rows[:, 0, :3].astype(f32))

    def to_heads(value, per_row):
        if per_row == 2:
            value = value.reshape(group, 2, half, HEADS, HEAD_DIM).transpose(3, 0, 2, 1, 4)
            return value.reshape(devices, half, LANES)
        return value

    def pair_to_heads(first, second):
        both = jnp.stack([first, second], axis=1).reshape(group, share, 2, HEADS, HEAD_DIM)
        return both.transpose(3, 0, 1, 2, 4).reshape(devices, share, LANES)

    def from_heads(value):
        value = value.reshape(HEADS, group, half, 2, HEAD_DIM).transpose(1, 3, 2, 0, 4)
        return value.reshape(capacity, HEADS * HEAD_DIM)

    def pair_from_heads(value):
        value = value.reshape(HEADS, group, share, 2, HEAD_DIM).transpose(3, 1, 2, 0, 4)
        value = value.reshape(2, capacity, HEADS * HEAD_DIM)
        return value[0], value[1]

    sent = jnp.concatenate([to_heads(queries, 2), pair_to_heads(keys, values), note(gate_sum)], axis=1)
    got = swap(sent)
    score_total = read_note(got[:, half + share :])
    chosen_total = jnp.sum(counts).astype(f32)
    ratio = chosen_total / score_total
    scaling = gate * ratio
    head_queries = got[:, :half].reshape(devices * half, LANES)
    kv = across_group(got[:, half : half + share].reshape(devices * share, LANES))
    mixed_packed, mixed_turned, lse = attend(factor, head_queries, kv, kpos, qpos, qlow)
    mixed = from_heads(swap(mixed_packed.reshape(devices, half, LANES)))

    attn_out = nn(mixed, w_out)
    middle = routed + attn_out
    normed_mlp = rms_scale(middle, mlp_gain).astype(bf16)
    dbranch = scaling[:, None] * upstream
    dmlp = dbranch.astype(bf16)
    gathered = lax.all_gather(
        jnp.concatenate([mixed, normed_mlp, dmlp], axis=1), "seq", axis=0, tiled=True
    )
    mixed_all = gathered[:, :width]
    normed_mlp_all = gathered[:, width : 2 * width]
    dmlp_all = gathered[:, 2 * width :]
    hidden = nn(normed_mlp, w_up)
    active = jax.nn.gelu(hidden, approximate=True).astype(bf16)
    branch = attn_out + nn(active, w_down)
    dweight = jnp.sum(upstream * branch, axis=1)

    def gelu_of(values):
        return jax.nn.gelu(values, approximate=True)

    dactive = nt(dmlp, w_down)
    dhidden = jax.vjp(gelu_of, hidden)[1](dactive)[0].astype(bf16)
    dnormed_mlp = nt(dhidden, w_up)
    dmiddle = jax.vjp(lambda v: rms_scale(v, mlp_gain), middle)[1](dnormed_mlp)[0]
    dattn = (dbranch + dmiddle).astype(bf16)
    dmixed = nt(dattn, w_out).astype(bf16)
    out_cols = width // devices
    dattn_split = dattn.reshape(capacity, devices, out_cols).swapaxes(0, 1)
    dattn_split = dattn_split.reshape(devices, capacity * out_cols // LANES, LANES)
    got = swap(
        jnp.concatenate(
            [to_heads(dmixed, 2), dattn_split, note(jnp.sum(jnp.where(live, dweight * gate, 0.0)))], axis=1
        )
    )
    dattn_own = got[:, half : half + capacity * out_cols // LANES].reshape(slots, out_cols)
    coefficient = read_note(got[:, half + capacity * out_cols // LANES :])
    dq_packed, dkv_parts = attend_back(
        factor,
        head_queries,
        got[:, :half].reshape(devices * half, LANES),
        kv,
        kpos,
        qpos,
        qlow,
        mixed_turned,
        lse,
    )
    dkv = sum_over_group(dkv_parts).astype(bf16)

    dscore = dweight * ratio - coefficient * chosen_total / (score_total * score_total)
    dlogit_router = jnp.where(live, dscore * gate * (1.0 - gate), 0.0)
    router_part = jnp.sum(dlogit_router[:, None] * routed, axis=0).reshape(devices, out_cols)
    router_parts = three_parts(router_part).swapaxes(0, 1).reshape(devices, 1, 3 * out_cols)
    router_note = jnp.pad(router_parts, ((0, 0), (0, 7), (0, LANES - 3 * out_cols)))
    got = swap(
        jnp.concatenate(
            [dq_packed.reshape(devices, half, LANES), dkv.reshape(devices, share, LANES), router_note], axis=1
        )
    )
    dquery = from_heads(got[:, :half])
    dkey, dvalue = pair_from_heads(got[:, half : half + share])
    grad_router = jnp.sum(got[:, half + share, : 3 * out_cols].astype(f32), axis=0)
    grad_router = jnp.sum(grad_router.reshape(3, out_cols), axis=0)

    normed_own = lax.dynamic_index_in_dim(normed_all.reshape(devices, group, share, width), member, 1, False)
    normed_own = normed_own.reshape(devices * share, width)
    dq_rows = dq_packed.reshape(devices, half, 2, HEAD_DIM).swapaxes(1, 2).reshape(devices * share, HEAD_DIM)
    dqkv = jnp.concatenate([dq_rows, dkv], axis=1)
    grad_qkv = lax.dot_general(normed_own, dqkv, (((0,), (0,)), ((), ())), preferred_element_type=f32)
    head_cols = 3 * HEAD_DIM // group
    grad_qkv = member_order(grad_qkv.reshape(width, group, head_cols).swapaxes(0, 1))
    grad_qkv = sum_over_group(grad_qkv).astype(bf16)
    grad_out = lax.dot_general(mixed_all, dattn_own, (((0,), (0,)), ((), ())), preferred_element_type=f32)

    hidden_cols = hidden_width // devices
    up_own = lax.dynamic_slice_in_dim(w_up, own * hidden_cols, hidden_cols, 1)
    down_own = lax.dynamic_slice_in_dim(w_down, own * hidden_cols, hidden_cols, 0)
    hidden_own = nn(normed_mlp_all, up_own)
    dactive_own = nt(dmlp_all, down_own)
    active_own, gelu_back = jax.vjp(gelu_of, hidden_own)
    dhidden_own = gelu_back(dactive_own)[0].astype(bf16)
    active_own = active_own.astype(bf16)
    grad_down = lax.dot_general(active_own, dmlp_all, (((0,), (0,)), ((), ())), preferred_element_type=f32)
    grad_up = lax.dot_general(
        normed_mlp_all, dhidden_own, (((0,), (0,)), ((), ())), preferred_element_type=f32
    )
    sent = jnp.concatenate([grad_up.astype(bf16), grad_qkv, grad_out.astype(bf16)], axis=1)
    got = swap(sent.reshape(devices, out_cols, sent.shape[1])).astype(f32)
    grad_up = got[:, :, :hidden_cols].swapaxes(0, 1).reshape(out_cols, hidden_width)
    grad_qkv = got[:, :, hidden_cols : hidden_cols + head_cols].reshape(HEADS, group, out_cols, head_cols)
    grad_qkv = grad_qkv.transpose(2, 0, 1, 3).reshape(out_cols, HEADS, 3, HEAD_DIM)
    grad_query = grad_qkv[:, :, 0].reshape(out_cols, width)
    grad_key = grad_qkv[:, :, 1].reshape(out_cols, width)
    grad_value = grad_qkv[:, :, 2].reshape(out_cols, width)
    grad_out = got[:, :, hidden_cols + head_cols :].swapaxes(0, 1).reshape(out_cols, width)

    def own_rows(value):
        return lax.dynamic_slice_in_dim(value, own * out_cols, out_cols, 0).astype(f32)

    grad_gain_attn = jnp.sum(
        own_rows(w_query) * grad_query + own_rows(w_key) * grad_key + own_rows(w_value) * grad_value, axis=1
    ) / own_rows(attn_gain)
    grad_gain_mlp = jnp.sum(own_rows(w_up) * grad_up, axis=1) / own_rows(mlp_gain)

    dnormed = nt(dquery, w_query) + nt(dkey, w_key) + nt(dvalue, w_value)
    drows = jax.vjp(lambda v: rms_scale(v, attn_gain), routed)[1](dnormed)[0]
    droutes = drows + dmiddle + dlogit_router[:, None] * w_router.astype(f32)[None, :]
    new_rows = (routed + scaling[:, None] * branch).astype(bf16)
    new_grads = (upstream + droutes).astype(bf16)
    put = (jnp.arange(tok_rows, dtype=jnp.int32)[:, None] == offsets[None, :]) & live[None, :]
    hit = jnp.any(put, axis=1, keepdims=True)
    put = put.astype(bf16)
    output = jnp.where(hit, nn(put, new_rows).astype(bf16), tokens_in)
    input_grad = jnp.where(hit, nn(put, new_grads).astype(bf16), out_grad)
    return (
        output,
        input_grad,
        grad_router,
        grad_gain_attn,
        grad_query,
        grad_key,
        grad_value,
        grad_out,
        grad_gain_mlp,
        grad_up,
        grad_down,
    )


SHARE = 64
HALF = 32
NOTE = 8
OUT_HALF = 16
OUT_ROWS = 32
TILES = 2
AT_OUT = TILES * OUT_ROWS
AT_QUERY = AT_OUT + OUT_HALF
AT_PAIR = AT_QUERY + OUT_HALF
AT_NOTE = AT_PAIR + OUT_ROWS
GRAD_ROWS = AT_NOTE + NOTE


def swapped(tile):
    return jnp.concatenate([tile[..., HEAD_DIM:], tile[..., :HEAD_DIM]], axis=-1)


def joined(left, right):
    return jnp.concatenate([left[..., :HEAD_DIM], right[..., HEAD_DIM:]], axis=-1)


def pack_rows(target, first, value):
    for pair in range(HEADS // 2):
        tile = value[:, pair * LANES : (pair + 1) * LANES]
        turned = swapped(tile)
        target[2 * pair, first : first + HALF, :] = joined(tile[:HALF], turned[HALF:])
        target[2 * pair + 1, first : first + HALF, :] = joined(turned[:HALF], tile[HALF:])


def pack_pairs(target, first, left, right):
    for pair in range(HEADS // 2):
        lanes = slice(pair * LANES, (pair + 1) * LANES)
        one, two = left[:, lanes], right[:, lanes]
        target[2 * pair, first : first + SHARE, :] = joined(one, swapped(two))
        target[2 * pair + 1, first : first + SHARE, :] = joined(swapped(one), two)


def unpack_rows(source, first, half):
    columns = []
    for pair in range(HEADS // 2):
        even = source[2 * pair, first : first + half, :]
        odd = source[2 * pair + 1, first : first + half, :]
        columns.append(jnp.concatenate([joined(even, swapped(odd)), joined(swapped(even), odd)], axis=0))
    return jnp.concatenate(columns, axis=1)


def unpack_pairs(source, first, rows):
    left, right = [], []
    for pair in range(HEADS // 2):
        even = source[2 * pair, first : first + rows, :]
        odd = source[2 * pair + 1, first : first + rows, :]
        left.append(joined(even, swapped(odd)))
        right.append(joined(swapped(even), odd))
    return jnp.concatenate(left, axis=1), jnp.concatenate(right, axis=1)


def in_parts(value):
    high = value.astype(bf16).astype(f32)
    rest = value - high
    middle = rest.astype(bf16).astype(f32)
    row = lax.broadcasted_iota(jnp.int32, value.shape, len(value.shape) - 2)
    parts = jnp.where(row == 0, high, jnp.where(row == 1, middle, jnp.where(row == 2, rest - middle, 0.0)))
    return parts.astype(bf16)


def write_note(target, first, value):
    rows = in_parts(jnp.broadcast_to(value, (NOTE, LANES)))
    for k in range(target.shape[0]):
        target[k, first : first + NOTE, :] = rows


def read_note(source, first):
    rows = source[:, first : first + NOTE, :].astype(f32)
    return jnp.sum(jnp.sum(rows, axis=0), axis=0, keepdims=True)[:, :1]


def slots_of(chosen_ref, device):
    row = chosen_ref[pl.ds(device // 2, 1), :]
    return jnp.where(device % 2 == 0, row[:, :SHARE], row[:, SHARE:])


def one_hot(own_ref, counts_ref, chosen_ref, tok_rows, live_only):
    offsets = slots_of(chosen_ref, own_ref[0])
    capacity = offsets.shape[1]
    rows = lax.broadcasted_iota(jnp.int32, (tok_rows, capacity), 0)
    hot = rows == offsets
    if live_only:
        slot = lax.broadcasted_iota(jnp.int32, (tok_rows, capacity), 1)
        hot = hot & (slot < counts_ref[own_ref[0]])
    return jnp.where(hot, 1.0, 0.0)


def live_column(own_ref, counts_ref, capacity):
    return lax.broadcasted_iota(jnp.int32, (capacity, 1), 0) < counts_ref[own_ref[0]]


def gate_of(rows, vectors_ref):
    return jax.nn.sigmoid(jnp.sum(rows * vectors_ref[0:1, :], axis=1, keepdims=True))


def inverse_rms(values):
    return lax.rsqrt(jnp.mean(values * values, axis=-1, keepdims=True) + eps_norm)


def total_count(counts_ref):
    return lax.fori_loop(0, counts_ref.shape[0], lambda i, s: s + counts_ref[i], 0).astype(f32)


def gelu_pair(u):
    c = 0.7978845608028654
    square = u * u
    t = jnp.tanh(c * (u + 0.044715 * (square * u)))
    value = 0.5 * u * (1.0 + t)
    slope = 0.5 * (1.0 + t) + (0.5 * u) * ((1.0 - t * t) * (c + (3.0 * 0.044715 * c) * square))
    return value, slope


def chip_of(own_ref, k):
    return jnp.bitwise_xor(own_ref[0] // 2, (k // 4) ^ (4 * (k % 4)))


def row_of(column):
    wide = jnp.broadcast_to(column, (column.shape[0], LANES))
    filled = jnp.concatenate([wide, jnp.zeros((LANES - column.shape[0], LANES), f32)], axis=0)
    return jnp.transpose(filled)[:1, : column.shape[0]]


def places_kernel(own_ref, counts_ref, lengths_ref, chosen_ref, kpos_ref, qpos_ref, qlow_ref):
    core = own_ref[0] % 2
    devices, capacity = 2 * chosen_ref.shape[0], SHARE
    tok_rows = lengths_ref[lengths_ref.shape[0] - 1]
    slot = lax.broadcasted_iota(jnp.int32, (1, capacity), 1)
    ends = []
    for k in range(lengths_ref.shape[0] - 1):
        ends.append(lengths_ref[k] + (ends[-1] if ends else 0))

    def place(device):
        value = device * tok_rows + slots_of(chosen_ref, device)
        return value, slot < counts_ref[device]

    def key_row(device):
        value, live = place(device)
        return jnp.where(live, value.astype(f32), far_away)

    for m in range(2):
        parity = jnp.bitwise_xor(core, m)
        for c in range(0, devices // 2, 2):
            tile = jnp.concatenate([key_row(2 * c + parity), key_row(2 * c + 2 + parity)], axis=1)
            kpos_ref[m : m + 1, c * capacity : (c + 2) * capacity] = tile
    blocks = qpos_ref.shape[0]
    sources = devices // 2 // blocks
    for b in range(blocks):
        lows, highs = [], []
        for c in range(b * sources, (b + 1) * sources):
            value, live = place(2 * c + core)
            low = jnp.zeros_like(value)
            for end in ends:
                low = jnp.maximum(low, jnp.where(value >= end, end, 0))
            both = jnp.concatenate([jnp.where(live, value, -1), low], axis=0).astype(f32)
            lows.append(both[:, :HALF])
            highs.append(both[:, HALF:])
        both = jnp.concatenate(lows + highs, axis=1)
        qpos_ref[b : b + 1, :] = both[:1]
        qlow_ref[b : b + 1, :] = both[1:]


def fetch_kernel(own_ref, counts_ref, chosen_ref, tokens_ref, grads_ref, both_ref, rows_ref, upstream_ref):
    hot = one_hot(own_ref, counts_ref, chosen_ref, tokens_ref.shape[0], False)
    capacity = hot.shape[1]
    pick = jnp.transpose(jnp.concatenate([hot, jnp.zeros_like(hot)], axis=1))[:capacity].astype(bf16)
    live = live_column(own_ref, counts_ref, capacity)
    rows = nn(pick, tokens_ref[...]).astype(bf16)
    upstream = jnp.where(live, nn(pick, grads_ref[...]), 0.0).astype(bf16)
    both_ref[0, :capacity, :] = rows
    both_ref[0, capacity:, :] = upstream
    rows_ref[0] = rows
    upstream_ref[0] = upstream


def project_kernel(own_ref, counts_ref, vectors_ref, wq, wk, wv, *rest):
    pieces, sent_ref = rest[:-1], rest[-1]
    head = own_ref[0] // 2
    core = own_ref[0] % 2
    even = head % 2 == 0
    k = 0
    weights = None
    for piece in pieces:
        blocks, capacity, width = piece.shape
        rows = piece[...].reshape(blocks * capacity, width).astype(f32)
        gate = gate_of(rows, vectors_ref)
        normed = (rows * inverse_rms(rows) * vectors_ref[1:2, :]).astype(bf16)
        if weights is None:
            w_pair = jnp.where(even, joined(wk[...], swapped(wv[...])), joined(swapped(wk[...]), wv[...]))
            weights = jnp.concatenate([w_pair, jnp.where(even, wq[...], swapped(wq[...]))], axis=1)
        product = nn(normed, weights)
        for j in range(blocks):
            chip = chip_of(own_ref, k)
            block = product[j * capacity : (j + 1) * capacity]
            query = block[:, LANES:]
            sent_ref[chip, :HALF, :] = joined(query[:HALF], swapped(query[HALF:])).astype(bf16)
            sent_ref[chip, HALF : HALF + SHARE, :] = block[:, :LANES].astype(bf16)
            slot = lax.broadcasted_iota(jnp.int32, (capacity, 1), 0)
            live = slot < counts_ref[2 * chip + core]
            part = jnp.where(live, gate[j * capacity : (j + 1) * capacity], 0.0)
            part = jnp.sum(part, axis=0, keepdims=True)
            sent_ref[chip, HALF + SHARE :, :] = in_parts(jnp.broadcast_to(part, (NOTE, LANES)))
            k += 1


def unpack_kernel(got_ref, mixed_ref):
    mixed_ref[0] = unpack_rows(got_ref, 0, HALF)


CHUNKS = 4
PIECES = (5, 4, 5)


def early_kernel(both_ref, down_ref, product_ref, w_down, sems):
    cols = down_ref.shape[0] // CHUNKS
    parts = [pl.ds(c * cols, cols) for c in range(CHUNKS)]
    copies = [pltpu.make_async_copy(down_ref.at[p, :], w_down.at[p, :], sems.at[c]) for c, p in enumerate(parts)]
    for copy in copies:
        copy.start()
    upstream = both_ref[0, both_ref.shape[1] // 2 :, :]
    for c, copy in enumerate(copies):
        copy.wait()
        part = slice(c * cols, (c + 1) * cols)
        product_ref[:, part] = nt(upstream, w_down[part, :])


def middle_kernel(
    own_ref, counts_ref, mixed_ref, total_ref, both_ref, vectors_ref, product_ref, out_ref, up_ref,
    sent_ref, active_ref, attn_ref, dmiddle_ref, dweight_ref, w_out, w_up, sems,
):
    width, total_cols = up_ref.shape
    cols = total_cols // CHUNKS
    copies = [pltpu.make_async_copy(out_ref, w_out, sems.at[0])]
    for c in range(CHUNKS):
        part = pl.ds(c * cols, cols)
        copies.append(pltpu.make_async_copy(up_ref.at[:, part], w_up.at[:, part], sems.at[1 + c]))
    for copy in copies:
        copy.start()
    capacity = mixed_ref.shape[1]
    rows = both_ref[0, :capacity, :].astype(f32)
    upstream = both_ref[0, capacity:, :].astype(f32)
    live = live_column(own_ref, counts_ref, capacity)
    gate = gate_of(rows, vectors_ref)
    ratio = total_count(counts_ref) / total_ref[:1, :1]
    scaling = gate * ratio
    gain = vectors_ref[2:3, :]
    dbranch = scaling * upstream
    copies[0].wait()
    attn_out = nn(mixed_ref[0], w_out[...])
    attn_ref[...] = attn_out
    dweight = jnp.sum(upstream * attn_out, axis=1, keepdims=True)
    middle = rows + attn_out
    scale = inverse_rms(middle)
    normed = (middle * scale * gain).astype(bf16)
    dnormed = jnp.zeros((capacity, width), f32)
    for c in range(CHUNKS):
        part = slice(c * cols, (c + 1) * cols)
        copies[1 + c].wait()
        value, slope = gelu_pair(nn(normed, w_up[:, part]))
        active = value.astype(bf16)
        active_ref[:, part] = active
        product = product_ref[:, part]
        dweight = dweight + jnp.sum(active.astype(f32) * product, axis=1, keepdims=True)
        dnormed = dnormed + nt((scaling * product * slope).astype(bf16), w_up[:, part])
    dweight_ref[...] = jnp.broadcast_to(dweight, dweight_ref.shape)
    scaled = gain * dnormed
    dmiddle = scale * scaled - middle * (scale * scale * scale) * jnp.mean(scaled * middle, axis=-1, keepdims=True)
    dmiddle_ref[...] = dmiddle
    dattn = (dbranch + dmiddle).astype(bf16)
    pack_rows(sent_ref, 0, nt(dattn, w_out[...]).astype(bf16))
    pack_rows(sent_ref, HALF, dattn)
    write_note(sent_ref, 2 * HALF, jnp.sum(jnp.where(live, dweight * gate, 0.0), axis=0, keepdims=True))


def put_kernel(
    own_ref, counts_ref, chosen_ref, total_ref, both_ref, vectors_ref, active_ref, attn_ref, old_ref, down_ref,
    result_ref, w_down, sems,
):
    rows_of_chunk = down_ref.shape[0] // CHUNKS
    parts = [pl.ds(c * rows_of_chunk, rows_of_chunk) for c in range(CHUNKS)]
    copies = [pltpu.make_async_copy(down_ref.at[p, :], w_down.at[p, :], sems.at[c]) for c, p in enumerate(parts)]
    for copy in copies:
        copy.start()
    rows = both_ref[0, : both_ref.shape[1] // 2, :].astype(f32)
    scaling = gate_of(rows, vectors_ref) * (total_count(counts_ref) / total_ref[:1, :1])
    mlp_out = jnp.zeros_like(rows)
    for c, copy in enumerate(copies):
        part = slice(c * rows_of_chunk, (c + 1) * rows_of_chunk)
        copy.wait()
        mlp_out = mlp_out + nn(active_ref[:, part], w_down[part, :])
    new = (rows + scaling * (attn_ref[...] + mlp_out)).astype(bf16)
    put_rows(own_ref, counts_ref, chosen_ref, old_ref, new, result_ref)


def put_rows(own_ref, counts_ref, chosen_ref, old_ref, new, result_ref):
    hot = one_hot(own_ref, counts_ref, chosen_ref, old_ref.shape[0], True)
    hit = jnp.sum(hot, axis=1, keepdims=True) > 0.5
    placed = nn(hot.astype(bf16), new)
    result_ref[...] = jnp.where(hit, placed, old_ref[...].astype(f32)).astype(bf16)


def router_slope(own_ref, counts_ref, rows, dweight_ref, total_ref, coef_ref, vectors_ref):
    gate = gate_of(rows, vectors_ref)
    live = live_column(own_ref, counts_ref, rows.shape[0])
    count = total_count(counts_ref)
    total = total_ref[:1, :1]
    dscore = dweight_ref[:, :1] * (count / total) - coef_ref[:1, :1] * count / (total * total)
    return jnp.where(live, dscore * gate * (1.0 - gate), 0.0)


def keys_kernel(dq_ref, dkv_ref, moved_ref, coef_ref, sent_ref, sum_ref):
    rows = dkv_ref.shape[0]
    sent_ref[:, :HALF, :] = dq_ref[...]
    dkv = dkv_ref[...] + moved_ref[:rows, :]
    sent_ref[:, HALF:, :] = dkv.astype(bf16).reshape(sent_ref.shape[0], SHARE, LANES)
    sum_ref[...] = coef_ref[...] + moved_ref[rows:, :]


def units_kernel(
    own_ref, counts_ref, got_ref, dqkv_ref, total_ref, coef_ref, vectors_ref, rows_ref, dweight_ref,
    out_ref, up_ref, down_ref, *rest,
):
    gathers = []
    for count in PIECES:
        gathers.append(rest[:count])
        rest = rest[count:]
    down_keep_ref, down_give_ref, keep_ref, give_ref, rest = *rest[:4], rest[4:]
    *slots, grad_up, grad_down, grad_out, grad_q, grad_kv, ratio_ref, sems = rest
    rows_slots, upstream_slots, mixed_slots = slots
    step = pl.program_id(0)
    steps = pl.num_programs(0)
    _, sources, capacity, width = mixed_slots.shape
    core = own_ref[0] % 2
    slot = step % 2

    def copies(k):
        result = []
        for i, pieces in enumerate(gathers):
            for side in range(2):
                piece = 2 * k + side
                if piece < 3 or len(pieces) == 4:
                    target = slots[i].at[k, 4 * side : 4 * side + 4]
                    result.append(pltpu.make_async_copy(pieces[piece], target, sems.at[k, i, side, 0]))
                    continue
                for half in range(2):
                    first = 4 * side + 2 * half
                    target = slots[i].at[k, first : first + 2]
                    result.append(pltpu.make_async_copy(pieces[piece + half], target, sems.at[k, i, side, half]))
        return result

    @pl.when(step == 0)
    def _():
        for k in range(2):
            for copy in copies(k):
                copy.start()

    @pl.when(step == 0)
    def _():
        for ref in (grad_up, grad_down, grad_out, grad_q, grad_kv):
            ref[...] = jnp.zeros_like(ref)
        ratio_ref[...] = jnp.broadcast_to(total_count(counts_ref) / total_ref[:1, :1], ratio_ref.shape)

    for k in range(2):

        @pl.when(step == k)
        def _(k=k):
            for copy in copies(k):
                copy.wait()

    def halves(ref, first):
        blocks = [ref[chip_of(own_ref, sources * step + j), first : first + HALF, :] for j in range(sources)]
        turned = jnp.transpose(jnp.concatenate(blocks, axis=0).astype(f32)).astype(bf16)
        return turned[:HEAD_DIM], turned[HEAD_DIM:]

    def low_high(value):
        value = value.reshape(sources, capacity, width)
        return value[:, :HALF, :].reshape(sources * HALF, width), value[:, HALF:, :].reshape(sources * HALF, width)

    rows = rows_slots[slot].reshape(sources * capacity, width).astype(f32)
    upstream = upstream_slots[slot].reshape(sources * capacity, width).astype(f32)
    mixed = mixed_slots[slot].reshape(sources * capacity, width)
    normed_attn = (rows * inverse_rms(rows) * vectors_ref[1:2, :]).astype(bf16)
    low_query, high_query = halves(dqkv_ref, 0)
    low_rows, high_rows = low_high(normed_attn)
    grad_q[...] += nn(low_query, low_rows) + nn(high_query, high_rows)
    blocks = [dqkv_ref[chip_of(own_ref, sources * step + j), HALF:, :] for j in range(sources)]
    pairs_turned = jnp.transpose(jnp.concatenate(blocks, axis=0).astype(f32)).astype(bf16)
    grad_kv[...] += nn(pairs_turned, normed_attn)
    low_attn, high_attn = halves(got_ref, HALF)
    low_mixed, high_mixed = low_high(mixed)
    grad_out[...] += nn(low_attn, low_mixed) + nn(high_attn, high_mixed)
    middle = rows + nn(mixed, out_ref[...])
    normed = (middle * inverse_rms(middle) * vectors_ref[2:3, :]).astype(bf16)
    dmlp = (gate_of(rows, vectors_ref) * ratio_ref[:1, :1] * upstream).astype(bf16)
    value, slope = gelu_pair(nn(normed, up_ref[...]))
    dhidden = nt(dmlp, down_ref[...]) * slope
    grad_down[...] += nn(jnp.transpose(value).astype(bf16), dmlp)
    grad_up[...] += nn(jnp.transpose(dhidden).astype(bf16), normed)

    @pl.when(step == steps - 1)
    def _():
        chips = keep_ref.shape[0]

        def split(value):
            value = value.reshape(chips, 2, OUT_ROWS, LANES)
            even, odd = value[:, 0], value[:, 1]
            return jnp.where(core == 0, even, odd), jnp.where(core == 0, odd, even)

        def store(first, kept, given):
            keep_ref[:, first : first + kept.shape[1], :] = kept.astype(bf16)
            give_ref[:, first : first + kept.shape[1], :] = given.astype(bf16)

        for t in range(TILES):
            store(t * OUT_ROWS, *split(jnp.transpose(grad_up[t * LANES : (t + 1) * LANES, :])))

        def two_in_one(value):
            return joined(value[:, :OUT_HALF], swapped(value[:, OUT_HALF:]))

        both_turned = jnp.transpose(jnp.concatenate([grad_out[...], grad_q[...]], axis=0))
        kept, given = split(both_turned)
        store(AT_OUT, two_in_one(kept), two_in_one(given))
        store(AT_QUERY, two_in_one(swapped(kept)), two_in_one(swapped(given)))
        store(AT_PAIR, *split(jnp.transpose(grad_kv[...])))
        own_rows = rows_ref[0, :capacity, :].astype(f32)
        dlogit = router_slope(own_ref, counts_ref, own_rows, dweight_ref, total_ref, coef_ref, vectors_ref)
        part = jnp.broadcast_to(jnp.sum(dlogit * own_rows, axis=0, keepdims=True), (NOTE, width))
        per_tile = LANES // OUT_ROWS
        for c in range(chips):
            tile = part[:, (2 * c) // per_tile * LANES : ((2 * c) // per_tile + 1) * LANES]
            shift = (2 * c) % per_tile * OUT_ROWS
            if shift:
                tile = jnp.concatenate([tile[:, shift:], tile[:, :shift]], axis=1)
            after = jnp.concatenate([tile[:, OUT_ROWS:], tile[:, :OUT_ROWS]], axis=1)
            keep_ref[c, AT_NOTE:, :] = in_parts(jnp.where(core == 0, tile, after))
            give_ref[c, AT_NOTE:, :] = in_parts(jnp.where(core == 0, after, tile))
        down = grad_down[...]
        half = down.shape[0] // 2
        down_keep_ref[...] = jnp.where(core == 0, down[:half], down[half:])
        down_give_ref[...] = jnp.where(core == 0, down[half:], down[:half]).astype(bf16)


def merge_kernel(keep_ref, moved_ref, sent_ref):
    total = keep_ref[...].astype(f32) + moved_ref[...].astype(f32)
    sent_ref[:, :AT_NOTE, :] = total[:, :AT_NOTE].astype(bf16)
    note = jnp.sum(total[:, AT_NOTE:], axis=1, keepdims=True)
    sent_ref[:, AT_NOTE:, :] = in_parts(jnp.broadcast_to(note, (note.shape[0], NOTE, LANES)))


def rows_kernel(
    own_ref, counts_ref, chosen_ref, got_ref, both_ref, dmiddle_ref, dweight_ref, total_ref, coef_ref, vectors_ref,
    old_ref, wq_ref, wk_ref, wv_ref, grads_ref, wq, wk, wv, sems,
):
    copies = [
        pltpu.make_async_copy(source, target, sems.at[i])
        for i, (source, target) in enumerate(((wq_ref, wq), (wk_ref, wk), (wv_ref, wv)))
    ]
    for copy in copies:
        copy.start()
    capacity = dmiddle_ref.shape[0]
    rows = both_ref[0, :capacity, :].astype(f32)
    upstream = both_ref[0, capacity:, :].astype(f32)
    gain = vectors_ref[1:2, :]
    dlogit = router_slope(own_ref, counts_ref, rows, dweight_ref, total_ref, coef_ref, vectors_ref)
    partial = upstream + dmiddle_ref[...] + dlogit * vectors_ref[0:1, :]
    dquery = unpack_rows(got_ref, 0, HALF)
    dkey, dvalue = unpack_pairs(got_ref, HALF, SHARE)
    copies[0].wait()
    dnormed = jnp.zeros_like(partial) + nt(dquery, wq[...])
    copies[1].wait()
    dnormed = dnormed + nt(dkey, wk[...])
    copies[2].wait()
    dnormed = dnormed + nt(dvalue, wv[...])
    scale = inverse_rms(rows)
    scaled = gain * dnormed
    drows = scale * scaled - rows * (scale * scale * scale) * jnp.mean(scaled * rows, axis=-1, keepdims=True)
    put_rows(own_ref, counts_ref, chosen_ref, old_ref, (partial + drows).astype(bf16), grads_ref)


def finish_kernel(
    got_ref, own_gain_ref, up_ref, wq_ref, wk_ref, wv_ref,
    grad_up_ref, grad_out_ref, grad_q_ref, grad_k_ref, grad_v_ref, router_ref, gain_attn_ref, gain_mlp_ref,
):
    total = jnp.zeros((OUT_ROWS, LANES), f32)
    for c in range(got_ref.shape[0]):
        for t in range(TILES):
            lanes = slice((TILES * c + t) * LANES, (TILES * c + t + 1) * LANES)
            part = got_ref[c, t * OUT_ROWS : (t + 1) * OUT_ROWS, :].astype(f32)
            grad_up_ref[:, lanes] = part
            total = total + part * up_ref[:, lanes].astype(f32)
    gain_mlp_ref[...] = row_of(jnp.sum(total, axis=1, keepdims=True)) / own_gain_ref[2:3, :]
    grad_out_ref[...] = unpack_rows(got_ref, AT_OUT, OUT_HALF).astype(f32)
    grad_q = unpack_rows(got_ref, AT_QUERY, OUT_HALF).astype(f32)
    grad_k, grad_v = (value.astype(f32) for value in unpack_pairs(got_ref, AT_PAIR, OUT_ROWS))
    grad_q_ref[...] = grad_q
    grad_k_ref[...] = grad_k
    grad_v_ref[...] = grad_v
    products = wq_ref[...].astype(f32) * grad_q + wk_ref[...].astype(f32) * grad_k + wv_ref[...].astype(f32) * grad_v
    gain_attn_ref[...] = row_of(jnp.sum(products, axis=1, keepdims=True)) / own_gain_ref[1:2, :]
    notes = jnp.sum(got_ref[:, AT_NOTE:, :].astype(f32), axis=0)
    router_ref[...] = jnp.sum(notes, axis=0, keepdims=True)[:, :OUT_ROWS]


def pair_attend_kernel(factor, got_ref, other_ref, kpos_ref, qpos_ref, qlow_ref, mixed_ref, turned_ref, lse_ref, total_ref):
    lists = (got_ref, other_ref)
    chips = got_ref.shape[0]
    blocks = chips * HALF // BLOCK
    sources = chips // blocks
    total = read_note(got_ref, HALF + SHARE) + read_note(other_ref, HALF + SHARE)
    total_ref[...] = jnp.broadcast_to(total, total_ref.shape)
    attend_core(
        factor,
        lambda b: got_ref[b * sources : (b + 1) * sources, :HALF, :].reshape(BLOCK, LANES),
        lambda m, extent: lists[m][: extent // SHARE, HALF : HALF + SHARE, :].reshape(extent, LANES),
        2, blocks, chips * SHARE, kpos_ref, qpos_ref, qlow_ref, mixed_ref, turned_ref, lse_ref,
    )


def pair_attend_back_kernel(
    factor, got_ref, other_ref, grad_ref, kpos_ref, qpos_ref, qlow_ref, turned_ref, lse_ref,
    dq_ref, own_ref, moved_ref, coef_ref,
):
    lists = (got_ref, other_ref)
    sums = (own_ref, moved_ref)
    chips = got_ref.shape[0]
    blocks = chips * HALF // BLOCK
    sources = chips // blocks
    coef = jnp.broadcast_to(read_note(grad_ref, 2 * HALF), coef_ref.shape)
    coef_ref[...] = coef
    moved_ref[chips * SHARE :, :] = coef

    def add_dkv(m, extent, first, update):
        if first:
            sums[m][:extent, :] = update
        else:
            sums[m][:extent, :] += update

    attend_back_core(
        factor,
        lambda b: got_ref[b * sources : (b + 1) * sources, :HALF, :].reshape(BLOCK, LANES),
        lambda b: grad_ref[b * sources : (b + 1) * sources, :HALF, :].reshape(BLOCK, LANES),
        lambda m, extent: lists[m][: extent // SHARE, HALF : HALF + SHARE, :].reshape(extent, LANES),
        2, blocks, chips * SHARE, kpos_ref, qpos_ref, qlow_ref, turned_ref, lse_ref, dq_ref, add_dkv,
    )


smem = pl.BlockSpec(memory_space=pltpu.SMEM)
hbm = pl.BlockSpec(memory_space=pl.ANY)
megabytes = {
    "places": 4, "early": 56, "fetch": 56, "project": 16, "attend": 20, "unpack": 4, "middle": 56, "put": 56, "attend_back": 24,
    "keys": 8, "units": 56, "merge": 10, "rows": 56, "finish": 12,
}


def params_of(name):
    return pltpu.CompilerParams(vmem_limit_bytes=megabytes[name] * 1024 * 1024)


def shaped(shape, dtype):
    return jax.ShapeDtypeStruct(shape, dtype)


microseconds = {
    "places": 1, "early": 5, "fetch": 3, "project": 4, "attend": 5, "unpack": 2, "middle": 11, "put": 6, "attend_back": 6, "keys": 2,
    "units": 16, "merge": 3, "rows": 7, "finish": 2,
}


def cost_of(name):
    return pl.CostEstimate(flops=0, transcendentals=0, bytes_accessed=microseconds[name] * 3_300_000)


def call(kernel, name, in_specs, out_shape, arguments, scratch=()):
    return pl.pallas_call(
        kernel,
        out_shape=out_shape,
        in_specs=in_specs,
        out_specs=jax.tree.map(lambda _: vmem, out_shape),
        scratch_shapes=list(scratch),
        compiler_params=params_of(name),
        cost_estimate=cost_of(name),
        name=name,
    )(*arguments)


def pairs(
    tokens_in,
    w_router,
    gain_attn,
    w_query,
    w_key,
    w_value,
    w_out,
    gain_mlp,
    w_up,
    w_down,
    out_grad,
    lengths,
    counts,
    chosen,
):
    devices = lax.axis_size("seq")
    chips = devices // 2
    own = lax.axis_index("seq")
    capacity = chosen.shape[0] // devices
    tok_rows, width = tokens_in.shape
    hidden_width = w_up.shape[1]
    out_rows = width // devices
    factor = HEAD_DIM ** (-0.5)
    core = own % 2
    own_id = own.astype(jnp.int32).reshape(1)
    chosen = chosen.reshape(chips, 2 * capacity)
    vectors = jnp.stack([w_router, gain_attn, gain_mlp]).astype(f32)
    own_gains = lax.dynamic_slice_in_dim(vectors, own * out_rows, out_rows, 1)
    cores = [[2 * c + k for c in range(chips)] for k in range(2)]

    def swap(value):
        return lax.all_to_all(value, "seq", split_axis=0, concat_axis=0, tiled=True, axis_index_groups=cores)

    def across(value, bits):
        return lax.ppermute(value, "seq", [(s, s ^ bits) for s in range(devices)])

    def line_of(block):
        return jnp.concatenate([block] + [across(block, 8 * k) for k in (1, 2, 3)], axis=0)

    def sides_of(line):
        return [line, across(line, 2), across(line, 4)]

    def gathered(sides):
        return sides + [across(sides[2][:2], 2), across(sides[1][2:], 4)]

    def gathered_whole(sides):
        return sides + [across(sides[2], 2)]

    blocks = chips * HALF // BLOCK
    square = pltpu.VMEM((width, width), bf16)
    block = shaped((1, capacity, width), bf16)
    both, own_rows, own_upstream = call(
        fetch_kernel, "fetch", [smem, smem] + [vmem] * 3, (shaped((1, 2 * capacity, width), bf16), block, block),
        (own_id, counts, chosen, tokens_in, out_grad),
    )
    rows_line = line_of(own_rows)
    product = call(
        early_kernel, "early", [vmem, hbm], shaped((capacity, hidden_width), f32), (both, w_down),
        [pltpu.VMEM((hidden_width, width), bf16), pltpu.SemaphoreType.DMA((CHUNKS,))],
    )
    chosen_after, product, rows_line = lax.optimization_barrier((chosen, product, rows_line))
    kpos, qpos, qlow = call(
        places_kernel, "places", [smem] * 3 + [vmem],
        (
            shaped((2, chips * SHARE), f32),
            shaped((blocks, 2 * BLOCK), f32),
            shaped((blocks, 2 * BLOCK), f32),
        ),
        (own_id, counts, jnp.append(lengths, tok_rows), chosen_after),
    )
    rows_all = gathered(sides_of(rows_line))
    column = own // 4 * LANES
    columns = [lax.dynamic_slice_in_dim(w, column, LANES, 1) for w in (w_query, w_key, w_value)]
    upstream_line = line_of(own_upstream)
    rows_all, upstream_line = lax.optimization_barrier((rows_all, upstream_line))
    kpos, qpos, qlow, columns, rows_all = lax.optimization_barrier((kpos, qpos, qlow, columns, rows_all))
    got = call(
        project_kernel, "project", [smem, smem] + [vmem] * 9,
        shaped((chips, HALF + SHARE + NOTE, LANES), bf16),
        (own_id, counts, vectors, *columns, *rows_all),
    )
    other = across(got, 1)
    upstream_sides = sides_of(upstream_line)
    mixed_packed, turned, lse, total = call(
        functools.partial(pair_attend_kernel, factor), "attend", [vmem] * 5,
        (
            shaped((chips * HALF, LANES), bf16),
            shaped((chips * HALF, LANES), f32),
            shaped((blocks, 2 * BLOCK), f32),
            shaped((8, LANES), f32),
        ),
        (got, other, kpos, qpos, qlow),
    )
    mixed_got = swap(mixed_packed.reshape(chips, HALF, LANES))
    upstream_sides, mixed_got = lax.optimization_barrier((upstream_sides, mixed_got))
    upstream_all = gathered_whole(upstream_sides)
    mixed = call(unpack_kernel, "unpack", [vmem], shaped((1, capacity, width), bf16), (mixed_got,))
    mixed_line = line_of(mixed)
    sent, active, attn_out, dmiddle, dweight = call(
        middle_kernel, "middle", [smem, smem] + [vmem] * 5 + [hbm] * 2,
        (
            shaped((chips, 2 * HALF + NOTE, LANES), bf16),
            shaped((capacity, hidden_width), bf16),
            shaped((capacity, width), f32),
            shaped((capacity, width), f32),
            shaped((capacity, LANES), f32),
        ),
        (own_id, counts, mixed, total, both, vectors, product, w_out, w_up),
        [
            square,
            pltpu.VMEM((width, hidden_width), bf16),
            pltpu.SemaphoreType.DMA((1 + CHUNKS,)),
        ],
    )
    mixed_line, sent = lax.optimization_barrier((mixed_line, sent))
    mixed_sides = sides_of(mixed_line)
    upstream_all, sent = lax.optimization_barrier((upstream_all, sent))
    grads_got = swap(sent)
    output = call(
        put_kernel, "put", [smem, smem] + [vmem] * 7 + [hbm], shaped((tok_rows, width), bf16),
        (own_id, counts, chosen, total, both, vectors, active, attn_out, tokens_in, w_down),
        [pltpu.VMEM((hidden_width, width), bf16), pltpu.SemaphoreType.DMA((CHUNKS,))],
    )
    mixed_all = gathered(mixed_sides)
    output, grads_got = lax.optimization_barrier((output, grads_got))
    dq, dkv_own, dkv_other, coef = call(
        functools.partial(pair_attend_back_kernel, factor), "attend_back", [vmem] * 8,
        (
            shaped((chips * HALF, LANES), bf16),
            shaped((chips * SHARE, LANES), f32),
            shaped((chips * SHARE + 8, LANES), f32),
            shaped((8, LANES), f32),
        ),
        (got, other, grads_got, kpos, qpos, qlow, turned, lse),
    )
    moved = across(dkv_other, 1)
    dqkv, coef = call(
        keys_kernel, "keys", [vmem] * 4,
        (shaped((chips, HALF + SHARE, LANES), bf16), shaped((8, LANES), f32)),
        (dq.reshape(chips, HALF, LANES), dkv_own, moved, coef),
    )
    got = swap(dqkv)
    sources = 8
    hidden_cols = hidden_width // chips
    whole = lambda *shape: pl.BlockSpec(shape, lambda i, o: (0,) * len(shape))
    down_keep, down_give, keep, give = pl.pallas_call(
        units_kernel,
        out_shape=(
            shaped((hidden_cols // 2, width), f32),
            shaped((hidden_cols // 2, width), bf16),
            shaped((chips, GRAD_ROWS, LANES), bf16),
            shaped((chips, GRAD_ROWS, LANES), bf16),
        ),
        grid_spec=pltpu.PrefetchScalarGridSpec(
            num_scalar_prefetch=1,
            grid=(chips // sources,),
            in_specs=[
                smem,
                whole(chips, 2 * HALF + NOTE, LANES),
                whole(chips, HALF + SHARE, LANES),
                whole(8, LANES),
                whole(8, LANES),
                whole(3, width),
                whole(1, 2 * capacity, width),
                whole(capacity, LANES),
                whole(width, width),
                pl.BlockSpec((width, hidden_cols), lambda i, o: (0, o[0] // 2)),
                pl.BlockSpec((hidden_cols, width), lambda i, o: (o[0] // 2, 0)),
            ]
            + [hbm] * sum(PIECES),
            out_specs=(
                whole(hidden_cols // 2, width),
                whole(hidden_cols // 2, width),
                whole(chips, GRAD_ROWS, LANES),
                whole(chips, GRAD_ROWS, LANES),
            ),
            scratch_shapes=[
                pltpu.VMEM((2, sources, capacity, width), bf16),
                pltpu.VMEM((2, sources, capacity, width), bf16),
                pltpu.VMEM((2, sources, capacity, width), bf16),
                pltpu.VMEM((hidden_cols, width), f32),
                pltpu.VMEM((hidden_cols, width), f32),
                pltpu.VMEM((HEAD_DIM, width), f32),
                pltpu.VMEM((HEAD_DIM, width), f32),
                pltpu.VMEM((2 * HEAD_DIM, width), f32),
                pltpu.VMEM((8, LANES), f32),
                pltpu.SemaphoreType.DMA((2, 3, 2, 2)),
            ],
        ),
        compiler_params=params_of("units"),
        cost_estimate=cost_of("units"),
        name="units",
    )(own_id, counts, grads_got, dqkv, total, coef, vectors, both, dweight, w_out, w_up, w_down, *rows_all, *upstream_all, *mixed_all)
    sent = call(
        merge_kernel, "merge", [vmem] * 2, shaped((chips, GRAD_ROWS, LANES), bf16), (keep, across(give, 1))
    )
    grad_down = down_keep + across(down_give, 1).astype(f32)
    last = swap(sent)
    input_grad = call(
        rows_kernel, "rows", [smem, smem] + [vmem] * 9 + [hbm] * 3, shaped((tok_rows, width), bf16),
        (
            own_id, counts, chosen, got, both, dmiddle, dweight, total, coef, vectors, out_grad,
            w_query, w_key, w_value,
        ),
        [square] * 3 + [pltpu.SemaphoreType.DMA((3,))],
    )
    block = shaped((out_rows, width), f32)
    row = shaped((1, out_rows), f32)
    first_row = own * out_rows
    grad_up, grad_out, grad_query, grad_key, grad_value, grad_router, grad_gain_attn, grad_gain_mlp = call(
        finish_kernel, "finish", [vmem] * 6,
        (shaped((out_rows, hidden_width), f32), block, block, block, block, row, row, row),
        (last, own_gains, *(lax.dynamic_slice_in_dim(w, first_row, out_rows) for w in (w_up, w_query, w_key, w_value))),
    )
    return (
        output,
        input_grad,
        grad_router.reshape(out_rows),
        grad_gain_attn.reshape(out_rows),
        grad_query,
        grad_key,
        grad_value,
        grad_out,
        grad_gain_mlp.reshape(out_rows),
        grad_up,
        grad_down,
    )


def per_device(*arguments):
    w_up, chosen = arguments[8], arguments[13]
    devices = lax.axis_size("seq")
    width, hidden_width = w_up.shape
    paired = (
        devices == 2 * HEADS
        and chosen.shape[0] == devices * SHARE
        and width == devices * OUT_ROWS
        and width == HEADS * HEAD_DIM
        and hidden_width == devices // 2 * TILES * LANES
    )
    return (pairs if paired else general)(*arguments)


def solution(mesh):
    placed = (P("seq", None),) + (P(),) * 9 + (P("seq", None),) + (P(),) * 3
    rows = P("seq", None)
    return jax.shard_map(
        per_device,
        mesh=mesh,
        in_specs=placed,
        out_specs=(rows, rows, P("seq"), P("seq"), rows, rows, rows, rows, P("seq"), rows, rows),
        check_vma=False,
    )
```
